32 devices in a mesh: ctx: 16 (over z, y, core), fsdp: 2 (over x).
Axes of the slice: x: 2, y: 2, z: 4, core: 2. Of those that a mesh axis runs over, the one named last changes fastest.
Arguments:
- hidden: bfloat16 [2, 4096, 5376], P('fsdp', 'ctx'), may hold values from -6 to 6
- queries: bfloat16 [2, 4096, 2048], P('fsdp', 'ctx'), may hold values from -23 to 23
- key_heads: bfloat16 [2, 4096, 1024], P('fsdp', 'ctx'), may hold values from -6 to 6
- w_value: bfloat16 [5376, 1024], P('fsdp'), may hold values from -0.078125 to 0.078125
- d_out: bfloat16 [2, 4096, 2048], P('fsdp', 'ctx'), may hold values from -6 to 6
- segments: int32 [2, 4096], P('fsdp', 'ctx'), may hold values from 0 to 3, never falling along the last dimension, each value on 1 to 2048 neighbouring positions
Outputs:
- attn_out: bfloat16 [2, 4096, 2048], P('fsdp', 'ctx')
- d_queries: bfloat16 [2, 4096, 2048], P('fsdp', 'ctx')
- d_keys: bfloat16 [2, 4096, 1024], P('fsdp', 'ctx')
- d_hidden: bfloat16 [2, 4096, 5376], P('fsdp', 'ctx')
- d_w_value: float32 [5376, 1024], P(('ctx', 'fsdp'))
The draws below stay inside these ranges and needn't reach their ends.
Inputs may be any that keep to these rules, and one draw needn't show every extreme that they name: `segments`: document ids never fall along a sequence; a document holds at most half of the 4096 tokens.
All inputs are finite; a program needn't handle non-finite values.
Results may differ from the reference program's by a relative error of at most 0.024.
Values may be sent and summed in bfloat16 or wider, within the bound.
No kernel may reach another device: no remote copies, remote signals or barrier semaphores. Data moves between devices by JAX's collectives and lax.ppermute only.
A program may use at most 256 MiB of HBM per device.

```python
import math
import jax
import jax.numpy as jnp
import numpy as np
from jax import lax

D = 5376
HQ = 16
HK = 8
HD = 128
WINDOW = 1024
TOK_DEV = 256
GROUP = 2
SPAN = 4096
BATCH = 2


def drawn_pair(key):
    query_key = jax.random.fold_in(key, 101)
    keys_key = jax.random.fold_in(key, 102)
    query_draw = jnp.clip(jax.random.normal(query_key, (BATCH, SPAN, HK, GROUP, HD), jnp.float32), -6.0, 6.0)
    key_draw = jnp.clip(jax.random.normal(keys_key, (BATCH, SPAN, HK, HD), jnp.float32), -6.0, 6.0)
    return (query_draw.reshape(BATCH, SPAN, HQ * HD), key_draw.reshape(BATCH, SPAN, HK * HD))


def draw_queries(key, part):
    return drawn_pair(key)[0].astype(jnp.bfloat16)


def draw_key_heads(key, part):
    return drawn_pair(key)[1].astype(jnp.bfloat16)


def spiked(entries, rng, source, target, blocks, factor):
    owner, partner = [(jnp.arange(entries.shape[axis_at]) // (entries.shape[axis_at] // blocks)).reshape([-1 if axis == axis_at else 1 for axis in range(entries.ndim)]) for axis_at in (source, target)]
    chosen = jax.random.permutation(rng, blocks)[partner]
    strong = (owner == chosen) | (owner == (partner + blocks // 2) % blocks)
    return jnp.where(strong, factor * entries, entries)


def block_scale(rng, extent, pieces, smallest, high):
    def one(axis_at, shards_of):
        heights = jax.random.uniform(jax.random.fold_in(jax.random.fold_in(rng, 6), axis_at), (shards_of,), jnp.float32, smallest / len(pieces), high / len(pieces))
        return jnp.repeat(jnp.exp(heights), extent[axis_at] // shards_of).reshape((-1,) + (1,) * (len(extent) - axis_at - 1))

    gain = one(*pieces[0])
    for cut in pieces[1:]:
        gain = gain * one(*cut)
    return gain


def length_profile(count, total, limit, skew):
    portions = [(1 << 20) // math.isqrt(standing ** skew) + 1 for standing in range(2, count + 1)]
    rest, counts = total - limit - (count - 1), [1] * (count - 1)
    while rest > 0:
        movable = [i for i in range(count - 1) if counts[i] < limit]
        mass, left = sum([portions[i] for i in movable]), rest
        for i in movable:
            addition = min(limit - counts[i], max(1, left * portions[i] // mass), rest)
            counts[i] = counts[i] + addition
            rest = rest - addition
    return np.array([limit] + counts)


def ragged_sizes(rng, count, total, reach, skew):
    if count == 2:
        one = jax.random.randint(rng, (), max(1, total - reach), min(reach, total - 1) + 1)
        return jnp.stack([one, total - one])
    sizes = jnp.asarray(length_profile(count, total, reach, skew), jnp.int32)
    couples = (count - 1) // 2
    source_of, taker = sizes[1:1 + 2 * couples:2], sizes[2:2 + 2 * couples:2]
    room = jnp.minimum(source_of - 1, reach - taker)
    moved = jax.random.randint(jax.random.fold_in(rng, 1), (couples,), 0, 1 << 20) % (room + 1)
    sizes = sizes.at[1:1 + 2 * couples:2].set(source_of - moved).at[2:2 + 2 * couples:2].set(taker + moved)
    return sizes[jax.random.permutation(jax.random.fold_in(rng, 2), count)]


def centred(rng, dims, width, most, split=(), kind=jnp.bfloat16):
    entries = width * jax.random.normal(rng, dims, jnp.float32)
    if split:
        entries = entries * block_scale(rng, dims, split, -0.22, 0.18)
    return jnp.clip(entries, -most, most).astype(kind)


def heavy_noise(own_key, dims, scale, reach, cuts, heavy, kind=jnp.bfloat16):
    drawn = scale * jax.random.normal(own_key, dims, jnp.float32)
    if cuts:
        drawn = drawn * block_scale(own_key, dims, cuts, -0.22, 0.18)
    return jnp.clip(spiked(drawn, jax.random.fold_in(own_key, 3), *heavy), -reach, reach).astype(kind)


def setup_inputs(seed: int = 0) -> dict:
    streams_of = jax.random.split(jax.random.key(seed), 7)
    hidden = heavy_noise(streams_of[0], (BATCH, SPAN, D), 1.0, 6.0, ((0, 2), (1, 16)), (1, 2, 16, 2.0))
    queries = draw_queries(jax.random.fold_in(streams_of[6], 71), 0)
    key_heads = draw_key_heads(jax.random.fold_in(streams_of[6], 71), 0)
    w_value = centred(streams_of[3], (D, HK * HD), D ** -0.5, 0.078125, ((0, 2),))
    d_out = centred(streams_of[4], (BATCH, SPAN, HQ * HD), 1.0, 6.0, ((0, 2), (1, 16)))
    segments = jax.vmap(lambda own: jnp.searchsorted(jnp.cumsum(ragged_sizes(own, 4, SPAN, SPAN // 2, 1)), jnp.arange(SPAN), side="right"))(jax.random.split(streams_of[5], BATCH)).reshape((BATCH, SPAN)).astype(jnp.int32)
    return dict(hidden=hidden, queries=queries, key_heads=key_heads, w_value=w_value, d_out=d_out, segments=segments)


score_scale = 1.0 / math.sqrt(168.0)

def one_sequence(tokens_in, query_all, key_all, w_value, grad_all, segment_ids):
    values = jnp.dot(tokens_in, w_value, preferred_element_type=jnp.float32).astype(jnp.bfloat16)
    kv_width = HK * HD
    span_rows = WINDOW + TOK_DEV
    pad_keys = jnp.concatenate([jnp.zeros((WINDOW, kv_width), key_all.dtype), key_all], 0)
    pad_values = jnp.concatenate([jnp.zeros((WINDOW, kv_width), values.dtype), values], 0)
    pad_segments = jnp.concatenate([jnp.full((WINDOW,), -1, jnp.int32), segment_ids.astype(jnp.int32)], 0)

    def block_step(carry, block_index):
        key_acc, value_acc = carry
        first_row = (block_index * TOK_DEV).astype(jnp.int32)
        query_rows = lax.dynamic_slice_in_dim(query_all, first_row, TOK_DEV, 0).reshape(TOK_DEV, HK, GROUP, HD).astype(jnp.float32)
        grad_heads = lax.dynamic_slice_in_dim(grad_all, first_row, TOK_DEV, 0).reshape(TOK_DEV, HK, GROUP, HD).astype(jnp.float32)
        window_keys = lax.dynamic_slice_in_dim(pad_keys, first_row, span_rows, 0).reshape(span_rows, HK, HD).astype(jnp.float32)
        window_values = lax.dynamic_slice_in_dim(pad_values, first_row, span_rows, 0).reshape(span_rows, HK, HD).astype(jnp.float32)
        window_tags = lax.dynamic_slice_in_dim(pad_segments, first_row, span_rows, 0)
        query_tags = lax.dynamic_slice_in_dim(segment_ids.astype(jnp.int32), first_row, TOK_DEV, 0)
        query_pos = first_row + jnp.arange(TOK_DEV, dtype=jnp.int32)
        key_pos = first_row - WINDOW + jnp.arange(span_rows, dtype=jnp.int32)
        distance = query_pos[:, None] - key_pos[None, :]
        allowed = (query_tags[:, None] == window_tags[None, :]) & (distance >= 0) & (distance < WINDOW) & (key_pos[None, :] >= 0)
        scores = jnp.einsum('tgrd,lgd->grtl', query_rows, window_keys) * score_scale
        scores = jnp.where(allowed, scores, -jnp.inf)
        highest = lax.optimization_barrier(jnp.max(scores, axis=-1, keepdims=True))
        raw_weights = jnp.exp(scores - highest)
        probs = raw_weights / lax.optimization_barrier(jnp.sum(raw_weights, axis=-1, keepdims=True))
        probs_low = probs.astype(jnp.bfloat16).astype(jnp.float32)
        out_heads = jnp.einsum('grtl,lgd->tgrd', probs_low, window_values).astype(jnp.bfloat16)
        grad_probs = jnp.einsum('tgrd,lgd->grtl', grad_heads, window_values)
        delta_sum = lax.optimization_barrier(jnp.sum(grad_heads * out_heads.astype(jnp.float32), axis=-1))
        delta_sum = jnp.transpose(delta_sum, (1, 2, 0))[..., None]
        grad_scores = (probs * (grad_probs - delta_sum)).astype(jnp.bfloat16).astype(jnp.float32)
        d_query_heads = (score_scale * jnp.einsum('grtl,lgd->tgrd', grad_scores, window_keys)).astype(jnp.bfloat16)
        key_terms = (score_scale * jnp.einsum('grtl,tgrd->lgd', grad_scores, query_rows)).astype(jnp.bfloat16)
        value_terms = jnp.einsum('grtl,tgrd->lgd', probs_low, grad_heads).astype(jnp.bfloat16)
        key_slice = lax.dynamic_slice_in_dim(key_acc, first_row, span_rows, 0) + key_terms.reshape(span_rows, kv_width).astype(jnp.float32)
        value_slice = lax.dynamic_slice_in_dim(value_acc, first_row, span_rows, 0) + value_terms.reshape(span_rows, kv_width).astype(jnp.float32)
        key_acc = lax.dynamic_update_slice_in_dim(key_acc, key_slice, first_row, 0)
        value_acc = lax.dynamic_update_slice_in_dim(value_acc, value_slice, first_row, 0)
        return ((key_acc, value_acc), (out_heads.reshape(TOK_DEV, HQ * HD), d_query_heads.reshape(TOK_DEV, HQ * HD)))
    start_acc = jnp.zeros((SPAN + WINDOW, kv_width), jnp.float32)
    (key_acc, value_acc), (out_blocks, query_blocks) = lax.scan(block_step, (start_acc, start_acc), jnp.arange(SPAN // TOK_DEV, dtype=jnp.int32))
    d_key_rows = key_acc[WINDOW:].astype(jnp.bfloat16)
    d_values = value_acc[WINDOW:]
    d_values_low = d_values.astype(jnp.bfloat16)
    d_tokens = lax.dot_general(d_values_low, w_value, (((1,), (1,)), ((), ())), preferred_element_type=jnp.float32).astype(jnp.bfloat16)
    weight_term = lax.dot_general(tokens_in, d_values_low, (((0,), (0,)), ((), ())), preferred_element_type=jnp.float32)
    return (out_blocks.reshape(SPAN, HQ * HD), query_blocks.reshape(SPAN, HQ * HD), d_key_rows, d_tokens, weight_term)

def reference(hidden, queries, key_heads, w_value, d_out, segments):

    def batch_step(weight_acc, members):
        tokens_in, query_all, key_all, grad_all, segment_ids = members
        out_rows, query_grads, key_grads, token_grads, weight_term = one_sequence(tokens_in, query_all, key_all, w_value, grad_all, segment_ids)
        return (weight_acc + weight_term, (out_rows, query_grads, key_grads, token_grads))
    weight_start = jnp.zeros((D, HK * HD), jnp.float32)
    d_w_value, (attn_out, d_queries, d_keys, d_hidden) = lax.scan(batch_step, weight_start, (hidden, queries, key_heads, d_out, segments))
    return (attn_out, d_queries, d_keys, d_hidden, d_w_value)
```

```python
import functools
import math

import jax
import jax.numpy as jnp
from jax import lax
from jax.experimental import pallas as pl
from jax.experimental.pallas import tpu as pltpu
from jax.sharding import PartitionSpec as P

HQ = 16
HK = 8
HD = 128
WINDOW = 1024
GROUP = 2
NEG = -1e30

score_scale = 1.0 / math.sqrt(168.0)
exp2_scale = score_scale / math.log(2.0)

BF16 = jnp.bfloat16
F32 = jnp.float32
NT = (((1,), (1,)), ((), ()))
TN = (((0,), (0,)), ((), ()))


def dot(a, b, dims=(((1,), (0,)), ((), ()))):
    return lax.dot_general(a, b, dims, preferred_element_type=F32)


def stacked(ref, rows):
    return jnp.concatenate([ref[rows, r * HD : (r + 1) * HD] for r in range(GROUP)], 0)


def probs_kernel(blk, n_back, low_ref, q_ref, do_ref, *refs):
    n_arr = n_back + 1
    k_refs = refs[:n_arr]
    e_ref, inv_ref, dot_ref = refs[n_arr : n_arr + 3]
    dv_refs = refs[n_arr + 3 : 2 * n_arr + 3]
    bias, s_scr, dv_acc = refs[2 * n_arr + 3 :]
    span_blocks = WINDOW // blk + 1

    @pl.when(pl.program_id(0) == 0)
    def _():
        for qb in range(2):
            kpos = lax.broadcasted_iota(jnp.int32, (span_blocks * blk, blk), 0) + qb * blk
            qpos = lax.broadcasted_iota(jnp.int32, (span_blocks * blk, blk), 1) + (qb * blk + WINDOW)
            low = low_ref[:, qb * blk : (qb + 1) * blk]
            ok = (kpos >= low) & (kpos <= qpos)
            bias[qb] = jnp.where(ok, 0.0, NEG)

    def key_block(j):
        return k_refs[j // 2][(j % 2) * blk : (j % 2 + 1) * blk, :]

    for qb in range(2):
        rows = slice(qb * blk, (qb + 1) * blk)
        qs = stacked(q_ref, rows)
        top = None
        for j in range(span_blocks):
            s = dot(key_block(qb + j), qs, NT)
            b = bias[qb, j * blk : (j + 1) * blk, :]
            s = s * exp2_scale + jnp.concatenate([b] * GROUP, 1)
            s_scr[j] = s
            part = jnp.max(s.reshape(blk // 8, 8, GROUP * blk), axis=0)
            top = part if top is None else jnp.maximum(top, part)
        top = jnp.max(top, axis=0, keepdims=True)
        total = None
        for j in range(span_blocks):
            e = jnp.exp2(s_scr[j] - top)
            part = jnp.sum(e.reshape(blk // 8, 8, GROUP * blk), axis=0)
            total = part if total is None else total + part
            e_ref[0, qb, j * blk : (j + 1) * blk, :] = e.astype(BF16)
        inv = 1.0 / jnp.sum(total, axis=0, keepdims=True)
        inv_ref[0, qb] = inv
        do_t = (stacked(do_ref, rows).astype(F32).T * inv).astype(BF16)
        dot_ref[0, qb] = do_t
        for j in range(span_blocks):
            term = dot(e_ref[0, qb, j * blk : (j + 1) * blk, :], do_t, NT)
            at = slice((qb + j) * blk, (qb + j + 1) * blk)
            if qb == 0 or j == span_blocks - 1:
                dv_acc[at, :] = term
            else:
                dv_acc[at, :] += term
    for a in range(n_arr):
        dv_refs[a][...] = dv_acc[a * 2 * blk : (a + 1) * 2 * blk, :].astype(BF16)


def grads_kernel(blk, n_back, e_ref, inv_ref, dot_ref, q_ref, *refs):
    n_arr = n_back + 1
    k_refs = refs[:n_arr]
    v_refs = refs[n_arr : 2 * n_arr]
    out_ref, dq_ref = refs[2 * n_arr : 2 * n_arr + 2]
    dk_refs = refs[2 * n_arr + 2 : 3 * n_arr + 2]
    (dk_acc,) = refs[3 * n_arr + 2 :]
    span_blocks = WINDOW // blk + 1

    def block_of(arrays, j):
        return arrays[j // 2][(j % 2) * blk : (j % 2 + 1) * blk, :]

    for qb in range(2):
        rows = slice(qb * blk, (qb + 1) * blk)
        qs = stacked(q_ref, rows)
        do_t = dot_ref[0, qb]
        out_t = None
        for j in range(span_blocks):
            e = e_ref[0, qb, j * blk : (j + 1) * blk, :]
            part = dot(block_of(v_refs, qb + j), e, TN)
            out_t = part if out_t is None else out_t + part
        out_t = (out_t * inv_ref[0, qb]).astype(BF16).astype(F32)
        delta = jnp.sum(out_t * do_t.astype(F32), axis=0, keepdims=True)
        out = out_t.T.astype(BF16)
        dq_t = None
        for j in range(span_blocks):
            e = e_ref[0, qb, j * blk : (j + 1) * blk, :].astype(F32)
            dp = dot(block_of(v_refs, qb + j), do_t)
            ds = (e * (dp - delta)).astype(BF16)
            term = dot(ds, qs)
            at = slice((qb + j) * blk, (qb + j + 1) * blk)
            if qb == 0 or j == span_blocks - 1:
                dk_acc[at, :] = term
            else:
                dk_acc[at, :] += term
            part = dot(block_of(k_refs, qb + j), ds, TN)
            dq_t = part if dq_t is None else dq_t + part
        dq = (dq_t * score_scale).T.astype(BF16)
        for r in range(GROUP):
            out_ref[rows, r * HD : (r + 1) * HD] = out[r * blk : (r + 1) * blk, :]
            dq_ref[rows, r * HD : (r + 1) * HD] = dq[r * blk : (r + 1) * blk, :]
    for a in range(n_arr):
        dk_refs[a][...] = (dk_acc[a * 2 * blk : (a + 1) * 2 * blk, :] * score_scale).astype(BF16)


def run_probs(low, q, do, keys):
    rows, width = keys[0].shape
    blk = rows // 2
    heads = width // HD
    n_arr = len(keys)
    span = WINDOW + blk
    lanes = GROUP * blk
    head_block = pl.BlockSpec((rows, HD), lambda g: (0, g))
    group_block = pl.BlockSpec((rows, GROUP * HD), lambda g: (0, g))
    return pl.pallas_call(
        functools.partial(probs_kernel, blk, n_arr - 1),
        grid=(heads,),
        in_specs=[pl.BlockSpec((1, rows), lambda g: (0, 0)), group_block, group_block] + [head_block] * n_arr,
        out_specs=[
            pl.BlockSpec((1, 2, span, lanes), lambda g: (g, 0, 0, 0)),
            pl.BlockSpec((1, 2, 1, lanes), lambda g: (g, 0, 0, 0)),
            pl.BlockSpec((1, 2, HD, lanes), lambda g: (g, 0, 0, 0)),
        ]
        + [head_block] * n_arr,
        out_shape=[
            jax.ShapeDtypeStruct((heads, 2, span, lanes), BF16),
            jax.ShapeDtypeStruct((heads, 2, 1, lanes), F32),
            jax.ShapeDtypeStruct((heads, 2, HD, lanes), BF16),
        ]
        + [jax.ShapeDtypeStruct((rows, width), BF16)] * n_arr,
        scratch_shapes=[
            pltpu.VMEM((2, span, blk), F32),
            pltpu.VMEM((span // blk, blk, lanes), F32),
            pltpu.VMEM((WINDOW + rows, HD), F32),
        ],
        compiler_params=pltpu.CompilerParams(vmem_limit_bytes=40 * 1024 * 1024),
        cost_estimate=pl.CostEstimate(
            flops=heads * 2 * span * lanes * HD * 2 * 2 * 6,
            bytes_accessed=heads * 2 * span * lanes * 2,
            transcendentals=0,
        ),
        name="probs",
    )(low, q, do, *keys)


def run_grads(e, inv, do_t, q, keys, values):
    rows, width = keys[0].shape
    blk = rows // 2
    heads = width // HD
    n_arr = len(keys)
    span = WINDOW + blk
    lanes = GROUP * blk
    head_block = pl.BlockSpec((rows, HD), lambda g: (0, g))
    group_block = pl.BlockSpec((rows, GROUP * HD), lambda g: (0, g))
    return pl.pallas_call(
        functools.partial(grads_kernel, blk, n_arr - 1),
        grid=(heads,),
        in_specs=[
            pl.BlockSpec((1, 2, span, lanes), lambda g: (g, 0, 0, 0)),
            pl.BlockSpec((1, 2, 1, lanes), lambda g: (g, 0, 0, 0)),
            pl.BlockSpec((1, 2, HD, lanes), lambda g: (g, 0, 0, 0)),
            group_block,
        ]
        + [head_block] * (2 * n_arr),
        out_specs=[group_block, group_block] + [head_block] * n_arr,
        out_shape=[jax.ShapeDtypeStruct((rows, GROUP * width), BF16)] * 2
        + [jax.ShapeDtypeStruct((rows, width), BF16)] * n_arr,
        scratch_shapes=[pltpu.VMEM((WINDOW + rows, HD), F32)],
        compiler_params=pltpu.CompilerParams(vmem_limit_bytes=40 * 1024 * 1024),
        cost_estimate=pl.CostEstimate(
            flops=heads * 2 * span * lanes * HD * 2 * 4 * 4,
            bytes_accessed=heads * 2 * span * lanes * 2,
            transcendentals=0,
        ),
        name="grads",
    )(e, inv, do_t, q, *keys, *values)


def shifted(x, axis, by):
    length = lax.axis_size(axis)
    return lax.ppermute(x, axis, [(i, i + by) for i in range(length) if 0 <= i + by < length])


def swapped(x):
    return lax.ppermute(x, "ctx", [(i, i ^ 1) for i in range(lax.axis_size("ctx"))])


def rotated(x, axis, by):
    length = lax.axis_size(axis)
    return lax.ppermute(x, axis, [(i, (i + by) % length) for i in range(length)])


def cols(x, at, width):
    return lax.dynamic_slice_in_dim(x, at * width, width, x.ndim - 1)


def pair(core, own, other, axis):
    return jnp.where(core == 0, jnp.concatenate([own, other], axis), jnp.concatenate([other, own], axis))


def to_heads(core, x):
    half = x.shape[1] // 2
    return pair(core, cols(x, core, half), swapped(cols(x, 1 - core, half)), 0)


def to_tokens(core, x):
    half = x.shape[0] // 2
    own = lax.dynamic_slice_in_dim(x, core * half, half, 0)
    other = swapped(lax.dynamic_slice_in_dim(x, (1 - core) * half, half, 0))
    return pair(core, own, other, 1)


def shards(hidden, queries, key_heads, w_value, d_out, segments):
    shard_rows = hidden.shape[1]
    model = hidden.shape[2]
    kv_width = w_value.shape[1]
    n_ctx = lax.axis_size("ctx")
    n_fsdp = lax.axis_size("fsdp")
    chip_rows = 2 * shard_rows
    n_back = WINDOW // chip_rows
    my_ctx = lax.axis_index("ctx")
    my_fsdp = lax.axis_index("fsdp")
    core = my_ctx % 2
    chip = my_ctx // 2
    half_kv = kv_width // 2
    slab = model // n_fsdp
    tokens = hidden[0]

    k_own = to_heads(core, key_heads[0])
    keys = [shifted(k_own, "ctx", 2 * d) for d in range(n_back, 0, -1)] + [k_own]
    q_chip = to_heads(core, queries[0])
    do_chip = to_heads(core, d_out[0])

    slabs = [cols(tokens, my_fsdp, slab)]
    for s in range(1, n_fsdp):
        slabs.append(rotated(cols(tokens, (my_fsdp + s) % n_fsdp, slab), "fsdp", s))
    value_sum = dot(slabs[0], w_value)
    for s in range(1, n_fsdp):
        back = rotated(dot(slabs[s], w_value).astype(BF16), "fsdp", -s)
        value_sum = value_sum + back.astype(F32)
    v_own = to_heads(core, value_sum.astype(BF16))
    vals = [shifted(v_own, "ctx", 2 * d) for d in range(n_back, 0, -1)] + [v_own]

    tags = lax.all_gather(segments[0], "ctx", axis=0, tiled=True)
    chip_tags = lax.dynamic_slice_in_dim(tags, chip * chip_rows, chip_rows, 0)
    doc_start = jnp.sum((tags[None, :] < chip_tags[:, None]).astype(jnp.int32), axis=1)
    first = chip * chip_rows
    q_pos = first + jnp.arange(chip_rows, dtype=jnp.int32)
    low = (jnp.maximum(doc_start, q_pos - (WINDOW - 1)) - (first - WINDOW))[None, :]

    e, inv, do_t, *dv_terms = run_probs(low, q_chip, do_chip, keys)
    dv_total = dv_terms[n_back].astype(F32)
    for d in range(1, n_back + 1):
        dv_total = dv_total + shifted(dv_terms[n_back - d], "ctx", -2 * d).astype(F32)
    dv_chip = dv_total.astype(BF16)

    part = half_kv // n_fsdp
    weight_term = None
    for s in range(n_fsdp):
        if s == 0:
            x_tokens = tokens
            dv_part = cols(dv_chip, my_fsdp, part)
        else:
            x_tokens = rotated(tokens, "fsdp", s)
            dv_part = rotated(cols(dv_chip, (my_fsdp + s) % n_fsdp, part), "fsdp", s)
        x_chip = pair(core, x_tokens, swapped(x_tokens), 0)
        term = dot(x_chip, dv_part, TN)
        weight_term = term if weight_term is None else weight_term + term
    groups = [list(range(c, n_ctx, 2)) for c in range(2)]
    rows_chip = lax.psum_scatter(
        weight_term.astype(BF16), "ctx", scatter_dimension=0, axis_index_groups=groups, tiled=True
    )
    rows_out = rows_chip.shape[0] // (2 * n_fsdp)
    blocks = rows_chip.reshape(2, n_fsdp * rows_out, part)
    own = lax.dynamic_index_in_dim(blocks, core, 0, keepdims=False)
    other = swapped(lax.dynamic_index_in_dim(blocks, 1 - core, 0, keepdims=False))
    both = pair(core, own[None], other[None], 0).reshape(2, n_fsdp, rows_out, part)
    gathered = jnp.zeros((n_fsdp, 2, rows_out, part), BF16)
    for s in range(n_fsdp):
        piece = lax.dynamic_index_in_dim(both, (my_fsdp + s) % n_fsdp, 1, keepdims=False)
        if s:
            piece = rotated(piece, "fsdp", s)
        gathered = lax.dynamic_update_index_in_dim(gathered, piece, (my_fsdp - s) % n_fsdp, 0)
    d_weight = jnp.transpose(gathered, (2, 1, 0, 3)).reshape(rows_out, kv_width).astype(F32)

    dv_low = to_tokens(core, dv_chip)
    d_tokens = jnp.zeros((shard_rows, model), BF16)
    for s in range(n_fsdp):
        dv_of = dv_low if s == 0 else rotated(dv_low, "fsdp", s)
        made = dot(dv_of, w_value, NT).astype(BF16)
        if s:
            made = rotated(made, "fsdp", -s)
        d_tokens = lax.dynamic_update_slice_in_dim(d_tokens, made, ((my_fsdp + s) % n_fsdp) * slab, 1)

    out_chip, dq_chip, *dk_terms = run_grads(e, inv, do_t, q_chip, keys, vals)
    dk_total = dk_terms[n_back].astype(F32)
    for d in range(1, n_back + 1):
        dk_total = dk_total + shifted(dk_terms[n_back - d], "ctx", -2 * d).astype(F32)
    return (
        to_tokens(core, out_chip)[None],
        to_tokens(core, dq_chip)[None],
        to_tokens(core, dk_total.astype(BF16))[None],
        d_tokens[None],
        d_weight,
    )


def solution(mesh):
    in_specs = (
        P("fsdp", "ctx", None),
        P("fsdp", "ctx", None),
        P("fsdp", "ctx", None),
        P("fsdp", None),
        P("fsdp", "ctx", None),
        P("fsdp", "ctx"),
    )
    out_specs = (
        P("fsdp", "ctx", None),
        P("fsdp", "ctx", None),
        P("fsdp", "ctx", None),
        P("fsdp", "ctx", None),
        P(("ctx", "fsdp"), None),
    )
    return jax.shard_map(shards, mesh=mesh, in_specs=in_specs, out_specs=out_specs, check_vma=False)
```

```python
import functools
import math

import jax
import jax.numpy as jnp
from jax import lax
from jax.experimental import pallas as pl
from jax.experimental.pallas import tpu as pltpu
from jax.sharding import PartitionSpec as P

HQ = 16
HK = 8
HD = 128
WINDOW = 1024
GROUP = 2
NEG = -1e30

score_scale = 1.0 / math.sqrt(168.0)
exp2_scale = score_scale / math.log(2.0)

BF16 = jnp.bfloat16
F32 = jnp.float32
NT = (((1,), (1,)), ((), ()))
TN = (((0,), (0,)), ((), ()))


def dot(a, b, dims=(((1,), (0,)), ((), ()))):
    return lax.dot_general(a, b, dims, preferred_element_type=F32)


def probs_kernel(blk, n_back, core_ref, low_ref, q_own, q_other, do_own, do_other, *refs):
    n_arr = n_back + 1
    k_refs = refs[:n_arr]
    e_ref, inv_ref, dot_ref = refs[n_arr : n_arr + 3]
    dv_refs = refs[n_arr + 3 : 2 * n_arr + 3]
    bias, s_scr, dv_acc, q_buf, do_buf = refs[2 * n_arr + 3 :]
    span_blocks = WINDOW // blk + 1
    core = core_ref[0]

    @pl.when(pl.program_id(0) == 0)
    def _():
        for qb in range(2):
            kpos = lax.broadcasted_iota(jnp.int32, (span_blocks * blk, blk), 0) + qb * blk
            qpos = lax.broadcasted_iota(jnp.int32, (span_blocks * blk, blk), 1) + (qb * blk + WINDOW)
            low = low_ref[:, qb * blk : (qb + 1) * blk]
            ok = (kpos >= low) & (kpos <= qpos)
            bias[qb] = jnp.where(ok, 0.0, NEG)

    q_buf[core] = q_own[...]
    q_buf[1 - core] = q_other[...]
    do_buf[core] = do_own[...]
    do_buf[1 - core] = do_other[...]

    def key_block(j):
        return k_refs[j // 2][(j % 2) * blk : (j % 2 + 1) * blk, :]

    def stacked(buf, qb):
        return jnp.concatenate([buf[qb, :, r * HD : (r + 1) * HD] for r in range(GROUP)], 0)

    for qb in range(2):
        qs = stacked(q_buf, qb)
        top = None
        for j in range(span_blocks):
            s = dot(key_block(qb + j), qs, NT)
            b = bias[qb, j * blk : (j + 1) * blk, :]
            s = s * exp2_scale + jnp.concatenate([b] * GROUP, 1)
            s_scr[j] = s
            part = jnp.max(s.reshape(blk // 8, 8, GROUP * blk), axis=0)
            top = part if top is None else jnp.maximum(top, part)
        top = jnp.max(top, axis=0, keepdims=True)
        total = None
        for j in range(span_blocks):
            e = jnp.exp2(s_scr[j] - top)
            part = jnp.sum(e.reshape(blk // 8, 8, GROUP * blk), axis=0)
            total = part if total is None else total + part
            e_ref[0, qb, j * blk : (j + 1) * blk, :] = e.astype(BF16)
        inv = 1.0 / jnp.sum(total, axis=0, keepdims=True)
        inv_ref[0, qb] = inv
        do_t = (stacked(do_buf, qb).astype(F32).T * inv).astype(BF16)
        dot_ref[0, qb] = do_t
        for j in range(span_blocks):
            term = dot(e_ref[0, qb, j * blk : (j + 1) * blk, :], do_t, NT)
            at = slice((qb + j) * blk, (qb + j + 1) * blk)
            if qb == 0 or j == span_blocks - 1:
                dv_acc[at, :] = term
            else:
                dv_acc[at, :] += term
    for a in range(n_arr):
        dv_refs[a][...] = dv_acc[a * 2 * blk : (a + 1) * 2 * blk, :].astype(BF16)


def grads_kernel(blk, n_back, core_ref, e_ref, inv_ref, dot_ref, q_own, q_other, *refs):
    n_arr = n_back + 1
    k_refs = refs[:n_arr]
    v_refs = refs[n_arr : 2 * n_arr]
    out_ref, dq_ref, other_ref = refs[2 * n_arr : 2 * n_arr + 3]
    dk_refs = refs[2 * n_arr + 3 : 3 * n_arr + 3]
    dk_acc, q_buf, out_buf, dq_buf = refs[3 * n_arr + 3 :]
    span_blocks = WINDOW // blk + 1
    core = core_ref[0]

    q_buf[core] = q_own[...]
    q_buf[1 - core] = q_other[...]

    def block_of(arrays, j):
        return arrays[j // 2][(j % 2) * blk : (j % 2 + 1) * blk, :]

    for qb in range(2):
        qs = jnp.concatenate([q_buf[qb, :, r * HD : (r + 1) * HD] for r in range(GROUP)], 0)
        do_t = dot_ref[0, qb]
        out_t = None
        for j in range(span_blocks):
            e = e_ref[0, qb, j * blk : (j + 1) * blk, :]
            part = dot(block_of(v_refs, qb + j), e, TN)
            out_t = part if out_t is None else out_t + part
        out_t = (out_t * inv_ref[0, qb]).astype(BF16).astype(F32)
        delta = jnp.sum(out_t * do_t.astype(F32), axis=0, keepdims=True)
        out = out_t.T.astype(BF16)
        dq_t = None
        for j in range(span_blocks):
            e = e_ref[0, qb, j * blk : (j + 1) * blk, :].astype(F32)
            dp = dot(block_of(v_refs, qb + j), do_t)
            ds = (e * (dp - delta)).astype(BF16)
            term = dot(ds, qs)
            at = slice((qb + j) * blk, (qb + j + 1) * blk)
            if qb == 0 or j == span_blocks - 1:
                dk_acc[at, :] = term
            else:
                dk_acc[at, :] += term
            part = dot(block_of(k_refs, qb + j), ds, TN)
            dq_t = part if dq_t is None else dq_t + part
        dq = (dq_t * score_scale).T.astype(BF16)
        for r in range(GROUP):
            out_buf[qb, :, r * HD : (r + 1) * HD] = out[r * blk : (r + 1) * blk, :]
            dq_buf[qb, :, r * HD : (r + 1) * HD] = dq[r * blk : (r + 1) * blk, :]
    out_ref[...] = out_buf[core]
    dq_ref[...] = dq_buf[core]
    other_ref[0] = out_buf[1 - core]
    other_ref[1] = dq_buf[1 - core]
    for a in range(n_arr):
        dk_refs[a][...] = (dk_acc[a * 2 * blk : (a + 1) * 2 * blk, :] * score_scale).astype(BF16)


def specs_of(rows, width):
    blk = rows // 2
    heads = width // HD
    span = WINDOW + blk
    lanes = GROUP * blk
    head = pl.BlockSpec((rows, HD), lambda g, c: (0, g))
    own = pl.BlockSpec((blk, GROUP * HD), lambda g, c: (0, c[0] * heads + g))
    return blk, heads, span, lanes, head, own


def run_probs(core, low, q, q_other, do, keys, rows, width):
    blk, heads, span, lanes, head, own = specs_of(rows, width)
    n_arr = len(keys)
    return pl.pallas_call(
        functools.partial(probs_kernel, blk, n_arr - 1),
        grid_spec=pltpu.PrefetchScalarGridSpec(
            num_scalar_prefetch=1,
            grid=(heads,),
            in_specs=[
                pl.BlockSpec((1, rows), lambda g, c: (0, 0)),
                own,
                pl.BlockSpec((blk, GROUP * HD), lambda g, c: (0, g)),
                own,
                pl.BlockSpec((blk, GROUP * HD), lambda g, c: (0, heads + g)),
            ]
            + [head] * n_arr,
            out_specs=[
                pl.BlockSpec((1, 2, span, lanes), lambda g, c: (g, 0, 0, 0)),
                pl.BlockSpec((1, 2, 1, lanes), lambda g, c: (g, 0, 0, 0)),
                pl.BlockSpec((1, 2, HD, lanes), lambda g, c: (g, 0, 0, 0)),
            ]
            + [head] * n_arr,
            scratch_shapes=[
                pltpu.VMEM((2, span, blk), F32),
                pltpu.VMEM((span // blk, blk, lanes), F32),
                pltpu.VMEM((WINDOW + rows, HD), F32),
                pltpu.VMEM((2, blk, GROUP * HD), BF16),
                pltpu.VMEM((2, blk, GROUP * HD), BF16),
            ],
        ),
        out_shape=[
            jax.ShapeDtypeStruct((heads, 2, span, lanes), BF16),
            jax.ShapeDtypeStruct((heads, 2, 1, lanes), F32),
            jax.ShapeDtypeStruct((heads, 2, HD, lanes), BF16),
        ]
        + [jax.ShapeDtypeStruct((rows, width), BF16)] * n_arr,
        compiler_params=pltpu.CompilerParams(vmem_limit_bytes=40 * 1024 * 1024),
        cost_estimate=pl.CostEstimate(
            flops=heads * 2 * span * lanes * HD * 2 * 2 * 6,
            bytes_accessed=heads * 2 * span * lanes * 2,
            transcendentals=0,
        ),
        name="probs",
    )(core, low, q, q_other, do, q_other, *keys)


def run_grads(core, e, inv, do_t, q, q_other, keys, values, rows, width):
    blk, heads, span, lanes, head, own = specs_of(rows, width)
    n_arr = len(keys)
    full = jax.ShapeDtypeStruct(q.shape, BF16)
    return pl.pallas_call(
        functools.partial(grads_kernel, blk, n_arr - 1),
        grid_spec=pltpu.PrefetchScalarGridSpec(
            num_scalar_prefetch=1,
            grid=(heads,),
            in_specs=[
                pl.BlockSpec((1, 2, span, lanes), lambda g, c: (g, 0, 0, 0)),
                pl.BlockSpec((1, 2, 1, lanes), lambda g, c: (g, 0, 0, 0)),
                pl.BlockSpec((1, 2, HD, lanes), lambda g, c: (g, 0, 0, 0)),
                own,
                pl.BlockSpec((blk, GROUP * HD), lambda g, c: (0, g)),
            ]
            + [head] * (2 * n_arr),
            out_specs=[own, own, pl.BlockSpec((2, blk, GROUP * HD), lambda g, c: (0, 0, g))] + [head] * n_arr,
            scratch_shapes=[
                pltpu.VMEM((WINDOW + rows, HD), F32),
                pltpu.VMEM((2, blk, GROUP * HD), BF16),
                pltpu.VMEM((2, blk, GROUP * HD), BF16),
                pltpu.VMEM((2, blk, GROUP * HD), BF16),
            ],
        ),
        out_shape=[full, full, jax.ShapeDtypeStruct((2, blk, GROUP * width), BF16)]
        + [jax.ShapeDtypeStruct((rows, width), BF16)] * n_arr,
        compiler_params=pltpu.CompilerParams(vmem_limit_bytes=40 * 1024 * 1024),
        cost_estimate=pl.CostEstimate(
            flops=heads * 2 * span * lanes * HD * 2 * 4 * 4,
            bytes_accessed=heads * 2 * span * lanes * 2,
            transcendentals=0,
        ),
        name="grads",
    )(core, e, inv, do_t, q, q_other, *keys, *values)


def shifted(x, by):
    length = lax.axis_size("ctx")
    return lax.ppermute(x, "ctx", [(i, i + by) for i in range(length) if 0 <= i + by < length])


def swapped(x):
    return lax.ppermute(x, "ctx", [(i, i ^ 1) for i in range(lax.axis_size("ctx"))])


def rotated(x, by):
    length = lax.axis_size("fsdp")
    return lax.ppermute(x, "fsdp", [(i, (i + by) % length) for i in range(length)])


def moved(x, flip, by):
    n_ctx, n_fsdp = lax.axis_size("ctx"), lax.axis_size("fsdp")
    pairs = [
        (c * n_fsdp + f, (c ^ (2 * flip)) * n_fsdp + (f + by) % n_fsdp)
        for c in range(n_ctx)
        for f in range(n_fsdp)
    ]
    return lax.ppermute(x, ("ctx", "fsdp"), pairs)


def cols(x, at, width):
    return lax.dynamic_slice_in_dim(x, at * width, width, x.ndim - 1)


def rows_of(x, at, count):
    return lax.dynamic_slice_in_dim(x, at * count, count, 0)


def placed(core, own, other, axis):
    both = jnp.concatenate([own, own], axis)
    return lax.dynamic_update_slice_in_dim(both, other, (1 - core) * own.shape[axis], axis)


def shards(hidden, queries, key_heads, w_value, d_out, segments):
    shard_rows = hidden.shape[1]
    model = hidden.shape[2]
    kv_width = w_value.shape[1]
    n_ctx = lax.axis_size("ctx")
    n_fsdp = lax.axis_size("fsdp")
    chip_rows = 2 * shard_rows
    n_back = WINDOW // chip_rows
    n_z = n_ctx // 4
    my_ctx = lax.axis_index("ctx")
    my_fsdp = lax.axis_index("fsdp")
    core = my_ctx % 2
    core_arg = core.astype(jnp.int32).reshape(1)
    chip = my_ctx // 2
    my_y = chip % 2
    my_z = chip // 2
    half_kv = kv_width // 2
    slab = model // n_fsdp
    tokens = hidden[0]
    first = chip * chip_rows

    sent = [rotated(cols(tokens, (my_fsdp + s) % n_fsdp, slab), s) for s in range(1, n_fsdp)]

    own_tags = segments[0].astype(BF16)
    tag_row = lax.dynamic_update_slice_in_dim(jnp.zeros((half_kv,), BF16), own_tags, core * shard_rows, 0)
    tag_rows = jnp.concatenate([tag_row[None], jnp.zeros((15, half_kv), BF16)], 0)
    got = swapped(jnp.concatenate([cols(key_heads[0], 1 - core, half_kv), tag_rows], 0))
    k_own = jnp.concatenate(
        [
            placed(core, cols(key_heads[0], core, half_kv), got[:shard_rows], 0),
            tag_rows + got[shard_rows:],
        ],
        0,
    )
    keys = [shifted(k_own, 2 * d) for d in range(n_back, 0, -1)] + [k_own]
    half_q = queries.shape[2] // 2
    q_other = swapped(jnp.concatenate([cols(queries[0], 1 - core, half_q), cols(d_out[0], 1 - core, half_q)], 1))

    out_rows = model // (n_ctx * n_fsdp)
    by_place = tokens.T.reshape(n_z, 2, 2, n_fsdp, out_rows, shard_rows)

    def rows_for(y, f):
        piece = lax.dynamic_index_in_dim(by_place, y, 1, keepdims=False)
        piece = lax.dynamic_index_in_dim(piece, f, 2, keepdims=False)
        return piece.reshape(n_z * 2 * out_rows, shard_rows)

    places = [(flip, s) for flip in range(2) for s in range(n_fsdp)]
    pieces = []
    for flip, s in places:
        piece = rows_for(my_y ^ flip, (my_fsdp + s) % n_fsdp)
        pieces.append(moved(piece, flip, s) if flip or s else piece)
    mine = jnp.concatenate(pieces, 1)
    theirs = swapped(mine)

    span_tags = jnp.concatenate([k[chip_rows, :chip_rows] for k in keys], 0)
    key_at = jnp.arange(WINDOW + chip_rows, dtype=jnp.int32)
    chip_tags = keys[n_back][chip_rows, :chip_rows]
    before = (span_tags[None, :] < chip_tags[:, None]) | (key_at + first < WINDOW)[None, :]
    low = jnp.sum(before.astype(jnp.int32), axis=1)
    low = jnp.maximum(low, jnp.arange(1, chip_rows + 1, dtype=jnp.int32))[None, :]

    e, inv, do_t, *dv_terms = run_probs(
        core_arg, low, queries[0], q_other, d_out[0], keys, chip_rows, half_kv
    )
    dv_total = dv_terms[n_back].astype(F32)
    for d in range(1, n_back + 1):
        dv_total = dv_total + shifted(dv_terms[n_back - d], -2 * d).astype(F32)
    dv_chip = dv_total.astype(BF16)

    value_sum = dot(cols(tokens, my_fsdp, slab), w_value)
    for s in range(1, n_fsdp):
        back = rotated(dot(sent[s - 1], w_value).astype(BF16), -s)
        value_sum = value_sum + back.astype(F32)
    own_values = value_sum.astype(BF16)
    v_own = placed(core, cols(own_values, core, half_kv), swapped(cols(own_values, 1 - core, half_kv)), 0)
    vals = [shifted(v_own, 2 * d) for d in range(n_back, 0, -1)] + [v_own]

    dv_places = [moved(dv_chip, flip, s) if flip or s else dv_chip for flip, s in places]
    weight_term = None
    for at, dv_of in enumerate(dv_places):
        window = slice(at * shard_rows, (at + 1) * shard_rows)
        term = dot(mine[:, window], rows_of(dv_of, core, shard_rows))
        term = term + dot(theirs[:, window], rows_of(dv_of, 1 - core, shard_rows))
        weight_term = term if weight_term is None else weight_term + term
    by_z = weight_term.astype(BF16).reshape(n_z, 2 * out_rows, half_kv)
    row_sum = lax.dynamic_index_in_dim(by_z, my_z, 0, keepdims=False).astype(F32)
    for d in range(1, n_z):
        piece = lax.dynamic_index_in_dim(by_z, (my_z + d) % n_z, 0, keepdims=False)
        piece = lax.ppermute(piece, "ctx", [(i, (i + 4 * d) % n_ctx) for i in range(n_ctx)])
        row_sum = row_sum + piece.astype(F32)
    d_weight = placed(core, rows_of(row_sum, core, out_rows), swapped(rows_of(row_sum, 1 - core, out_rows)), 1)

    dv_fsdp = [dv_places[s] for s in range(n_fsdp)]
    dv_other = swapped(jnp.concatenate([rows_of(x, 1 - core, shard_rows) for x in dv_fsdp], 0))
    dv_rows = placed(
        core, jnp.concatenate([rows_of(x, core, shard_rows) for x in dv_fsdp], 0), dv_other, 1
    )
    made = dot(dv_rows, w_value, NT).astype(BF16)
    d_tokens = jnp.concatenate([made[:shard_rows]] * n_fsdp, 1)
    for s in range(1, n_fsdp):
        back = rotated(made[s * shard_rows : (s + 1) * shard_rows], -s)
        d_tokens = lax.dynamic_update_slice_in_dim(d_tokens, back, ((my_fsdp + s) % n_fsdp) * slab, 1)

    out, dq, other, *dk_terms = run_grads(
        core_arg, e, inv, do_t, queries[0], q_other, keys, vals, chip_rows, half_kv
    )
    dk_total = dk_terms[n_back].astype(F32)
    for d in range(1, n_back + 1):
        dk_total = dk_total + shifted(dk_terms[n_back - d], -2 * d).astype(F32)
    dk_chip = dk_total.astype(BF16)
    d_keys = placed(core, rows_of(dk_chip, core, shard_rows), swapped(rows_of(dk_chip, 1 - core, shard_rows)), 1)
    other = swapped(other)
    out = lax.dynamic_update_slice_in_dim(out, other[0], (1 - core) * half_q, 1)
    dq = lax.dynamic_update_slice_in_dim(dq, other[1], (1 - core) * half_q, 1)
    return (out[None], dq[None], d_keys[None], d_tokens[None], d_weight)


def solution(mesh):
    in_specs = (
        P("fsdp", "ctx", None),
        P("fsdp", "ctx", None),
        P("fsdp", "ctx", None),
        P("fsdp", None),
        P("fsdp", "ctx", None),
        P("fsdp", "ctx"),
    )
    out_specs = (
        P("fsdp", "ctx", None),
        P("fsdp", "ctx", None),
        P("fsdp", "ctx", None),
        P("fsdp", "ctx", None),
        P(("ctx", "fsdp"), None),
    )
    return jax.shard_map(shards, mesh=mesh, in_specs=in_specs, out_specs=out_specs, check_vma=False)
```

```python
import functools
import math

import jax
import jax.numpy as jnp
from jax import lax
from jax.experimental import pallas as pl
from jax.experimental.pallas import tpu as pltpu
from jax.sharding import PartitionSpec as P

HQ = 16
HK = 8
HD = 128
WINDOW = 1024
GROUP = 2
NEG = -1e30

score_scale = 1.0 / math.sqrt(168.0)
exp2_scale = score_scale / math.log(2.0)

BF16 = jnp.bfloat16
F32 = jnp.float32
NT = (((1,), (1,)), ((), ()))
TN = (((0,), (0,)), ((), ()))


def dot(a, b, dims=(((1,), (0,)), ((), ()))):
    return lax.dot_general(a, b, dims, preferred_element_type=F32)


def probs_kernel(blk, n_back, core_ref, low_ref, q_own, q_other, do_own, do_other, *refs):
    n_arr = n_back + 1
    k_refs = refs[:n_arr]
    e_ref, inv_ref, dot_ref = refs[n_arr : n_arr + 3]
    dv_refs = refs[n_arr + 3 : 2 * n_arr + 3]
    bias, s_scr, dv_acc, q_buf, do_buf = refs[2 * n_arr + 3 :]
    span_blocks = WINDOW // blk + 1
    core = core_ref[0]

    @pl.when(pl.program_id(0) == 0)
    def _():
        for qb in range(2):
            kpos = lax.broadcasted_iota(jnp.int32, (span_blocks * blk, blk), 0) + qb * blk
            qpos = lax.broadcasted_iota(jnp.int32, (span_blocks * blk, blk), 1) + (qb * blk + WINDOW)
            low = low_ref[:, qb * blk : (qb + 1) * blk]
            ok = (kpos >= low) & (kpos <= qpos)
            bias[qb] = jnp.where(ok, 0.0, NEG)

    q_buf[core] = q_own[...]
    q_buf[1 - core] = q_other[...]
    do_buf[core] = do_own[...]
    do_buf[1 - core] = do_other[...]

    def key_block(j):
        return k_refs[j // 2][(j % 2) * blk : (j % 2 + 1) * blk, :]

    def stacked(buf, qb):
        return jnp.concatenate([buf[qb, :, r * HD : (r + 1) * HD] for r in range(GROUP)], 0)

    for qb in range(2):
        qs = stacked(q_buf, qb)
        top = None
        for j in range(span_blocks):
            s = dot(key_block(qb + j), qs, NT)
            b = bias[qb, j * blk : (j + 1) * blk, :]
            s = s * exp2_scale + jnp.concatenate([b] * GROUP, 1)
            s_scr[j] = s
            part = jnp.max(s.reshape(blk // 8, 8, GROUP * blk), axis=0)
            top = part if top is None else jnp.maximum(top, part)
        top = jnp.max(top, axis=0, keepdims=True)
        total = None
        for j in range(span_blocks):
            e = jnp.exp2(s_scr[j] - top)
            part = jnp.sum(e.reshape(blk // 8, 8, GROUP * blk), axis=0)
            total = part if total is None else total + part
            e_ref[0, qb, j * blk : (j + 1) * blk, :] = e.astype(BF16)
        inv = 1.0 / jnp.sum(total, axis=0, keepdims=True)
        inv_ref[0, qb] = inv
        do_t = (stacked(do_buf, qb).astype(F32).T * inv).astype(BF16)
        dot_ref[0, qb] = do_t
        for j in range(span_blocks):
            term = dot(e_ref[0, qb, j * blk : (j + 1) * blk, :], do_t, NT)
            at = slice((qb + j) * blk, (qb + j + 1) * blk)
            if qb == 0 or j == span_blocks - 1:
                dv_acc[at, :] = term
            else:
                dv_acc[at, :] += term
    for a in range(n_arr):
        dv_refs[a][...] = dv_acc[a * 2 * blk : (a + 1) * 2 * blk, :].astype(BF16)


def grads_kernel(blk, n_back, core_ref, e_ref, inv_ref, dot_ref, q_own, q_other, *refs):
    n_arr = n_back + 1
    k_refs = refs[:n_arr]
    v_refs = refs[n_arr : 2 * n_arr]
    out_ref, dq_ref, other_ref = refs[2 * n_arr : 2 * n_arr + 3]
    dk_refs = refs[2 * n_arr + 3 : 3 * n_arr + 3]
    dk_acc, q_buf, out_buf, dq_buf = refs[3 * n_arr + 3 :]
    span_blocks = WINDOW // blk + 1
    core = core_ref[0]

    q_buf[core] = q_own[...]
    q_buf[1 - core] = q_other[...]

    def block_of(arrays, j):
        return arrays[j // 2][(j % 2) * blk : (j % 2 + 1) * blk, :]

    for qb in range(2):
        qs = jnp.concatenate([q_buf[qb, :, r * HD : (r + 1) * HD] for r in range(GROUP)], 0)
        do_t = dot_ref[0, qb]
        out_t = None
        for j in range(span_blocks):
            e = e_ref[0, qb, j * blk : (j + 1) * blk, :]
            part = dot(block_of(v_refs, qb + j), e, TN)
            out_t = part if out_t is None else out_t + part
        out_t = (out_t * inv_ref[0, qb]).astype(BF16).astype(F32)
        delta = jnp.sum(out_t * do_t.astype(F32), axis=0, keepdims=True)
        out = out_t.T.astype(BF16)
        dq_t = None
        for j in range(span_blocks):
            e = e_ref[0, qb, j * blk : (j + 1) * blk, :].astype(F32)
            dp = dot(block_of(v_refs, qb + j), do_t)
            ds = (e * (dp - delta)).astype(BF16)
            term = dot(ds, qs)
            at = slice((qb + j) * blk, (qb + j + 1) * blk)
            if qb == 0 or j == span_blocks - 1:
                dk_acc[at, :] = term
            else:
                dk_acc[at, :] += term
            part = dot(block_of(k_refs, qb + j), ds, TN)
            dq_t = part if dq_t is None else dq_t + part
        dq = (dq_t * score_scale).T.astype(BF16)
        for r in range(GROUP):
            out_buf[qb, :, r * HD : (r + 1) * HD] = out[r * blk : (r + 1) * blk, :]
            dq_buf[qb, :, r * HD : (r + 1) * HD] = dq[r * blk : (r + 1) * blk, :]
    out_ref[...] = out_buf[core]
    dq_ref[...] = dq_buf[core]
    other_ref[0] = out_buf[1 - core]
    other_ref[1] = dq_buf[1 - core]
    for a in range(n_arr):
        dk_refs[a][...] = (dk_acc[a * 2 * blk : (a + 1) * 2 * blk, :] * score_scale).astype(BF16)


def specs_of(rows, width):
    blk = rows // 2
    heads = width // HD
    span = WINDOW + blk
    lanes = GROUP * blk
    head = pl.BlockSpec((rows, HD), lambda g, c: (0, g))
    own = pl.BlockSpec((blk, GROUP * HD), lambda g, c: (0, c[0] * heads + g))
    return blk, heads, span, lanes, head, own


def run_probs(core, low, q, q_other, do, keys, rows, width):
    blk, heads, span, lanes, head, own = specs_of(rows, width)
    n_arr = len(keys)
    return pl.pallas_call(
        functools.partial(probs_kernel, blk, n_arr - 1),
        grid_spec=pltpu.PrefetchScalarGridSpec(
            num_scalar_prefetch=1,
            grid=(heads,),
            in_specs=[
                pl.BlockSpec((1, rows), lambda g, c: (0, 0)),
                own,
                pl.BlockSpec((blk, GROUP * HD), lambda g, c: (0, g)),
                own,
                pl.BlockSpec((blk, GROUP * HD), lambda g, c: (0, heads + g)),
            ]
            + [head] * n_arr,
            out_specs=[
                pl.BlockSpec((1, 2, span, lanes), lambda g, c: (g, 0, 0, 0)),
                pl.BlockSpec((1, 2, 1, lanes), lambda g, c: (g, 0, 0, 0)),
                pl.BlockSpec((1, 2, HD, lanes), lambda g, c: (g, 0, 0, 0)),
            ]
            + [head] * n_arr,
            scratch_shapes=[
                pltpu.VMEM((2, span, blk), F32),
                pltpu.VMEM((span // blk, blk, lanes), F32),
                pltpu.VMEM((WINDOW + rows, HD), F32),
                pltpu.VMEM((2, blk, GROUP * HD), BF16),
                pltpu.VMEM((2, blk, GROUP * HD), BF16),
            ],
        ),
        out_shape=[
            jax.ShapeDtypeStruct((heads, 2, span, lanes), BF16),
            jax.ShapeDtypeStruct((heads, 2, 1, lanes), F32),
            jax.ShapeDtypeStruct((heads, 2, HD, lanes), BF16),
        ]
        + [jax.ShapeDtypeStruct((rows, width), BF16)] * n_arr,
        compiler_params=pltpu.CompilerParams(vmem_limit_bytes=40 * 1024 * 1024),
        cost_estimate=pl.CostEstimate(
            flops=heads * 2 * span * lanes * HD // 16,
            bytes_accessed=heads * span * lanes // 16,
            transcendentals=0,
        ),
        name="probs",
    )(core, low, q, q_other, do, q_other, *keys)


def run_grads(core, e, inv, do_t, q, q_other, keys, values, rows, width):
    blk, heads, span, lanes, head, own = specs_of(rows, width)
    n_arr = len(keys)
    full = jax.ShapeDtypeStruct(q.shape, BF16)
    return pl.pallas_call(
        functools.partial(grads_kernel, blk, n_arr - 1),
        grid_spec=pltpu.PrefetchScalarGridSpec(
            num_scalar_prefetch=1,
            grid=(heads,),
            in_specs=[
                pl.BlockSpec((1, 2, span, lanes), lambda g, c: (g, 0, 0, 0)),
                pl.BlockSpec((1, 2, 1, lanes), lambda g, c: (g, 0, 0, 0)),
                pl.BlockSpec((1, 2, HD, lanes), lambda g, c: (g, 0, 0, 0)),
                own,
                pl.BlockSpec((blk, GROUP * HD), lambda g, c: (0, g)),
            ]
            + [head] * (2 * n_arr),
            out_specs=[own, own, pl.BlockSpec((2, blk, GROUP * HD), lambda g, c: (0, 0, g))] + [head] * n_arr,
            scratch_shapes=[
                pltpu.VMEM((WINDOW + rows, HD), F32),
                pltpu.VMEM((2, blk, GROUP * HD), BF16),
                pltpu.VMEM((2, blk, GROUP * HD), BF16),
                pltpu.VMEM((2, blk, GROUP * HD), BF16),
            ],
        ),
        out_shape=[full, full, jax.ShapeDtypeStruct((2, blk, GROUP * width), BF16)]
        + [jax.ShapeDtypeStruct((rows, width), BF16)] * n_arr,
        compiler_params=pltpu.CompilerParams(vmem_limit_bytes=40 * 1024 * 1024),
        cost_estimate=pl.CostEstimate(
            flops=heads * 2 * span * lanes * HD // 16,
            bytes_accessed=heads * span * lanes // 16,
            transcendentals=0,
        ),
        name="grads",
    )(core, e, inv, do_t, q, q_other, *keys, *values)


def shifted(x, by):
    length = lax.axis_size("ctx")
    return lax.ppermute(x, "ctx", [(i, i + by) for i in range(length) if 0 <= i + by < length])


def swapped(x):
    return lax.ppermute(x, "ctx", [(i, i ^ 1) for i in range(lax.axis_size("ctx"))])


def rotated(x, by):
    length = lax.axis_size("fsdp")
    return lax.ppermute(x, "fsdp", [(i, (i + by) % length) for i in range(length)])


def moved(x, flip, by):
    n_ctx, n_fsdp = lax.axis_size("ctx"), lax.axis_size("fsdp")
    pairs = [
        (c * n_fsdp + f, (c ^ (2 * flip)) * n_fsdp + (f + by) % n_fsdp)
        for c in range(n_ctx)
        for f in range(n_fsdp)
    ]
    return lax.ppermute(x, ("ctx", "fsdp"), pairs)


def cols(x, at, width):
    return lax.dynamic_slice_in_dim(x, at * width, width, x.ndim - 1)


def rows_of(x, at, count):
    return lax.dynamic_slice_in_dim(x, at * count, count, 0)


def placed(core, own, other, axis):
    both = jnp.concatenate([own, own], axis)
    return lax.dynamic_update_slice_in_dim(both, other, (1 - core) * own.shape[axis], axis)


def shards(hidden, queries, key_heads, w_value, d_out, segments):
    shard_rows = hidden.shape[1]
    model = hidden.shape[2]
    kv_width = w_value.shape[1]
    n_ctx = lax.axis_size("ctx")
    n_fsdp = lax.axis_size("fsdp")
    chip_rows = 2 * shard_rows
    n_back = WINDOW // chip_rows
    n_z = n_ctx // 4
    my_ctx = lax.axis_index("ctx")
    my_fsdp = lax.axis_index("fsdp")
    core = my_ctx % 2
    core_arg = core.astype(jnp.int32).reshape(1)
    chip = my_ctx // 2
    my_y = chip % 2
    my_z = chip // 2
    half_kv = kv_width // 2
    slab = model // n_fsdp
    tokens = hidden[0]
    first = chip * chip_rows

    sent = [rotated(cols(tokens, (my_fsdp + s) % n_fsdp, slab), s) for s in range(1, n_fsdp)]

    own_tags = segments[0].astype(BF16)
    tag_row = lax.dynamic_update_slice_in_dim(jnp.zeros((half_kv,), BF16), own_tags, core * shard_rows, 0)
    tag_rows = jnp.concatenate([tag_row[None], jnp.zeros((15, half_kv), BF16)], 0)
    got = swapped(jnp.concatenate([cols(key_heads[0], 1 - core, half_kv), tag_rows], 0))
    k_own = jnp.concatenate(
        [
            placed(core, cols(key_heads[0], core, half_kv), got[:shard_rows], 0),
            tag_rows + got[shard_rows:],
        ],
        0,
    )
    keys = [shifted(k_own, 2 * d) for d in range(n_back, 0, -1)] + [k_own]
    half_q = queries.shape[2] // 2
    q_other = swapped(jnp.concatenate([cols(queries[0], 1 - core, half_q), cols(d_out[0], 1 - core, half_q)], 1))

    out_rows = model // (n_ctx * n_fsdp)
    by_place = tokens.T.reshape(n_z, 2, 2, n_fsdp, out_rows, shard_rows)

    def rows_for(y, f):
        piece = lax.dynamic_index_in_dim(by_place, y, 1, keepdims=False)
        piece = lax.dynamic_index_in_dim(piece, f, 2, keepdims=False)
        return piece.reshape(n_z * 2 * out_rows, shard_rows)

    places = [(flip, s) for flip in range(2) for s in range(n_fsdp)]
    pieces = []
    for flip, s in places:
        piece = rows_for(my_y ^ flip, (my_fsdp + s) % n_fsdp)
        pieces.append(moved(piece, flip, s) if flip or s else piece)
    mine = jnp.concatenate(pieces, 1)
    theirs = swapped(mine)

    span_tags = jnp.concatenate([k[chip_rows, :chip_rows] for k in keys], 0)
    key_at = jnp.arange(WINDOW + chip_rows, dtype=jnp.int32)
    chip_tags = keys[n_back][chip_rows, :chip_rows]
    before = (span_tags[None, :] < chip_tags[:, None]) | (key_at + first < WINDOW)[None, :]
    low = jnp.sum(before.astype(jnp.int32), axis=1)
    low = jnp.maximum(low, jnp.arange(1, chip_rows + 1, dtype=jnp.int32))[None, :]

    e, inv, do_t, *dv_terms = run_probs(
        core_arg, low, queries[0], q_other, d_out[0], keys, chip_rows, half_kv
    )
    dv_total = dv_terms[n_back].astype(F32)
    for d in range(1, n_back + 1):
        dv_total = dv_total + shifted(dv_terms[n_back - d], -2 * d).astype(F32)
    dv_chip = dv_total.astype(BF16)

    value_sum = dot(cols(tokens, my_fsdp, slab), w_value)
    for s in range(1, n_fsdp):
        back = rotated(dot(sent[s - 1], w_value).astype(BF16), -s)
        value_sum = value_sum + back.astype(F32)
    own_values = value_sum.astype(BF16)
    v_own = placed(core, cols(own_values, core, half_kv), swapped(cols(own_values, 1 - core, half_kv)), 0)
    vals = [shifted(v_own, 2 * d) for d in range(n_back, 0, -1)] + [v_own]

    dv_places = [moved(dv_chip, flip, s) if flip or s else dv_chip for flip, s in places]
    weight_term = None
    for at, dv_of in enumerate(dv_places):
        window = slice(at * shard_rows, (at + 1) * shard_rows)
        term = dot(mine[:, window], rows_of(dv_of, core, shard_rows))
        term = term + dot(theirs[:, window], rows_of(dv_of, 1 - core, shard_rows))
        weight_term = term if weight_term is None else weight_term + term
    by_z = weight_term.astype(BF16).reshape(n_z, 2 * out_rows, half_kv)
    row_sum = lax.dynamic_index_in_dim(by_z, my_z, 0, keepdims=False).astype(F32)
    for d in range(1, n_z):
        piece = lax.dynamic_index_in_dim(by_z, (my_z + d) % n_z, 0, keepdims=False)
        piece = lax.ppermute(piece, "ctx", [(i, (i + 4 * d) % n_ctx) for i in range(n_ctx)])
        row_sum = row_sum + piece.astype(F32)
    d_weight = placed(core, rows_of(row_sum, core, out_rows), swapped(rows_of(row_sum, 1 - core, out_rows)), 1)

    dv_fsdp = [dv_places[s] for s in range(n_fsdp)]
    dv_other = swapped(jnp.concatenate([rows_of(x, 1 - core, shard_rows) for x in dv_fsdp], 0))
    dv_rows = placed(
        core, jnp.concatenate([rows_of(x, core, shard_rows) for x in dv_fsdp], 0), dv_other, 1
    )
    made = dot(dv_rows, w_value, NT).astype(BF16)
    d_tokens = jnp.concatenate([made[:shard_rows]] * n_fsdp, 1)
    for s in range(1, n_fsdp):
        back = rotated(made[s * shard_rows : (s + 1) * shard_rows], -s)
        d_tokens = lax.dynamic_update_slice_in_dim(d_tokens, back, ((my_fsdp + s) % n_fsdp) * slab, 1)

    out, dq, other, *dk_terms = run_grads(
        core_arg, e, inv, do_t, queries[0], q_other, keys, vals, chip_rows, half_kv
    )
    dk_back = [shifted(dk_terms[n_back - d], -2 * d) for d in range(1, n_back + 1)]
    dk_back, by_z = lax.optimization_barrier((dk_back, by_z))
    dk_total = dk_terms[n_back].astype(F32)
    for term in dk_back:
        dk_total = dk_total + term.astype(F32)
    dk_chip = dk_total.astype(BF16)
    d_keys = placed(core, rows_of(dk_chip, core, shard_rows), swapped(rows_of(dk_chip, 1 - core, shard_rows)), 1)
    other = swapped(other)
    out = lax.dynamic_update_slice_in_dim(out, other[0], (1 - core) * half_q, 1)
    dq = lax.dynamic_update_slice_in_dim(dq, other[1], (1 - core) * half_q, 1)
    return (out[None], dq[None], d_keys[None], d_tokens[None], d_weight)


def solution(mesh):
    in_specs = (
        P("fsdp", "ctx", None),
        P("fsdp", "ctx", None),
        P("fsdp", "ctx", None),
        P("fsdp", None),
        P("fsdp", "ctx", None),
        P("fsdp", "ctx"),
    )
    out_specs = (
        P("fsdp", "ctx", None),
        P("fsdp", "ctx", None),
        P("fsdp", "ctx", None),
        P("fsdp", "ctx", None),
        P(("ctx", "fsdp"), None),
    )
    return jax.shard_map(shards, mesh=mesh, in_specs=in_specs, out_specs=out_specs, check_vma=False)
```

```python
import functools
import math

import jax
import jax.numpy as jnp
from jax import lax
from jax.experimental import pallas as pl
from jax.experimental.pallas import tpu as pltpu
from jax.sharding import PartitionSpec as P

HQ = 16
HK = 8
HD = 128
WINDOW = 1024
GROUP = 2
NEG = -1e30

score_scale = 1.0 / math.sqrt(168.0)
exp2_scale = score_scale / math.log(2.0)

BF16 = jnp.bfloat16
F32 = jnp.float32
NT = (((1,), (1,)), ((), ()))
TN = (((0,), (0,)), ((), ()))


def dot(a, b, dims=(((1,), (0,)), ((), ()))):
    return lax.dot_general(a, b, dims, preferred_element_type=F32)


def probs_kernel(blk, n_back, core_ref, low_ref, q_own, q_other, do_own, do_other, *refs):
    n_arr = n_back + 1
    k_refs = refs[:n_arr]
    e_ref, inv_ref, dot_ref = refs[n_arr : n_arr + 3]
    dv_refs = refs[n_arr + 3 : 2 * n_arr + 3]
    bias, s_scr, dv_acc, q_buf, do_buf = refs[2 * n_arr + 3 :]
    span_blocks = WINDOW // blk + 1
    core = core_ref[0]

    @pl.when(pl.program_id(0) == 0)
    def _():
        for qb in range(2):
            kpos = lax.broadcasted_iota(jnp.int32, (span_blocks * blk, blk), 0) + qb * blk
            qpos = lax.broadcasted_iota(jnp.int32, (span_blocks * blk, blk), 1) + (qb * blk + WINDOW)
            low = low_ref[:, qb * blk : (qb + 1) * blk]
            ok = (kpos >= low) & (kpos <= qpos)
            bias[qb] = jnp.where(ok, 0.0, NEG)

    q_buf[core] = q_own[...]
    q_buf[1 - core] = q_other[...]
    do_buf[core] = do_own[...]
    do_buf[1 - core] = do_other[...]

    def key_block(j):
        return k_refs[j // 2][(j % 2) * blk : (j % 2 + 1) * blk, :]

    def stacked(buf, qb):
        return jnp.concatenate([buf[qb, :, r * HD : (r + 1) * HD] for r in range(GROUP)], 0)

    for qb in range(2):
        qs = stacked(q_buf, qb)
        top = None
        for j in range(span_blocks):
            s = dot(key_block(qb + j), qs, NT)
            b = bias[qb, j * blk : (j + 1) * blk, :]
            s = s * exp2_scale + jnp.concatenate([b] * GROUP, 1)
            s_scr[j] = s
            part = jnp.max(s.reshape(blk // 8, 8, GROUP * blk), axis=0)
            top = part if top is None else jnp.maximum(top, part)
        top = jnp.max(top, axis=0, keepdims=True)
        total = None
        for j in range(span_blocks):
            e = jnp.exp2(s_scr[j] - top)
            part = jnp.sum(e.reshape(blk // 8, 8, GROUP * blk), axis=0)
            total = part if total is None else total + part
            e_ref[0, qb, j * blk : (j + 1) * blk, :] = e.astype(BF16)
        inv = 1.0 / jnp.sum(total, axis=0, keepdims=True)
        inv_ref[0, qb] = inv
        do_t = (stacked(do_buf, qb).astype(F32).T * inv).astype(BF16)
        dot_ref[0, qb] = do_t
        for j in range(span_blocks):
            term = dot(e_ref[0, qb, j * blk : (j + 1) * blk, :], do_t, NT)
            at = slice((qb + j) * blk, (qb + j + 1) * blk)
            if qb == 0 or j == span_blocks - 1:
                dv_acc[at, :] = term
            else:
                dv_acc[at, :] += term
    for a in range(n_arr):
        dv_refs[a][...] = dv_acc[a * 2 * blk : (a + 1) * 2 * blk, :].astype(BF16)


def grads_kernel(blk, n_back, core_ref, e_ref, inv_ref, dot_ref, q_own, q_other, *refs):
    n_arr = n_back + 1
    k_refs = refs[:n_arr]
    v_refs = refs[n_arr : 2 * n_arr]
    out_ref, dq_ref, other_ref = refs[2 * n_arr : 2 * n_arr + 3]
    dk_refs = refs[2 * n_arr + 3 : 3 * n_arr + 3]
    dk_acc, q_buf, out_buf, dq_buf = refs[3 * n_arr + 3 :]
    span_blocks = WINDOW // blk + 1
    core = core_ref[0]

    q_buf[core] = q_own[...]
    q_buf[1 - core] = q_other[...]

    def block_of(arrays, j):
        return arrays[j // 2][(j % 2) * blk : (j % 2 + 1) * blk, :]

    for qb in range(2):
        qs = jnp.concatenate([q_buf[qb, :, r * HD : (r + 1) * HD] for r in range(GROUP)], 0)
        do_t = dot_ref[0, qb]
        out_t = None
        for j in range(span_blocks):
            e = e_ref[0, qb, j * blk : (j + 1) * blk, :]
            part = dot(block_of(v_refs, qb + j), e, TN)
            out_t = part if out_t is None else out_t + part
        out_t = (out_t * inv_ref[0, qb]).astype(BF16).astype(F32)
        delta = jnp.sum(out_t * do_t.astype(F32), axis=0, keepdims=True)
        out = out_t.T.astype(BF16)
        dq_t = None
        for j in range(span_blocks):
            e = e_ref[0, qb, j * blk : (j + 1) * blk, :].astype(F32)
            dp = dot(block_of(v_refs, qb + j), do_t)
            ds = (e * (dp - delta)).astype(BF16)
            term = dot(ds, qs)
            at = slice((qb + j) * blk, (qb + j + 1) * blk)
            if qb == 0 or j == span_blocks - 1:
                dk_acc[at, :] = term
            else:
                dk_acc[at, :] += term
            part = dot(block_of(k_refs, qb + j), ds, TN)
            dq_t = part if dq_t is None else dq_t + part
        dq = (dq_t * score_scale).T.astype(BF16)
        for r in range(GROUP):
            out_buf[qb, :, r * HD : (r + 1) * HD] = out[r * blk : (r + 1) * blk, :]
            dq_buf[qb, :, r * HD : (r + 1) * HD] = dq[r * blk : (r + 1) * blk, :]
    out_ref[...] = out_buf[core]
    dq_ref[...] = dq_buf[core]
    other_ref[0] = out_buf[1 - core]
    other_ref[1] = dq_buf[1 - core]
    for a in range(n_arr):
        dk_refs[a][...] = (dk_acc[a * 2 * blk : (a + 1) * 2 * blk, :] * score_scale).astype(BF16)


def specs_of(rows, width):
    blk = rows // 2
    heads = width // HD
    span = WINDOW + blk
    lanes = GROUP * blk
    head = pl.BlockSpec((rows, HD), lambda g, c: (0, g))
    own = pl.BlockSpec((blk, GROUP * HD), lambda g, c: (0, c[0] * heads + g))
    return blk, heads, span, lanes, head, own


def run_probs(core, low, q, q_other, do, keys, rows, width):
    blk, heads, span, lanes, head, own = specs_of(rows, width)
    n_arr = len(keys)
    return pl.pallas_call(
        functools.partial(probs_kernel, blk, n_arr - 1),
        grid_spec=pltpu.PrefetchScalarGridSpec(
            num_scalar_prefetch=1,
            grid=(heads,),
            in_specs=[
                pl.BlockSpec((1, rows), lambda g, c: (0, 0)),
                own,
                pl.BlockSpec((blk, GROUP * HD), lambda g, c: (0, g)),
                own,
                pl.BlockSpec((blk, GROUP * HD), lambda g, c: (0, heads + g)),
            ]
            + [head] * n_arr,
            out_specs=[
                pl.BlockSpec((1, 2, span, lanes), lambda g, c: (g, 0, 0, 0)),
                pl.BlockSpec((1, 2, 1, lanes), lambda g, c: (g, 0, 0, 0)),
                pl.BlockSpec((1, 2, HD, lanes), lambda g, c: (g, 0, 0, 0)),
            ]
            + [head] * n_arr,
            scratch_shapes=[
                pltpu.VMEM((2, span, blk), F32),
                pltpu.VMEM((span // blk, blk, lanes), F32),
                pltpu.VMEM((WINDOW + rows, HD), F32),
                pltpu.VMEM((2, blk, GROUP * HD), BF16),
                pltpu.VMEM((2, blk, GROUP * HD), BF16),
            ],
        ),
        out_shape=[
            jax.ShapeDtypeStruct((heads, 2, span, lanes), BF16),
            jax.ShapeDtypeStruct((heads, 2, 1, lanes), F32),
            jax.ShapeDtypeStruct((heads, 2, HD, lanes), BF16),
        ]
        + [jax.ShapeDtypeStruct((rows, width), BF16)] * n_arr,
        compiler_params=pltpu.CompilerParams(vmem_limit_bytes=40 * 1024 * 1024),
        cost_estimate=pl.CostEstimate(
            flops=heads * 2 * span * lanes * HD // 16,
            bytes_accessed=heads * span * lanes // 16,
            transcendentals=0,
        ),
        name="probs",
    )(core, low, q, q_other, do, q_other, *keys)


def run_grads(core, e, inv, do_t, q, q_other, keys, values, rows, width):
    blk, heads, span, lanes, head, own = specs_of(rows, width)
    n_arr = len(keys)
    full = jax.ShapeDtypeStruct(q.shape, BF16)
    return pl.pallas_call(
        functools.partial(grads_kernel, blk, n_arr - 1),
        grid_spec=pltpu.PrefetchScalarGridSpec(
            num_scalar_prefetch=1,
            grid=(heads,),
            in_specs=[
                pl.BlockSpec((1, 2, span, lanes), lambda g, c: (g, 0, 0, 0)),
                pl.BlockSpec((1, 2, 1, lanes), lambda g, c: (g, 0, 0, 0)),
                pl.BlockSpec((1, 2, HD, lanes), lambda g, c: (g, 0, 0, 0)),
                own,
                pl.BlockSpec((blk, GROUP * HD), lambda g, c: (0, g)),
            ]
            + [head] * (2 * n_arr),
            out_specs=[own, own, pl.BlockSpec((2, blk, GROUP * HD), lambda g, c: (0, 0, g))] + [head] * n_arr,
            scratch_shapes=[
                pltpu.VMEM((WINDOW + rows, HD), F32),
                pltpu.VMEM((2, blk, GROUP * HD), BF16),
                pltpu.VMEM((2, blk, GROUP * HD), BF16),
                pltpu.VMEM((2, blk, GROUP * HD), BF16),
            ],
        ),
        out_shape=[full, full, jax.ShapeDtypeStruct((2, blk, GROUP * width), BF16)]
        + [jax.ShapeDtypeStruct((rows, width), BF16)] * n_arr,
        compiler_params=pltpu.CompilerParams(vmem_limit_bytes=40 * 1024 * 1024),
        cost_estimate=pl.CostEstimate(
            flops=heads * 2 * span * lanes * HD // 16,
            bytes_accessed=heads * span * lanes // 16,
            transcendentals=0,
        ),
        name="grads",
    )(core, e, inv, do_t, q, q_other, *keys, *values)


def shifted(x, by):
    length = lax.axis_size("ctx")
    return lax.ppermute(x, "ctx", [(i, i + by) for i in range(length) if 0 <= i + by < length])


def swapped(x):
    return lax.ppermute(x, "ctx", [(i, i ^ 1) for i in range(lax.axis_size("ctx"))])


def rotated(x, by):
    length = lax.axis_size("fsdp")
    return lax.ppermute(x, "fsdp", [(i, (i + by) % length) for i in range(length)])


def moved(x, flip, by):
    n_ctx, n_fsdp = lax.axis_size("ctx"), lax.axis_size("fsdp")
    pairs = [
        (c * n_fsdp + f, (c ^ (2 * flip)) * n_fsdp + (f + by) % n_fsdp)
        for c in range(n_ctx)
        for f in range(n_fsdp)
    ]
    return lax.ppermute(x, ("ctx", "fsdp"), pairs)


def cols(x, at, width):
    return lax.dynamic_slice_in_dim(x, at * width, width, x.ndim - 1)


def rows_of(x, at, count):
    return lax.dynamic_slice_in_dim(x, at * count, count, 0)


def placed(core, own, other, axis):
    both = jnp.concatenate([own, own], axis)
    return lax.dynamic_update_slice_in_dim(both, other, (1 - core) * own.shape[axis], axis)


def after(x, *earlier):
    return lax.optimization_barrier((x, *earlier))[0]


def shards(hidden, queries, key_heads, w_value, d_out, segments):
    shard_rows = hidden.shape[1]
    model = hidden.shape[2]
    kv_width = w_value.shape[1]
    n_ctx = lax.axis_size("ctx")
    n_fsdp = lax.axis_size("fsdp")
    chip_rows = 2 * shard_rows
    n_back = WINDOW // chip_rows
    n_z = n_ctx // 4
    my_ctx = lax.axis_index("ctx")
    my_fsdp = lax.axis_index("fsdp")
    core = my_ctx % 2
    core_arg = core.astype(jnp.int32).reshape(1)
    chip = my_ctx // 2
    my_y = chip % 2
    my_z = chip // 2
    half_kv = kv_width // 2
    slab = model // n_fsdp
    tokens = hidden[0]
    first = chip * chip_rows

    own_tags = segments[0].astype(BF16)
    tag_row = lax.dynamic_update_slice_in_dim(jnp.zeros((half_kv,), BF16), own_tags, core * shard_rows, 0)
    tag_rows = jnp.concatenate([tag_row[None], jnp.zeros((15, half_kv), BF16)], 0)
    k_sent = jnp.concatenate([cols(key_heads[0], 1 - core, half_kv), tag_rows], 0)
    got = swapped(k_sent)

    slabs = [after(cols(tokens, (my_fsdp + s) % n_fsdp, slab), k_sent) for s in range(1, n_fsdp)]
    sent = [rotated(x, s + 1) for s, x in enumerate(slabs)]
    half_q = queries.shape[2] // 2
    q_sent = jnp.concatenate([cols(queries[0], 1 - core, half_q), cols(d_out[0], 1 - core, half_q)], 1)
    q_other = swapped(after(q_sent, *slabs))

    k_own = jnp.concatenate(
        [
            placed(core, cols(key_heads[0], core, half_kv), got[:shard_rows], 0),
            tag_rows + got[shard_rows:],
        ],
        0,
    )
    keys = [shifted(k_own, 2 * d) for d in range(n_back, 0, -1)] + [k_own]
    value_own = after(dot(cols(tokens, my_fsdp, slab), w_value), k_own)

    out_rows = model // (n_ctx * n_fsdp)
    by_place = after(tokens.T, k_own).reshape(n_z, 2, 2, n_fsdp, out_rows, shard_rows)

    def rows_for(y, f):
        piece = lax.dynamic_index_in_dim(by_place, y, 1, keepdims=False)
        piece = lax.dynamic_index_in_dim(piece, f, 2, keepdims=False)
        return piece.reshape(n_z * 2 * out_rows, shard_rows)

    places = [(flip, s) for flip in range(2) for s in range(n_fsdp)]
    pieces = [rows_for(my_y ^ flip, (my_fsdp + s) % n_fsdp) for flip, s in places]

    span_tags = jnp.concatenate([k[chip_rows, :chip_rows] for k in keys], 0)
    key_at = jnp.arange(WINDOW + chip_rows, dtype=jnp.int32)
    chip_tags = keys[n_back][chip_rows, :chip_rows]
    before = (span_tags[None, :] < chip_tags[:, None]) | (key_at + first < WINDOW)[None, :]
    low = jnp.sum(before.astype(jnp.int32), axis=1)
    low = jnp.maximum(low, jnp.arange(1, chip_rows + 1, dtype=jnp.int32))[None, :]

    partial = [dot(x, w_value).astype(BF16) for x in sent]
    low = after(low, value_own, *pieces, *partial)
    e, inv, do_t, *dv_terms = run_probs(
        core_arg, low, queries[0], q_other, d_out[0], keys, chip_rows, half_kv
    )
    dv_back = [shifted(dv_terms[n_back - d], -2 * d) for d in range(1, n_back + 1)]

    value_sum = value_own
    for s, x in enumerate(partial):
        value_sum = value_sum + rotated(x, -s - 1).astype(F32)
    own_values = value_sum.astype(BF16)
    v_own = placed(core, cols(own_values, core, half_kv), swapped(cols(own_values, 1 - core, half_kv)), 0)
    vals = [shifted(v_own, 2 * d) for d in range(n_back, 0, -1)] + [v_own]

    *pieces, _ = lax.optimization_barrier((*pieces, own_values))
    pieces = [moved(x, flip, s) if flip or s else x for x, (flip, s) in zip(pieces, places)]
    mine = jnp.concatenate(pieces, 1)
    theirs = swapped(mine)

    *dv_back, _ = lax.optimization_barrier((*dv_back, v_own))
    dv_total = dv_terms[n_back].astype(F32)
    for term in dv_back:
        dv_total = dv_total + term.astype(F32)
    dv_chip = dv_total.astype(BF16)

    dv_places = [moved(dv_chip, flip, s) if flip or s else dv_chip for flip, s in places]
    weight_term = None
    for at, dv_of in enumerate(dv_places):
        window = slice(at * shard_rows, (at + 1) * shard_rows)
        term = dot(mine[:, window], rows_of(dv_of, core, shard_rows))
        term = term + dot(theirs[:, window], rows_of(dv_of, 1 - core, shard_rows))
        weight_term = term if weight_term is None else weight_term + term
    by_z = weight_term.astype(BF16).reshape(n_z, 2 * out_rows, half_kv)
    row_sum = lax.dynamic_index_in_dim(by_z, my_z, 0, keepdims=False).astype(F32)
    for d in range(1, n_z):
        piece = lax.dynamic_index_in_dim(by_z, (my_z + d) % n_z, 0, keepdims=False)
        piece = lax.ppermute(piece, "ctx", [(i, (i + 4 * d) % n_ctx) for i in range(n_ctx)])
        row_sum = row_sum + piece.astype(F32)
    d_weight = placed(core, rows_of(row_sum, core, out_rows), swapped(rows_of(row_sum, 1 - core, out_rows)), 1)

    dv_fsdp = [dv_places[s] for s in range(n_fsdp)]
    dv_other = swapped(jnp.concatenate([rows_of(x, 1 - core, shard_rows) for x in dv_fsdp], 0))
    dv_rows = placed(
        core, jnp.concatenate([rows_of(x, core, shard_rows) for x in dv_fsdp], 0), dv_other, 1
    )
    made = dot(dv_rows, w_value, NT).astype(BF16)
    d_tokens = jnp.concatenate([made[:shard_rows]] * n_fsdp, 1)
    for s in range(1, n_fsdp):
        back = rotated(made[s * shard_rows : (s + 1) * shard_rows], -s)
        d_tokens = lax.dynamic_update_slice_in_dim(d_tokens, back, ((my_fsdp + s) % n_fsdp) * slab, 1)

    out, dq, other, *dk_terms = run_grads(
        core_arg, e, inv, do_t, queries[0], q_other, keys, vals, chip_rows, half_kv
    )
    dk_back = [shifted(dk_terms[n_back - d], -2 * d) for d in range(1, n_back + 1)]
    *dk_back, _ = lax.optimization_barrier((*dk_back, by_z))
    dk_total = dk_terms[n_back].astype(F32)
    for term in dk_back:
        dk_total = dk_total + term.astype(F32)
    dk_chip = dk_total.astype(BF16)
    d_keys = placed(core, rows_of(dk_chip, core, shard_rows), swapped(rows_of(dk_chip, 1 - core, shard_rows)), 1)
    other = swapped(other)
    out = lax.dynamic_update_slice_in_dim(out, other[0], (1 - core) * half_q, 1)
    dq = lax.dynamic_update_slice_in_dim(dq, other[1], (1 - core) * half_q, 1)
    return (out[None], dq[None], d_keys[None], d_tokens[None], d_weight)


def solution(mesh):
    in_specs = (
        P("fsdp", "ctx", None),
        P("fsdp", "ctx", None),
        P("fsdp", "ctx", None),
        P("fsdp", None),
        P("fsdp", "ctx", None),
        P("fsdp", "ctx"),
    )
    out_specs = (
        P("fsdp", "ctx", None),
        P("fsdp", "ctx", None),
        P("fsdp", "ctx", None),
        P("fsdp", "ctx", None),
        P(("ctx", "fsdp"), None),
    )
    return jax.shard_map(shards, mesh=mesh, in_specs=in_specs, out_specs=out_specs, check_vma=False)
```

```python
import functools
import math

import jax
import jax.numpy as jnp
from jax import lax
from jax.experimental import pallas as pl
from jax.experimental.pallas import tpu as pltpu
from jax.sharding import PartitionSpec as P

HQ = 16
HK = 8
HD = 128
WINDOW = 1024
GROUP = 2
NEG = -1e30

score_scale = 1.0 / math.sqrt(168.0)
exp2_scale = score_scale / math.log(2.0)

BF16 = jnp.bfloat16
F32 = jnp.float32
NT = (((1,), (1,)), ((), ()))
TN = (((0,), (0,)), ((), ()))


def dot(a, b, dims=(((1,), (0,)), ((), ()))):
    return lax.dot_general(a, b, dims, preferred_element_type=F32)


def probs_kernel(blk, n_back, core_ref, low_ref, q_own, q_other, do_own, do_other, *refs):
    n_arr = n_back + 1
    k_refs = refs[:n_arr]
    e_ref, inv_ref, dot_ref = refs[n_arr : n_arr + 3]
    dv_refs = refs[n_arr + 3 : 2 * n_arr + 3]
    bias, s_scr, dv_acc, q_buf, do_buf = refs[2 * n_arr + 3 :]
    span_blocks = WINDOW // blk + 1
    core = core_ref[0]

    @pl.when(pl.program_id(0) == 0)
    def _():
        for qb in range(2):
            kpos = lax.broadcasted_iota(jnp.int32, (span_blocks * blk, blk), 0) + qb * blk
            qpos = lax.broadcasted_iota(jnp.int32, (span_blocks * blk, blk), 1) + (qb * blk + WINDOW)
            low = low_ref[:, qb * blk : (qb + 1) * blk]
            ok = (kpos >= low) & (kpos <= qpos)
            bias[qb] = jnp.where(ok, 0.0, NEG)

    q_buf[core] = q_own[...]
    q_buf[1 - core] = q_other[...]
    do_buf[core] = do_own[...]
    do_buf[1 - core] = do_other[...]

    def key_block(j):
        return k_refs[j // 2][(j % 2) * blk : (j % 2 + 1) * blk, :]

    def stacked(buf, qb):
        return jnp.concatenate([buf[qb, :, r * HD : (r + 1) * HD] for r in range(GROUP)], 0)

    for qb in range(2):
        qs = stacked(q_buf, qb)
        top = None
        for j in range(span_blocks):
            s = dot(key_block(qb + j), qs, NT)
            b = bias[qb, j * blk : (j + 1) * blk, :]
            s = s * exp2_scale + jnp.concatenate([b] * GROUP, 1)
            s_scr[j] = s
            part = jnp.max(s.reshape(blk // 8, 8, GROUP * blk), axis=0)
            top = part if top is None else jnp.maximum(top, part)
        top = jnp.max(top, axis=0, keepdims=True)
        total = None
        for j in range(span_blocks):
            e = jnp.exp2(s_scr[j] - top)
            part = jnp.sum(e.reshape(blk // 8, 8, GROUP * blk), axis=0)
            total = part if total is None else total + part
            e_ref[0, qb, j * blk : (j + 1) * blk, :] = e.astype(BF16)
        inv = 1.0 / jnp.sum(total, axis=0, keepdims=True)
        inv_ref[0, qb] = inv
        do_t = (stacked(do_buf, qb).astype(F32).T * inv).astype(BF16)
        dot_ref[0, qb] = do_t
        for j in range(span_blocks):
            term = dot(e_ref[0, qb, j * blk : (j + 1) * blk, :], do_t, NT)
            at = slice((qb + j) * blk, (qb + j + 1) * blk)
            if qb == 0 or j == span_blocks - 1:
                dv_acc[at, :] = term
            else:
                dv_acc[at, :] += term
    for a in range(n_arr):
        dv_refs[a][...] = dv_acc[a * 2 * blk : (a + 1) * 2 * blk, :].astype(BF16)


def grads_kernel(blk, n_back, core_ref, e_ref, inv_ref, dot_ref, q_own, q_other, *refs):
    n_arr = n_back + 1
    k_refs = refs[:n_arr]
    v_refs = refs[n_arr : 2 * n_arr]
    out_ref, dq_ref, other_ref = refs[2 * n_arr : 2 * n_arr + 3]
    dk_refs = refs[2 * n_arr + 3 : 3 * n_arr + 3]
    dk_acc, q_buf, out_buf, dq_buf = refs[3 * n_arr + 3 :]
    span_blocks = WINDOW // blk + 1
    core = core_ref[0]

    q_buf[core] = q_own[...]
    q_buf[1 - core] = q_other[...]

    def block_of(arrays, j):
        return arrays[j // 2][(j % 2) * blk : (j % 2 + 1) * blk, :]

    for qb in range(2):
        qs = jnp.concatenate([q_buf[qb, :, r * HD : (r + 1) * HD] for r in range(GROUP)], 0)
        do_t = dot_ref[0, qb]
        out_t = None
        for j in range(span_blocks):
            e = e_ref[0, qb, j * blk : (j + 1) * blk, :]
            part = dot(block_of(v_refs, qb + j), e, TN)
            out_t = part if out_t is None else out_t + part
        out_t = (out_t * inv_ref[0, qb]).astype(BF16).astype(F32)
        delta = jnp.sum(out_t * do_t.astype(F32), axis=0, keepdims=True)
        out = out_t.T.astype(BF16)
        dq_t = None
        for j in range(span_blocks):
            e = e_ref[0, qb, j * blk : (j + 1) * blk, :].astype(F32)
            dp = dot(block_of(v_refs, qb + j), do_t)
            ds = (e * (dp - delta)).astype(BF16)
            term = dot(ds, qs)
            at = slice((qb + j) * blk, (qb + j + 1) * blk)
            if qb == 0 or j == span_blocks - 1:
                dk_acc[at, :] = term
            else:
                dk_acc[at, :] += term
            part = dot(block_of(k_refs, qb + j), ds, TN)
            dq_t = part if dq_t is None else dq_t + part
        dq = (dq_t * score_scale).T.astype(BF16)
        for r in range(GROUP):
            out_buf[qb, :, r * HD : (r + 1) * HD] = out[r * blk : (r + 1) * blk, :]
            dq_buf[qb, :, r * HD : (r + 1) * HD] = dq[r * blk : (r + 1) * blk, :]
    out_ref[...] = out_buf[core]
    dq_ref[...] = dq_buf[core]
    other_ref[0] = out_buf[1 - core]
    other_ref[1] = dq_buf[1 - core]
    for a in range(n_arr):
        dk_refs[a][...] = (dk_acc[a * 2 * blk : (a + 1) * 2 * blk, :] * score_scale).astype(BF16)


def specs_of(rows, width):
    blk = rows // 2
    heads = width // HD
    span = WINDOW + blk
    lanes = GROUP * blk
    head = pl.BlockSpec((rows, HD), lambda g, c: (0, g))
    own = pl.BlockSpec((blk, GROUP * HD), lambda g, c: (0, c[0] * heads + g))
    return blk, heads, span, lanes, head, own


def run_probs(core, low, q, q_other, do, keys, rows, width):
    blk, heads, span, lanes, head, own = specs_of(rows, width)
    n_arr = len(keys)
    return pl.pallas_call(
        functools.partial(probs_kernel, blk, n_arr - 1),
        grid_spec=pltpu.PrefetchScalarGridSpec(
            num_scalar_prefetch=1,
            grid=(heads,),
            in_specs=[
                pl.BlockSpec((1, rows), lambda g, c: (0, 0)),
                own,
                pl.BlockSpec((blk, GROUP * HD), lambda g, c: (0, g)),
                own,
                pl.BlockSpec((blk, GROUP * HD), lambda g, c: (0, heads + g)),
            ]
            + [head] * n_arr,
            out_specs=[
                pl.BlockSpec((1, 2, span, lanes), lambda g, c: (g, 0, 0, 0)),
                pl.BlockSpec((1, 2, 1, lanes), lambda g, c: (g, 0, 0, 0)),
                pl.BlockSpec((1, 2, HD, lanes), lambda g, c: (g, 0, 0, 0)),
            ]
            + [head] * n_arr,
            scratch_shapes=[
                pltpu.VMEM((2, span, blk), F32),
                pltpu.VMEM((span // blk, blk, lanes), F32),
                pltpu.VMEM((WINDOW + rows, HD), F32),
                pltpu.VMEM((2, blk, GROUP * HD), BF16),
                pltpu.VMEM((2, blk, GROUP * HD), BF16),
            ],
        ),
        out_shape=[
            jax.ShapeDtypeStruct((heads, 2, span, lanes), BF16),
            jax.ShapeDtypeStruct((heads, 2, 1, lanes), F32),
            jax.ShapeDtypeStruct((heads, 2, HD, lanes), BF16),
        ]
        + [jax.ShapeDtypeStruct((rows, width), BF16)] * n_arr,
        compiler_params=pltpu.CompilerParams(vmem_limit_bytes=40 * 1024 * 1024),
        cost_estimate=small_cost(),
        name="probs",
    )(core, low, q, q_other, do, q_other, *keys)


def run_grads(core, e, inv, do_t, q, q_other, keys, values, rows, width, head_range, earlier):
    blk, heads, span, lanes, _, _ = specs_of(rows, width)
    n_arr = len(keys)
    low, high = head_range
    full = jax.ShapeDtypeStruct(q.shape, BF16)
    head = pl.BlockSpec((rows, HD), lambda g, c: (0, low + g))
    own = pl.BlockSpec((blk, GROUP * HD), lambda g, c: (0, c[0] * heads + low + g))
    n_in = 5 + 2 * n_arr

    def kernel(*refs):
        grads_kernel(blk, n_arr - 1, *refs[: 1 + n_in], *refs[1 + n_in + len(earlier) :])

    return pl.pallas_call(
        kernel,
        grid_spec=pltpu.PrefetchScalarGridSpec(
            num_scalar_prefetch=1,
            grid=(high - low,),
            in_specs=[
                pl.BlockSpec((1, 2, span, lanes), lambda g, c: (low + g, 0, 0, 0)),
                pl.BlockSpec((1, 2, 1, lanes), lambda g, c: (low + g, 0, 0, 0)),
                pl.BlockSpec((1, 2, HD, lanes), lambda g, c: (low + g, 0, 0, 0)),
                own,
                pl.BlockSpec((blk, GROUP * HD), lambda g, c: (0, low + g)),
            ]
            + [head] * (2 * n_arr)
            + [pl.BlockSpec(memory_space=pl.ANY)] * len(earlier),
            out_specs=[own, own, pl.BlockSpec((2, blk, GROUP * HD), lambda g, c: (0, 0, low + g))] + [head] * n_arr,
            scratch_shapes=[
                pltpu.VMEM((WINDOW + rows, HD), F32),
                pltpu.VMEM((2, blk, GROUP * HD), BF16),
                pltpu.VMEM((2, blk, GROUP * HD), BF16),
                pltpu.VMEM((2, blk, GROUP * HD), BF16),
            ],
        ),
        out_shape=[full, full, jax.ShapeDtypeStruct((2, blk, GROUP * width), BF16)]
        + [jax.ShapeDtypeStruct((rows, width), BF16)] * n_arr,
        input_output_aliases={1 + n_in + i: i for i in range(len(earlier))},
        compiler_params=pltpu.CompilerParams(vmem_limit_bytes=40 * 1024 * 1024),
        cost_estimate=small_cost(),
        name="grads",
    )(core, e, inv, do_t, q, q_other, *keys, *values, *earlier)


def small_cost():
    return pl.CostEstimate(flops=1 << 20, bytes_accessed=1 << 12, transcendentals=0)


def whole():
    return pl.BlockSpec(memory_space=pltpu.VMEM)


def pieces_kernel(dims, at_ref, x_ref, *refs):
    n_z, n_fsdp, out_rows = dims
    outs = refs[: 2 * n_fsdp]
    turned = refs[2 * n_fsdp]
    my_y, my_fsdp = at_ref[0], at_ref[1]
    for c in range(x_ref.shape[1] // HD):
        turned[c * HD : (c + 1) * HD, :] = x_ref[:, c * HD : (c + 1) * HD].astype(F32).T
    for p, out in enumerate(outs):
        flip, s = p // n_fsdp, p % n_fsdp
        y = lax.rem(my_y + flip, 2)
        f = lax.rem(my_fsdp + s, n_fsdp)
        for z in range(n_z):
            parts = []
            for core in range(2):
                block = ((z * 2 + y) * 2 + core) * n_fsdp + f
                parts.append(turned[pl.ds(pl.multiple_of(block * out_rows, 8), out_rows), :])
            out[z * 2 * out_rows : (z + 1) * 2 * out_rows, :] = jnp.concatenate(parts, 0).astype(BF16)


def run_pieces(at, tokens, n_z, n_fsdp, out_rows):
    rows, model = tokens.shape
    shape = jax.ShapeDtypeStruct((n_z * 2 * out_rows, rows), BF16)
    return pl.pallas_call(
        functools.partial(pieces_kernel, (n_z, n_fsdp, out_rows)),
        in_specs=[pl.BlockSpec(memory_space=pltpu.SMEM), whole()],
        out_specs=[whole()] * (2 * n_fsdp),
        out_shape=[shape] * (2 * n_fsdp),
        scratch_shapes=[pltpu.VMEM((model, rows), F32)],
        compiler_params=pltpu.CompilerParams(vmem_limit_bytes=32 * 1024 * 1024),
        cost_estimate=small_cost(),
        name="pieces",
    )(at, tokens)


def product_kernel(at_ref, x_ref, w_ref, o_ref):
    o_ref[...] = dot(x_ref[...], w_ref[...]).astype(o_ref.dtype)


def run_product(at, x, w, kind):
    rows = x.shape[0]
    depth, width = w.shape
    tile = 512
    return pl.pallas_call(
        product_kernel,
        grid_spec=pltpu.PrefetchScalarGridSpec(
            num_scalar_prefetch=1,
            grid=(width // tile,),
            in_specs=[
                pl.BlockSpec((rows, depth), lambda j, at: (0, at[0])),
                pl.BlockSpec((depth, tile), lambda j, at: (0, j)),
            ],
            out_specs=pl.BlockSpec((rows, tile), lambda j, at: (0, j)),
        ),
        out_shape=jax.ShapeDtypeStruct((rows, width), kind),
        compiler_params=pltpu.CompilerParams(vmem_limit_bytes=32 * 1024 * 1024),
        cost_estimate=small_cost(),
        name="product",
    )(at, x, w)


def weight_kernel(n_z, at_ref, *refs):
    n = (len(refs) - 1 - n_z) // 2
    mine, theirs = refs[:n], refs[n]
    dv_refs = refs[n + 1 : 2 * n + 1]
    outs = refs[2 * n + 1 :]
    core, my_z = at_ref[0], at_ref[1]
    count = mine[0].shape[0] // n_z
    rows = mine[0].shape[1]
    for d, out in enumerate(outs):
        z = lax.rem(my_z + d, n_z)
        at = pl.ds(pl.multiple_of(z * count, 16), count)
        total = None
        for p in range(n):
            own = pl.ds(pl.multiple_of(core * rows, rows), rows)
            other = pl.ds(pl.multiple_of((1 - core) * rows, rows), rows)
            term = dot(mine[p][at, :], dv_refs[p][own, :])
            term = term + dot(theirs[at, p * rows : (p + 1) * rows], dv_refs[p][other, :])
            total = term if total is None else total + term
        out[...] = total.astype(out.dtype)


def run_weight(at, mine, theirs, dv_places, n_z):
    count = theirs.shape[0] // n_z
    width = dv_places[0].shape[1]
    shapes = [jax.ShapeDtypeStruct((count, width), F32 if d == 0 else BF16) for d in range(n_z)]
    return pl.pallas_call(
        functools.partial(weight_kernel, n_z),
        in_specs=[pl.BlockSpec(memory_space=pltpu.SMEM)] + [whole()] * (2 * len(mine) + 1),
        out_specs=[whole()] * n_z,
        out_shape=shapes,
        compiler_params=pltpu.CompilerParams(vmem_limit_bytes=40 * 1024 * 1024),
        cost_estimate=small_cost(),
        name="weight",
    )(at, *mine, theirs, *dv_places)


def tokens_kernel(n_fsdp, at_ref, dv_ref, w_ref, own_ref, *others):
    made = dot(dv_ref[...], w_ref[...], NT).astype(BF16)
    rows = own_ref.shape[0]
    own_ref[...] = made[:rows]
    for s, ref in enumerate(others):
        ref[...] = made[(s + 1) * rows : (s + 2) * rows]


def run_tokens(at, dv_rows, w, n_fsdp):
    slab, width = w.shape
    rows = dv_rows.shape[0] // n_fsdp
    tile = slab // 3 if slab % (3 * HD) == 0 else slab
    n_tiles = slab // tile
    return pl.pallas_call(
        functools.partial(tokens_kernel, n_fsdp),
        grid_spec=pltpu.PrefetchScalarGridSpec(
            num_scalar_prefetch=1,
            grid=(n_tiles,),
            in_specs=[
                pl.BlockSpec(dv_rows.shape, lambda j, at: (0, 0)),
                pl.BlockSpec((tile, width), lambda j, at: (j, 0)),
            ],
            out_specs=[pl.BlockSpec((rows, tile), lambda j, at: (0, at[0] * n_tiles + j))]
            + [pl.BlockSpec((rows, tile), lambda j, at: (0, j))] * (n_fsdp - 1),
        ),
        out_shape=[jax.ShapeDtypeStruct((rows, slab * n_fsdp), BF16)]
        + [jax.ShapeDtypeStruct((rows, slab), BF16)] * (n_fsdp - 1),
        compiler_params=pltpu.CompilerParams(vmem_limit_bytes=40 * 1024 * 1024),
        cost_estimate=small_cost(),
        name="tokens",
    )(at, dv_rows, w)


def shifted(x, by):
    length = lax.axis_size("ctx")
    return lax.ppermute(x, "ctx", [(i, i + by) for i in range(length) if 0 <= i + by < length])


def swapped(x):
    return lax.ppermute(x, "ctx", [(i, i ^ 1) for i in range(lax.axis_size("ctx"))])


def rotated(x, by):
    length = lax.axis_size("fsdp")
    return lax.ppermute(x, "fsdp", [(i, (i + by) % length) for i in range(length)])


def moved(x, flip, by):
    n_ctx, n_fsdp = lax.axis_size("ctx"), lax.axis_size("fsdp")
    pairs = [
        (c * n_fsdp + f, (c ^ (2 * flip)) * n_fsdp + (f + by) % n_fsdp)
        for c in range(n_ctx)
        for f in range(n_fsdp)
    ]
    return lax.ppermute(x, ("ctx", "fsdp"), pairs)


def cols(x, at, width):
    return lax.dynamic_slice_in_dim(x, at * width, width, x.ndim - 1)


def rows_of(x, at, count):
    return lax.dynamic_slice_in_dim(x, at * count, count, 0)


def placed(core, own, other, axis):
    both = jnp.concatenate([own, own], axis)
    return lax.dynamic_update_slice_in_dim(both, other, (1 - core) * own.shape[axis], axis)


def after(x, *earlier):
    return lax.optimization_barrier((x, *earlier))[0]


def shards(hidden, queries, key_heads, w_value, d_out, segments):
    shard_rows = hidden.shape[1]
    model = hidden.shape[2]
    kv_width = w_value.shape[1]
    n_ctx = lax.axis_size("ctx")
    n_fsdp = lax.axis_size("fsdp")
    chip_rows = 2 * shard_rows
    n_back = WINDOW // chip_rows
    n_z = n_ctx // 4
    my_ctx = lax.axis_index("ctx")
    my_fsdp = lax.axis_index("fsdp")
    core = my_ctx % 2
    core_arg = core.astype(jnp.int32).reshape(1)
    chip = my_ctx // 2
    my_y = chip % 2
    my_z = chip // 2
    half_kv = kv_width // 2
    slab = model // n_fsdp
    tokens = hidden[0]
    first = chip * chip_rows

    own_tags = segments[0].astype(BF16)
    tag_row = lax.dynamic_update_slice_in_dim(jnp.zeros((half_kv,), BF16), own_tags, core * shard_rows, 0)
    tag_rows = jnp.concatenate([tag_row[None], jnp.zeros((15, half_kv), BF16)], 0)
    k_sent = jnp.concatenate([cols(key_heads[0], 1 - core, half_kv), tag_rows], 0)
    got = swapped(k_sent)

    slabs = [after(cols(tokens, (my_fsdp + s) % n_fsdp, slab), k_sent) for s in range(1, n_fsdp)]
    sent = [rotated(x, s + 1) for s, x in enumerate(slabs)]
    half_q = queries.shape[2] // 2
    q_sent = jnp.concatenate([cols(queries[0], 1 - core, half_q), cols(d_out[0], 1 - core, half_q)], 1)
    q_other = swapped(after(q_sent, *slabs))

    k_own = jnp.concatenate(
        [
            placed(core, cols(key_heads[0], core, half_kv), got[:shard_rows], 0),
            tag_rows + got[shard_rows:],
        ],
        0,
    )
    keys = [shifted(k_own, 2 * d) for d in range(n_back, 0, -1)] + [k_own]
    aligned = slab % HD == 0
    fsdp_arg = my_fsdp.astype(jnp.int32).reshape(1)
    zero_arg = jnp.zeros((1,), jnp.int32)
    if aligned:
        value_own = run_product(after(fsdp_arg, k_own), tokens, w_value, F32)
    else:
        value_own = dot(cols(tokens, my_fsdp, slab), w_value)

    out_rows = model // (n_ctx * n_fsdp)
    places = [(flip, s) for flip in range(2) for s in range(n_fsdp)]
    if out_rows % 8 == 0:
        at = jnp.stack([my_y, my_fsdp]).astype(jnp.int32)
        pieces = run_pieces(after(at, k_own), tokens, n_z, n_fsdp, out_rows)
    else:
        by_place = tokens.T.reshape(n_z, 2, 2, n_fsdp, out_rows, shard_rows)
        pieces = []
        for flip, s in places:
            piece = lax.dynamic_index_in_dim(by_place, my_y ^ flip, 1, keepdims=False)
            piece = lax.dynamic_index_in_dim(piece, (my_fsdp + s) % n_fsdp, 2, keepdims=False)
            pieces.append(piece.reshape(n_z * 2 * out_rows, shard_rows))

    span_tags = jnp.concatenate([k[chip_rows, :chip_rows] for k in keys], 0)
    key_at = jnp.arange(WINDOW + chip_rows, dtype=jnp.int32)
    chip_tags = keys[n_back][chip_rows, :chip_rows]
    before = (span_tags[None, :] < chip_tags[:, None]) | (key_at + first < WINDOW)[None, :]
    low = jnp.sum(before.astype(jnp.int32), axis=1)
    low = jnp.maximum(low, jnp.arange(1, chip_rows + 1, dtype=jnp.int32))[None, :]

    if aligned:
        partial = [run_product(zero_arg, x, w_value, BF16) for x in sent]
    else:
        partial = [dot(x, w_value).astype(BF16) for x in sent]
    low = after(low, value_own, *pieces, *partial)
    e, inv, do_t, *dv_terms = run_probs(
        core_arg, low, queries[0], q_other, d_out[0], keys, chip_rows, half_kv
    )
    dv_back = [shifted(dv_terms[n_back - d], -2 * d) for d in range(1, n_back + 1)]

    value_back = [rotated(x, -s - 1) for s, x in enumerate(partial)]
    *value_back, _ = lax.optimization_barrier((*value_back, dv_terms[n_back]))
    value_sum = value_own
    for x in value_back:
        value_sum = value_sum + x.astype(F32)
    own_values = value_sum.astype(BF16)
    v_own = placed(core, cols(own_values, core, half_kv), swapped(cols(own_values, 1 - core, half_kv)), 0)
    vals = [shifted(v_own, 2 * d) for d in range(n_back, 0, -1)] + [v_own]

    *pieces, _ = lax.optimization_barrier((*pieces, partial))
    pieces = [moved(x, flip, s) if flip or s else x for x, (flip, s) in zip(pieces, places)]
    *pieces, _ = lax.optimization_barrier((*pieces, v_own))
    mine = jnp.concatenate(pieces, 1)
    theirs = swapped(mine)

    *dv_back, _ = lax.optimization_barrier((*dv_back, (vals[n_back - 1], pieces)))
    dv_total = dv_terms[n_back].astype(F32)
    for term in dv_back:
        dv_total = dv_total + term.astype(F32)
    dv_chip = dv_total.astype(BF16)

    dv_places = [moved(dv_chip, flip, s) if flip or s else dv_chip for flip, s in places]
    if out_rows % 8 == 0:
        by_z = run_weight(jnp.stack([core, my_z]).astype(jnp.int32), pieces, theirs, dv_places, n_z)
    else:
        weight_term = None
        for at, dv_of in enumerate(dv_places):
            window = slice(at * shard_rows, (at + 1) * shard_rows)
            term = dot(mine[:, window], rows_of(dv_of, core, shard_rows))
            term = term + dot(theirs[:, window], rows_of(dv_of, 1 - core, shard_rows))
            weight_term = term if weight_term is None else weight_term + term
        weight_term = weight_term.reshape(n_z, 2 * out_rows, half_kv)
        by_z = [
            lax.dynamic_index_in_dim(weight_term, (my_z + d) % n_z, 0, keepdims=False).astype(BF16 if d else F32)
            for d in range(n_z)
        ]
    row_sum = by_z[0]
    for d in range(1, n_z):
        piece = lax.ppermute(by_z[d], "ctx", [(i, (i + 4 * d) % n_ctx) for i in range(n_ctx)])
        row_sum = row_sum + piece.astype(F32)
    d_weight = placed(core, rows_of(row_sum, core, out_rows), swapped(rows_of(row_sum, 1 - core, out_rows)), 1)

    dv_fsdp = [dv_places[s] for s in range(n_fsdp)]
    dv_other = swapped(jnp.concatenate([rows_of(x, 1 - core, shard_rows) for x in dv_fsdp], 0))
    dv_rows = placed(
        core, jnp.concatenate([rows_of(x, core, shard_rows) for x in dv_fsdp], 0), dv_other, 1
    )
    if aligned:
        d_tokens, *made = run_tokens(fsdp_arg, dv_rows, w_value, n_fsdp)
    else:
        made = dot(dv_rows, w_value, NT).astype(BF16)
        made = [made[s * shard_rows : (s + 1) * shard_rows] for s in range(n_fsdp)]
        d_tokens = jnp.concatenate([made[0]] * n_fsdp, 1)
        made = made[1:]
    for s in range(1, n_fsdp):
        back = rotated(made[s - 1], -s)
        d_tokens = lax.dynamic_update_slice_in_dim(d_tokens, back, ((my_fsdp + s) % n_fsdp) * slab, 1)

    n_heads = half_kv // HD
    grad_args = (e, inv, do_t, queries[0], q_other, keys, vals, chip_rows, half_kv)
    early = run_grads(core_arg, *grad_args, (0, n_heads // 2), ())
    core_late = after(core_arg, *dv_places, *made)
    out, dq, other, *dk_terms = run_grads(core_late, *grad_args, (n_heads // 2, n_heads), early)
    dk_back = [shifted(dk_terms[n_back - d], -2 * d) for d in range(1, n_back + 1)]
    *dk_back, _ = lax.optimization_barrier((*dk_back, by_z[0]))
    dk_total = dk_terms[n_back].astype(F32)
    for term in dk_back:
        dk_total = dk_total + term.astype(F32)
    dk_chip = dk_total.astype(BF16)
    d_keys = placed(core, rows_of(dk_chip, core, shard_rows), swapped(rows_of(dk_chip, 1 - core, shard_rows)), 1)
    other = swapped(other)
    out = lax.dynamic_update_slice_in_dim(out, other[0], (1 - core) * half_q, 1)
    dq = lax.dynamic_update_slice_in_dim(dq, other[1], (1 - core) * half_q, 1)
    return (out[None], dq[None], d_keys[None], d_tokens[None], d_weight)


def solution(mesh):
    in_specs = (
        P("fsdp", "ctx", None),
        P("fsdp", "ctx", None),
        P("fsdp", "ctx", None),
        P("fsdp", None),
        P("fsdp", "ctx", None),
        P("fsdp", "ctx"),
    )
    out_specs = (
        P("fsdp", "ctx", None),
        P("fsdp", "ctx", None),
        P("fsdp", "ctx", None),
        P("fsdp", "ctx", None),
        P(("ctx", "fsdp"), None),
    )
    return jax.shard_map(shards, mesh=mesh, in_specs=in_specs, out_specs=out_specs, check_vma=False)
```

```python
import functools
import math

import jax
import jax.numpy as jnp
from jax import lax
from jax.experimental import pallas as pl
from jax.experimental.pallas import tpu as pltpu
from jax.sharding import PartitionSpec as P

HQ = 16
HK = 8
HD = 128
WINDOW = 1024
GROUP = 2
NEG = -1e30

score_scale = 1.0 / math.sqrt(168.0)
exp2_scale = score_scale / math.log(2.0)

BF16 = jnp.bfloat16
F32 = jnp.float32
NT = (((1,), (1,)), ((), ()))
TN = (((0,), (0,)), ((), ()))


def dot(a, b, dims=(((1,), (0,)), ((), ()))):
    return lax.dot_general(a, b, dims, preferred_element_type=F32)


def probs_kernel(blk, n_back, core_ref, low_ref, q_own, q_other, do_own, do_other, *refs):
    n_arr = n_back + 1
    k_refs = refs[:n_arr]
    e_ref, inv_ref, dot_ref = refs[n_arr : n_arr + 3]
    dv_refs = refs[n_arr + 3 : 2 * n_arr + 3]
    bias, s_scr, dv_acc, q_buf, do_buf = refs[2 * n_arr + 3 :]
    span_blocks = WINDOW // blk + 1
    core = core_ref[0]

    @pl.when(pl.program_id(0) == 0)
    def _():
        for qb in range(2):
            kpos = lax.broadcasted_iota(jnp.int32, (span_blocks * blk, blk), 0) + qb * blk
            qpos = lax.broadcasted_iota(jnp.int32, (span_blocks * blk, blk), 1) + (qb * blk + WINDOW)
            low = low_ref[:, qb * blk : (qb + 1) * blk]
            ok = (kpos >= low) & (kpos <= qpos)
            bias[qb] = jnp.where(ok, 0.0, NEG)

    q_buf[core] = q_own[...]
    q_buf[1 - core] = q_other[...]
    do_buf[core] = do_own[...]
    do_buf[1 - core] = do_other[...]

    def key_block(j):
        return k_refs[j // 2][(j % 2) * blk : (j % 2 + 1) * blk, :]

    def stacked(buf, qb):
        return jnp.concatenate([buf[qb, :, r * HD : (r + 1) * HD] for r in range(GROUP)], 0)

    for qb in range(2):
        qs = stacked(q_buf, qb)
        top = None
        for j in range(span_blocks):
            s = dot(key_block(qb + j), qs, NT)
            b = bias[qb, j * blk : (j + 1) * blk, :]
            s = s * exp2_scale + jnp.concatenate([b] * GROUP, 1)
            s_scr[j] = s
            part = jnp.max(s.reshape(blk // 8, 8, GROUP * blk), axis=0)
            top = part if top is None else jnp.maximum(top, part)
        top = jnp.max(top, axis=0, keepdims=True)
        total = None
        for j in range(span_blocks):
            e = jnp.exp2(s_scr[j] - top)
            part = jnp.sum(e.reshape(blk // 8, 8, GROUP * blk), axis=0)
            total = part if total is None else total + part
            e_ref[0, qb, j * blk : (j + 1) * blk, :] = e.astype(BF16)
        inv = 1.0 / jnp.sum(total, axis=0, keepdims=True)
        inv_ref[0, qb] = inv
        do_t = (stacked(do_buf, qb).astype(F32).T * inv).astype(BF16)
        dot_ref[0, qb] = do_t
        for j in range(span_blocks):
            term = dot(e_ref[0, qb, j * blk : (j + 1) * blk, :], do_t, NT)
            at = slice((qb + j) * blk, (qb + j + 1) * blk)
            if qb == 0 or j == span_blocks - 1:
                dv_acc[at, :] = term
            else:
                dv_acc[at, :] += term
    for a in range(n_arr):
        dv_refs[a][...] = dv_acc[a * 2 * blk : (a + 1) * 2 * blk, :].astype(BF16)


def grads_kernel(blk, n_back, core_ref, e_ref, inv_ref, dot_ref, q_own, q_other, *refs):
    n_arr = n_back + 1
    k_refs = refs[:n_arr]
    v_refs = refs[n_arr : 2 * n_arr]
    out_ref, dq_ref, other_ref = refs[2 * n_arr : 2 * n_arr + 3]
    dk_refs = refs[2 * n_arr + 3 : 3 * n_arr + 3]
    dk_acc, q_buf, out_buf, dq_buf = refs[3 * n_arr + 3 :]
    span_blocks = WINDOW // blk + 1
    core = core_ref[0]

    q_buf[core] = q_own[...]
    q_buf[1 - core] = q_other[...]

    def block_of(arrays, j):
        return arrays[j // 2][(j % 2) * blk : (j % 2 + 1) * blk, :]

    for qb in range(2):
        qs = jnp.concatenate([q_buf[qb, :, r * HD : (r + 1) * HD] for r in range(GROUP)], 0)
        do_t = dot_ref[0, qb]
        out_t = None
        for j in range(span_blocks):
            e = e_ref[0, qb, j * blk : (j + 1) * blk, :]
            part = dot(block_of(v_refs, qb + j), e, TN)
            out_t = part if out_t is None else out_t + part
        out_t = (out_t * inv_ref[0, qb]).astype(BF16).astype(F32)
        delta = jnp.sum(out_t * do_t.astype(F32), axis=0, keepdims=True)
        out = out_t.T.astype(BF16)
        dq_t = None
        for j in range(span_blocks):
            e = e_ref[0, qb, j * blk : (j + 1) * blk, :].astype(F32)
            dp = dot(block_of(v_refs, qb + j), do_t)
            ds = (e * (dp - delta)).astype(BF16)
            term = dot(ds, qs)
            at = slice((qb + j) * blk, (qb + j + 1) * blk)
            if qb == 0 or j == span_blocks - 1:
                dk_acc[at, :] = term
            else:
                dk_acc[at, :] += term
            part = dot(block_of(k_refs, qb + j), ds, TN)
            dq_t = part if dq_t is None else dq_t + part
        dq = (dq_t * score_scale).T.astype(BF16)
        for r in range(GROUP):
            out_buf[qb, :, r * HD : (r + 1) * HD] = out[r * blk : (r + 1) * blk, :]
            dq_buf[qb, :, r * HD : (r + 1) * HD] = dq[r * blk : (r + 1) * blk, :]
    out_ref[...] = out_buf[core]
    dq_ref[...] = dq_buf[core]
    other_ref[0] = out_buf[1 - core]
    other_ref[1] = dq_buf[1 - core]
    for a in range(n_arr):
        dk_refs[a][...] = (dk_acc[a * 2 * blk : (a + 1) * 2 * blk, :] * score_scale).astype(BF16)


def specs_of(rows, width):
    blk = rows // 2
    heads = width // HD
    span = WINDOW + blk
    lanes = GROUP * blk
    head = pl.BlockSpec((rows, HD), lambda g, c: (0, g))
    own = pl.BlockSpec((blk, GROUP * HD), lambda g, c: (0, c[0] * heads + g))
    return blk, heads, span, lanes, head, own


def run_probs(core, low, q, q_other, do, keys, rows, width):
    blk, heads, span, lanes, head, own = specs_of(rows, width)
    n_arr = len(keys)
    return pl.pallas_call(
        functools.partial(probs_kernel, blk, n_arr - 1),
        grid_spec=pltpu.PrefetchScalarGridSpec(
            num_scalar_prefetch=1,
            grid=(heads,),
            in_specs=[
                pl.BlockSpec((1, rows), lambda g, c: (0, 0)),
                own,
                pl.BlockSpec((blk, GROUP * HD), lambda g, c: (0, g)),
                own,
                pl.BlockSpec((blk, GROUP * HD), lambda g, c: (0, heads + g)),
            ]
            + [head] * n_arr,
            out_specs=[
                pl.BlockSpec((1, 2, span, lanes), lambda g, c: (g, 0, 0, 0)),
                pl.BlockSpec((1, 2, 1, lanes), lambda g, c: (g, 0, 0, 0)),
                pl.BlockSpec((1, 2, HD, lanes), lambda g, c: (g, 0, 0, 0)),
            ]
            + [head] * n_arr,
            scratch_shapes=[
                pltpu.VMEM((2, span, blk), F32),
                pltpu.VMEM((span // blk, blk, lanes), F32),
                pltpu.VMEM((WINDOW + rows, HD), F32),
                pltpu.VMEM((2, blk, GROUP * HD), BF16),
                pltpu.VMEM((2, blk, GROUP * HD), BF16),
            ],
        ),
        out_shape=[
            jax.ShapeDtypeStruct((heads, 2, span, lanes), BF16),
            jax.ShapeDtypeStruct((heads, 2, 1, lanes), F32),
            jax.ShapeDtypeStruct((heads, 2, HD, lanes), BF16),
        ]
        + [jax.ShapeDtypeStruct((rows, width), BF16)] * n_arr,
        compiler_params=pltpu.CompilerParams(vmem_limit_bytes=40 * 1024 * 1024),
        cost_estimate=small_cost(),
        name="probs",
    )(core, low, q, q_other, do, q_other, *keys)


def run_grads(core, e, inv, do_t, q, q_other, keys, values, rows, width, head_range, earlier):
    blk, heads, span, lanes, _, _ = specs_of(rows, width)
    n_arr = len(keys)
    low, high = head_range
    full = jax.ShapeDtypeStruct(q.shape, BF16)
    head = pl.BlockSpec((rows, HD), lambda g, c: (0, low + g))
    own = pl.BlockSpec((blk, GROUP * HD), lambda g, c: (0, c[0] * heads + low + g))
    n_in = 5 + 2 * n_arr

    def kernel(*refs):
        grads_kernel(blk, n_arr - 1, *refs[: 1 + n_in], *refs[1 + n_in + len(earlier) :])

    return pl.pallas_call(
        kernel,
        grid_spec=pltpu.PrefetchScalarGridSpec(
            num_scalar_prefetch=1,
            grid=(high - low,),
            in_specs=[
                pl.BlockSpec((1, 2, span, lanes), lambda g, c: (low + g, 0, 0, 0)),
                pl.BlockSpec((1, 2, 1, lanes), lambda g, c: (low + g, 0, 0, 0)),
                pl.BlockSpec((1, 2, HD, lanes), lambda g, c: (low + g, 0, 0, 0)),
                own,
                pl.BlockSpec((blk, GROUP * HD), lambda g, c: (0, low + g)),
            ]
            + [head] * (2 * n_arr)
            + [pl.BlockSpec(memory_space=pl.ANY)] * len(earlier),
            out_specs=[own, own, pl.BlockSpec((2, blk, GROUP * HD), lambda g, c: (0, 0, low + g))] + [head] * n_arr,
            scratch_shapes=[
                pltpu.VMEM((WINDOW + rows, HD), F32),
                pltpu.VMEM((2, blk, GROUP * HD), BF16),
                pltpu.VMEM((2, blk, GROUP * HD), BF16),
                pltpu.VMEM((2, blk, GROUP * HD), BF16),
            ],
        ),
        out_shape=[full, full, jax.ShapeDtypeStruct((2, blk, GROUP * width), BF16)]
        + [jax.ShapeDtypeStruct((rows, width), BF16)] * n_arr,
        input_output_aliases={1 + n_in + i: i for i in range(len(earlier))},
        compiler_params=pltpu.CompilerParams(vmem_limit_bytes=40 * 1024 * 1024),
        cost_estimate=small_cost(),
        name="grads",
    )(core, e, inv, do_t, q, q_other, *keys, *values, *earlier)


def small_cost():
    return pl.CostEstimate(flops=1 << 20, bytes_accessed=1 << 12, transcendentals=0)


def whole():
    return pl.BlockSpec(memory_space=pltpu.VMEM)


def pieces_kernel(dims, at_ref, x_ref, *refs):
    n_z, n_fsdp, out_rows = dims
    outs = refs[: 2 * n_fsdp]
    turned = refs[2 * n_fsdp]
    my_y, my_fsdp = at_ref[0], at_ref[1]
    for c in range(x_ref.shape[1] // HD):
        turned[c * HD : (c + 1) * HD, :] = x_ref[:, c * HD : (c + 1) * HD].astype(F32).T
    for p, out in enumerate(outs):
        flip, s = p // n_fsdp, p % n_fsdp
        y = lax.rem(my_y + flip, 2)
        f = lax.rem(my_fsdp + s, n_fsdp)
        for z in range(n_z):
            parts = []
            for core in range(2):
                block = ((z * 2 + y) * 2 + core) * n_fsdp + f
                parts.append(turned[pl.ds(pl.multiple_of(block * out_rows, 8), out_rows), :])
            out[z * 2 * out_rows : (z + 1) * 2 * out_rows, :] = jnp.concatenate(parts, 0).astype(BF16)


def run_pieces(at, tokens, n_z, n_fsdp, out_rows):
    rows, model = tokens.shape
    shape = jax.ShapeDtypeStruct((n_z * 2 * out_rows, rows), BF16)
    return pl.pallas_call(
        functools.partial(pieces_kernel, (n_z, n_fsdp, out_rows)),
        in_specs=[pl.BlockSpec(memory_space=pltpu.SMEM), whole()],
        out_specs=[whole()] * (2 * n_fsdp),
        out_shape=[shape] * (2 * n_fsdp),
        scratch_shapes=[pltpu.VMEM((model, rows), F32)],
        compiler_params=pltpu.CompilerParams(vmem_limit_bytes=32 * 1024 * 1024),
        cost_estimate=small_cost(),
        name="pieces",
    )(at, tokens)


def product_kernel(at_ref, x_ref, w_ref, o_ref):
    o_ref[...] = dot(x_ref[...], w_ref[...]).astype(o_ref.dtype)


def run_product(at, x, w, kind):
    rows = x.shape[0]
    depth, width = w.shape
    tile = 512
    return pl.pallas_call(
        product_kernel,
        grid_spec=pltpu.PrefetchScalarGridSpec(
            num_scalar_prefetch=1,
            grid=(width // tile,),
            in_specs=[
                pl.BlockSpec((rows, depth), lambda j, at: (0, at[0])),
                pl.BlockSpec((depth, tile), lambda j, at: (0, j)),
            ],
            out_specs=pl.BlockSpec((rows, tile), lambda j, at: (0, j)),
        ),
        out_shape=jax.ShapeDtypeStruct((rows, width), kind),
        compiler_params=pltpu.CompilerParams(vmem_limit_bytes=32 * 1024 * 1024),
        cost_estimate=small_cost(),
        name="product",
    )(at, x, w)


def weight_kernel(n_z, at_ref, *refs):
    n = (len(refs) - 1 - n_z) // 2
    mine, theirs = refs[:n], refs[n]
    dv_refs = refs[n + 1 : 2 * n + 1]
    outs = refs[2 * n + 1 :]
    core, my_z = at_ref[0], at_ref[1]
    count = mine[0].shape[0] // n_z
    rows = mine[0].shape[1]
    for d, out in enumerate(outs):
        z = lax.rem(my_z + d, n_z)
        at = pl.ds(pl.multiple_of(z * count, 16), count)
        total = None
        for p in range(n):
            own = pl.ds(pl.multiple_of(core * rows, rows), rows)
            other = pl.ds(pl.multiple_of((1 - core) * rows, rows), rows)
            term = dot(mine[p][at, :], dv_refs[p][own, :])
            term = term + dot(theirs[at, p * rows : (p + 1) * rows], dv_refs[p][other, :])
            total = term if total is None else total + term
        out[...] = total.astype(out.dtype)


def run_weight(at, mine, theirs, dv_places, n_z):
    count = theirs.shape[0] // n_z
    width = dv_places[0].shape[1]
    shapes = [jax.ShapeDtypeStruct((count, width), F32 if d == 0 else BF16) for d in range(n_z)]
    return pl.pallas_call(
        functools.partial(weight_kernel, n_z),
        in_specs=[pl.BlockSpec(memory_space=pltpu.SMEM)] + [whole()] * (2 * len(mine) + 1),
        out_specs=[whole()] * n_z,
        out_shape=shapes,
        compiler_params=pltpu.CompilerParams(vmem_limit_bytes=40 * 1024 * 1024),
        cost_estimate=small_cost(),
        name="weight",
    )(at, *mine, theirs, *dv_places)


def tokens_kernel(n_fsdp, at_ref, dv_ref, w_ref, own_ref, *others):
    made = dot(dv_ref[...], w_ref[...], NT).astype(BF16)
    rows = own_ref.shape[0]
    own_ref[...] = made[:rows]
    for s, ref in enumerate(others):
        ref[...] = made[(s + 1) * rows : (s + 2) * rows]


def run_tokens(at, dv_rows, w, n_fsdp):
    slab, width = w.shape
    rows = dv_rows.shape[0] // n_fsdp
    tile = slab // 3 if slab % (3 * HD) == 0 else slab
    n_tiles = slab // tile
    return pl.pallas_call(
        functools.partial(tokens_kernel, n_fsdp),
        grid_spec=pltpu.PrefetchScalarGridSpec(
            num_scalar_prefetch=1,
            grid=(n_tiles,),
            in_specs=[
                pl.BlockSpec(dv_rows.shape, lambda j, at: (0, 0)),
                pl.BlockSpec((tile, width), lambda j, at: (j, 0)),
            ],
            out_specs=[pl.BlockSpec((rows, tile), lambda j, at: (0, at[0] * n_tiles + j))]
            + [pl.BlockSpec((rows, tile), lambda j, at: (0, j))] * (n_fsdp - 1),
        ),
        out_shape=[jax.ShapeDtypeStruct((rows, slab * n_fsdp), BF16)]
        + [jax.ShapeDtypeStruct((rows, slab), BF16)] * (n_fsdp - 1),
        compiler_params=pltpu.CompilerParams(vmem_limit_bytes=40 * 1024 * 1024),
        cost_estimate=small_cost(),
        name="tokens",
    )(at, dv_rows, w)


def shifted(x, by):
    length = lax.axis_size("ctx")
    return lax.ppermute(x, "ctx", [(i, i + by) for i in range(length) if 0 <= i + by < length])


def swapped(x):
    return lax.ppermute(x, "ctx", [(i, i ^ 1) for i in range(lax.axis_size("ctx"))])


def rotated(x, by):
    length = lax.axis_size("fsdp")
    return lax.ppermute(x, "fsdp", [(i, (i + by) % length) for i in range(length)])


def moved(x, flip, by):
    n_ctx, n_fsdp = lax.axis_size("ctx"), lax.axis_size("fsdp")
    pairs = [
        (c * n_fsdp + f, (c ^ (2 * flip)) * n_fsdp + (f + by) % n_fsdp)
        for c in range(n_ctx)
        for f in range(n_fsdp)
    ]
    return lax.ppermute(x, ("ctx", "fsdp"), pairs)


def relayed(my_y, far, got):
    return (far.astype(F32) + jnp.where(my_y == 1, got.astype(F32), 0.0)).astype(BF16)


def gathered_terms(my_y, mine, got, back):
    return (mine.astype(F32) + back.astype(F32) + jnp.where(my_y == 0, got.astype(F32), 0.0)).astype(BF16)


def cols(x, at, width):
    return lax.dynamic_slice_in_dim(x, at * width, width, x.ndim - 1)


def rows_of(x, at, count):
    return lax.dynamic_slice_in_dim(x, at * count, count, 0)


def placed(core, own, other, axis):
    both = jnp.concatenate([own, own], axis)
    return lax.dynamic_update_slice_in_dim(both, other, (1 - core) * own.shape[axis], axis)


def flipped(x):
    return lax.ppermute(x, "ctx", [(i, i ^ 2) for i in range(lax.axis_size("ctx"))])


def after(x, *earlier):
    return lax.optimization_barrier((x, *earlier))[0]


def shards(hidden, queries, key_heads, w_value, d_out, segments):
    shard_rows = hidden.shape[1]
    model = hidden.shape[2]
    kv_width = w_value.shape[1]
    n_ctx = lax.axis_size("ctx")
    n_fsdp = lax.axis_size("fsdp")
    chip_rows = 2 * shard_rows
    n_z = n_ctx // 4
    assert WINDOW == 2 * chip_rows
    my_ctx = lax.axis_index("ctx")
    my_fsdp = lax.axis_index("fsdp")
    core = my_ctx % 2
    core_arg = core.astype(jnp.int32).reshape(1)
    chip = my_ctx // 2
    my_y = chip % 2
    my_z = chip // 2
    half_kv = kv_width // 2
    slab = model // n_fsdp
    tokens = hidden[0]
    first = chip * chip_rows

    aligned = slab % HD == 0
    fsdp_arg = my_fsdp.astype(jnp.int32).reshape(1)
    zero_arg = jnp.zeros((1,), jnp.int32)
    half_q = queries.shape[2] // 2
    out_rows = model // (n_ctx * n_fsdp)
    places = [(flip, s) for flip in range(2) for s in range(n_fsdp)]

    own_tags = segments[0].astype(BF16)
    tag_row = lax.dynamic_update_slice_in_dim(jnp.zeros((half_kv,), BF16), own_tags, core * shard_rows, 0)
    tag_rows = jnp.concatenate([tag_row[None], jnp.zeros((15, half_kv), BF16)], 0)
    k_sent = jnp.concatenate([cols(key_heads[0], 1 - core, half_kv), tag_rows], 0)
    got = swapped(k_sent)

    slabs = [after(cols(tokens, (my_fsdp + s) % n_fsdp, slab), k_sent) for s in range(1, n_fsdp)]
    sent = [rotated(x, s + 1) for s, x in enumerate(slabs)]

    if out_rows % 8 == 0:
        at = jnp.stack([my_y, my_fsdp]).astype(jnp.int32)
        pieces = run_pieces(after(at, *slabs), tokens, n_z, n_fsdp, out_rows)
    else:
        turned = tokens.T.reshape(n_z, 2, 2, n_fsdp, out_rows, shard_rows)
        pieces = []
        for flip, s in places:
            piece = lax.dynamic_index_in_dim(turned, my_y ^ flip, 1, keepdims=False)
            piece = lax.dynamic_index_in_dim(piece, (my_fsdp + s) % n_fsdp, 2, keepdims=False)
            pieces.append(piece.reshape(n_z * 2 * out_rows, shard_rows))
    by_place = dict(zip(places, pieces))

    k_own = jnp.concatenate(
        [
            placed(core, cols(key_heads[0], core, half_kv), got[:shard_rows], 0),
            tag_rows + got[shard_rows:],
        ],
        0,
    )
    k_own = after(k_own, *pieces)
    k_far = shifted(k_own, 4)
    over_y = {s: flipped(after(by_place[1, s], k_own)) for s in range(1, n_fsdp)}
    q_sent = jnp.concatenate([cols(queries[0], 1 - core, half_q), cols(d_out[0], 1 - core, half_q)], 1)
    q_other = swapped(after(q_sent, k_own))
    if aligned:
        value_own = run_product(after(fsdp_arg, q_sent), tokens, w_value, F32)
    else:
        value_own = dot(cols(tokens, my_fsdp, slab), w_value)
    k_far, over_y, _ = lax.optimization_barrier((k_far, over_y, value_own))
    k_near = flipped(jnp.where(my_y == 0, k_own, k_far))
    keys = [k_far, k_near, k_own]

    span_tags = jnp.concatenate([k[chip_rows, :chip_rows] for k in keys], 0)
    key_at = jnp.arange(WINDOW + chip_rows, dtype=jnp.int32)
    chip_tags = k_own[chip_rows, :chip_rows]
    before = (span_tags[None, :] < chip_tags[:, None]) | (key_at + first < WINDOW)[None, :]
    low = jnp.sum(before.astype(jnp.int32), axis=1)
    low = jnp.maximum(low, jnp.arange(1, chip_rows + 1, dtype=jnp.int32))[None, :]

    if aligned:
        partial = [run_product(zero_arg, x, w_value, BF16) for x in sent]
    else:
        partial = [dot(x, w_value).astype(BF16) for x in sent]
    low = after(low, *partial)
    e, inv, do_t, dv_far, dv_near, dv_mine = run_probs(
        core_arg, low, queries[0], q_other, d_out[0], keys, chip_rows, half_kv
    )
    dv_got = flipped(dv_near)

    value_back = [rotated(x, -s - 1) for s, x in enumerate(partial)]
    *value_back, _ = lax.optimization_barrier((*value_back, dv_near))
    value_sum = value_own
    for x in value_back:
        value_sum = value_sum + x.astype(F32)
    own_values = value_sum.astype(BF16)
    v_own = placed(core, cols(own_values, core, half_kv), swapped(cols(own_values, 1 - core, half_kv)), 0)

    over_y[0] = flipped(after(by_place[1, 0], k_near))
    v_own, over_y[0] = lax.optimization_barrier((v_own, over_y[0]))
    v_far = shifted(v_own, 4)
    over_fsdp = {}
    for s in range(1, n_fsdp):
        both = jnp.concatenate([by_place[0, s], over_y[s]], 1)
        over_fsdp[s] = rotated(after(both, own_values), s)

    dv_got = after(dv_got, v_own)
    dv_back = shifted(relayed(my_y, dv_far, dv_got), -4)
    v_sent = jnp.where(my_y == 0, v_own, v_far)
    v_near = flipped(v_sent)
    vals = [v_far, v_near, v_own]
    dv_chip = gathered_terms(my_y, dv_mine, dv_got, after(dv_back, v_sent))
    dv_places = [moved(dv_chip, flip, s) if flip or s else dv_chip for flip, s in places]

    n_heads = half_kv // HD
    grad_args = (e, inv, do_t, queries[0], q_other, keys, vals, chip_rows, half_kv)
    early = run_grads(core_arg, *grad_args, (0, n_heads // 2), ())

    over_fsdp, dv_places, _ = lax.optimization_barrier((over_fsdp, dv_places, early[0]))
    arrived = {(0, 0): by_place[0, 0], (1, 0): over_y[0]}
    for s in range(1, n_fsdp):
        arrived[0, s] = over_fsdp[s][:, :shard_rows]
        arrived[1, s] = over_fsdp[s][:, shard_rows:]
    pieces = [arrived[place] for place in places]
    theirs = swapped(jnp.concatenate(pieces, 1))

    dv_fsdp = dv_places[:n_fsdp]
    dv_other = swapped(jnp.concatenate([rows_of(x, 1 - core, shard_rows) for x in dv_fsdp], 0))
    dv_rows = placed(
        core, jnp.concatenate([rows_of(x, core, shard_rows) for x in dv_fsdp], 0), dv_other, 1
    )
    if aligned:
        d_tokens, *made = run_tokens(fsdp_arg, dv_rows, w_value, n_fsdp)
    else:
        made = dot(dv_rows, w_value, NT).astype(BF16)
        made = [made[s * shard_rows : (s + 1) * shard_rows] for s in range(n_fsdp)]
        d_tokens = jnp.concatenate([made[0]] * n_fsdp, 1)
        made = made[1:]
    for s in range(1, n_fsdp):
        back = rotated(made[s - 1], -s)
        d_tokens = lax.dynamic_update_slice_in_dim(d_tokens, back, ((my_fsdp + s) % n_fsdp) * slab, 1)

    if out_rows % 8 == 0:
        at = after(jnp.stack([core, my_z]).astype(jnp.int32), *made)
        by_z = run_weight(at, pieces, theirs, dv_places, n_z)
    else:
        weight_term = None
        for at, dv_of in enumerate(dv_places):
            window = slice(at * shard_rows, (at + 1) * shard_rows)
            term = dot(pieces[at], rows_of(dv_of, core, shard_rows))
            term = term + dot(theirs[:, window], rows_of(dv_of, 1 - core, shard_rows))
            weight_term = term if weight_term is None else weight_term + term
        weight_term = weight_term.reshape(n_z, 2 * out_rows, half_kv)
        by_z = [
            lax.dynamic_index_in_dim(weight_term, (my_z + d) % n_z, 0, keepdims=False).astype(BF16 if d else F32)
            for d in range(n_z)
        ]
    over_z = [
        lax.ppermute(by_z[d], "ctx", [(i, (i + 4 * d) % n_ctx) for i in range(n_ctx)]) for d in range(1, n_z)
    ]

    core_late = after(core_arg, by_z[0])
    out, dq, other, dk_far, dk_near, dk_mine = run_grads(core_late, *grad_args, (n_heads // 2, n_heads), early)
    dk_got = flipped(dk_near)
    dk_sent = relayed(my_y, dk_far, dk_got)
    dk_back = shifted(dk_sent, -4)

    over_z, _ = lax.optimization_barrier((over_z, dk_sent))
    row_sum = by_z[0]
    for x in over_z:
        row_sum = row_sum + x.astype(F32)
    d_weight = placed(core, rows_of(row_sum, core, out_rows), swapped(rows_of(row_sum, 1 - core, out_rows)), 1)

    dk_chip = gathered_terms(my_y, dk_mine, dk_got, dk_back)
    d_keys = placed(core, rows_of(dk_chip, core, shard_rows), swapped(rows_of(dk_chip, 1 - core, shard_rows)), 1)
    other = swapped(other)
    out = lax.dynamic_update_slice_in_dim(out, other[0], (1 - core) * half_q, 1)
    dq = lax.dynamic_update_slice_in_dim(dq, other[1], (1 - core) * half_q, 1)
    return (out[None], dq[None], d_keys[None], d_tokens[None], d_weight)


def solution(mesh):
    in_specs = (
        P("fsdp", "ctx", None),
        P("fsdp", "ctx", None),
        P("fsdp", "ctx", None),
        P("fsdp", None),
        P("fsdp", "ctx", None),
        P("fsdp", "ctx"),
    )
    out_specs = (
        P("fsdp", "ctx", None),
        P("fsdp", "ctx", None),
        P("fsdp", "ctx", None),
        P("fsdp", "ctx", None),
        P(("ctx", "fsdp"), None),
    )
    return jax.shard_map(shards, mesh=mesh, in_specs=in_specs, out_specs=out_specs, check_vma=False)
```

```python
import functools
import math

import jax
import jax.numpy as jnp
from jax import lax
from jax.experimental import pallas as pl
from jax.experimental.pallas import tpu as pltpu
from jax.sharding import PartitionSpec as P

HQ = 16
HK = 8
HD = 128
WINDOW = 1024
GROUP = 2
NEG = -1e30

score_scale = 1.0 / math.sqrt(168.0)
exp2_scale = score_scale / math.log(2.0)

BF16 = jnp.bfloat16
F32 = jnp.float32
NT = (((1,), (1,)), ((), ()))
TN = (((0,), (0,)), ((), ()))


def dot(a, b, dims=(((1,), (0,)), ((), ()))):
    return lax.dot_general(a, b, dims, preferred_element_type=F32)


def probs_kernel(blk, n_back, core_ref, low_ref, q_own, q_other, do_own, do_other, *refs):
    n_arr = n_back + 1
    k_refs = refs[:n_arr]
    e_ref, inv_ref, dot_ref = refs[n_arr : n_arr + 3]
    dv_refs = refs[n_arr + 3 : 2 * n_arr + 3]
    bias, s_scr, dv_acc, q_buf, do_buf = refs[2 * n_arr + 3 :]
    span_blocks = WINDOW // blk + 1
    core = core_ref[0]

    @pl.when(pl.program_id(0) == 0)
    def _():
        for qb in range(2):
            kpos = lax.broadcasted_iota(jnp.int32, (span_blocks * blk, blk), 0) + qb * blk
            qpos = lax.broadcasted_iota(jnp.int32, (span_blocks * blk, blk), 1) + (qb * blk + WINDOW)
            low = low_ref[:, qb * blk : (qb + 1) * blk]
            ok = (kpos >= low) & (kpos <= qpos)
            bias[qb] = jnp.where(ok, 0.0, NEG)

    q_buf[core] = q_own[...]
    q_buf[1 - core] = q_other[...]
    do_buf[core] = do_own[...]
    do_buf[1 - core] = do_other[...]

    def key_block(j):
        return k_refs[j // 2][(j % 2) * blk : (j % 2 + 1) * blk, :]

    def stacked(buf, qb):
        return jnp.concatenate([buf[qb, :, r * HD : (r + 1) * HD] for r in range(GROUP)], 0)

    for qb in range(2):
        qs = stacked(q_buf, qb)
        top = None
        for j in range(span_blocks):
            s = dot(key_block(qb + j), qs, NT)
            b = bias[qb, j * blk : (j + 1) * blk, :]
            s = s * exp2_scale + jnp.concatenate([b] * GROUP, 1)
            s_scr[j] = s
            part = jnp.max(s.reshape(blk // 8, 8, GROUP * blk), axis=0)
            top = part if top is None else jnp.maximum(top, part)
        top = jnp.max(top, axis=0, keepdims=True)
        total = None
        for j in range(span_blocks):
            e = jnp.exp2(s_scr[j] - top)
            part = jnp.sum(e.reshape(blk // 8, 8, GROUP * blk), axis=0)
            total = part if total is None else total + part
            e_ref[0, qb, j * blk : (j + 1) * blk, :] = e.astype(BF16)
        inv = 1.0 / jnp.sum(total, axis=0, keepdims=True)
        inv_ref[0, qb] = inv
        do_t = (stacked(do_buf, qb).astype(F32).T * inv).astype(BF16)
        dot_ref[0, qb] = do_t
        for j in range(span_blocks):
            term = dot(e_ref[0, qb, j * blk : (j + 1) * blk, :], do_t, NT)
            at = slice((qb + j) * blk, (qb + j + 1) * blk)
            if qb == 0 or j == span_blocks - 1:
                dv_acc[at, :] = term
            else:
                dv_acc[at, :] += term
    for a in range(n_arr):
        dv_refs[a][...] = dv_acc[a * 2 * blk : (a + 1) * 2 * blk, :].astype(BF16)


def grads_kernel(blk, n_back, core_ref, e_ref, inv_ref, dot_ref, q_own, q_other, *refs):
    n_arr = n_back + 1
    k_refs = refs[:n_arr]
    v_refs = refs[n_arr : 2 * n_arr]
    out_ref, dq_ref, other_ref = refs[2 * n_arr : 2 * n_arr + 3]
    dk_refs = refs[2 * n_arr + 3 : 3 * n_arr + 3]
    dk_acc, q_buf, out_buf, dq_buf = refs[3 * n_arr + 3 :]
    span_blocks = WINDOW // blk + 1
    core = core_ref[0]

    q_buf[core] = q_own[...]
    q_buf[1 - core] = q_other[...]

    def block_of(arrays, j):
        return arrays[j // 2][(j % 2) * blk : (j % 2 + 1) * blk, :]

    for qb in range(2):
        qs = jnp.concatenate([q_buf[qb, :, r * HD : (r + 1) * HD] for r in range(GROUP)], 0)
        do_t = dot_ref[0, qb]
        out_t = None
        for j in range(span_blocks):
            e = e_ref[0, qb, j * blk : (j + 1) * blk, :]
            part = dot(block_of(v_refs, qb + j), e, TN)
            out_t = part if out_t is None else out_t + part
        out_t = (out_t * inv_ref[0, qb]).astype(BF16).astype(F32)
        delta = jnp.sum(out_t * do_t.astype(F32), axis=0, keepdims=True)
        out = out_t.T.astype(BF16)
        dq_t = None
        for j in range(span_blocks):
            e = e_ref[0, qb, j * blk : (j + 1) * blk, :].astype(F32)
            dp = dot(block_of(v_refs, qb + j), do_t)
            ds = (e * (dp - delta)).astype(BF16)
            term = dot(ds, qs)
            at = slice((qb + j) * blk, (qb + j + 1) * blk)
            if qb == 0 or j == span_blocks - 1:
                dk_acc[at, :] = term
            else:
                dk_acc[at, :] += term
            part = dot(block_of(k_refs, qb + j), ds, TN)
            dq_t = part if dq_t is None else dq_t + part
        dq = (dq_t * score_scale).T.astype(BF16)
        for r in range(GROUP):
            out_buf[qb, :, r * HD : (r + 1) * HD] = out[r * blk : (r + 1) * blk, :]
            dq_buf[qb, :, r * HD : (r + 1) * HD] = dq[r * blk : (r + 1) * blk, :]
    out_ref[...] = out_buf[core]
    dq_ref[...] = dq_buf[core]
    other_ref[0] = out_buf[1 - core]
    other_ref[1] = dq_buf[1 - core]
    for a in range(n_arr):
        dk_refs[a][...] = (dk_acc[a * 2 * blk : (a + 1) * 2 * blk, :] * score_scale).astype(BF16)


def specs_of(rows, width):
    blk = rows // 2
    heads = width // HD
    span = WINDOW + blk
    lanes = GROUP * blk
    head = pl.BlockSpec((rows, HD), lambda g, c: (0, g))
    own = pl.BlockSpec((blk, GROUP * HD), lambda g, c: (0, c[0] * heads + g))
    return blk, heads, span, lanes, head, own


def run_probs(core, low, q, q_other, do, keys, rows, width):
    blk, heads, span, lanes, head, own = specs_of(rows, width)
    n_arr = len(keys)
    return pl.pallas_call(
        functools.partial(probs_kernel, blk, n_arr - 1),
        grid_spec=pltpu.PrefetchScalarGridSpec(
            num_scalar_prefetch=1,
            grid=(heads,),
            in_specs=[
                pl.BlockSpec((1, rows), lambda g, c: (0, 0)),
                own,
                pl.BlockSpec((blk, GROUP * HD), lambda g, c: (0, g)),
                own,
                pl.BlockSpec((blk, GROUP * HD), lambda g, c: (0, heads + g)),
            ]
            + [head] * n_arr,
            out_specs=[
                pl.BlockSpec((1, 2, span, lanes), lambda g, c: (g, 0, 0, 0)),
                pl.BlockSpec((1, 2, 1, lanes), lambda g, c: (g, 0, 0, 0)),
                pl.BlockSpec((1, 2, HD, lanes), lambda g, c: (g, 0, 0, 0)),
            ]
            + [head] * n_arr,
            scratch_shapes=[
                pltpu.VMEM((2, span, blk), F32),
                pltpu.VMEM((span // blk, blk, lanes), F32),
                pltpu.VMEM((WINDOW + rows, HD), F32),
                pltpu.VMEM((2, blk, GROUP * HD), BF16),
                pltpu.VMEM((2, blk, GROUP * HD), BF16),
            ],
        ),
        out_shape=[
            jax.ShapeDtypeStruct((heads, 2, span, lanes), BF16),
            jax.ShapeDtypeStruct((heads, 2, 1, lanes), F32),
            jax.ShapeDtypeStruct((heads, 2, HD, lanes), BF16),
        ]
        + [jax.ShapeDtypeStruct((rows, width), BF16)] * n_arr,
        compiler_params=pltpu.CompilerParams(vmem_limit_bytes=40 * 1024 * 1024),
        cost_estimate=small_cost(),
        name="probs",
    )(core, low, q, q_other, do, q_other, *keys)


def run_grads(core, e, inv, do_t, q, q_other, keys, values, rows, width, low, high):
    blk, heads, span, lanes, _, _ = specs_of(rows, width)
    n_arr = len(keys)
    count = high - low
    head = pl.BlockSpec((rows, HD), lambda g, c: (0, low + g))
    head_out = pl.BlockSpec((rows, HD), lambda g, c: (0, g))
    group_out = pl.BlockSpec((blk, GROUP * HD), lambda g, c: (0, g))
    return pl.pallas_call(
        functools.partial(grads_kernel, blk, n_arr - 1),
        grid_spec=pltpu.PrefetchScalarGridSpec(
            num_scalar_prefetch=1,
            grid=(count,),
            in_specs=[
                pl.BlockSpec((1, 2, span, lanes), lambda g, c: (low + g, 0, 0, 0)),
                pl.BlockSpec((1, 2, 1, lanes), lambda g, c: (low + g, 0, 0, 0)),
                pl.BlockSpec((1, 2, HD, lanes), lambda g, c: (low + g, 0, 0, 0)),
                pl.BlockSpec((blk, GROUP * HD), lambda g, c: (0, c[0] * heads + low + g)),
                pl.BlockSpec((blk, GROUP * HD), lambda g, c: (0, low + g)),
            ]
            + [head] * (2 * n_arr),
            out_specs=[group_out, group_out, pl.BlockSpec((2, blk, GROUP * HD), lambda g, c: (0, 0, g))]
            + [head_out] * n_arr,
            scratch_shapes=[
                pltpu.VMEM((WINDOW + rows, HD), F32),
                pltpu.VMEM((2, blk, GROUP * HD), BF16),
                pltpu.VMEM((2, blk, GROUP * HD), BF16),
                pltpu.VMEM((2, blk, GROUP * HD), BF16),
            ],
        ),
        out_shape=[jax.ShapeDtypeStruct((blk, GROUP * HD * count), BF16)] * 2
        + [jax.ShapeDtypeStruct((2, blk, GROUP * HD * count), BF16)]
        + [jax.ShapeDtypeStruct((rows, HD * count), BF16)] * n_arr,
        compiler_params=pltpu.CompilerParams(vmem_limit_bytes=40 * 1024 * 1024),
        cost_estimate=small_cost(),
        name="grads",
    )(core, e, inv, do_t, q, q_other, *keys, *values)


def small_cost():
    return pl.CostEstimate(flops=1 << 20, bytes_accessed=1 << 12, transcendentals=0)


def whole():
    return pl.BlockSpec(memory_space=pltpu.VMEM)


def pieces_kernel(dims, at_ref, x_ref, *refs):
    n_z, n_fsdp, out_rows = dims
    outs = refs[: 2 * n_fsdp]
    turned = refs[2 * n_fsdp]
    my_y, my_fsdp = at_ref[0], at_ref[1]
    for c in range(x_ref.shape[1] // HD):
        turned[c * HD : (c + 1) * HD, :] = x_ref[:, c * HD : (c + 1) * HD].astype(F32).T
    for p, out in enumerate(outs):
        flip, s = p // n_fsdp, p % n_fsdp
        y = lax.rem(my_y + flip, 2)
        f = lax.rem(my_fsdp + s, n_fsdp)
        for z in range(n_z):
            parts = []
            for core in range(2):
                block = ((z * 2 + y) * 2 + core) * n_fsdp + f
                parts.append(turned[pl.ds(pl.multiple_of(block * out_rows, 8), out_rows), :])
            out[z * 2 * out_rows : (z + 1) * 2 * out_rows, :] = jnp.concatenate(parts, 0).astype(BF16)


def run_pieces(at, tokens, n_z, n_fsdp, out_rows):
    rows, model = tokens.shape
    shape = jax.ShapeDtypeStruct((n_z * 2 * out_rows, rows), BF16)
    return pl.pallas_call(
        functools.partial(pieces_kernel, (n_z, n_fsdp, out_rows)),
        in_specs=[pl.BlockSpec(memory_space=pltpu.SMEM), whole()],
        out_specs=[whole()] * (2 * n_fsdp),
        out_shape=[shape] * (2 * n_fsdp),
        scratch_shapes=[pltpu.VMEM((model, rows), F32)],
        compiler_params=pltpu.CompilerParams(vmem_limit_bytes=32 * 1024 * 1024),
        cost_estimate=small_cost(),
        name="pieces",
    )(at, tokens)


def product_kernel(at_ref, x_ref, w_ref, o_ref):
    o_ref[...] = dot(x_ref[...], w_ref[...]).astype(o_ref.dtype)


def run_product(at, x, w, kind):
    rows = x.shape[0]
    depth, width = w.shape
    tile = 512
    return pl.pallas_call(
        product_kernel,
        grid_spec=pltpu.PrefetchScalarGridSpec(
            num_scalar_prefetch=1,
            grid=(width // tile,),
            in_specs=[
                pl.BlockSpec((rows, depth), lambda j, at: (0, at[0])),
                pl.BlockSpec((depth, tile), lambda j, at: (0, j)),
            ],
            out_specs=pl.BlockSpec((rows, tile), lambda j, at: (0, j)),
        ),
        out_shape=jax.ShapeDtypeStruct((rows, width), kind),
        compiler_params=pltpu.CompilerParams(vmem_limit_bytes=32 * 1024 * 1024),
        cost_estimate=small_cost(),
        name="product",
    )(at, x, w)


def weight_kernel(n_z, n, at_ref, *refs):
    own_pairs, other_pairs = refs[:n], refs[n : 2 * n]
    dv_refs = refs[2 * n : 4 * n]
    outs = refs[4 * n :]
    core = at_ref[0]
    step = pl.program_id(0)
    rows = own_pairs[0].shape[1] // 2
    own = pl.ds(pl.multiple_of(core * rows, rows), rows)
    other = pl.ds(pl.multiple_of((1 - core) * rows, rows), rows)
    total = None
    for p in range(n):
        for flip in range(2):
            window = slice(flip * rows, (flip + 1) * rows)
            term = dot(own_pairs[p][:, window], dv_refs[2 * p + flip][own, :])
            term = term + dot(other_pairs[p][:, window], dv_refs[2 * p + flip][other, :])
            total = term if total is None else total + term
    for d, out in enumerate(outs):

        @pl.when(step == (n_z - 1 if d == 0 else d - 1))
        def _():
            out[...] = total.astype(out.dtype)


def run_weight(at, own_pairs, other_pairs, dv_pairs, n_z):
    n = len(own_pairs)
    count = own_pairs[0].shape[0] // n_z
    rows2 = own_pairs[0].shape[1]
    dvs = [x for pair_of in dv_pairs for x in pair_of]
    width = dvs[0].shape[1]
    shapes = [jax.ShapeDtypeStruct((count, width), F32 if d == 0 else BF16) for d in range(n_z)]
    pair_block = pl.BlockSpec((count, rows2), lambda d, at: (lax.rem(at[1] + d + 1, n_z), 0))
    return pl.pallas_call(
        functools.partial(weight_kernel, n_z, n),
        grid_spec=pltpu.PrefetchScalarGridSpec(
            num_scalar_prefetch=1,
            grid=(n_z,),
            in_specs=[pair_block] * (2 * n) + [pl.BlockSpec(dvs[0].shape, lambda d, at: (0, 0))] * (2 * n),
            out_specs=[pl.BlockSpec((count, width), lambda d, at: (0, 0))] * n_z,
        ),
        out_shape=shapes,
        compiler_params=pltpu.CompilerParams(vmem_limit_bytes=40 * 1024 * 1024),
        cost_estimate=small_cost(),
        name="weight",
    )(at, *own_pairs, *other_pairs, *dvs)


def tokens_kernel(n_fsdp, at_ref, dv_ref, w_ref, own_ref, *others):
    made = dot(dv_ref[...], w_ref[...], NT).astype(BF16)
    rows = own_ref.shape[0]
    own_ref[...] = made[:rows]
    for s, ref in enumerate(others):
        ref[...] = made[(s + 1) * rows : (s + 2) * rows]


def run_tokens(at, dv_rows, w, n_fsdp):
    slab, width = w.shape
    rows = dv_rows.shape[0] // n_fsdp
    tile = slab // 3 if slab % (3 * HD) == 0 else slab
    n_tiles = slab // tile
    return pl.pallas_call(
        functools.partial(tokens_kernel, n_fsdp),
        grid_spec=pltpu.PrefetchScalarGridSpec(
            num_scalar_prefetch=1,
            grid=(n_tiles,),
            in_specs=[
                pl.BlockSpec(dv_rows.shape, lambda j, at: (0, 0)),
                pl.BlockSpec((tile, width), lambda j, at: (j, 0)),
            ],
            out_specs=[pl.BlockSpec((rows, tile), lambda j, at: (0, at[0] * n_tiles + j))]
            + [pl.BlockSpec((rows, tile), lambda j, at: (0, j))] * (n_fsdp - 1),
        ),
        out_shape=[jax.ShapeDtypeStruct((rows, slab * n_fsdp), BF16)]
        + [jax.ShapeDtypeStruct((rows, slab), BF16)] * (n_fsdp - 1),
        compiler_params=pltpu.CompilerParams(vmem_limit_bytes=40 * 1024 * 1024),
        cost_estimate=small_cost(),
        name="tokens",
    )(at, dv_rows, w)


def shifted(x, by):
    length = lax.axis_size("ctx")
    return lax.ppermute(x, "ctx", [(i, i + by) for i in range(length) if 0 <= i + by < length])


def swapped(x):
    return lax.ppermute(x, "ctx", [(i, i ^ 1) for i in range(lax.axis_size("ctx"))])


def rotated(x, by):
    length = lax.axis_size("fsdp")
    return lax.ppermute(x, "fsdp", [(i, (i + by) % length) for i in range(length)])


def moved(x, flip, by):
    n_ctx, n_fsdp = lax.axis_size("ctx"), lax.axis_size("fsdp")
    pairs = [
        (c * n_fsdp + f, (c ^ (2 * flip)) * n_fsdp + (f + by) % n_fsdp)
        for c in range(n_ctx)
        for f in range(n_fsdp)
    ]
    return lax.ppermute(x, ("ctx", "fsdp"), pairs)


def relayed(my_y, far, got):
    return (far.astype(F32) + jnp.where(my_y == 1, got.astype(F32), 0.0)).astype(BF16)


def gathered_terms(my_y, mine, got, back):
    return (mine.astype(F32) + back.astype(F32) + jnp.where(my_y == 0, got.astype(F32), 0.0)).astype(BF16)


def cols(x, at, width):
    return lax.dynamic_slice_in_dim(x, at * width, width, x.ndim - 1)


def rows_of(x, at, count):
    return lax.dynamic_slice_in_dim(x, at * count, count, 0)


def placed(core, own, other, axis):
    both = jnp.concatenate([own, own], axis)
    return lax.dynamic_update_slice_in_dim(both, other, (1 - core) * own.shape[axis], axis)


def flipped(x):
    return lax.ppermute(x, "ctx", [(i, i ^ 2) for i in range(lax.axis_size("ctx"))])


def after(x, *earlier):
    return lax.optimization_barrier((x, *earlier))[0]


def shards(hidden, queries, key_heads, w_value, d_out, segments):
    shard_rows = hidden.shape[1]
    model = hidden.shape[2]
    kv_width = w_value.shape[1]
    n_ctx = lax.axis_size("ctx")
    n_fsdp = lax.axis_size("fsdp")
    chip_rows = 2 * shard_rows
    n_z = n_ctx // 4
    assert WINDOW == 2 * chip_rows
    my_ctx = lax.axis_index("ctx")
    my_fsdp = lax.axis_index("fsdp")
    core = my_ctx % 2
    core_arg = core.astype(jnp.int32).reshape(1)
    chip = my_ctx // 2
    my_y = chip % 2
    my_z = chip // 2
    half_kv = kv_width // 2
    slab = model // n_fsdp
    tokens = hidden[0]
    first = chip * chip_rows

    aligned = slab % HD == 0
    fsdp_arg = my_fsdp.astype(jnp.int32).reshape(1)
    zero_arg = jnp.zeros((1,), jnp.int32)
    half_q = queries.shape[2] // 2
    out_rows = model // (n_ctx * n_fsdp)
    places = [(flip, s) for flip in range(2) for s in range(n_fsdp)]

    slabs = [cols(tokens, (my_fsdp + s) % n_fsdp, slab) for s in range(1, n_fsdp)]
    sent = [rotated(x, s + 1) for s, x in enumerate(slabs)]

    own_tags = segments[0].astype(BF16)
    tag_row = lax.dynamic_update_slice_in_dim(jnp.zeros((half_kv,), BF16), own_tags, core * shard_rows, 0)
    tag_rows = jnp.concatenate([tag_row[None], jnp.zeros((15, half_kv), BF16)], 0)
    k_sent = jnp.concatenate([cols(key_heads[0], 1 - core, half_kv), tag_rows], 0)
    got = swapped(after(k_sent, *slabs))

    if out_rows % 8 == 0:
        at = jnp.stack([my_y, my_fsdp]).astype(jnp.int32)
        pieces = run_pieces(after(at, k_sent), tokens, n_z, n_fsdp, out_rows)
    else:
        turned = tokens.T.reshape(n_z, 2, 2, n_fsdp, out_rows, shard_rows)
        pieces = []
        for flip, s in places:
            piece = lax.dynamic_index_in_dim(turned, my_y ^ flip, 1, keepdims=False)
            piece = lax.dynamic_index_in_dim(piece, (my_fsdp + s) % n_fsdp, 2, keepdims=False)
            pieces.append(piece.reshape(n_z * 2 * out_rows, shard_rows))
    by_place = dict(zip(places, pieces))

    k_own = jnp.concatenate(
        [
            placed(core, cols(key_heads[0], core, half_kv), got[:shard_rows], 0),
            tag_rows + got[shard_rows:],
        ],
        0,
    )
    k_own = after(k_own, *pieces)
    k_far = shifted(k_own, 4)
    over_y = {s: flipped(after(by_place[1, s], k_own)) for s in range(1, n_fsdp)}
    q_sent = jnp.concatenate([cols(queries[0], 1 - core, half_q), cols(d_out[0], 1 - core, half_q)], 1)
    q_other = swapped(after(q_sent, k_own))
    if aligned:
        value_own = run_product(after(fsdp_arg, q_sent), tokens, w_value, F32)
    else:
        value_own = dot(cols(tokens, my_fsdp, slab), w_value)
    k_far, over_y, _ = lax.optimization_barrier((k_far, over_y, value_own))
    k_near = flipped(jnp.where(my_y == 0, k_own, k_far))
    keys = [k_far, k_near, k_own]

    span_tags = jnp.concatenate([k[chip_rows, :chip_rows] for k in keys], 0)
    key_at = jnp.arange(WINDOW + chip_rows, dtype=jnp.int32)
    chip_tags = k_own[chip_rows, :chip_rows]
    before = (span_tags[None, :] < chip_tags[:, None]) | (key_at + first < WINDOW)[None, :]
    low = jnp.sum(before.astype(jnp.int32), axis=1)
    low = jnp.maximum(low, jnp.arange(1, chip_rows + 1, dtype=jnp.int32))[None, :]

    if aligned:
        partial = [run_product(zero_arg, x, w_value, BF16) for x in sent]
    else:
        partial = [dot(x, w_value).astype(BF16) for x in sent]
    low = after(low, *partial)
    e, inv, do_t, dv_far, dv_near, dv_mine = run_probs(
        core_arg, low, queries[0], q_other, d_out[0], keys, chip_rows, half_kv
    )
    dv_got = flipped(dv_near)

    value_back = [rotated(x, -s - 1) for s, x in enumerate(partial)]
    *value_back, _ = lax.optimization_barrier((*value_back, dv_near))
    value_sum = value_own
    for x in value_back:
        value_sum = value_sum + x.astype(F32)
    own_values = value_sum.astype(BF16)
    v_own = placed(core, cols(own_values, core, half_kv), swapped(cols(own_values, 1 - core, half_kv)), 0)

    over_y[0] = flipped(after(by_place[1, 0], k_near))
    v_own, over_y[0] = lax.optimization_barrier((v_own, over_y[0]))
    v_far = shifted(v_own, 4)
    own_pairs = [jnp.concatenate([by_place[0, 0], over_y[0]], 1)]
    other_pairs = [swapped(after(own_pairs[0], v_own))]
    for s in range(1, n_fsdp):
        both = jnp.concatenate([by_place[0, s], over_y[s]], 1)
        own_pairs.append(rotated(after(both, own_values), s))

    dv_got = after(dv_got, v_own)
    dv_back = shifted(relayed(my_y, dv_far, dv_got), -4)
    v_sent = jnp.where(my_y == 0, v_own, v_far)
    v_near = flipped(v_sent)
    vals = [v_far, v_near, v_own]
    dv_chip = gathered_terms(my_y, dv_mine, dv_got, after(dv_back, v_sent))
    dv_fsdp = [dv_chip] + [rotated(dv_chip, s) for s in range(1, n_fsdp)]
    dv_over_y = [flipped(dv_chip)]
    n_heads = half_kv // HD
    grad_args = (e, inv, do_t, queries[0], q_other, keys, vals, chip_rows, half_kv)
    early = run_grads(after(core_arg, *own_pairs), *grad_args, 0, n_heads // 2)
    dv_fsdp[1:], dv_over_y[0], _ = lax.optimization_barrier((dv_fsdp[1:], dv_over_y[0], early[0]))
    dv_over_y += [flipped(x) for x in dv_fsdp[1:]]
    core_late = after(core_arg, dv_over_y[0], *dv_fsdp)
    late = run_grads(core_late, *grad_args, n_heads // 2, n_heads)
    dk_got = [flipped(early[4]), flipped(late[4])]

    dv_other = swapped(jnp.concatenate([rows_of(x, 1 - core, shard_rows) for x in dv_fsdp], 0))
    dv_rows = placed(
        core, jnp.concatenate([rows_of(x, core, shard_rows) for x in dv_fsdp], 0), dv_other, 1
    )
    other_pairs += [swapped(after(x, early[0])) for x in own_pairs[1:]]
    dv_rows, dv_over_y, _ = lax.optimization_barrier((dv_rows, dv_over_y, late[0]))
    if aligned:
        d_tokens, *made = run_tokens(fsdp_arg, dv_rows, w_value, n_fsdp)
    else:
        made = dot(dv_rows, w_value, NT).astype(BF16)
        made = [made[s * shard_rows : (s + 1) * shard_rows] for s in range(n_fsdp)]
        d_tokens = jnp.concatenate([made[0]] * n_fsdp, 1)
        made = made[1:]
    for s in range(1, n_fsdp):
        back = rotated(made[s - 1], -s)
        d_tokens = lax.dynamic_update_slice_in_dim(d_tokens, back, ((my_fsdp + s) % n_fsdp) * slab, 1)

    dv_pairs = list(zip(dv_fsdp, dv_over_y))
    if out_rows % 8 == 0:
        at = after(jnp.stack([core, my_z]).astype(jnp.int32), *made)
        by_z = run_weight(at, own_pairs, other_pairs, dv_pairs, n_z)
    else:
        weight_term = 0.0
        for p in range(n_fsdp):
            for flip in range(2):
                window = slice(flip * shard_rows, (flip + 1) * shard_rows)
                weight_term += dot(own_pairs[p][:, window], rows_of(dv_pairs[p][flip], core, shard_rows))
                weight_term += dot(other_pairs[p][:, window], rows_of(dv_pairs[p][flip], 1 - core, shard_rows))
        weight_term = weight_term.reshape(n_z, 2 * out_rows, half_kv)
        by_z = [
            lax.dynamic_index_in_dim(weight_term, (my_z + d) % n_z, 0, keepdims=False).astype(BF16 if d else F32)
            for d in range(n_z)
        ]
    over_z = [
        lax.ppermute(by_z[d], "ctx", [(i, (i + 4 * d) % n_ctx) for i in range(n_ctx)]) for d in range(1, n_z)
    ]

    *dk_got, _ = lax.optimization_barrier((*dk_got, by_z[0]))
    dk_got, dk_far, dk_mine = [jnp.concatenate(x, 1) for x in (dk_got, (early[3], late[3]), (early[5], late[5]))]
    dk_sent = relayed(my_y, dk_far, dk_got)
    dk_back = shifted(dk_sent, -4)

    over_z, _ = lax.optimization_barrier((over_z, dk_sent))
    row_sum = by_z[0]
    for x in over_z:
        row_sum = row_sum + x.astype(F32)
    d_weight = placed(core, rows_of(row_sum, core, out_rows), swapped(rows_of(row_sum, 1 - core, out_rows)), 1)

    dk_chip = gathered_terms(my_y, dk_mine, dk_got, dk_back)
    d_keys = placed(core, rows_of(dk_chip, core, shard_rows), swapped(rows_of(dk_chip, 1 - core, shard_rows)), 1)
    early, late, _ = lax.optimization_barrier((early, late, made))
    out, dq, other = [jnp.concatenate((early[i], late[i]), early[i].ndim - 1) for i in range(3)]
    other = swapped(other)
    out = placed(core, out, other[0], 1)
    dq = placed(core, dq, other[1], 1)
    return (out[None], dq[None], d_keys[None], d_tokens[None], d_weight)


def solution(mesh):
    in_specs = (
        P("fsdp", "ctx", None),
        P("fsdp", "ctx", None),
        P("fsdp", "ctx", None),
        P("fsdp", None),
        P("fsdp", "ctx", None),
        P("fsdp", "ctx"),
    )
    out_specs = (
        P("fsdp", "ctx", None),
        P("fsdp", "ctx", None),
        P("fsdp", "ctx", None),
        P("fsdp", "ctx", None),
        P(("ctx", "fsdp"), None),
    )
    return jax.shard_map(shards, mesh=mesh, in_specs=in_specs, out_specs=out_specs, check_vma=False)
```

```python
import functools
import math

import jax
import jax.numpy as jnp
from jax import lax
from jax.experimental import pallas as pl
from jax.experimental.pallas import tpu as pltpu
from jax.sharding import PartitionSpec as P

HQ = 16
HK = 8
HD = 128
WINDOW = 1024
GROUP = 2
NEG = -1e30

score_scale = 1.0 / math.sqrt(168.0)
exp2_scale = score_scale / math.log(2.0)

BF16 = jnp.bfloat16
F32 = jnp.float32
NT = (((1,), (1,)), ((), ()))
TN = (((0,), (0,)), ((), ()))


def dot(a, b, dims=(((1,), (0,)), ((), ()))):
    return lax.dot_general(a, b, dims, preferred_element_type=F32)


def probs_kernel(blk, n_back, core_ref, low_ref, q_own, q_other, do_own, do_other, *refs):
    n_arr = n_back + 1
    k_refs = refs[:n_arr]
    e_ref, inv_ref, dot_ref = refs[n_arr : n_arr + 3]
    dv_refs = refs[n_arr + 3 : 2 * n_arr + 3]
    bias, s_scr, dv_acc, q_buf, do_buf = refs[2 * n_arr + 3 :]
    span_blocks = WINDOW // blk + 1
    core = core_ref[0]

    @pl.when(pl.program_id(0) == 0)
    def _():
        for qb in range(2):
            kpos = lax.broadcasted_iota(jnp.int32, (span_blocks * blk, blk), 0) + qb * blk
            qpos = lax.broadcasted_iota(jnp.int32, (span_blocks * blk, blk), 1) + (qb * blk + WINDOW)
            low = low_ref[:, qb * blk : (qb + 1) * blk]
            ok = (kpos >= low) & (kpos <= qpos)
            bias[qb] = jnp.where(ok, 0.0, NEG)

    q_buf[core] = q_own[...]
    q_buf[1 - core] = q_other[...]
    do_buf[core] = do_own[...]
    do_buf[1 - core] = do_other[...]

    def key_block(j):
        return k_refs[j // 2][(j % 2) * blk : (j % 2 + 1) * blk, :]

    def stacked(buf, qb):
        return jnp.concatenate([buf[qb, :, r * HD : (r + 1) * HD] for r in range(GROUP)], 0)

    for qb in range(2):
        qs = stacked(q_buf, qb)
        top = None
        for j in range(span_blocks):
            s = dot(key_block(qb + j), qs, NT)
            b = bias[qb, j * blk : (j + 1) * blk, :]
            s = s * exp2_scale + jnp.concatenate([b] * GROUP, 1)
            s_scr[j] = s
            part = jnp.max(s.reshape(blk // 8, 8, GROUP * blk), axis=0)
            top = part if top is None else jnp.maximum(top, part)
        top = jnp.max(top, axis=0, keepdims=True)
        total = None
        for j in range(span_blocks):
            e = jnp.exp2(s_scr[j] - top)
            part = jnp.sum(e.reshape(blk // 8, 8, GROUP * blk), axis=0)
            total = part if total is None else total + part
            e_ref[0, qb, j * blk : (j + 1) * blk, :] = e.astype(BF16)
        inv = 1.0 / jnp.sum(total, axis=0, keepdims=True)
        inv_ref[0, qb] = inv
        do_t = (stacked(do_buf, qb).astype(F32).T * inv).astype(BF16)
        dot_ref[0, qb] = do_t
        for j in range(span_blocks):
            term = dot(e_ref[0, qb, j * blk : (j + 1) * blk, :], do_t, NT)
            at = slice((qb + j) * blk, (qb + j + 1) * blk)
            if qb == 0 or j == span_blocks - 1:
                dv_acc[at, :] = term
            else:
                dv_acc[at, :] += term
    for a in range(n_arr):
        dv_refs[a][...] = dv_acc[a * 2 * blk : (a + 1) * 2 * blk, :].astype(BF16)


def grads_kernel(blk, n_back, core_ref, e_ref, inv_ref, dot_ref, q_own, q_other, *refs):
    n_arr = n_back + 1
    k_refs = refs[:n_arr]
    v_refs = refs[n_arr : 2 * n_arr]
    out_ref, dq_ref, other_ref = refs[2 * n_arr : 2 * n_arr + 3]
    dk_refs = refs[2 * n_arr + 3 : 3 * n_arr + 3]
    dk_acc, q_buf, out_buf, dq_buf = refs[3 * n_arr + 3 :]
    span_blocks = WINDOW // blk + 1
    core = core_ref[0]

    q_buf[core] = q_own[...]
    q_buf[1 - core] = q_other[...]

    def block_of(arrays, j):
        return arrays[j // 2][(j % 2) * blk : (j % 2 + 1) * blk, :]

    for qb in range(2):
        qs = jnp.concatenate([q_buf[qb, :, r * HD : (r + 1) * HD] for r in range(GROUP)], 0)
        do_t = dot_ref[0, qb]
        out_t = None
        for j in range(span_blocks):
            e = e_ref[0, qb, j * blk : (j + 1) * blk, :]
            part = dot(block_of(v_refs, qb + j), e, TN)
            out_t = part if out_t is None else out_t + part
        out_t = (out_t * inv_ref[0, qb]).astype(BF16).astype(F32)
        delta = jnp.sum(out_t * do_t.astype(F32), axis=0, keepdims=True)
        out = out_t.T.astype(BF16)
        dq_t = None
        for j in range(span_blocks):
            e = e_ref[0, qb, j * blk : (j + 1) * blk, :].astype(F32)
            dp = dot(block_of(v_refs, qb + j), do_t)
            ds = (e * (dp - delta)).astype(BF16)
            term = dot(ds, qs)
            at = slice((qb + j) * blk, (qb + j + 1) * blk)
            if qb == 0 or j == span_blocks - 1:
                dk_acc[at, :] = term
            else:
                dk_acc[at, :] += term
            part = dot(block_of(k_refs, qb + j), ds, TN)
            dq_t = part if dq_t is None else dq_t + part
        dq = (dq_t * score_scale).T.astype(BF16)
        for r in range(GROUP):
            out_buf[qb, :, r * HD : (r + 1) * HD] = out[r * blk : (r + 1) * blk, :]
            dq_buf[qb, :, r * HD : (r + 1) * HD] = dq[r * blk : (r + 1) * blk, :]
    out_ref[...] = out_buf[core]
    dq_ref[...] = dq_buf[core]
    other_ref[0] = out_buf[1 - core]
    other_ref[1] = dq_buf[1 - core]
    for a in range(n_arr):
        dk_refs[a][...] = (dk_acc[a * 2 * blk : (a + 1) * 2 * blk, :] * score_scale).astype(BF16)


def specs_of(rows, width):
    blk = rows // 2
    heads = width // HD
    span = WINDOW + blk
    lanes = GROUP * blk
    head = pl.BlockSpec((rows, HD), lambda g, c: (0, g))
    own = pl.BlockSpec((blk, GROUP * HD), lambda g, c: (0, c[0] * heads + g))
    return blk, heads, span, lanes, head, own


def run_probs(core, low, q, q_other, do, keys, rows, width):
    blk, heads, span, lanes, head, own = specs_of(rows, width)
    n_arr = len(keys)
    return pl.pallas_call(
        functools.partial(probs_kernel, blk, n_arr - 1),
        grid_spec=pltpu.PrefetchScalarGridSpec(
            num_scalar_prefetch=1,
            grid=(heads,),
            in_specs=[
                pl.BlockSpec((1, rows), lambda g, c: (0, 0)),
                own,
                pl.BlockSpec((blk, GROUP * HD), lambda g, c: (0, g)),
                own,
                pl.BlockSpec((blk, GROUP * HD), lambda g, c: (0, heads + g)),
            ]
            + [head] * n_arr,
            out_specs=[
                pl.BlockSpec((1, 2, span, lanes), lambda g, c: (g, 0, 0, 0)),
                pl.BlockSpec((1, 2, 1, lanes), lambda g, c: (g, 0, 0, 0)),
                pl.BlockSpec((1, 2, HD, lanes), lambda g, c: (g, 0, 0, 0)),
            ]
            + [head] * n_arr,
            scratch_shapes=[
                pltpu.VMEM((2, span, blk), F32),
                pltpu.VMEM((span // blk, blk, lanes), F32),
                pltpu.VMEM((WINDOW + rows, HD), F32),
                pltpu.VMEM((2, blk, GROUP * HD), BF16),
                pltpu.VMEM((2, blk, GROUP * HD), BF16),
            ],
        ),
        out_shape=[
            jax.ShapeDtypeStruct((heads, 2, span, lanes), BF16),
            jax.ShapeDtypeStruct((heads, 2, 1, lanes), F32),
            jax.ShapeDtypeStruct((heads, 2, HD, lanes), BF16),
        ]
        + [jax.ShapeDtypeStruct((rows, width), BF16)] * n_arr,
        compiler_params=pltpu.CompilerParams(vmem_limit_bytes=40 * 1024 * 1024),
        cost_estimate=small_cost(),
        name="probs",
    )(core, low, q, q_other, do, q_other, *keys)


def run_grads(core, e, inv, do_t, q, q_other, keys, values, rows, width):
    blk, heads, span, lanes, head, own = specs_of(rows, width)
    n_arr = len(keys)
    full = jax.ShapeDtypeStruct(q.shape, BF16)
    return pl.pallas_call(
        functools.partial(grads_kernel, blk, n_arr - 1),
        grid_spec=pltpu.PrefetchScalarGridSpec(
            num_scalar_prefetch=1,
            grid=(heads,),
            in_specs=[
                pl.BlockSpec((1, 2, span, lanes), lambda g, c: (g, 0, 0, 0)),
                pl.BlockSpec((1, 2, 1, lanes), lambda g, c: (g, 0, 0, 0)),
                pl.BlockSpec((1, 2, HD, lanes), lambda g, c: (g, 0, 0, 0)),
                own,
                pl.BlockSpec((blk, GROUP * HD), lambda g, c: (0, g)),
            ]
            + [head] * (2 * n_arr),
            out_specs=[own, own, pl.BlockSpec((2, blk, GROUP * HD), lambda g, c: (0, 0, g))] + [head] * n_arr,
            scratch_shapes=[
                pltpu.VMEM((WINDOW + rows, HD), F32),
                pltpu.VMEM((2, blk, GROUP * HD), BF16),
                pltpu.VMEM((2, blk, GROUP * HD), BF16),
                pltpu.VMEM((2, blk, GROUP * HD), BF16),
            ],
        ),
        out_shape=[full, full, jax.ShapeDtypeStruct((2, blk, GROUP * width), BF16)]
        + [jax.ShapeDtypeStruct((rows, width), BF16)] * n_arr,
        compiler_params=pltpu.CompilerParams(vmem_limit_bytes=40 * 1024 * 1024),
        cost_estimate=small_cost(),
        name="grads",
    )(core, e, inv, do_t, q, q_other, *keys, *values)


def small_cost():
    return pl.CostEstimate(flops=1 << 20, bytes_accessed=1 << 12, transcendentals=0)


def whole():
    return pl.BlockSpec(memory_space=pltpu.VMEM)


def pieces_kernel(dims, at_ref, x_ref, *refs):
    n_z, n_fsdp, out_rows = dims
    outs = refs[: 2 * n_fsdp]
    turned = refs[2 * n_fsdp]
    my_y, my_fsdp = at_ref[0], at_ref[1]
    for c in range(x_ref.shape[1] // HD):
        turned[c * HD : (c + 1) * HD, :] = x_ref[:, c * HD : (c + 1) * HD].astype(F32).T
    for p, out in enumerate(outs):
        flip, s = p // n_fsdp, p % n_fsdp
        y = lax.rem(my_y + flip, 2)
        f = lax.rem(my_fsdp + s, n_fsdp)
        for z in range(n_z):
            parts = []
            for core in range(2):
                block = ((z * 2 + y) * 2 + core) * n_fsdp + f
                parts.append(turned[pl.ds(pl.multiple_of(block * out_rows, 8), out_rows), :])
            out[z * 2 * out_rows : (z + 1) * 2 * out_rows, :] = jnp.concatenate(parts, 0).astype(BF16)


def run_pieces(at, tokens, n_z, n_fsdp, out_rows):
    rows, model = tokens.shape
    shape = jax.ShapeDtypeStruct((n_z * 2 * out_rows, rows), BF16)
    return pl.pallas_call(
        functools.partial(pieces_kernel, (n_z, n_fsdp, out_rows)),
        in_specs=[pl.BlockSpec(memory_space=pltpu.SMEM), whole()],
        out_specs=[whole()] * (2 * n_fsdp),
        out_shape=[shape] * (2 * n_fsdp),
        scratch_shapes=[pltpu.VMEM((model, rows), F32)],
        compiler_params=pltpu.CompilerParams(vmem_limit_bytes=32 * 1024 * 1024),
        cost_estimate=small_cost(),
        name="pieces",
    )(at, tokens)


def product_kernel(at_ref, *refs):
    *x_refs, w_ref, o_ref = refs
    total, first = None, 0
    for x in x_refs:
        term = dot(x[...], w_ref[first : first + x.shape[1], :])
        total = term if total is None else total + term
        first += x.shape[1]
    o_ref[...] = total.astype(o_ref.dtype)


def run_product(at, parts, w, kind):
    rows = parts[0].shape[0]
    depth, width = w.shape
    tile = 512
    if len(parts) == 1:
        x_specs = [pl.BlockSpec((rows, depth), lambda j, at: (0, at[0]))]
    else:
        x_specs = [pl.BlockSpec(x.shape, lambda j, at: (0, 0)) for x in parts]
    return pl.pallas_call(
        product_kernel,
        grid_spec=pltpu.PrefetchScalarGridSpec(
            num_scalar_prefetch=1,
            grid=(width // tile,),
            in_specs=x_specs + [pl.BlockSpec((depth, tile), lambda j, at: (0, j))],
            out_specs=pl.BlockSpec((rows, tile), lambda j, at: (0, j)),
        ),
        out_shape=jax.ShapeDtypeStruct((rows, width), kind),
        compiler_params=pltpu.CompilerParams(vmem_limit_bytes=32 * 1024 * 1024),
        cost_estimate=small_cost(),
        name="product",
    )(at, *parts, w)


def weight_kernel(n_z, n, at_ref, *refs):
    own_pairs, other_pairs = refs[:n], refs[n : 2 * n]
    dv_refs = refs[2 * n : 4 * n]
    outs = refs[4 * n :]
    core = at_ref[0]
    step = pl.program_id(0)
    rows = own_pairs[0].shape[1] // 2
    own = pl.ds(pl.multiple_of(core * rows, rows), rows)
    other = pl.ds(pl.multiple_of((1 - core) * rows, rows), rows)
    total = None
    for p in range(n):
        for flip in range(2):
            window = slice(flip * rows, (flip + 1) * rows)
            term = dot(own_pairs[p][:, window], dv_refs[2 * p + flip][own, :])
            term = term + dot(other_pairs[p][:, window], dv_refs[2 * p + flip][other, :])
            total = term if total is None else total + term
    for d, out in enumerate(outs):

        @pl.when(step == (n_z - 1 if d == 0 else d - 1))
        def _():
            out[...] = total.astype(out.dtype)


def run_weight(at, own_pairs, other_pairs, dv_pairs, n_z):
    n = len(own_pairs)
    count = own_pairs[0].shape[0] // n_z
    rows2 = own_pairs[0].shape[1]
    dvs = [x for pair_of in dv_pairs for x in pair_of]
    width = dvs[0].shape[1]
    shapes = [jax.ShapeDtypeStruct((count, width), F32 if d == 0 else BF16) for d in range(n_z)]
    pair_block = pl.BlockSpec((count, rows2), lambda d, at: (lax.rem(at[1] + d + 1, n_z), 0))
    return pl.pallas_call(
        functools.partial(weight_kernel, n_z, n),
        grid_spec=pltpu.PrefetchScalarGridSpec(
            num_scalar_prefetch=1,
            grid=(n_z,),
            in_specs=[pair_block] * (2 * n) + [pl.BlockSpec(dvs[0].shape, lambda d, at: (0, 0))] * (2 * n),
            out_specs=[pl.BlockSpec((count, width), lambda d, at: (0, 0))] * n_z,
        ),
        out_shape=shapes,
        compiler_params=pltpu.CompilerParams(vmem_limit_bytes=40 * 1024 * 1024),
        cost_estimate=small_cost(),
        name="weight",
    )(at, *own_pairs, *other_pairs, *dvs)


def tokens_kernel(n_fsdp, at_ref, dv_ref, w_ref, own_ref, *others):
    made = dot(dv_ref[...], w_ref[...], NT).astype(BF16)
    rows = own_ref.shape[0]
    own_ref[...] = made[:rows]
    for s, ref in enumerate(others):
        ref[...] = made[(s + 1) * rows : (s + 2) * rows]


def run_tokens(at, dv_rows, w, n_fsdp):
    slab, width = w.shape
    rows = dv_rows.shape[0] // n_fsdp
    tile = slab // 3 if slab % (3 * HD) == 0 else slab
    n_tiles = slab // tile
    return pl.pallas_call(
        functools.partial(tokens_kernel, n_fsdp),
        grid_spec=pltpu.PrefetchScalarGridSpec(
            num_scalar_prefetch=1,
            grid=(n_tiles,),
            in_specs=[
                pl.BlockSpec(dv_rows.shape, lambda j, at: (0, 0)),
                pl.BlockSpec((tile, width), lambda j, at: (j, 0)),
            ],
            out_specs=[pl.BlockSpec((rows, tile), lambda j, at: (0, at[0] * n_tiles + j))]
            + [pl.BlockSpec((rows, tile), lambda j, at: (0, j))] * (n_fsdp - 1),
        ),
        out_shape=[jax.ShapeDtypeStruct((rows, slab * n_fsdp), BF16)]
        + [jax.ShapeDtypeStruct((rows, slab), BF16)] * (n_fsdp - 1),
        compiler_params=pltpu.CompilerParams(vmem_limit_bytes=40 * 1024 * 1024),
        cost_estimate=small_cost(),
        name="tokens",
    )(at, dv_rows, w)


def shifted(x, by):
    length = lax.axis_size("ctx")
    return lax.ppermute(x, "ctx", [(i, i + by) for i in range(length) if 0 <= i + by < length])


def swapped(x):
    return lax.ppermute(x, "ctx", [(i, i ^ 1) for i in range(lax.axis_size("ctx"))])


def rotated(x, by):
    length = lax.axis_size("fsdp")
    return lax.ppermute(x, "fsdp", [(i, (i + by) % length) for i in range(length)])


def moved(x, flip, by):
    n_ctx, n_fsdp = lax.axis_size("ctx"), lax.axis_size("fsdp")
    pairs = [
        (c * n_fsdp + f, (c ^ (2 * flip)) * n_fsdp + (f + by) % n_fsdp)
        for c in range(n_ctx)
        for f in range(n_fsdp)
    ]
    return lax.ppermute(x, ("ctx", "fsdp"), pairs)


def relayed(my_y, far, got):
    return (far.astype(F32) + jnp.where(my_y == 1, got.astype(F32), 0.0)).astype(BF16)


def gathered_terms(my_y, mine, got, back):
    return (mine.astype(F32) + back.astype(F32) + jnp.where(my_y == 0, got.astype(F32), 0.0)).astype(BF16)


def cols(x, at, width):
    return lax.dynamic_slice_in_dim(x, at * width, width, x.ndim - 1)


def rows_of(x, at, count):
    return lax.dynamic_slice_in_dim(x, at * count, count, 0)


def placed(core, own, other, axis):
    both = jnp.concatenate([own, own], axis)
    return lax.dynamic_update_slice_in_dim(both, other, (1 - core) * own.shape[axis], axis)


def flipped(x):
    return lax.ppermute(x, "ctx", [(i, i ^ 2) for i in range(lax.axis_size("ctx"))])


def after(x, *earlier):
    return lax.optimization_barrier((x, *earlier))[0]


def shards(hidden, queries, key_heads, w_value, d_out, segments):
    shard_rows = hidden.shape[1]
    model = hidden.shape[2]
    kv_width = w_value.shape[1]
    n_ctx = lax.axis_size("ctx")
    n_fsdp = lax.axis_size("fsdp")
    chip_rows = 2 * shard_rows
    n_z = n_ctx // 4
    assert WINDOW == 2 * chip_rows
    my_ctx = lax.axis_index("ctx")
    my_fsdp = lax.axis_index("fsdp")
    core = my_ctx % 2
    core_arg = core.astype(jnp.int32).reshape(1)
    chip = my_ctx // 2
    my_y = chip % 2
    my_z = chip // 2
    half_kv = kv_width // 2
    slab = model // n_fsdp
    tokens = hidden[0]
    first = chip * chip_rows

    aligned = slab % HD == 0
    fsdp_arg = my_fsdp.astype(jnp.int32).reshape(1)
    zero_arg = jnp.zeros((1,), jnp.int32)
    half_q = queries.shape[2] // 2
    out_rows = model // (n_ctx * n_fsdp)
    places = [(flip, s) for flip in range(2) for s in range(n_fsdp)]

    cut = slab // HD // 2 * HD if aligned else slab
    parts_at = [(0, cut), (cut, slab)] if aligned else [(0, slab)]
    slabs = [
        [
            lax.dynamic_slice_in_dim(tokens, (my_fsdp + s) % n_fsdp * slab + low, high - low, 1)
            for low, high in parts_at
        ]
        for s in range(1, n_fsdp)
    ]
    sent = [[rotated(x, s + 1) for x in parts] for s, parts in enumerate(slabs)]

    own_tags = segments[0].astype(BF16)
    tag_row = lax.dynamic_update_slice_in_dim(jnp.zeros((half_kv,), BF16), own_tags, core * shard_rows, 0)
    tag_rows = jnp.concatenate([tag_row[None], jnp.zeros((15, half_kv), BF16)], 0)
    k_sent = jnp.concatenate([cols(key_heads[0], 1 - core, half_kv), tag_rows], 0)
    got = swapped(after(k_sent, *[parts[0] for parts in slabs]))

    if out_rows % 8 == 0:
        at = jnp.stack([my_y, my_fsdp]).astype(jnp.int32)
        pieces = run_pieces(after(at, k_sent), tokens, n_z, n_fsdp, out_rows)
    else:
        turned = tokens.T.reshape(n_z, 2, 2, n_fsdp, out_rows, shard_rows)
        pieces = []
        for flip, s in places:
            piece = lax.dynamic_index_in_dim(turned, my_y ^ flip, 1, keepdims=False)
            piece = lax.dynamic_index_in_dim(piece, (my_fsdp + s) % n_fsdp, 2, keepdims=False)
            pieces.append(piece.reshape(n_z * 2 * out_rows, shard_rows))
    by_place = dict(zip(places, pieces))

    k_own = jnp.concatenate(
        [
            placed(core, cols(key_heads[0], core, half_kv), got[:shard_rows], 0),
            tag_rows + got[shard_rows:],
        ],
        0,
    )
    k_own = after(k_own, *pieces)
    k_far = shifted(k_own, 4)
    over_y = {s: flipped(after(by_place[1, s], k_own)) for s in range(1, n_fsdp)}
    q_sent = jnp.concatenate([cols(queries[0], 1 - core, half_q), cols(d_out[0], 1 - core, half_q)], 1)
    q_other = swapped(after(q_sent, k_own))
    if aligned:
        value_own = run_product(after(fsdp_arg, q_sent), [tokens], w_value, F32)
    else:
        value_own = dot(cols(tokens, my_fsdp, slab), w_value)
    firsts = [parts[0] for parts in sent]
    k_far, over_y, firsts, _ = lax.optimization_barrier((k_far, over_y, firsts, value_own))
    sent = [[x, *parts[1:]] for x, parts in zip(firsts, sent)]
    k_near = flipped(jnp.where(my_y == 0, k_own, k_far))
    keys = [k_far, k_near, k_own]

    span_tags = jnp.concatenate([k[chip_rows, :chip_rows] for k in keys], 0)
    key_at = jnp.arange(WINDOW + chip_rows, dtype=jnp.int32)
    chip_tags = k_own[chip_rows, :chip_rows]
    before = (span_tags[None, :] < chip_tags[:, None]) | (key_at + first < WINDOW)[None, :]
    low = jnp.sum(before.astype(jnp.int32), axis=1)
    low = jnp.maximum(low, jnp.arange(1, chip_rows + 1, dtype=jnp.int32))[None, :]

    if aligned:
        partial = [run_product(zero_arg, parts, w_value, BF16) for parts in sent]
    else:
        partial = [dot(parts[0], w_value).astype(BF16) for parts in sent]
    low = after(low, *partial)
    e, inv, do_t, dv_far, dv_near, dv_mine = run_probs(
        core_arg, low, queries[0], q_other, d_out[0], keys, chip_rows, half_kv
    )
    dv_got = flipped(dv_near)

    value_back = [rotated(x, -s - 1) for s, x in enumerate(partial)]
    over_fsdp = {s: rotated(after(by_place[0, s], *partial), s) for s in range(1, n_fsdp)}
    value_back, over_fsdp, _ = lax.optimization_barrier((value_back, over_fsdp, dv_near))
    value_sum = value_own
    for x in value_back:
        value_sum = value_sum + x.astype(F32)
    own_values = value_sum.astype(BF16)
    v_own = placed(core, cols(own_values, core, half_kv), swapped(cols(own_values, 1 - core, half_kv)), 0)

    over_y[0] = flipped(after(by_place[1, 0], k_near))
    v_own, over_y[0] = lax.optimization_barrier((v_own, over_y[0]))
    v_far = shifted(v_own, 4)
    own_pairs = [jnp.concatenate([by_place[0, 0], over_y[0]], 1)]
    other_pairs = [swapped(after(own_pairs[0], v_own))]
    relayed_y = {s: rotated(after(over_y[s], own_values), s) for s in range(1, n_fsdp)}

    dv_got = after(dv_got, v_own)
    dv_sent = relayed(my_y, dv_far, dv_got)
    dv_back = shifted(dv_sent, -4)
    v_sent = after(jnp.where(my_y == 0, v_own, v_far), dv_sent)
    v_near = flipped(v_sent)
    vals = [v_far, v_near, v_own]
    dv_chip = gathered_terms(my_y, dv_mine, dv_got, after(dv_back, v_sent))
    dv_fsdp = [dv_chip] + [rotated(dv_chip, s) for s in range(1, n_fsdp)]
    dv_over_y = [moved(dv_chip, 1, s) for s in range(n_fsdp)]
    relayed_y, v_near = lax.optimization_barrier((relayed_y, v_near))
    for s in range(1, n_fsdp):
        own_pairs.append(jnp.concatenate([over_fsdp[s], relayed_y[s]], 1))
        other_pairs.append(swapped(own_pairs[s]))
    vals = [v_far, v_near, v_own]
    out, dq, other, dk_far, dk_near, dk_mine = run_grads(
        after(core_arg, dv_chip, *own_pairs), e, inv, do_t, queries[0], q_other, keys, vals, chip_rows, half_kv
    )
    dk_got = flipped(dk_near)

    dv_fsdp, dv_over_y, other_pairs, _ = lax.optimization_barrier((dv_fsdp, dv_over_y, other_pairs, dk_near))
    dv_other = swapped(jnp.concatenate([rows_of(x, 1 - core, shard_rows) for x in dv_fsdp], 0))
    dv_rows = placed(
        core, jnp.concatenate([rows_of(x, core, shard_rows) for x in dv_fsdp], 0), dv_other, 1
    )
    if aligned:
        d_tokens, *made = run_tokens(fsdp_arg, dv_rows, w_value, n_fsdp)
    else:
        made = dot(dv_rows, w_value, NT).astype(BF16)
        made = [made[s * shard_rows : (s + 1) * shard_rows] for s in range(n_fsdp)]
        d_tokens = jnp.concatenate([made[0]] * n_fsdp, 1)
        made = made[1:]
    for s in range(1, n_fsdp):
        back = rotated(made[s - 1], -s)
        d_tokens = lax.dynamic_update_slice_in_dim(d_tokens, back, ((my_fsdp + s) % n_fsdp) * slab, 1)

    dv_pairs = list(zip(dv_fsdp, dv_over_y))
    if out_rows % 8 == 0:
        at = after(jnp.stack([core, my_z]).astype(jnp.int32), dk_got, *made)
        by_z = run_weight(at, own_pairs, other_pairs, dv_pairs, n_z)
    else:
        weight_term = 0.0
        for p in range(n_fsdp):
            for flip in range(2):
                window = slice(flip * shard_rows, (flip + 1) * shard_rows)
                weight_term += dot(own_pairs[p][:, window], rows_of(dv_pairs[p][flip], core, shard_rows))
                weight_term += dot(other_pairs[p][:, window], rows_of(dv_pairs[p][flip], 1 - core, shard_rows))
        weight_term = weight_term.reshape(n_z, 2 * out_rows, half_kv)
        by_z = [
            lax.dynamic_index_in_dim(weight_term, (my_z + d) % n_z, 0, keepdims=False).astype(BF16 if d else F32)
            for d in range(n_z)
        ]
    over_z = [
        lax.ppermute(by_z[d], "ctx", [(i, (i + 4 * d) % n_ctx) for i in range(n_ctx)]) for d in range(1, n_z)
    ]

    dk_got = after(dk_got, by_z[0])
    dk_sent = relayed(my_y, dk_far, dk_got)
    dk_back = shifted(dk_sent, -4)

    over_z, _ = lax.optimization_barrier((over_z, dk_sent))
    row_sum = by_z[0]
    for x in over_z:
        row_sum = row_sum + x.astype(F32)
    d_weight = placed(core, rows_of(row_sum, core, out_rows), swapped(rows_of(row_sum, 1 - core, out_rows)), 1)

    dk_chip = gathered_terms(my_y, dk_mine, dk_got, dk_back)
    d_keys = placed(core, rows_of(dk_chip, core, shard_rows), swapped(rows_of(dk_chip, 1 - core, shard_rows)), 1)
    other = swapped(after(other, *made))
    out = lax.dynamic_update_slice_in_dim(out, other[0], (1 - core) * half_q, 1)
    dq = lax.dynamic_update_slice_in_dim(dq, other[1], (1 - core) * half_q, 1)
    return (out[None], dq[None], d_keys[None], d_tokens[None], d_weight)


def solution(mesh):
    in_specs = (
        P("fsdp", "ctx", None),
        P("fsdp", "ctx", None),
        P("fsdp", "ctx", None),
        P("fsdp", None),
        P("fsdp", "ctx", None),
        P("fsdp", "ctx"),
    )
    out_specs = (
        P("fsdp", "ctx", None),
        P("fsdp", "ctx", None),
        P("fsdp", "ctx", None),
        P("fsdp", "ctx", None),
        P(("ctx", "fsdp"), None),
    )
    return jax.shard_map(shards, mesh=mesh, in_specs=in_specs, out_specs=out_specs, check_vma=False)
```

```python
import functools
import math

import jax
import jax.numpy as jnp
from jax import lax
from jax.experimental import pallas as pl
from jax.experimental.pallas import tpu as pltpu
from jax.sharding import PartitionSpec as P

HQ = 16
HK = 8
HD = 128
WINDOW = 1024
GROUP = 2
NEG = -1e30
VMEM_BYTES = 58 * 1024 * 1024

score_scale = 1.0 / math.sqrt(168.0)
exp2_scale = score_scale / math.log(2.0)

BF16 = jnp.bfloat16
F32 = jnp.float32
NT = (((1,), (1,)), ((), ()))
TN = (((0,), (0,)), ((), ()))


def dot(a, b, dims=(((1,), (0,)), ((), ()))):
    return lax.dot_general(a, b, dims, preferred_element_type=F32)


def probs_kernel(blk, n_back, core_ref, low_ref, q_own, q_other, do_own, do_other, *refs):
    n_arr = n_back + 1
    k_refs = refs[:n_arr]
    e_ref, inv_ref, dot_ref = refs[n_arr : n_arr + 3]
    dv_refs = refs[n_arr + 3 : 2 * n_arr + 3]
    bias, s_scr, dv_acc, q_buf, do_buf = refs[2 * n_arr + 3 :]
    span_blocks = WINDOW // blk + 1
    core = core_ref[0]

    @pl.when(pl.program_id(0) == 0)
    def _():
        for qb in range(2):
            kpos = lax.broadcasted_iota(jnp.int32, (span_blocks * blk, blk), 0) + qb * blk
            qpos = lax.broadcasted_iota(jnp.int32, (span_blocks * blk, blk), 1) + (qb * blk + WINDOW)
            low = low_ref[:, qb * blk : (qb + 1) * blk]
            ok = (kpos >= low) & (kpos <= qpos)
            bias[qb] = jnp.where(ok, 0.0, NEG)

    q_buf[core] = q_own[...]
    q_buf[1 - core] = q_other[...]
    do_buf[core] = do_own[...]
    do_buf[1 - core] = do_other[...]

    def key_block(j):
        return k_refs[j // 2][(j % 2) * blk : (j % 2 + 1) * blk, :]

    def stacked(buf, qb):
        return jnp.concatenate([buf[qb, :, r * HD : (r + 1) * HD] for r in range(GROUP)], 0)

    for qb in range(2):
        qs = stacked(q_buf, qb)
        top = None
        for j in range(span_blocks):
            s = dot(key_block(qb + j), qs, NT)
            b = bias[qb, j * blk : (j + 1) * blk, :]
            s = s * exp2_scale + jnp.concatenate([b] * GROUP, 1)
            s_scr[j] = s
            part = jnp.max(s.reshape(blk // 8, 8, GROUP * blk), axis=0)
            top = part if top is None else jnp.maximum(top, part)
        top = jnp.max(top, axis=0, keepdims=True)
        total = None
        for j in range(span_blocks):
            e = jnp.exp2(s_scr[j] - top)
            part = jnp.sum(e.reshape(blk // 8, 8, GROUP * blk), axis=0)
            total = part if total is None else total + part
            e_ref[0, qb, j * blk : (j + 1) * blk, :] = e.astype(BF16)
        inv = 1.0 / jnp.sum(total, axis=0, keepdims=True)
        inv_ref[0, qb] = inv
        do_t = (stacked(do_buf, qb).astype(F32).T * inv).astype(BF16)
        dot_ref[0, qb] = do_t
        for j in range(span_blocks):
            term = dot(e_ref[0, qb, j * blk : (j + 1) * blk, :], do_t, NT)
            at = slice((qb + j) * blk, (qb + j + 1) * blk)
            if qb == 0 or j == span_blocks - 1:
                dv_acc[at, :] = term
            else:
                dv_acc[at, :] += term
    for a in range(n_arr):
        dv_refs[a][...] = dv_acc[a * 2 * blk : (a + 1) * 2 * blk, :].astype(BF16)


def grads_kernel(blk, n_back, core_ref, e_ref, inv_ref, dot_ref, q_own, q_other, *refs):
    n_arr = n_back + 1
    k_refs = refs[:n_arr]
    v_refs = refs[n_arr : 2 * n_arr]
    out_ref, dq_ref, other_ref = refs[2 * n_arr : 2 * n_arr + 3]
    dk_refs = refs[2 * n_arr + 3 : 3 * n_arr + 3]
    dk_acc, q_buf, out_buf, dq_buf = refs[3 * n_arr + 3 :]
    span_blocks = WINDOW // blk + 1
    core = core_ref[0]

    q_buf[core] = q_own[...]
    q_buf[1 - core] = q_other[...]

    def block_of(arrays, j):
        return arrays[j // 2][(j % 2) * blk : (j % 2 + 1) * blk, :]

    for qb in range(2):
        qs = jnp.concatenate([q_buf[qb, :, r * HD : (r + 1) * HD] for r in range(GROUP)], 0)
        do_t = dot_ref[0, qb]
        out_t = None
        for j in range(span_blocks):
            e = e_ref[0, qb, j * blk : (j + 1) * blk, :]
            part = dot(block_of(v_refs, qb + j), e, TN)
            out_t = part if out_t is None else out_t + part
        out_t = (out_t * inv_ref[0, qb]).astype(BF16).astype(F32)
        delta = jnp.sum(out_t * do_t.astype(F32), axis=0, keepdims=True)
        out = out_t.T.astype(BF16)
        dq_t = None
        for j in range(span_blocks):
            e = e_ref[0, qb, j * blk : (j + 1) * blk, :].astype(F32)
            dp = dot(block_of(v_refs, qb + j), do_t)
            ds = (e * (dp - delta)).astype(BF16)
            term = dot(ds, qs)
            at = slice((qb + j) * blk, (qb + j + 1) * blk)
            if qb == 0 or j == span_blocks - 1:
                dk_acc[at, :] = term
            else:
                dk_acc[at, :] += term
            part = dot(block_of(k_refs, qb + j), ds, TN)
            dq_t = part if dq_t is None else dq_t + part
        dq = (dq_t * score_scale).T.astype(BF16)
        for r in range(GROUP):
            out_buf[qb, :, r * HD : (r + 1) * HD] = out[r * blk : (r + 1) * blk, :]
            dq_buf[qb, :, r * HD : (r + 1) * HD] = dq[r * blk : (r + 1) * blk, :]
    out_ref[...] = out_buf[core]
    dq_ref[...] = dq_buf[core]
    other_ref[0] = out_buf[1 - core]
    other_ref[1] = dq_buf[1 - core]
    for a in range(n_arr):
        dk_refs[a][...] = (dk_acc[a * 2 * blk : (a + 1) * 2 * blk, :] * score_scale).astype(BF16)


def specs_of(rows, width):
    blk = rows // 2
    heads = width // HD
    span = WINDOW + blk
    lanes = GROUP * blk
    head = pl.BlockSpec((rows, HD), lambda g, c: (0, g))
    own = pl.BlockSpec((blk, GROUP * HD), lambda g, c: (0, c[0] * heads + g))
    return blk, heads, span, lanes, head, own


def run_probs(core, low, q, q_other, do, keys, rows, width):
    blk, heads, span, lanes, head, own = specs_of(rows, width)
    n_arr = len(keys)
    return pl.pallas_call(
        functools.partial(probs_kernel, blk, n_arr - 1),
        grid_spec=pltpu.PrefetchScalarGridSpec(
            num_scalar_prefetch=1,
            grid=(heads,),
            in_specs=[
                pl.BlockSpec((1, rows), lambda g, c: (0, 0)),
                own,
                pl.BlockSpec((blk, GROUP * HD), lambda g, c: (0, g)),
                own,
                pl.BlockSpec((blk, GROUP * HD), lambda g, c: (0, heads + g)),
            ]
            + [head] * n_arr,
            out_specs=[
                pl.BlockSpec((1, 2, span, lanes), lambda g, c: (g, 0, 0, 0)),
                pl.BlockSpec((1, 2, 1, lanes), lambda g, c: (g, 0, 0, 0)),
                pl.BlockSpec((1, 2, HD, lanes), lambda g, c: (g, 0, 0, 0)),
            ]
            + [head] * n_arr,
            scratch_shapes=[
                pltpu.VMEM((2, span, blk), F32),
                pltpu.VMEM((span // blk, blk, lanes), F32),
                pltpu.VMEM((WINDOW + rows, HD), F32),
                pltpu.VMEM((2, blk, GROUP * HD), BF16),
                pltpu.VMEM((2, blk, GROUP * HD), BF16),
            ],
        ),
        out_shape=[
            jax.ShapeDtypeStruct((heads, 2, span, lanes), BF16),
            jax.ShapeDtypeStruct((heads, 2, 1, lanes), F32),
            jax.ShapeDtypeStruct((heads, 2, HD, lanes), BF16),
        ]
        + [jax.ShapeDtypeStruct((rows, width), BF16)] * n_arr,
        compiler_params=pltpu.CompilerParams(vmem_limit_bytes=VMEM_BYTES),
        cost_estimate=small_cost(),
        name="probs",
    )(core, low, q, q_other, do, q_other, *keys)


def run_grads(core, e, inv, do_t, q, q_other, keys, values, rows, width):
    blk, heads, span, lanes, head, own = specs_of(rows, width)
    n_arr = len(keys)
    full = jax.ShapeDtypeStruct(q.shape, BF16)
    return pl.pallas_call(
        functools.partial(grads_kernel, blk, n_arr - 1),
        grid_spec=pltpu.PrefetchScalarGridSpec(
            num_scalar_prefetch=1,
            grid=(heads,),
            in_specs=[
                pl.BlockSpec((1, 2, span, lanes), lambda g, c: (g, 0, 0, 0)),
                pl.BlockSpec((1, 2, 1, lanes), lambda g, c: (g, 0, 0, 0)),
                pl.BlockSpec((1, 2, HD, lanes), lambda g, c: (g, 0, 0, 0)),
                own,
                pl.BlockSpec((blk, GROUP * HD), lambda g, c: (0, g)),
            ]
            + [head] * (2 * n_arr),
            out_specs=[own, own, pl.BlockSpec((2, blk, GROUP * HD), lambda g, c: (0, 0, g))] + [head] * n_arr,
            scratch_shapes=[
                pltpu.VMEM((WINDOW + rows, HD), F32),
                pltpu.VMEM((2, blk, GROUP * HD), BF16),
                pltpu.VMEM((2, blk, GROUP * HD), BF16),
                pltpu.VMEM((2, blk, GROUP * HD), BF16),
            ],
        ),
        out_shape=[full, full, jax.ShapeDtypeStruct((2, blk, GROUP * width), BF16)]
        + [jax.ShapeDtypeStruct((rows, width), BF16)] * n_arr,
        compiler_params=pltpu.CompilerParams(vmem_limit_bytes=VMEM_BYTES),
        cost_estimate=small_cost(),
        name="grads",
    )(core, e, inv, do_t, q, q_other, *keys, *values)


def small_cost():
    return pl.CostEstimate(flops=1 << 20, bytes_accessed=1 << 12, transcendentals=0)


def whole():
    return pl.BlockSpec(memory_space=pltpu.VMEM)


def pieces_kernel(dims, at_ref, x_ref, *refs):
    n_z, n_fsdp, out_rows = dims
    outs = refs[: 2 * n_fsdp]
    turned = refs[2 * n_fsdp]
    my_y, my_fsdp = at_ref[0], at_ref[1]
    for c in range(x_ref.shape[1] // HD):
        turned[c * HD : (c + 1) * HD, :] = x_ref[:, c * HD : (c + 1) * HD].astype(F32).T
    for p, out in enumerate(outs):
        flip, s = p // n_fsdp, p % n_fsdp
        y = lax.rem(my_y + flip, 2)
        f = lax.rem(my_fsdp + s, n_fsdp)
        for z in range(n_z):
            parts = []
            for core in range(2):
                block = ((z * 2 + y) * 2 + core) * n_fsdp + f
                parts.append(turned[pl.ds(pl.multiple_of(block * out_rows, 8), out_rows), :])
            out[z * 2 * out_rows : (z + 1) * 2 * out_rows, :] = jnp.concatenate(parts, 0).astype(BF16)


def run_pieces(at, tokens, n_z, n_fsdp, out_rows):
    rows, model = tokens.shape
    shape = jax.ShapeDtypeStruct((n_z * 2 * out_rows, rows), BF16)
    return pl.pallas_call(
        functools.partial(pieces_kernel, (n_z, n_fsdp, out_rows)),
        in_specs=[pl.BlockSpec(memory_space=pltpu.SMEM), whole()],
        out_specs=[whole()] * (2 * n_fsdp),
        out_shape=[shape] * (2 * n_fsdp),
        scratch_shapes=[pltpu.VMEM((model, rows), F32)],
        compiler_params=pltpu.CompilerParams(vmem_limit_bytes=VMEM_BYTES),
        cost_estimate=small_cost(),
        name="pieces",
    )(at, tokens)


def product_kernel(at_ref, *refs):
    *x_refs, w_ref, o_ref = refs
    total, first = None, 0
    for x in x_refs:
        term = dot(x[...], w_ref[first : first + x.shape[1], :])
        total = term if total is None else total + term
        first += x.shape[1]
    o_ref[...] = total.astype(o_ref.dtype)


def run_product(at, parts, w, kind):
    rows = parts[0].shape[0]
    depth, width = w.shape
    tile = 512
    if len(parts) == 1:
        x_specs = [pl.BlockSpec((rows, depth), lambda j, at: (0, at[0]))]
    else:
        x_specs = [pl.BlockSpec(x.shape, lambda j, at: (0, 0)) for x in parts]
    return pl.pallas_call(
        product_kernel,
        grid_spec=pltpu.PrefetchScalarGridSpec(
            num_scalar_prefetch=1,
            grid=(width // tile,),
            in_specs=x_specs + [pl.BlockSpec((depth, tile), lambda j, at: (0, j))],
            out_specs=pl.BlockSpec((rows, tile), lambda j, at: (0, j)),
        ),
        out_shape=jax.ShapeDtypeStruct((rows, width), kind),
        compiler_params=pltpu.CompilerParams(vmem_limit_bytes=VMEM_BYTES),
        cost_estimate=small_cost(),
        name="product",
    )(at, *parts, w)


def weight_kernel(n_z, n, at_ref, *refs):
    own_pairs, other_pairs = refs[:n], refs[n : 2 * n]
    dv_refs = refs[2 * n : 4 * n]
    outs = refs[4 * n :]
    core = at_ref[0]
    step = pl.program_id(0)
    rows = own_pairs[0].shape[1] // 2
    own = pl.ds(pl.multiple_of(core * rows, rows), rows)
    other = pl.ds(pl.multiple_of((1 - core) * rows, rows), rows)
    total = None
    for p in range(n):
        for flip in range(2):
            window = slice(flip * rows, (flip + 1) * rows)
            term = dot(own_pairs[p][:, window], dv_refs[2 * p + flip][own, :])
            term = term + dot(other_pairs[p][:, window], dv_refs[2 * p + flip][other, :])
            total = term if total is None else total + term
    for d, out in enumerate(outs):

        @pl.when(step == (n_z - 1 if d == 0 else d - 1))
        def _():
            out[...] = total.astype(out.dtype)


def run_weight(at, own_pairs, other_pairs, dv_pairs, n_z):
    n = len(own_pairs)
    count = own_pairs[0].shape[0] // n_z
    rows2 = own_pairs[0].shape[1]
    dvs = [x for pair_of in dv_pairs for x in pair_of]
    width = dvs[0].shape[1]
    shapes = [jax.ShapeDtypeStruct((count, width), F32 if d == 0 else BF16) for d in range(n_z)]
    pair_block = pl.BlockSpec((count, rows2), lambda d, at: (lax.rem(at[1] + d + 1, n_z), 0))
    return pl.pallas_call(
        functools.partial(weight_kernel, n_z, n),
        grid_spec=pltpu.PrefetchScalarGridSpec(
            num_scalar_prefetch=1,
            grid=(n_z,),
            in_specs=[pair_block] * (2 * n) + [pl.BlockSpec(dvs[0].shape, lambda d, at: (0, 0))] * (2 * n),
            out_specs=[pl.BlockSpec((count, width), lambda d, at: (0, 0))] * n_z,
        ),
        out_shape=shapes,
        compiler_params=pltpu.CompilerParams(vmem_limit_bytes=VMEM_BYTES),
        cost_estimate=small_cost(),
        name="weight",
    )(at, *own_pairs, *other_pairs, *dvs)


def tokens_kernel(n_fsdp, at_ref, dv_ref, w_ref, own_ref, *others):
    made = dot(dv_ref[...], w_ref[...], NT).astype(BF16)
    rows = own_ref.shape[0]
    own_ref[...] = made[:rows]
    for s, ref in enumerate(others):
        ref[...] = made[(s + 1) * rows : (s + 2) * rows]


def run_tokens(at, dv_rows, w, n_fsdp):
    slab, width = w.shape
    rows = dv_rows.shape[0] // n_fsdp
    tile = slab // 3 if slab % (3 * HD) == 0 else slab
    n_tiles = slab // tile
    return pl.pallas_call(
        functools.partial(tokens_kernel, n_fsdp),
        grid_spec=pltpu.PrefetchScalarGridSpec(
            num_scalar_prefetch=1,
            grid=(n_tiles,),
            in_specs=[
                pl.BlockSpec(dv_rows.shape, lambda j, at: (0, 0)),
                pl.BlockSpec((tile, width), lambda j, at: (j, 0)),
            ],
            out_specs=[pl.BlockSpec((rows, tile), lambda j, at: (0, at[0] * n_tiles + j))]
            + [pl.BlockSpec((rows, tile), lambda j, at: (0, j))] * (n_fsdp - 1),
        ),
        out_shape=[jax.ShapeDtypeStruct((rows, slab * n_fsdp), BF16)]
        + [jax.ShapeDtypeStruct((rows, slab), BF16)] * (n_fsdp - 1),
        compiler_params=pltpu.CompilerParams(vmem_limit_bytes=VMEM_BYTES),
        cost_estimate=small_cost(),
        name="tokens",
    )(at, dv_rows, w)


def shifted(x, by):
    length = lax.axis_size("ctx")
    return lax.ppermute(x, "ctx", [(i, i + by) for i in range(length) if 0 <= i + by < length])


def swapped(x):
    return lax.ppermute(x, "ctx", [(i, i ^ 1) for i in range(lax.axis_size("ctx"))])


def rotated(x, by):
    length = lax.axis_size("fsdp")
    return lax.ppermute(x, "fsdp", [(i, (i + by) % length) for i in range(length)])


def moved(x, flip, by):
    n_ctx, n_fsdp = lax.axis_size("ctx"), lax.axis_size("fsdp")
    pairs = [
        (c * n_fsdp + f, (c ^ (2 * flip)) * n_fsdp + (f + by) % n_fsdp)
        for c in range(n_ctx)
        for f in range(n_fsdp)
    ]
    return lax.ppermute(x, ("ctx", "fsdp"), pairs)


def relayed(my_y, far, got):
    return (far.astype(F32) + jnp.where(my_y == 1, got.astype(F32), 0.0)).astype(BF16)


def gathered_terms(my_y, mine, got, back):
    return (mine.astype(F32) + back.astype(F32) + jnp.where(my_y == 0, got.astype(F32), 0.0)).astype(BF16)


def cols(x, at, width):
    return lax.dynamic_slice_in_dim(x, at * width, width, x.ndim - 1)


def rows_of(x, at, count):
    return lax.dynamic_slice_in_dim(x, at * count, count, 0)


def placed(core, own, other, axis):
    both = jnp.concatenate([own, own], axis)
    return lax.dynamic_update_slice_in_dim(both, other, (1 - core) * own.shape[axis], axis)


def flipped(x):
    return lax.ppermute(x, "ctx", [(i, i ^ 2) for i in range(lax.axis_size("ctx"))])


def after(x, *earlier):
    return lax.optimization_barrier((x, *earlier))[0]


def shards(hidden, queries, key_heads, w_value, d_out, segments):
    shard_rows = hidden.shape[1]
    model = hidden.shape[2]
    kv_width = w_value.shape[1]
    n_ctx = lax.axis_size("ctx")
    n_fsdp = lax.axis_size("fsdp")
    chip_rows = 2 * shard_rows
    n_z = n_ctx // 4
    assert WINDOW == 2 * chip_rows
    my_ctx = lax.axis_index("ctx")
    my_fsdp = lax.axis_index("fsdp")
    core = my_ctx % 2
    core_arg = core.astype(jnp.int32).reshape(1)
    chip = my_ctx // 2
    my_y = chip % 2
    my_z = chip // 2
    half_kv = kv_width // 2
    slab = model // n_fsdp
    tokens = hidden[0]
    first = chip * chip_rows

    aligned = slab % HD == 0
    fsdp_arg = my_fsdp.astype(jnp.int32).reshape(1)
    zero_arg = jnp.zeros((1,), jnp.int32)
    half_q = queries.shape[2] // 2
    out_rows = model // (n_ctx * n_fsdp)
    places = [(flip, s) for flip in range(2) for s in range(n_fsdp)]

    cut = slab // HD // 2 * HD if aligned else slab
    parts_at = [(0, cut), (cut, slab)] if aligned else [(0, slab)]
    slabs = [
        [
            lax.dynamic_slice_in_dim(tokens, (my_fsdp + s) % n_fsdp * slab + low, high - low, 1)
            for low, high in parts_at
        ]
        for s in range(1, n_fsdp)
    ]
    sent = [[rotated(x, s + 1) for x in parts] for s, parts in enumerate(slabs)]

    own_tags = segments[0].astype(BF16)
    tag_row = lax.dynamic_update_slice_in_dim(jnp.zeros((half_kv,), BF16), own_tags, core * shard_rows, 0)
    tag_rows = jnp.concatenate([tag_row[None], jnp.zeros((15, half_kv), BF16)], 0)
    k_sent = jnp.concatenate([cols(key_heads[0], 1 - core, half_kv), tag_rows], 0)
    got = swapped(after(k_sent, *[parts[0] for parts in slabs]))

    if out_rows % 8 == 0:
        at = jnp.stack([my_y, my_fsdp]).astype(jnp.int32)
        pieces = run_pieces(after(at, k_sent), tokens, n_z, n_fsdp, out_rows)
    else:
        turned = tokens.T.reshape(n_z, 2, 2, n_fsdp, out_rows, shard_rows)
        pieces = []
        for flip, s in places:
            piece = lax.dynamic_index_in_dim(turned, my_y ^ flip, 1, keepdims=False)
            piece = lax.dynamic_index_in_dim(piece, (my_fsdp + s) % n_fsdp, 2, keepdims=False)
            pieces.append(piece.reshape(n_z * 2 * out_rows, shard_rows))
    by_place = dict(zip(places, pieces))

    k_own = jnp.concatenate(
        [
            placed(core, cols(key_heads[0], core, half_kv), got[:shard_rows], 0),
            tag_rows + got[shard_rows:],
        ],
        0,
    )
    k_own = after(k_own, *pieces)
    k_far = shifted(k_own, 4)
    over_y = {s: flipped(after(by_place[1, s], k_own)) for s in range(1, n_fsdp)}
    q_sent = jnp.concatenate([cols(queries[0], 1 - core, half_q), cols(d_out[0], 1 - core, half_q)], 1)
    q_other = swapped(after(q_sent, k_own))
    if aligned:
        value_own = run_product(after(fsdp_arg, q_sent), [tokens], w_value, F32)
    else:
        value_own = dot(cols(tokens, my_fsdp, slab), w_value)
    firsts = [parts[0] for parts in sent]
    k_far, over_y, firsts, _ = lax.optimization_barrier((k_far, over_y, firsts, value_own))
    sent = [[x, *parts[1:]] for x, parts in zip(firsts, sent)]
    k_near = flipped(jnp.where(my_y == 0, k_own, k_far))
    keys = [k_far, k_near, k_own]

    span_tags = jnp.concatenate([k[chip_rows, :chip_rows] for k in keys], 0)
    key_at = jnp.arange(WINDOW + chip_rows, dtype=jnp.int32)
    chip_tags = k_own[chip_rows, :chip_rows]
    before = (span_tags[None, :] < chip_tags[:, None]) | (key_at + first < WINDOW)[None, :]
    low = jnp.sum(before.astype(jnp.int32), axis=1)
    low = jnp.maximum(low, jnp.arange(1, chip_rows + 1, dtype=jnp.int32))[None, :]

    if aligned:
        partial = [run_product(zero_arg, parts, w_value, BF16) for parts in sent]
    else:
        partial = [dot(parts[0], w_value).astype(BF16) for parts in sent]
    low = after(low, *partial)
    e, inv, do_t, dv_far, dv_near, dv_mine = run_probs(
        core_arg, low, queries[0], q_other, d_out[0], keys, chip_rows, half_kv
    )
    dv_got = flipped(dv_near)

    value_back = [rotated(x, -s - 1) for s, x in enumerate(partial)]
    *value_back, _ = lax.optimization_barrier((*value_back, dv_near))
    value_sum = value_own
    for x in value_back:
        value_sum = value_sum + x.astype(F32)
    own_values = value_sum.astype(BF16)
    v_own = placed(core, cols(own_values, core, half_kv), swapped(cols(own_values, 1 - core, half_kv)), 0)

    over_y[0] = flipped(after(by_place[1, 0], k_near))
    v_own, over_y[0] = lax.optimization_barrier((v_own, over_y[0]))
    v_far = shifted(v_own, 4)
    own_pairs = [jnp.concatenate([by_place[0, 0], over_y[0]], 1)]
    other_pairs = [swapped(after(own_pairs[0], v_own))]
    for s in range(1, n_fsdp):
        both = jnp.concatenate([by_place[0, s], over_y[s]], 1)
        own_pairs.append(rotated(after(both, own_values), s))

    dv_got = after(dv_got, v_own)
    dv_sent = relayed(my_y, dv_far, dv_got)
    dv_back = shifted(dv_sent, -4)
    v_sent = after(jnp.where(my_y == 0, v_own, v_far), dv_sent)
    v_near = flipped(v_sent)
    vals = [v_far, v_near, v_own]
    dv_chip = gathered_terms(my_y, dv_mine, dv_got, after(dv_back, v_sent))
    dv_fsdp = [dv_chip] + [rotated(dv_chip, s) for s in range(1, n_fsdp)]
    dv_over_y = [moved(dv_chip, 1, s) for s in range(n_fsdp)]
    own_pairs[1:] = [after(x, dv_chip) for x in own_pairs[1:]]
    v_near = after(v_near, dv_chip)
    other_pairs += [swapped(x) for x in own_pairs[1:]]
    vals = [v_far, v_near, v_own]
    out, dq, other, dk_far, dk_near, dk_mine = run_grads(
        core_arg, e, inv, do_t, queries[0], q_other, keys, vals, chip_rows, half_kv
    )
    dk_got = flipped(dk_near)

    dv_fsdp = [after(x, dk_near) for x in dv_fsdp]
    dv_over_y = [after(x, dk_near) for x in dv_over_y]
    dv_other = swapped(jnp.concatenate([rows_of(x, 1 - core, shard_rows) for x in dv_fsdp], 0))
    dv_rows = placed(
        core, jnp.concatenate([rows_of(x, core, shard_rows) for x in dv_fsdp], 0), dv_other, 1
    )
    if aligned:
        d_tokens, *made = run_tokens(fsdp_arg, dv_rows, w_value, n_fsdp)
    else:
        made = dot(dv_rows, w_value, NT).astype(BF16)
        made = [made[s * shard_rows : (s + 1) * shard_rows] for s in range(n_fsdp)]
        d_tokens = jnp.concatenate([made[0]] * n_fsdp, 1)
        made = made[1:]
    for s in range(1, n_fsdp):
        back = rotated(made[s - 1], -s)
        d_tokens = lax.dynamic_update_slice_in_dim(d_tokens, back, ((my_fsdp + s) % n_fsdp) * slab, 1)

    dv_pairs = list(zip(dv_fsdp, dv_over_y))
    if out_rows % 8 == 0:
        at = after(jnp.stack([core, my_z]).astype(jnp.int32), *made)
        by_z = run_weight(at, own_pairs, other_pairs, dv_pairs, n_z)
    else:
        weight_term = 0.0
        for p in range(n_fsdp):
            for flip in range(2):
                window = slice(flip * shard_rows, (flip + 1) * shard_rows)
                weight_term += dot(own_pairs[p][:, window], rows_of(dv_pairs[p][flip], core, shard_rows))
                weight_term += dot(other_pairs[p][:, window], rows_of(dv_pairs[p][flip], 1 - core, shard_rows))
        weight_term = weight_term.reshape(n_z, 2 * out_rows, half_kv)
        by_z = [
            lax.dynamic_index_in_dim(weight_term, (my_z + d) % n_z, 0, keepdims=False).astype(BF16 if d else F32)
            for d in range(n_z)
        ]
    over_z = [
        lax.ppermute(by_z[d], "ctx", [(i, (i + 4 * d) % n_ctx) for i in range(n_ctx)]) for d in range(1, n_z)
    ]

    dk_got = after(dk_got, by_z[0])
    dk_sent = relayed(my_y, dk_far, dk_got)
    dk_back = shifted(dk_sent, -4)

    over_z, _ = lax.optimization_barrier((over_z, dk_sent))
    row_sum = by_z[0]
    for x in over_z:
        row_sum = row_sum + x.astype(F32)
    d_weight = placed(core, rows_of(row_sum, core, out_rows), swapped(rows_of(row_sum, 1 - core, out_rows)), 1)

    dk_chip = gathered_terms(my_y, dk_mine, dk_got, dk_back)
    d_keys = placed(core, rows_of(dk_chip, core, shard_rows), swapped(rows_of(dk_chip, 1 - core, shard_rows)), 1)
    other = swapped(after(other, *made))
    out = lax.dynamic_update_slice_in_dim(out, other[0], (1 - core) * half_q, 1)
    dq = lax.dynamic_update_slice_in_dim(dq, other[1], (1 - core) * half_q, 1)
    return (out[None], dq[None], d_keys[None], d_tokens[None], d_weight)


def solution(mesh):
    in_specs = (
        P("fsdp", "ctx", None),
        P("fsdp", "ctx", None),
        P("fsdp", "ctx", None),
        P("fsdp", None),
        P("fsdp", "ctx", None),
        P("fsdp", "ctx"),
    )
    out_specs = (
        P("fsdp", "ctx", None),
        P("fsdp", "ctx", None),
        P("fsdp", "ctx", None),
        P("fsdp", "ctx", None),
        P(("ctx", "fsdp"), None),
    )
    return jax.shard_map(shards, mesh=mesh, in_specs=in_specs, out_specs=out_specs, check_vma=False)
```

```python
import functools
import math

import jax
import jax.numpy as jnp
from jax import lax
from jax.experimental import pallas as pl
from jax.experimental.pallas import tpu as pltpu
from jax.sharding import PartitionSpec as P

HQ = 16
HK = 8
HD = 128
WINDOW = 1024
GROUP = 2
NEG = -1e30
VMEM_BYTES = 58 * 1024 * 1024

score_scale = 1.0 / math.sqrt(168.0)
exp2_scale = score_scale / math.log(2.0)

BF16 = jnp.bfloat16
F32 = jnp.float32
NT = (((1,), (1,)), ((), ()))
TN = (((0,), (0,)), ((), ()))


def dot(a, b, dims=(((1,), (0,)), ((), ()))):
    return lax.dot_general(a, b, dims, preferred_element_type=F32)


def probs_kernel(blk, n_back, core_ref, low_ref, q_own, q_other, do_own, do_other, *refs):
    n_arr = n_back + 1
    k_refs = refs[:n_arr]
    e_ref, inv_ref, dot_ref = refs[n_arr : n_arr + 3]
    dv_refs = refs[n_arr + 3 : 2 * n_arr + 3]
    bias, s_scr, dv_acc, q_buf, do_buf = refs[2 * n_arr + 3 :]
    span_blocks = WINDOW // blk + 1
    core = core_ref[0]

    @pl.when(pl.program_id(0) == 0)
    def _():
        for qb in range(2):
            kpos = lax.broadcasted_iota(jnp.int32, (span_blocks * blk, blk), 0) + qb * blk
            qpos = lax.broadcasted_iota(jnp.int32, (span_blocks * blk, blk), 1) + (qb * blk + WINDOW)
            low = low_ref[:, qb * blk : (qb + 1) * blk]
            ok = (kpos >= low) & (kpos <= qpos)
            bias[qb] = jnp.where(ok, 0.0, NEG)

    q_buf[core] = q_own[...]
    q_buf[1 - core] = q_other[...]
    do_buf[core] = do_own[...]
    do_buf[1 - core] = do_other[...]

    def key_block(j):
        return k_refs[j // 2][(j % 2) * blk : (j % 2 + 1) * blk, :]

    def stacked(buf, qb):
        return jnp.concatenate([buf[qb, :, r * HD : (r + 1) * HD] for r in range(GROUP)], 0)

    for qb in range(2):
        qs = stacked(q_buf, qb)
        top = None
        for j in range(span_blocks):
            s = dot(key_block(qb + j), qs, NT)
            b = bias[qb, j * blk : (j + 1) * blk, :]
            s = s * exp2_scale + jnp.concatenate([b] * GROUP, 1)
            s_scr[j] = s
            part = jnp.max(s.reshape(blk // 8, 8, GROUP * blk), axis=0)
            top = part if top is None else jnp.maximum(top, part)
        top = jnp.max(top, axis=0, keepdims=True)
        total = None
        for j in range(span_blocks):
            e = jnp.exp2(s_scr[j] - top)
            part = jnp.sum(e.reshape(blk // 8, 8, GROUP * blk), axis=0)
            total = part if total is None else total + part
            e_ref[0, qb, j * blk : (j + 1) * blk, :] = e.astype(BF16)
        inv = 1.0 / jnp.sum(total, axis=0, keepdims=True)
        inv_ref[0, qb] = inv
        do_t = (stacked(do_buf, qb).astype(F32).T * inv).astype(BF16)
        dot_ref[0, qb] = do_t
        for j in range(span_blocks):
            term = dot(e_ref[0, qb, j * blk : (j + 1) * blk, :], do_t, NT)
            at = slice((qb + j) * blk, (qb + j + 1) * blk)
            if qb == 0 or j == span_blocks - 1:
                dv_acc[at, :] = term
            else:
                dv_acc[at, :] += term
    for a in range(n_arr):
        dv_refs[a][...] = dv_acc[a * 2 * blk : (a + 1) * 2 * blk, :].astype(BF16)


def grads_kernel(blk, n_back, core_ref, e_ref, inv_ref, dot_ref, q_own, q_other, *refs):
    n_arr = n_back + 1
    k_refs = refs[:n_arr]
    v_refs = refs[n_arr : 2 * n_arr]
    out_ref, dq_ref, other_ref = refs[2 * n_arr : 2 * n_arr + 3]
    dk_refs = refs[2 * n_arr + 3 : 3 * n_arr + 3]
    dk_acc, q_buf, out_buf, dq_buf = refs[3 * n_arr + 3 :]
    span_blocks = WINDOW // blk + 1
    core = core_ref[0]

    q_buf[core] = q_own[...]
    q_buf[1 - core] = q_other[...]

    def block_of(arrays, j):
        return arrays[j // 2][(j % 2) * blk : (j % 2 + 1) * blk, :]

    for qb in range(2):
        qs = jnp.concatenate([q_buf[qb, :, r * HD : (r + 1) * HD] for r in range(GROUP)], 0)
        do_t = dot_ref[0, qb]
        out_t = None
        for j in range(span_blocks):
            e = e_ref[0, qb, j * blk : (j + 1) * blk, :]
            part = dot(block_of(v_refs, qb + j), e, TN)
            out_t = part if out_t is None else out_t + part
        out_t = (out_t * inv_ref[0, qb]).astype(BF16).astype(F32)
        delta = jnp.sum(out_t * do_t.astype(F32), axis=0, keepdims=True)
        out = out_t.T.astype(BF16)
        dq_t = None
        for j in range(span_blocks):
            e = e_ref[0, qb, j * blk : (j + 1) * blk, :].astype(F32)
            dp = dot(block_of(v_refs, qb + j), do_t)
            ds = (e * (dp - delta)).astype(BF16)
            term = dot(ds, qs)
            at = slice((qb + j) * blk, (qb + j + 1) * blk)
            if qb == 0 or j == span_blocks - 1:
                dk_acc[at, :] = term
            else:
                dk_acc[at, :] += term
            part = dot(block_of(k_refs, qb + j), ds, TN)
            dq_t = part if dq_t is None else dq_t + part
        dq = (dq_t * score_scale).T.astype(BF16)
        for r in range(GROUP):
            out_buf[qb, :, r * HD : (r + 1) * HD] = out[r * blk : (r + 1) * blk, :]
            dq_buf[qb, :, r * HD : (r + 1) * HD] = dq[r * blk : (r + 1) * blk, :]
    out_ref[...] = out_buf[core]
    dq_ref[...] = dq_buf[core]
    other_ref[0] = out_buf[1 - core]
    other_ref[1] = dq_buf[1 - core]
    for a in range(n_arr):
        dk_refs[a][...] = (dk_acc[a * 2 * blk : (a + 1) * 2 * blk, :] * score_scale).astype(BF16)


def specs_of(rows, width):
    blk = rows // 2
    heads = width // HD
    span = WINDOW + blk
    lanes = GROUP * blk
    head = pl.BlockSpec((rows, HD), lambda g, c: (0, g))
    own = pl.BlockSpec((blk, GROUP * HD), lambda g, c: (0, c[0] * heads + g))
    return blk, heads, span, lanes, head, own


def run_probs(core, low, q, q_other, do, keys, rows, width):
    blk, heads, span, lanes, head, own = specs_of(rows, width)
    n_arr = len(keys)
    return pl.pallas_call(
        functools.partial(probs_kernel, blk, n_arr - 1),
        grid_spec=pltpu.PrefetchScalarGridSpec(
            num_scalar_prefetch=1,
            grid=(heads,),
            in_specs=[
                pl.BlockSpec((1, rows), lambda g, c: (0, 0)),
                own,
                pl.BlockSpec((blk, GROUP * HD), lambda g, c: (0, g)),
                own,
                pl.BlockSpec((blk, GROUP * HD), lambda g, c: (0, heads + g)),
            ]
            + [head] * n_arr,
            out_specs=[
                pl.BlockSpec((1, 2, span, lanes), lambda g, c: (g, 0, 0, 0)),
                pl.BlockSpec((1, 2, 1, lanes), lambda g, c: (g, 0, 0, 0)),
                pl.BlockSpec((1, 2, HD, lanes), lambda g, c: (g, 0, 0, 0)),
            ]
            + [head] * n_arr,
            scratch_shapes=[
                pltpu.VMEM((2, span, blk), F32),
                pltpu.VMEM((span // blk, blk, lanes), F32),
                pltpu.VMEM((WINDOW + rows, HD), F32),
                pltpu.VMEM((2, blk, GROUP * HD), BF16),
                pltpu.VMEM((2, blk, GROUP * HD), BF16),
            ],
        ),
        out_shape=[
            jax.ShapeDtypeStruct((heads, 2, span, lanes), BF16),
            jax.ShapeDtypeStruct((heads, 2, 1, lanes), F32),
            jax.ShapeDtypeStruct((heads, 2, HD, lanes), BF16),
        ]
        + [jax.ShapeDtypeStruct((rows, width), BF16)] * n_arr,
        compiler_params=pltpu.CompilerParams(vmem_limit_bytes=VMEM_BYTES),
        cost_estimate=small_cost(),
        name="probs",
    )(core, low, q, q_other, do, q_other, *keys)


def run_grads(core, e, inv, do_t, q, q_other, keys, values, rows, width):
    blk, heads, span, lanes, head, own = specs_of(rows, width)
    n_arr = len(keys)
    full = jax.ShapeDtypeStruct(q.shape, BF16)
    return pl.pallas_call(
        functools.partial(grads_kernel, blk, n_arr - 1),
        grid_spec=pltpu.PrefetchScalarGridSpec(
            num_scalar_prefetch=1,
            grid=(heads,),
            in_specs=[
                pl.BlockSpec((1, 2, span, lanes), lambda g, c: (g, 0, 0, 0)),
                pl.BlockSpec((1, 2, 1, lanes), lambda g, c: (g, 0, 0, 0)),
                pl.BlockSpec((1, 2, HD, lanes), lambda g, c: (g, 0, 0, 0)),
                own,
                pl.BlockSpec((blk, GROUP * HD), lambda g, c: (0, g)),
            ]
            + [head] * (2 * n_arr),
            out_specs=[own, own, pl.BlockSpec((2, blk, GROUP * HD), lambda g, c: (0, 0, g))] + [head] * n_arr,
            scratch_shapes=[
                pltpu.VMEM((WINDOW + rows, HD), F32),
                pltpu.VMEM((2, blk, GROUP * HD), BF16),
                pltpu.VMEM((2, blk, GROUP * HD), BF16),
                pltpu.VMEM((2, blk, GROUP * HD), BF16),
            ],
        ),
        out_shape=[full, full, jax.ShapeDtypeStruct((2, blk, GROUP * width), BF16)]
        + [jax.ShapeDtypeStruct((rows, width), BF16)] * n_arr,
        compiler_params=pltpu.CompilerParams(vmem_limit_bytes=VMEM_BYTES),
        cost_estimate=small_cost(),
        name="grads",
    )(core, e, inv, do_t, q, q_other, *keys, *values)


def small_cost():
    return pl.CostEstimate(flops=1 << 20, bytes_accessed=1 << 12, transcendentals=0)


def whole():
    return pl.BlockSpec(memory_space=pltpu.VMEM)


def pieces_kernel(dims, at_ref, x_ref, *refs):
    n_z, n_fsdp, out_rows = dims
    outs = refs[: 2 * n_fsdp]
    turned = refs[2 * n_fsdp]
    my_y, my_fsdp = at_ref[0], at_ref[1]
    for c in range(x_ref.shape[1] // HD):
        turned[c * HD : (c + 1) * HD, :] = x_ref[:, c * HD : (c + 1) * HD].astype(F32).T
    for p, out in enumerate(outs):
        flip, s = p // n_fsdp, p % n_fsdp
        y = lax.rem(my_y + flip, 2)
        f = lax.rem(my_fsdp + s, n_fsdp)
        for z in range(n_z):
            parts = []
            for core in range(2):
                block = ((z * 2 + y) * 2 + core) * n_fsdp + f
                parts.append(turned[pl.ds(pl.multiple_of(block * out_rows, 8), out_rows), :])
            out[z * 2 * out_rows : (z + 1) * 2 * out_rows, :] = jnp.concatenate(parts, 0).astype(BF16)


def run_pieces(at, tokens, n_z, n_fsdp, out_rows):
    rows, model = tokens.shape
    shape = jax.ShapeDtypeStruct((n_z * 2 * out_rows, rows), BF16)
    return pl.pallas_call(
        functools.partial(pieces_kernel, (n_z, n_fsdp, out_rows)),
        in_specs=[pl.BlockSpec(memory_space=pltpu.SMEM), whole()],
        out_specs=[whole()] * (2 * n_fsdp),
        out_shape=[shape] * (2 * n_fsdp),
        scratch_shapes=[pltpu.VMEM((model, rows), F32)],
        compiler_params=pltpu.CompilerParams(vmem_limit_bytes=VMEM_BYTES),
        cost_estimate=small_cost(),
        name="pieces",
    )(at, tokens)


def product_kernel(at_ref, *refs):
    *x_refs, w_ref, o_ref = refs
    total, first = None, 0
    for x in x_refs:
        term = dot(x[...], w_ref[first : first + x.shape[1], :])
        total = term if total is None else total + term
        first += x.shape[1]
    o_ref[...] = total.astype(o_ref.dtype)


def run_product(at, parts, w, kind):
    rows = parts[0].shape[0]
    depth, width = w.shape
    tile = 256
    if len(parts) == 1:
        x_specs = [pl.BlockSpec((rows, depth), lambda j, at: (0, at[0]))]
    else:
        x_specs = [pl.BlockSpec(x.shape, lambda j, at: (0, 0)) for x in parts]
    return pl.pallas_call(
        product_kernel,
        grid_spec=pltpu.PrefetchScalarGridSpec(
            num_scalar_prefetch=1,
            grid=(width // tile,),
            in_specs=x_specs + [pl.BlockSpec((depth, tile), lambda j, at: (0, j))],
            out_specs=pl.BlockSpec((rows, tile), lambda j, at: (0, j)),
        ),
        out_shape=jax.ShapeDtypeStruct((rows, width), kind),
        compiler_params=pltpu.CompilerParams(vmem_limit_bytes=VMEM_BYTES),
        cost_estimate=small_cost(),
        name="product",
    )(at, *parts, w)


def weight_kernel(n_z, n, at_ref, *refs):
    own_pairs, other_pairs = refs[:n], refs[n : 2 * n]
    dv_refs = refs[2 * n : 4 * n]
    outs = refs[4 * n :]
    core = at_ref[0]
    step = pl.program_id(0)
    rows = own_pairs[0].shape[1] // 2
    own = pl.ds(pl.multiple_of(core * rows, rows), rows)
    other = pl.ds(pl.multiple_of((1 - core) * rows, rows), rows)
    total = None
    for p in range(n):
        for flip in range(2):
            window = slice(flip * rows, (flip + 1) * rows)
            term = dot(own_pairs[p][:, window], dv_refs[2 * p + flip][own, :])
            term = term + dot(other_pairs[p][:, window], dv_refs[2 * p + flip][other, :])
            total = term if total is None else total + term
    for d, out in enumerate(outs):

        @pl.when(step == (n_z - 1 if d == 0 else d - 1))
        def _():
            out[...] = total.astype(out.dtype)


def run_weight(at, own_pairs, other_pairs, dv_pairs, n_z):
    n = len(own_pairs)
    count = own_pairs[0].shape[0] // n_z
    rows2 = own_pairs[0].shape[1]
    dvs = [x for pair_of in dv_pairs for x in pair_of]
    width = dvs[0].shape[1]
    shapes = [jax.ShapeDtypeStruct((count, width), F32 if d == 0 else BF16) for d in range(n_z)]
    pair_block = pl.BlockSpec((count, rows2), lambda d, at: (lax.rem(at[1] + d + 1, n_z), 0))
    return pl.pallas_call(
        functools.partial(weight_kernel, n_z, n),
        grid_spec=pltpu.PrefetchScalarGridSpec(
            num_scalar_prefetch=1,
            grid=(n_z,),
            in_specs=[pair_block] * (2 * n) + [pl.BlockSpec(dvs[0].shape, lambda d, at: (0, 0))] * (2 * n),
            out_specs=[pl.BlockSpec((count, width), lambda d, at: (0, 0))] * n_z,
        ),
        out_shape=shapes,
        compiler_params=pltpu.CompilerParams(vmem_limit_bytes=VMEM_BYTES),
        cost_estimate=small_cost(),
        name="weight",
    )(at, *own_pairs, *other_pairs, *dvs)


def tokens_kernel(n_fsdp, at_ref, dv_ref, w_ref, own_ref, *others):
    made = dot(dv_ref[...], w_ref[...], NT).astype(BF16)
    rows = own_ref.shape[0]
    own_ref[...] = made[:rows]
    for s, ref in enumerate(others):
        ref[...] = made[(s + 1) * rows : (s + 2) * rows]


def run_tokens(at, dv_rows, w, n_fsdp):
    slab, width = w.shape
    rows = dv_rows.shape[0] // n_fsdp
    tile = 3 * HD if slab % (3 * HD) == 0 else slab
    n_tiles = slab // tile
    return pl.pallas_call(
        functools.partial(tokens_kernel, n_fsdp),
        grid_spec=pltpu.PrefetchScalarGridSpec(
            num_scalar_prefetch=1,
            grid=(n_tiles,),
            in_specs=[
                pl.BlockSpec(dv_rows.shape, lambda j, at: (0, 0)),
                pl.BlockSpec((tile, width), lambda j, at: (j, 0)),
            ],
            out_specs=[pl.BlockSpec((rows, tile), lambda j, at: (0, at[0] * n_tiles + j))]
            + [pl.BlockSpec((rows, tile), lambda j, at: (0, j))] * (n_fsdp - 1),
        ),
        out_shape=[jax.ShapeDtypeStruct((rows, slab * n_fsdp), BF16)]
        + [jax.ShapeDtypeStruct((rows, slab), BF16)] * (n_fsdp - 1),
        compiler_params=pltpu.CompilerParams(vmem_limit_bytes=VMEM_BYTES),
        cost_estimate=small_cost(),
        name="tokens",
    )(at, dv_rows, w)


def shifted(x, by):
    length = lax.axis_size("ctx")
    return lax.ppermute(x, "ctx", [(i, i + by) for i in range(length) if 0 <= i + by < length])


def swapped(x):
    return lax.ppermute(x, "ctx", [(i, i ^ 1) for i in range(lax.axis_size("ctx"))])


def rotated(x, by):
    length = lax.axis_size("fsdp")
    return lax.ppermute(x, "fsdp", [(i, (i + by) % length) for i in range(length)])


def moved(x, flip, by):
    n_ctx, n_fsdp = lax.axis_size("ctx"), lax.axis_size("fsdp")
    pairs = [
        (c * n_fsdp + f, (c ^ (2 * flip)) * n_fsdp + (f + by) % n_fsdp)
        for c in range(n_ctx)
        for f in range(n_fsdp)
    ]
    return lax.ppermute(x, ("ctx", "fsdp"), pairs)


def relayed(my_y, far, got):
    return (far.astype(F32) + jnp.where(my_y == 1, got.astype(F32), 0.0)).astype(BF16)


def gathered_terms(my_y, mine, got, back):
    return (mine.astype(F32) + back.astype(F32) + jnp.where(my_y == 0, got.astype(F32), 0.0)).astype(BF16)


def cols(x, at, width):
    return lax.dynamic_slice_in_dim(x, at * width, width, x.ndim - 1)


def rows_of(x, at, count):
    return lax.dynamic_slice_in_dim(x, at * count, count, 0)


def placed(core, own, other, axis):
    both = jnp.concatenate([own, own], axis)
    return lax.dynamic_update_slice_in_dim(both, other, (1 - core) * own.shape[axis], axis)


def flipped(x):
    return lax.ppermute(x, "ctx", [(i, i ^ 2) for i in range(lax.axis_size("ctx"))])


def after(x, *earlier):
    return lax.optimization_barrier((x, *earlier))[0]


def shards(hidden, queries, key_heads, w_value, d_out, segments):
    shard_rows = hidden.shape[1]
    model = hidden.shape[2]
    kv_width = w_value.shape[1]
    n_ctx = lax.axis_size("ctx")
    n_fsdp = lax.axis_size("fsdp")
    chip_rows = 2 * shard_rows
    n_z = n_ctx // 4
    assert WINDOW == 2 * chip_rows
    my_ctx = lax.axis_index("ctx")
    my_fsdp = lax.axis_index("fsdp")
    core = my_ctx % 2
    core_arg = core.astype(jnp.int32).reshape(1)
    chip = my_ctx // 2
    my_y = chip % 2
    my_z = chip // 2
    half_kv = kv_width // 2
    slab = model // n_fsdp
    tokens = hidden[0]
    first = chip * chip_rows

    aligned = slab % HD == 0
    fsdp_arg = my_fsdp.astype(jnp.int32).reshape(1)
    zero_arg = jnp.zeros((1,), jnp.int32)
    half_q = queries.shape[2] // 2
    out_rows = model // (n_ctx * n_fsdp)
    places = [(flip, s) for flip in range(2) for s in range(n_fsdp)]

    cut = slab // HD // 2 * HD if aligned else slab
    parts_at = [(0, cut), (cut, slab)] if aligned else [(0, slab)]
    slabs = [
        [
            lax.dynamic_slice_in_dim(tokens, (my_fsdp + s) % n_fsdp * slab + low, high - low, 1)
            for low, high in parts_at
        ]
        for s in range(1, n_fsdp)
    ]
    sent = [[rotated(x, s + 1) for x in parts] for s, parts in enumerate(slabs)]

    own_tags = segments[0].astype(BF16)
    tag_row = lax.dynamic_update_slice_in_dim(jnp.zeros((half_kv,), BF16), own_tags, core * shard_rows, 0)
    tag_rows = jnp.concatenate([tag_row[None], jnp.zeros((15, half_kv), BF16)], 0)
    k_sent = jnp.concatenate([cols(key_heads[0], 1 - core, half_kv), tag_rows], 0)
    got = swapped(after(k_sent, *[parts[0] for parts in slabs]))

    if out_rows % 8 == 0:
        at = jnp.stack([my_y, my_fsdp]).astype(jnp.int32)
        pieces = run_pieces(after(at, k_sent, got), tokens, n_z, n_fsdp, out_rows)
    else:
        turned = tokens.T.reshape(n_z, 2, 2, n_fsdp, out_rows, shard_rows)
        pieces = []
        for flip, s in places:
            piece = lax.dynamic_index_in_dim(turned, my_y ^ flip, 1, keepdims=False)
            piece = lax.dynamic_index_in_dim(piece, (my_fsdp + s) % n_fsdp, 2, keepdims=False)
            pieces.append(piece.reshape(n_z * 2 * out_rows, shard_rows))
    by_place = dict(zip(places, pieces))

    k_own = jnp.concatenate(
        [
            placed(core, cols(key_heads[0], core, half_kv), got[:shard_rows], 0),
            tag_rows + got[shard_rows:],
        ],
        0,
    )
    k_far = shifted(k_own, 4)
    k_near = shifted(k_own, 2)
    over_y = {s: flipped(after(by_place[1, s], k_own)) for s in range(1, n_fsdp)}
    q_sent = jnp.concatenate([cols(queries[0], 1 - core, half_q), cols(d_out[0], 1 - core, half_q)], 1)
    q_other = swapped(after(q_sent, k_own))
    if aligned:
        value_own = run_product(after(fsdp_arg, q_sent), [tokens], w_value, F32)
    else:
        value_own = dot(cols(tokens, my_fsdp, slab), w_value)
    keys = [k_far, k_near, k_own]

    span_tags = jnp.concatenate([k[chip_rows, :chip_rows] for k in keys], 0)
    key_at = jnp.arange(WINDOW + chip_rows, dtype=jnp.int32)
    chip_tags = k_own[chip_rows, :chip_rows]
    before = (span_tags[None, :] < chip_tags[:, None]) | (key_at + first < WINDOW)[None, :]
    low = jnp.sum(before.astype(jnp.int32), axis=1)
    low = jnp.maximum(low, jnp.arange(1, chip_rows + 1, dtype=jnp.int32))[None, :]

    if aligned:
        partial = [run_product(zero_arg, parts, w_value, BF16) for parts in sent]
    else:
        partial = [dot(parts[0], w_value).astype(BF16) for parts in sent]
    low = after(low, *partial, *over_y.values())
    e, inv, do_t, dv_far, dv_near, dv_mine = run_probs(
        core_arg, low, queries[0], q_other, d_out[0], keys, chip_rows, half_kv
    )
    dv_got = flipped(dv_near)

    value_back = [rotated(x, -s - 1) for s, x in enumerate(partial)]
    *value_back, _ = lax.optimization_barrier((*value_back, dv_near))
    value_sum = value_own
    for x in value_back:
        value_sum = value_sum + x.astype(F32)
    own_values = value_sum.astype(BF16)
    v_own = placed(core, cols(own_values, core, half_kv), swapped(cols(own_values, 1 - core, half_kv)), 0)

    over_y[0] = flipped(after(by_place[1, 0], k_near))
    both_y = [
        after(jnp.concatenate([by_place[0, s], over_y[s]], 1), own_values) for s in range(1, n_fsdp)
    ]
    v_own, over_y[0], both_y = lax.optimization_barrier((v_own, over_y[0], both_y))
    v_far = shifted(v_own, 4)
    own_pairs = [jnp.concatenate([by_place[0, 0], over_y[0]], 1)]
    other_pairs = [swapped(after(own_pairs[0], v_own))]
    own_pairs += [rotated(x, s + 1) for s, x in enumerate(both_y)]

    dv_got = after(dv_got, v_own)
    dv_sent = relayed(my_y, dv_far, dv_got)
    dv_back = shifted(dv_sent, -4)
    v_sent = after(jnp.where(my_y == 0, v_own, v_far), dv_sent)
    v_near = flipped(v_sent)
    vals = [v_far, v_near, v_own]
    dv_chip = gathered_terms(my_y, dv_mine, dv_got, after(dv_back, v_sent))
    dv_fsdp = [dv_chip] + [rotated(dv_chip, s) for s in range(1, n_fsdp)]
    dv_over_y = [moved(dv_chip, 1, s) for s in range(n_fsdp)]
    v_near = after(v_near, dv_chip)
    vals = [v_far, v_near, v_own]
    out, dq, other, dk_far, dk_near, dk_mine = run_grads(
        core_arg, e, inv, do_t, queries[0], q_other, keys, vals, chip_rows, half_kv
    )
    dk_got = flipped(dk_near)
    own_pairs[1:] = [after(x, dk_near) for x in own_pairs[1:]]
    other_pairs += [swapped(x) for x in own_pairs[1:]]

    dv_fsdp = [after(x, dk_near) for x in dv_fsdp]
    dv_over_y = [after(x, dk_near) for x in dv_over_y]
    dv_other = swapped(jnp.concatenate([rows_of(x, 1 - core, shard_rows) for x in dv_fsdp], 0))
    dv_rows = placed(
        core, jnp.concatenate([rows_of(x, core, shard_rows) for x in dv_fsdp], 0), dv_other, 1
    )
    dv_rows = after(dv_rows, *dv_over_y)
    if aligned:
        d_tokens, *made = run_tokens(fsdp_arg, dv_rows, w_value, n_fsdp)
    else:
        made = dot(dv_rows, w_value, NT).astype(BF16)
        made = [made[s * shard_rows : (s + 1) * shard_rows] for s in range(n_fsdp)]
        d_tokens = jnp.concatenate([made[0]] * n_fsdp, 1)
        made = made[1:]
    for s in range(1, n_fsdp):
        back = rotated(made[s - 1], -s)
        d_tokens = lax.dynamic_update_slice_in_dim(d_tokens, back, ((my_fsdp + s) % n_fsdp) * slab, 1)

    dk_sent = relayed(my_y, dk_far, after(dk_got, *made))
    dk_back = shifted(dk_sent, -4)

    dv_pairs = list(zip(dv_fsdp, dv_over_y))
    if out_rows % 8 == 0:
        at = after(jnp.stack([core, my_z]).astype(jnp.int32), dk_sent)
        by_z = run_weight(at, own_pairs, other_pairs, dv_pairs, n_z)
    else:
        weight_term = 0.0
        for p in range(n_fsdp):
            for flip in range(2):
                window = slice(flip * shard_rows, (flip + 1) * shard_rows)
                weight_term += dot(own_pairs[p][:, window], rows_of(dv_pairs[p][flip], core, shard_rows))
                weight_term += dot(other_pairs[p][:, window], rows_of(dv_pairs[p][flip], 1 - core, shard_rows))
        weight_term = weight_term.reshape(n_z, 2 * out_rows, half_kv)
        by_z = [
            lax.dynamic_index_in_dim(weight_term, (my_z + d) % n_z, 0, keepdims=False).astype(BF16 if d else F32)
            for d in range(n_z)
        ]
    over_z = [
        lax.ppermute(by_z[d], "ctx", [(i, (i + 4 * d) % n_ctx) for i in range(n_ctx)]) for d in range(1, n_z)
    ]

    row_sum = by_z[0]
    for x in over_z:
        row_sum = row_sum + x.astype(F32)
    d_weight = placed(core, rows_of(row_sum, core, out_rows), swapped(rows_of(row_sum, 1 - core, out_rows)), 1)

    dk_chip = gathered_terms(my_y, dk_mine, dk_got, after(dk_back, *over_z[:1]))
    d_keys = placed(core, rows_of(dk_chip, core, shard_rows), swapped(rows_of(dk_chip, 1 - core, shard_rows)), 1)
    other = swapped(after(other, *made))
    out = lax.dynamic_update_slice_in_dim(out, other[0], (1 - core) * half_q, 1)
    dq = lax.dynamic_update_slice_in_dim(dq, other[1], (1 - core) * half_q, 1)
    return (out[None], dq[None], d_keys[None], d_tokens[None], d_weight)


def solution(mesh):
    in_specs = (
        P("fsdp", "ctx", None),
        P("fsdp", "ctx", None),
        P("fsdp", "ctx", None),
        P("fsdp", None),
        P("fsdp", "ctx", None),
        P("fsdp", "ctx"),
    )
    out_specs = (
        P("fsdp", "ctx", None),
        P("fsdp", "ctx", None),
        P("fsdp", "ctx", None),
        P("fsdp", "ctx", None),
        P(("ctx", "fsdp"), None),
    )
    return jax.shard_map(shards, mesh=mesh, in_specs=in_specs, out_specs=out_specs, check_vma=False)
```

```python
import functools
import math

import jax
import jax.numpy as jnp
from jax import lax
from jax.experimental import pallas as pl
from jax.experimental.pallas import tpu as pltpu
from jax.sharding import PartitionSpec as P

HQ = 16
HK = 8
HD = 128
WINDOW = 1024
GROUP = 2
NEG = -1e30
VMEM_BYTES = 58 * 1024 * 1024

score_scale = 1.0 / math.sqrt(168.0)
exp2_scale = score_scale / math.log(2.0)

BF16 = jnp.bfloat16
F32 = jnp.float32
NT = (((1,), (1,)), ((), ()))
TN = (((0,), (0,)), ((), ()))


def dot(a, b, dims=(((1,), (0,)), ((), ()))):
    return lax.dot_general(a, b, dims, preferred_element_type=F32)


def probs_kernel(blk, n_back, core_ref, low_ref, q_own, q_other, do_own, do_other, *refs):
    n_arr = n_back + 1
    k_refs = refs[:n_arr]
    e_ref, inv_ref, dot_ref = refs[n_arr : n_arr + 3]
    dv_refs = refs[n_arr + 3 : 2 * n_arr + 3]
    bias, s_scr, dv_acc, q_buf, do_buf = refs[2 * n_arr + 3 :]
    span_blocks = WINDOW // blk + 1
    core = core_ref[0]

    @pl.when(pl.program_id(0) == 0)
    def _():
        for qb in range(2):
            kpos = lax.broadcasted_iota(jnp.int32, (span_blocks * blk, blk), 0) + qb * blk
            qpos = lax.broadcasted_iota(jnp.int32, (span_blocks * blk, blk), 1) + (qb * blk + WINDOW)
            low = low_ref[:, qb * blk : (qb + 1) * blk]
            ok = (kpos >= low) & (kpos <= qpos)
            bias[qb] = jnp.where(ok, 0.0, NEG)

    q_buf[core] = q_own[...]
    q_buf[1 - core] = q_other[...]
    do_buf[core] = do_own[...]
    do_buf[1 - core] = do_other[...]

    def key_block(j):
        return k_refs[j // 2][(j % 2) * blk : (j % 2 + 1) * blk, :]

    def stacked(buf, qb):
        return jnp.concatenate([buf[qb, :, r * HD : (r + 1) * HD] for r in range(GROUP)], 0)

    for qb in range(2):
        qs = stacked(q_buf, qb)
        top = None
        for j in range(span_blocks):
            s = dot(key_block(qb + j), qs, NT)
            b = bias[qb, j * blk : (j + 1) * blk, :]
            s = s * exp2_scale + jnp.concatenate([b] * GROUP, 1)
            s_scr[j] = s
            part = jnp.max(s.reshape(blk // 8, 8, GROUP * blk), axis=0)
            top = part if top is None else jnp.maximum(top, part)
        top = jnp.max(top, axis=0, keepdims=True)
        total = None
        for j in range(span_blocks):
            e = jnp.exp2(s_scr[j] - top)
            part = jnp.sum(e.reshape(blk // 8, 8, GROUP * blk), axis=0)
            total = part if total is None else total + part
            e_ref[0, qb, j * blk : (j + 1) * blk, :] = e.astype(BF16)
        inv = 1.0 / jnp.sum(total, axis=0, keepdims=True)
        inv_ref[0, qb] = inv
        do_t = (stacked(do_buf, qb).astype(F32).T * inv).astype(BF16)
        dot_ref[0, qb] = do_t
        for j in range(span_blocks):
            term = dot(e_ref[0, qb, j * blk : (j + 1) * blk, :], do_t, NT)
            at = slice((qb + j) * blk, (qb + j + 1) * blk)
            if qb == 0 or j == span_blocks - 1:
                dv_acc[at, :] = term
            else:
                dv_acc[at, :] += term
    for a in range(n_arr):
        dv_refs[a][...] = dv_acc[a * 2 * blk : (a + 1) * 2 * blk, :].astype(BF16)


def grads_kernel(blk, n_back, core_ref, e_ref, inv_ref, dot_ref, q_own, q_other, *refs):
    n_arr = n_back + 1
    k_refs = refs[:n_arr]
    v_refs = refs[n_arr : 2 * n_arr]
    out_ref, dq_ref, other_ref = refs[2 * n_arr : 2 * n_arr + 3]
    dk_refs = refs[2 * n_arr + 3 : 3 * n_arr + 3]
    dk_acc, q_buf, out_buf, dq_buf = refs[3 * n_arr + 3 :]
    span_blocks = WINDOW // blk + 1
    core = core_ref[0]

    q_buf[core] = q_own[...]
    q_buf[1 - core] = q_other[...]

    def block_of(arrays, j):
        return arrays[j // 2][(j % 2) * blk : (j % 2 + 1) * blk, :]

    for qb in range(2):
        qs = jnp.concatenate([q_buf[qb, :, r * HD : (r + 1) * HD] for r in range(GROUP)], 0)
        do_t = dot_ref[0, qb]
        out_t = None
        for j in range(span_blocks):
            e = e_ref[0, qb, j * blk : (j + 1) * blk, :]
            part = dot(block_of(v_refs, qb + j), e, TN)
            out_t = part if out_t is None else out_t + part
        out_t = (out_t * inv_ref[0, qb]).astype(BF16).astype(F32)
        delta = jnp.sum(out_t * do_t.astype(F32), axis=0, keepdims=True)
        out = out_t.T.astype(BF16)
        dq_t = None
        for j in range(span_blocks):
            e = e_ref[0, qb, j * blk : (j + 1) * blk, :].astype(F32)
            dp = dot(block_of(v_refs, qb + j), do_t)
            ds = (e * (dp - delta)).astype(BF16)
            term = dot(ds, qs)
            at = slice((qb + j) * blk, (qb + j + 1) * blk)
            if qb == 0 or j == span_blocks - 1:
                dk_acc[at, :] = term
            else:
                dk_acc[at, :] += term
            part = dot(block_of(k_refs, qb + j), ds, TN)
            dq_t = part if dq_t is None else dq_t + part
        dq = (dq_t * score_scale).T.astype(BF16)
        for r in range(GROUP):
            out_buf[qb, :, r * HD : (r + 1) * HD] = out[r * blk : (r + 1) * blk, :]
            dq_buf[qb, :, r * HD : (r + 1) * HD] = dq[r * blk : (r + 1) * blk, :]
    out_ref[...] = out_buf[core]
    dq_ref[...] = dq_buf[core]
    other_ref[0] = out_buf[1 - core]
    other_ref[1] = dq_buf[1 - core]
    for a in range(n_arr):
        dk_refs[a][...] = (dk_acc[a * 2 * blk : (a + 1) * 2 * blk, :] * score_scale).astype(BF16)


def specs_of(rows, width):
    blk = rows // 2
    heads = width // HD
    span = WINDOW + blk
    lanes = GROUP * blk
    head = pl.BlockSpec((rows, HD), lambda g, c: (0, g))
    own = pl.BlockSpec((blk, GROUP * HD), lambda g, c: (0, c[0] * heads + g))
    return blk, heads, span, lanes, head, own


def run_probs(core, low, q, q_other, do, keys, rows, width):
    blk, heads, span, lanes, head, own = specs_of(rows, width)
    n_arr = len(keys)
    return pl.pallas_call(
        functools.partial(probs_kernel, blk, n_arr - 1),
        grid_spec=pltpu.PrefetchScalarGridSpec(
            num_scalar_prefetch=1,
            grid=(heads,),
            in_specs=[
                pl.BlockSpec((1, rows), lambda g, c: (0, 0)),
                own,
                pl.BlockSpec((blk, GROUP * HD), lambda g, c: (0, g)),
                own,
                pl.BlockSpec((blk, GROUP * HD), lambda g, c: (0, heads + g)),
            ]
            + [head] * n_arr,
            out_specs=[
                pl.BlockSpec((1, 2, span, lanes), lambda g, c: (g, 0, 0, 0)),
                pl.BlockSpec((1, 2, 1, lanes), lambda g, c: (g, 0, 0, 0)),
                pl.BlockSpec((1, 2, HD, lanes), lambda g, c: (g, 0, 0, 0)),
            ]
            + [head] * n_arr,
            scratch_shapes=[
                pltpu.VMEM((2, span, blk), F32),
                pltpu.VMEM((span // blk, blk, lanes), F32),
                pltpu.VMEM((WINDOW + rows, HD), F32),
                pltpu.VMEM((2, blk, GROUP * HD), BF16),
                pltpu.VMEM((2, blk, GROUP * HD), BF16),
            ],
        ),
        out_shape=[
            jax.ShapeDtypeStruct((heads, 2, span, lanes), BF16),
            jax.ShapeDtypeStruct((heads, 2, 1, lanes), F32),
            jax.ShapeDtypeStruct((heads, 2, HD, lanes), BF16),
        ]
        + [jax.ShapeDtypeStruct((rows, width), BF16)] * n_arr,
        compiler_params=pltpu.CompilerParams(vmem_limit_bytes=VMEM_BYTES),
        cost_estimate=small_cost(),
        name="probs",
    )(core, low, q, q_other, do, q_other, *keys)


def run_grads(core, e, inv, do_t, q, q_other, keys, values, rows, width):
    blk, heads, span, lanes, head, own = specs_of(rows, width)
    n_arr = len(keys)
    full = jax.ShapeDtypeStruct(q.shape, BF16)
    return pl.pallas_call(
        functools.partial(grads_kernel, blk, n_arr - 1),
        grid_spec=pltpu.PrefetchScalarGridSpec(
            num_scalar_prefetch=1,
            grid=(heads,),
            in_specs=[
                pl.BlockSpec((1, 2, span, lanes), lambda g, c: (g, 0, 0, 0)),
                pl.BlockSpec((1, 2, 1, lanes), lambda g, c: (g, 0, 0, 0)),
                pl.BlockSpec((1, 2, HD, lanes), lambda g, c: (g, 0, 0, 0)),
                own,
                pl.BlockSpec((blk, GROUP * HD), lambda g, c: (0, g)),
            ]
            + [head] * (2 * n_arr),
            out_specs=[own, own, pl.BlockSpec((2, blk, GROUP * HD), lambda g, c: (0, 0, g))] + [head] * n_arr,
            scratch_shapes=[
                pltpu.VMEM((WINDOW + rows, HD), F32),
                pltpu.VMEM((2, blk, GROUP * HD), BF16),
                pltpu.VMEM((2, blk, GROUP * HD), BF16),
                pltpu.VMEM((2, blk, GROUP * HD), BF16),
            ],
        ),
        out_shape=[full, full, jax.ShapeDtypeStruct((2, blk, GROUP * width), BF16)]
        + [jax.ShapeDtypeStruct((rows, width), BF16)] * n_arr,
        compiler_params=pltpu.CompilerParams(vmem_limit_bytes=VMEM_BYTES),
        cost_estimate=small_cost(),
        name="grads",
    )(core, e, inv, do_t, q, q_other, *keys, *values)


def small_cost():
    return pl.CostEstimate(flops=1 << 20, bytes_accessed=1 << 12, transcendentals=0)


def whole():
    return pl.BlockSpec(memory_space=pltpu.VMEM)


def pieces_kernel(dims, at_ref, x_ref, *refs):
    n_z, n_fsdp, out_rows = dims
    outs = refs[: 2 * n_fsdp]
    turned = refs[2 * n_fsdp]
    my_y, my_fsdp = at_ref[0], at_ref[1]
    for c in range(x_ref.shape[1] // HD):
        turned[c * HD : (c + 1) * HD, :] = x_ref[:, c * HD : (c + 1) * HD].astype(F32).T
    for p, out in enumerate(outs):
        flip, s = p // n_fsdp, p % n_fsdp
        y = lax.rem(my_y + flip, 2)
        f = lax.rem(my_fsdp + s, n_fsdp)
        for z in range(n_z):
            parts = []
            for core in range(2):
                block = ((z * 2 + y) * 2 + core) * n_fsdp + f
                parts.append(turned[pl.ds(pl.multiple_of(block * out_rows, 8), out_rows), :])
            out[z * 2 * out_rows : (z + 1) * 2 * out_rows, :] = jnp.concatenate(parts, 0).astype(BF16)


def run_pieces(at, tokens, n_z, n_fsdp, out_rows):
    rows, model = tokens.shape
    shape = jax.ShapeDtypeStruct((n_z * 2 * out_rows, rows), BF16)
    return pl.pallas_call(
        functools.partial(pieces_kernel, (n_z, n_fsdp, out_rows)),
        in_specs=[pl.BlockSpec(memory_space=pltpu.SMEM), whole()],
        out_specs=[whole()] * (2 * n_fsdp),
        out_shape=[shape] * (2 * n_fsdp),
        scratch_shapes=[pltpu.VMEM((model, rows), F32)],
        compiler_params=pltpu.CompilerParams(vmem_limit_bytes=VMEM_BYTES),
        cost_estimate=small_cost(),
        name="pieces",
    )(at, tokens)


def product_kernel(at_ref, *refs):
    *x_refs, w_ref, o_ref = refs
    total, first = None, 0
    for x in x_refs:
        term = dot(x[...], w_ref[first : first + x.shape[1], :])
        total = term if total is None else total + term
        first += x.shape[1]
    o_ref[...] = total.astype(o_ref.dtype)


def run_product(at, parts, w, kind):
    rows = parts[0].shape[0]
    depth, width = w.shape
    tile = 512
    if len(parts) == 1:
        x_specs = [pl.BlockSpec((rows, depth), lambda j, at: (0, at[0]))]
    else:
        x_specs = [pl.BlockSpec(x.shape, lambda j, at: (0, 0)) for x in parts]
    return pl.pallas_call(
        product_kernel,
        grid_spec=pltpu.PrefetchScalarGridSpec(
            num_scalar_prefetch=1,
            grid=(width // tile,),
            in_specs=x_specs + [pl.BlockSpec((depth, tile), lambda j, at: (0, j))],
            out_specs=pl.BlockSpec((rows, tile), lambda j, at: (0, j)),
        ),
        out_shape=jax.ShapeDtypeStruct((rows, width), kind),
        compiler_params=pltpu.CompilerParams(vmem_limit_bytes=VMEM_BYTES),
        cost_estimate=small_cost(),
        name="product",
    )(at, *parts, w)


def weight_kernel(n_z, n, at_ref, *refs):
    own_pairs, other_pairs = refs[:n], refs[n : 2 * n]
    dv_refs = refs[2 * n : 4 * n]
    outs = refs[4 * n :]
    core = at_ref[0]
    step = pl.program_id(0)
    rows = own_pairs[0].shape[1] // 2
    own = pl.ds(pl.multiple_of(core * rows, rows), rows)
    other = pl.ds(pl.multiple_of((1 - core) * rows, rows), rows)
    total = None
    for p in range(n):
        for flip in range(2):
            window = slice(flip * rows, (flip + 1) * rows)
            term = dot(own_pairs[p][:, window], dv_refs[2 * p + flip][own, :])
            term = term + dot(other_pairs[p][:, window], dv_refs[2 * p + flip][other, :])
            total = term if total is None else total + term
    for d, out in enumerate(outs):

        @pl.when(step == (n_z - 1 if d == 0 else d - 1))
        def _():
            out[...] = total.astype(out.dtype)


def run_weight(at, own_pairs, other_pairs, dv_pairs, n_z):
    n = len(own_pairs)
    count = own_pairs[0].shape[0] // n_z
    rows2 = own_pairs[0].shape[1]
    dvs = [x for pair_of in dv_pairs for x in pair_of]
    width = dvs[0].shape[1]
    shapes = [jax.ShapeDtypeStruct((count, width), F32 if d == 0 else BF16) for d in range(n_z)]
    pair_block = pl.BlockSpec((count, rows2), lambda d, at: (lax.rem(at[1] + d + 1, n_z), 0))
    return pl.pallas_call(
        functools.partial(weight_kernel, n_z, n),
        grid_spec=pltpu.PrefetchScalarGridSpec(
            num_scalar_prefetch=1,
            grid=(n_z,),
            in_specs=[pair_block] * (2 * n) + [pl.BlockSpec(dvs[0].shape, lambda d, at: (0, 0))] * (2 * n),
            out_specs=[pl.BlockSpec((count, width), lambda d, at: (0, 0))] * n_z,
        ),
        out_shape=shapes,
        compiler_params=pltpu.CompilerParams(vmem_limit_bytes=VMEM_BYTES),
        cost_estimate=small_cost(),
        name="weight",
    )(at, *own_pairs, *other_pairs, *dvs)


def tokens_kernel(n_fsdp, at_ref, dv_ref, w_ref, own_ref, *others):
    made = dot(dv_ref[...], w_ref[...], NT).astype(BF16)
    rows = own_ref.shape[0]
    own_ref[...] = made[:rows]
    for s, ref in enumerate(others):
        ref[...] = made[(s + 1) * rows : (s + 2) * rows]


def run_tokens(at, dv_rows, w, n_fsdp):
    slab, width = w.shape
    rows = dv_rows.shape[0] // n_fsdp
    tile = slab // 3 if slab % (3 * HD) == 0 else slab
    n_tiles = slab // tile
    return pl.pallas_call(
        functools.partial(tokens_kernel, n_fsdp),
        grid_spec=pltpu.PrefetchScalarGridSpec(
            num_scalar_prefetch=1,
            grid=(n_tiles,),
            in_specs=[
                pl.BlockSpec(dv_rows.shape, lambda j, at: (0, 0)),
                pl.BlockSpec((tile, width), lambda j, at: (j, 0)),
            ],
            out_specs=[pl.BlockSpec((rows, tile), lambda j, at: (0, at[0] * n_tiles + j))]
            + [pl.BlockSpec((rows, tile), lambda j, at: (0, j))] * (n_fsdp - 1),
        ),
        out_shape=[jax.ShapeDtypeStruct((rows, slab * n_fsdp), BF16)]
        + [jax.ShapeDtypeStruct((rows, slab), BF16)] * (n_fsdp - 1),
        compiler_params=pltpu.CompilerParams(vmem_limit_bytes=VMEM_BYTES),
        cost_estimate=small_cost(),
        name="tokens",
    )(at, dv_rows, w)


def shifted(x, by):
    length = lax.axis_size("ctx")
    return lax.ppermute(x, "ctx", [(i, i + by) for i in range(length) if 0 <= i + by < length])


def swapped(x):
    return lax.ppermute(x, "ctx", [(i, i ^ 1) for i in range(lax.axis_size("ctx"))])


def rotated(x, by):
    length = lax.axis_size("fsdp")
    return lax.ppermute(x, "fsdp", [(i, (i + by) % length) for i in range(length)])


def moved(x, flip, by):
    n_ctx, n_fsdp = lax.axis_size("ctx"), lax.axis_size("fsdp")
    pairs = [
        (c * n_fsdp + f, (c ^ (2 * flip)) * n_fsdp + (f + by) % n_fsdp)
        for c in range(n_ctx)
        for f in range(n_fsdp)
    ]
    return lax.ppermute(x, ("ctx", "fsdp"), pairs)


def relayed(my_y, far, got):
    return (far.astype(F32) + jnp.where(my_y == 1, got.astype(F32), 0.0)).astype(BF16)


def gathered_terms(my_y, mine, got, back):
    return (mine.astype(F32) + back.astype(F32) + jnp.where(my_y == 0, got.astype(F32), 0.0)).astype(BF16)


def cols(x, at, width):
    return lax.dynamic_slice_in_dim(x, at * width, width, x.ndim - 1)


def rows_of(x, at, count):
    return lax.dynamic_slice_in_dim(x, at * count, count, 0)


def placed(core, own, other, axis):
    both = jnp.concatenate([own, own], axis)
    return lax.dynamic_update_slice_in_dim(both, other, (1 - core) * own.shape[axis], axis)


def flipped(x):
    return lax.ppermute(x, "ctx", [(i, i ^ 2) for i in range(lax.axis_size("ctx"))])


def after(x, *earlier):
    return lax.optimization_barrier((x, *earlier))[0]


def shards(hidden, queries, key_heads, w_value, d_out, segments):
    shard_rows = hidden.shape[1]
    model = hidden.shape[2]
    kv_width = w_value.shape[1]
    n_ctx = lax.axis_size("ctx")
    n_fsdp = lax.axis_size("fsdp")
    chip_rows = 2 * shard_rows
    n_z = n_ctx // 4
    assert WINDOW == 2 * chip_rows
    my_ctx = lax.axis_index("ctx")
    my_fsdp = lax.axis_index("fsdp")
    core = my_ctx % 2
    core_arg = core.astype(jnp.int32).reshape(1)
    chip = my_ctx // 2
    my_y = chip % 2
    my_z = chip // 2
    half_kv = kv_width // 2
    slab = model // n_fsdp
    tokens = hidden[0]
    first = chip * chip_rows

    aligned = slab % HD == 0
    fsdp_arg = my_fsdp.astype(jnp.int32).reshape(1)
    zero_arg = jnp.zeros((1,), jnp.int32)
    half_q = queries.shape[2] // 2
    out_rows = model // (n_ctx * n_fsdp)
    places = [(flip, s) for flip in range(2) for s in range(n_fsdp)]

    cut = slab // HD // 2 * HD if aligned else slab
    parts_at = [(0, cut), (cut, slab)] if aligned else [(0, slab)]
    slabs = [
        [
            lax.dynamic_slice_in_dim(tokens, (my_fsdp + s) % n_fsdp * slab + low, high - low, 1)
            for low, high in parts_at
        ]
        for s in range(1, n_fsdp)
    ]
    sent = [[rotated(x, s + 1) for x in parts] for s, parts in enumerate(slabs)]

    own_tags = segments[0].astype(BF16)
    tag_row = lax.dynamic_update_slice_in_dim(jnp.zeros((half_kv,), BF16), own_tags, core * shard_rows, 0)
    tag_rows = jnp.concatenate([tag_row[None], jnp.zeros((15, half_kv), BF16)], 0)
    k_sent = jnp.concatenate([cols(key_heads[0], 1 - core, half_kv), tag_rows], 0)
    got = swapped(after(k_sent, *[parts[0] for parts in slabs]))

    if out_rows % 8 == 0:
        at = jnp.stack([my_y, my_fsdp]).astype(jnp.int32)
        pieces = run_pieces(after(at, k_sent, got), tokens, n_z, n_fsdp, out_rows)
    else:
        turned = tokens.T.reshape(n_z, 2, 2, n_fsdp, out_rows, shard_rows)
        pieces = []
        for flip, s in places:
            piece = lax.dynamic_index_in_dim(turned, my_y ^ flip, 1, keepdims=False)
            piece = lax.dynamic_index_in_dim(piece, (my_fsdp + s) % n_fsdp, 2, keepdims=False)
            pieces.append(piece.reshape(n_z * 2 * out_rows, shard_rows))
    by_place = dict(zip(places, pieces))

    k_own = jnp.concatenate(
        [
            placed(core, cols(key_heads[0], core, half_kv), got[:shard_rows], 0),
            tag_rows + got[shard_rows:],
        ],
        0,
    )
    k_far = shifted(k_own, 4)
    k_near = shifted(k_own, 2)
    over_y = {s: flipped(after(by_place[1, s], k_own)) for s in range(1, n_fsdp)}
    q_sent = jnp.concatenate([cols(queries[0], 1 - core, half_q), cols(d_out[0], 1 - core, half_q)], 1)
    q_other = swapped(after(q_sent, k_own))
    if aligned:
        value_own = run_product(after(fsdp_arg, q_sent, *pieces), [tokens], w_value, F32)
    else:
        value_own = dot(cols(tokens, my_fsdp, slab), w_value)
    keys = [k_far, k_near, k_own]

    span_tags = jnp.concatenate([k[chip_rows, :chip_rows] for k in keys], 0)
    key_at = jnp.arange(WINDOW + chip_rows, dtype=jnp.int32)
    chip_tags = k_own[chip_rows, :chip_rows]
    before = (span_tags[None, :] < chip_tags[:, None]) | (key_at + first < WINDOW)[None, :]
    low = jnp.sum(before.astype(jnp.int32), axis=1)
    low = jnp.maximum(low, jnp.arange(1, chip_rows + 1, dtype=jnp.int32))[None, :]

    if aligned:
        partial = [run_product(zero_arg, parts, w_value, BF16) for parts in sent]
    else:
        partial = [dot(parts[0], w_value).astype(BF16) for parts in sent]
    low = after(low, *partial, *over_y.values())
    e, inv, do_t, dv_far, dv_near, dv_mine = run_probs(
        core_arg, low, queries[0], q_other, d_out[0], keys, chip_rows, half_kv
    )
    dv_got = flipped(dv_near)

    value_back = [rotated(x, -s - 1) for s, x in enumerate(partial)]
    over_fsdp = {s: rotated(after(by_place[0, s], sent), s) for s in range(1, n_fsdp)}
    value_back = [after(x, dv_near) for x in value_back]
    value_back[0] = after(value_back[0], over_fsdp)
    value_sum = value_own
    for x in value_back:
        value_sum = value_sum + x.astype(F32)
    own_values = value_sum.astype(BF16)
    v_own = placed(core, cols(own_values, core, half_kv), swapped(cols(own_values, 1 - core, half_kv)), 0)

    over_y[0] = flipped(after(by_place[1, 0], k_near))
    v_own, over_y[0] = lax.optimization_barrier((v_own, over_y[0]))
    v_far = shifted(v_own, 4)
    own_pairs = [jnp.concatenate([by_place[0, 0], over_y[0]], 1)]
    other_pairs = [swapped(after(own_pairs[0], v_own))]
    relayed_y = {s: rotated(after(over_y[s], own_values), s) for s in range(1, n_fsdp)}

    dv_got = after(dv_got, v_own)
    dv_sent = relayed(my_y, dv_far, dv_got)
    dv_back = shifted(dv_sent, -4)
    v_sent = after(jnp.where(my_y == 0, v_own, v_far), dv_sent)
    v_near = flipped(v_sent)
    vals = [v_far, v_near, v_own]
    dv_chip = gathered_terms(my_y, dv_mine, dv_got, after(dv_back, v_sent))
    dv_fsdp = [dv_chip] + [rotated(dv_chip, s) for s in range(1, n_fsdp)]
    dv_over_y = [moved(dv_chip, 1, s) for s in range(n_fsdp)]
    for s in range(1, n_fsdp):
        own_pairs.append(jnp.concatenate([over_fsdp[s], after(relayed_y[s], dv_chip)], 1))
        other_pairs.append(swapped(own_pairs[s]))
    v_near = after(v_near, dv_chip)
    vals = [v_far, v_near, v_own]
    out, dq, other, dk_far, dk_near, dk_mine = run_grads(
        core_arg, e, inv, do_t, queries[0], q_other, keys, vals, chip_rows, half_kv
    )
    dk_back = [shifted(dk_near, -2), shifted(dk_far, -4)]

    dv_fsdp = [after(x, dk_near) for x in dv_fsdp]
    dv_over_y = [after(x, dk_near) for x in dv_over_y]
    dv_other = swapped(jnp.concatenate([rows_of(x, 1 - core, shard_rows) for x in dv_fsdp], 0))
    dv_rows = placed(
        core, jnp.concatenate([rows_of(x, core, shard_rows) for x in dv_fsdp], 0), dv_other, 1
    )
    dv_rows = after(dv_rows, *dv_over_y)
    if aligned:
        d_tokens, *made = run_tokens(fsdp_arg, dv_rows, w_value, n_fsdp)
    else:
        made = dot(dv_rows, w_value, NT).astype(BF16)
        made = [made[s * shard_rows : (s + 1) * shard_rows] for s in range(n_fsdp)]
        d_tokens = jnp.concatenate([made[0]] * n_fsdp, 1)
        made = made[1:]
    for s in range(1, n_fsdp):
        back = rotated(made[s - 1], -s)
        d_tokens = lax.dynamic_update_slice_in_dim(d_tokens, back, ((my_fsdp + s) % n_fsdp) * slab, 1)

    dv_pairs = list(zip(dv_fsdp, dv_over_y))
    if out_rows % 8 == 0:
        at = after(jnp.stack([core, my_z]).astype(jnp.int32), *made)
        by_z = run_weight(at, own_pairs, other_pairs, dv_pairs, n_z)
    else:
        weight_term = 0.0
        for p in range(n_fsdp):
            for flip in range(2):
                window = slice(flip * shard_rows, (flip + 1) * shard_rows)
                weight_term += dot(own_pairs[p][:, window], rows_of(dv_pairs[p][flip], core, shard_rows))
                weight_term += dot(other_pairs[p][:, window], rows_of(dv_pairs[p][flip], 1 - core, shard_rows))
        weight_term = weight_term.reshape(n_z, 2 * out_rows, half_kv)
        by_z = [
            lax.dynamic_index_in_dim(weight_term, (my_z + d) % n_z, 0, keepdims=False).astype(BF16 if d else F32)
            for d in range(n_z)
        ]
    by_z, dk_back = lax.optimization_barrier((list(by_z), dk_back))
    over_z = [
        lax.ppermute(by_z[d], "ctx", [(i, (i + 4 * d) % n_ctx) for i in range(n_ctx)]) for d in range(1, n_z)
    ]

    row_sum = by_z[0]
    for x in over_z:
        row_sum = row_sum + x.astype(F32)
    d_weight = placed(core, rows_of(row_sum, core, out_rows), swapped(rows_of(row_sum, 1 - core, out_rows)), 1)

    dk_chip = (dk_mine.astype(F32) + dk_back[0].astype(F32) + dk_back[1].astype(F32)).astype(BF16)
    d_keys = placed(core, rows_of(dk_chip, core, shard_rows), swapped(rows_of(dk_chip, 1 - core, shard_rows)), 1)
    other = swapped(after(other, *made))
    out = lax.dynamic_update_slice_in_dim(out, other[0], (1 - core) * half_q, 1)
    dq = lax.dynamic_update_slice_in_dim(dq, other[1], (1 - core) * half_q, 1)
    return (out[None], dq[None], d_keys[None], d_tokens[None], d_weight)


def solution(mesh):
    in_specs = (
        P("fsdp", "ctx", None),
        P("fsdp", "ctx", None),
        P("fsdp", "ctx", None),
        P("fsdp", None),
        P("fsdp", "ctx", None),
        P("fsdp", "ctx"),
    )
    out_specs = (
        P("fsdp", "ctx", None),
        P("fsdp", "ctx", None),
        P("fsdp", "ctx", None),
        P("fsdp", "ctx", None),
        P(("ctx", "fsdp"), None),
    )
    return jax.shard_map(shards, mesh=mesh, in_specs=in_specs, out_specs=out_specs, check_vma=False)
```

```python
import functools
import math

import jax
import jax.numpy as jnp
from jax import lax
from jax.experimental import pallas as pl
from jax.experimental.pallas import tpu as pltpu
from jax.sharding import PartitionSpec as P

HQ = 16
HK = 8
HD = 128
WINDOW = 1024
GROUP = 2
NEG = -1e30
VMEM_BYTES = 58 * 1024 * 1024

score_scale = 1.0 / math.sqrt(168.0)
exp2_scale = score_scale / math.log(2.0)

BF16 = jnp.bfloat16
F32 = jnp.float32
NT = (((1,), (1,)), ((), ()))
TN = (((0,), (0,)), ((), ()))


def dot(a, b, dims=(((1,), (0,)), ((), ()))):
    return lax.dot_general(a, b, dims, preferred_element_type=F32)


def probs_kernel(blk, n_back, core_ref, low_ref, q_own, q_other, do_own, do_other, *refs):
    n_arr = n_back + 1
    k_refs = refs[:n_arr]
    e_ref, inv_ref, dot_ref = refs[n_arr : n_arr + 3]
    dv_refs = refs[n_arr + 3 : 2 * n_arr + 3]
    bias, s_scr, dv_acc, q_buf, do_buf = refs[2 * n_arr + 3 :]
    span_blocks = WINDOW // blk + 1
    core = core_ref[0]

    @pl.when(pl.program_id(0) == 0)
    def _():
        for qb in range(2):
            kpos = lax.broadcasted_iota(jnp.int32, (span_blocks * blk, blk), 0) + qb * blk
            qpos = lax.broadcasted_iota(jnp.int32, (span_blocks * blk, blk), 1) + (qb * blk + WINDOW)
            low = low_ref[:, qb * blk : (qb + 1) * blk]
            ok = (kpos >= low) & (kpos <= qpos)
            bias[qb] = jnp.where(ok, 0.0, NEG)

    q_buf[core] = q_own[...]
    q_buf[1 - core] = q_other[...]
    do_buf[core] = do_own[...]
    do_buf[1 - core] = do_other[...]

    def key_block(j):
        return k_refs[j // 2][(j % 2) * blk : (j % 2 + 1) * blk, :]

    def stacked(buf, qb):
        return jnp.concatenate([buf[qb, :, r * HD : (r + 1) * HD] for r in range(GROUP)], 0)

    for qb in range(2):
        qs = stacked(q_buf, qb)
        top = None
        for j in range(span_blocks):
            s = dot(key_block(qb + j), qs, NT)
            b = bias[qb, j * blk : (j + 1) * blk, :]
            s = s * exp2_scale + jnp.concatenate([b] * GROUP, 1)
            s_scr[j] = s
            part = jnp.max(s.reshape(blk // 8, 8, GROUP * blk), axis=0)
            top = part if top is None else jnp.maximum(top, part)
        top = jnp.max(top, axis=0, keepdims=True)
        total = None
        for j in range(span_blocks):
            e = jnp.exp2(s_scr[j] - top)
            part = jnp.sum(e.reshape(blk // 8, 8, GROUP * blk), axis=0)
            total = part if total is None else total + part
            e_ref[0, qb, j * blk : (j + 1) * blk, :] = e.astype(BF16)
        inv = 1.0 / jnp.sum(total, axis=0, keepdims=True)
        inv_ref[0, qb] = inv
        do_t = (stacked(do_buf, qb).astype(F32).T * inv).astype(BF16)
        dot_ref[0, qb] = do_t
        for j in range(span_blocks):
            term = dot(e_ref[0, qb, j * blk : (j + 1) * blk, :], do_t, NT)
            at = slice((qb + j) * blk, (qb + j + 1) * blk)
            if qb == 0 or j == span_blocks - 1:
                dv_acc[at, :] = term
            else:
                dv_acc[at, :] += term
    for a in range(n_arr):
        dv_refs[a][...] = dv_acc[a * 2 * blk : (a + 1) * 2 * blk, :].astype(BF16)


def grads_kernel(blk, n_back, core_ref, e_ref, inv_ref, dot_ref, q_own, q_other, *refs):
    n_arr = n_back + 1
    k_refs = refs[:n_arr]
    v_refs = refs[n_arr : 2 * n_arr]
    out_ref, dq_ref, other_ref = refs[2 * n_arr : 2 * n_arr + 3]
    dk_refs = refs[2 * n_arr + 3 : 3 * n_arr + 3]
    dk_acc, q_buf, out_buf, dq_buf = refs[3 * n_arr + 3 :]
    span_blocks = WINDOW // blk + 1
    core = core_ref[0]

    q_buf[core] = q_own[...]
    q_buf[1 - core] = q_other[...]

    def block_of(arrays, j):
        return arrays[j // 2][(j % 2) * blk : (j % 2 + 1) * blk, :]

    for qb in range(2):
        qs = jnp.concatenate([q_buf[qb, :, r * HD : (r + 1) * HD] for r in range(GROUP)], 0)
        do_t = dot_ref[0, qb]
        out_t = None
        for j in range(span_blocks):
            e = e_ref[0, qb, j * blk : (j + 1) * blk, :]
            part = dot(block_of(v_refs, qb + j), e, TN)
            out_t = part if out_t is None else out_t + part
        out_t = (out_t * inv_ref[0, qb]).astype(BF16).astype(F32)
        delta = jnp.sum(out_t * do_t.astype(F32), axis=0, keepdims=True)
        out = out_t.T.astype(BF16)
        dq_t = None
        for j in range(span_blocks):
            e = e_ref[0, qb, j * blk : (j + 1) * blk, :].astype(F32)
            dp = dot(block_of(v_refs, qb + j), do_t)
            ds = (e * (dp - delta)).astype(BF16)
            term = dot(ds, qs)
            at = slice((qb + j) * blk, (qb + j + 1) * blk)
            if qb == 0 or j == span_blocks - 1:
                dk_acc[at, :] = term
            else:
                dk_acc[at, :] += term
            part = dot(block_of(k_refs, qb + j), ds, TN)
            dq_t = part if dq_t is None else dq_t + part
        dq = (dq_t * score_scale).T.astype(BF16)
        for r in range(GROUP):
            out_buf[qb, :, r * HD : (r + 1) * HD] = out[r * blk : (r + 1) * blk, :]
            dq_buf[qb, :, r * HD : (r + 1) * HD] = dq[r * blk : (r + 1) * blk, :]
    out_ref[...] = out_buf[core]
    dq_ref[...] = dq_buf[core]
    other_ref[0] = out_buf[1 - core]
    other_ref[1] = dq_buf[1 - core]
    for a in range(n_arr):
        dk_refs[a][...] = (dk_acc[a * 2 * blk : (a + 1) * 2 * blk, :] * score_scale).astype(BF16)


def specs_of(rows, width):
    blk = rows // 2
    heads = width // HD
    span = WINDOW + blk
    lanes = GROUP * blk
    head = pl.BlockSpec((rows, HD), lambda g, c: (0, g))
    own = pl.BlockSpec((blk, GROUP * HD), lambda g, c: (0, c[0] * heads + g))
    return blk, heads, span, lanes, head, own


def run_probs(core, low, q, q_other, do, keys, rows, width):
    blk, heads, span, lanes, head, own = specs_of(rows, width)
    n_arr = len(keys)
    return pl.pallas_call(
        functools.partial(probs_kernel, blk, n_arr - 1),
        grid_spec=pltpu.PrefetchScalarGridSpec(
            num_scalar_prefetch=1,
            grid=(heads,),
            in_specs=[
                pl.BlockSpec((1, rows), lambda g, c: (0, 0)),
                own,
                pl.BlockSpec((blk, GROUP * HD), lambda g, c: (0, g)),
                own,
                pl.BlockSpec((blk, GROUP * HD), lambda g, c: (0, heads + g)),
            ]
            + [head] * n_arr,
            out_specs=[
                pl.BlockSpec((1, 2, span, lanes), lambda g, c: (g, 0, 0, 0)),
                pl.BlockSpec((1, 2, 1, lanes), lambda g, c: (g, 0, 0, 0)),
                pl.BlockSpec((1, 2, HD, lanes), lambda g, c: (g, 0, 0, 0)),
            ]
            + [head] * n_arr,
            scratch_shapes=[
                pltpu.VMEM((2, span, blk), F32),
                pltpu.VMEM((span // blk, blk, lanes), F32),
                pltpu.VMEM((WINDOW + rows, HD), F32),
                pltpu.VMEM((2, blk, GROUP * HD), BF16),
                pltpu.VMEM((2, blk, GROUP * HD), BF16),
            ],
        ),
        out_shape=[
            jax.ShapeDtypeStruct((heads, 2, span, lanes), BF16),
            jax.ShapeDtypeStruct((heads, 2, 1, lanes), F32),
            jax.ShapeDtypeStruct((heads, 2, HD, lanes), BF16),
        ]
        + [jax.ShapeDtypeStruct((rows, width), BF16)] * n_arr,
        compiler_params=pltpu.CompilerParams(vmem_limit_bytes=VMEM_BYTES),
        cost_estimate=small_cost(),
        name="probs",
    )(core, low, q, q_other, do, q_other, *keys)


def run_grads(core, e, inv, do_t, q, q_other, keys, values, rows, width):
    blk, heads, span, lanes, head, own = specs_of(rows, width)
    n_arr = len(keys)
    full = jax.ShapeDtypeStruct(q.shape, BF16)
    return pl.pallas_call(
        functools.partial(grads_kernel, blk, n_arr - 1),
        grid_spec=pltpu.PrefetchScalarGridSpec(
            num_scalar_prefetch=1,
            grid=(heads,),
            in_specs=[
                pl.BlockSpec((1, 2, span, lanes), lambda g, c: (g, 0, 0, 0)),
                pl.BlockSpec((1, 2, 1, lanes), lambda g, c: (g, 0, 0, 0)),
                pl.BlockSpec((1, 2, HD, lanes), lambda g, c: (g, 0, 0, 0)),
                own,
                pl.BlockSpec((blk, GROUP * HD), lambda g, c: (0, g)),
            ]
            + [head] * (2 * n_arr),
            out_specs=[own, own, pl.BlockSpec((2, blk, GROUP * HD), lambda g, c: (0, 0, g))] + [head] * n_arr,
            scratch_shapes=[
                pltpu.VMEM((WINDOW + rows, HD), F32),
                pltpu.VMEM((2, blk, GROUP * HD), BF16),
                pltpu.VMEM((2, blk, GROUP * HD), BF16),
                pltpu.VMEM((2, blk, GROUP * HD), BF16),
            ],
        ),
        out_shape=[full, full, jax.ShapeDtypeStruct((2, blk, GROUP * width), BF16)]
        + [jax.ShapeDtypeStruct((rows, width), BF16)] * n_arr,
        compiler_params=pltpu.CompilerParams(vmem_limit_bytes=VMEM_BYTES),
        cost_estimate=small_cost(),
        name="grads",
    )(core, e, inv, do_t, q, q_other, *keys, *values)


def small_cost():
    return pl.CostEstimate(flops=1 << 20, bytes_accessed=1 << 12, transcendentals=0)


def whole():
    return pl.BlockSpec(memory_space=pltpu.VMEM)


def pieces_kernel(dims, at_ref, x_ref, *refs):
    n_z, n_fsdp, out_rows = dims
    outs = refs[: 2 * n_fsdp]
    turned = refs[2 * n_fsdp]
    my_y, my_fsdp = at_ref[0], at_ref[1]
    for c in range(x_ref.shape[1] // HD):
        turned[c * HD : (c + 1) * HD, :] = x_ref[:, c * HD : (c + 1) * HD].astype(F32).T
    for p, out in enumerate(outs):
        flip, s = p // n_fsdp, p % n_fsdp
        y = lax.rem(my_y + flip, 2)
        f = lax.rem(my_fsdp + s, n_fsdp)
        for z in range(n_z):
            parts = []
            for core in range(2):
                block = ((z * 2 + y) * 2 + core) * n_fsdp + f
                parts.append(turned[pl.ds(pl.multiple_of(block * out_rows, 8), out_rows), :])
            out[z * 2 * out_rows : (z + 1) * 2 * out_rows, :] = jnp.concatenate(parts, 0).astype(BF16)


def run_pieces(at, tokens, n_z, n_fsdp, out_rows):
    rows, model = tokens.shape
    shape = jax.ShapeDtypeStruct((n_z * 2 * out_rows, rows), BF16)
    return pl.pallas_call(
        functools.partial(pieces_kernel, (n_z, n_fsdp, out_rows)),
        in_specs=[pl.BlockSpec(memory_space=pltpu.SMEM), whole()],
        out_specs=[whole()] * (2 * n_fsdp),
        out_shape=[shape] * (2 * n_fsdp),
        scratch_shapes=[pltpu.VMEM((model, rows), F32)],
        compiler_params=pltpu.CompilerParams(vmem_limit_bytes=VMEM_BYTES),
        cost_estimate=small_cost(),
        name="pieces",
    )(at, tokens)


def product_kernel(at_ref, *refs):
    *x_refs, w_ref, o_ref = refs
    total, first = None, 0
    for x in x_refs:
        term = dot(x[...], w_ref[first : first + x.shape[1], :])
        total = term if total is None else total + term
        first += x.shape[1]
    o_ref[...] = total.astype(o_ref.dtype)


def run_product(at, parts, w, kind):
    rows = parts[0].shape[0]
    depth, width = w.shape
    tile = 512
    if len(parts) == 1:
        x_specs = [pl.BlockSpec((rows, depth), lambda j, at: (0, at[0]))]
    else:
        x_specs = [pl.BlockSpec(x.shape, lambda j, at: (0, 0)) for x in parts]
    return pl.pallas_call(
        product_kernel,
        grid_spec=pltpu.PrefetchScalarGridSpec(
            num_scalar_prefetch=1,
            grid=(width // tile,),
            in_specs=x_specs + [pl.BlockSpec((depth, tile), lambda j, at: (0, j))],
            out_specs=pl.BlockSpec((rows, tile), lambda j, at: (0, j)),
        ),
        out_shape=jax.ShapeDtypeStruct((rows, width), kind),
        compiler_params=pltpu.CompilerParams(vmem_limit_bytes=VMEM_BYTES),
        cost_estimate=small_cost(),
        name="product",
    )(at, *parts, w)


def weight_kernel(n_z, n, at_ref, *refs):
    own_pairs, other_pairs = refs[:n], refs[n : 2 * n]
    dv_refs = refs[2 * n : 4 * n]
    outs = refs[4 * n :]
    core = at_ref[0]
    step = pl.program_id(0)
    rows = own_pairs[0].shape[1] // 2
    own = pl.ds(pl.multiple_of(core * rows, rows), rows)
    other = pl.ds(pl.multiple_of((1 - core) * rows, rows), rows)
    total = None
    for p in range(n):
        for flip in range(2):
            window = slice(flip * rows, (flip + 1) * rows)
            term = dot(own_pairs[p][:, window], dv_refs[2 * p + flip][own, :])
            term = term + dot(other_pairs[p][:, window], dv_refs[2 * p + flip][other, :])
            total = term if total is None else total + term
    for d, out in enumerate(outs):

        @pl.when(step == (n_z - 1 if d == 0 else d - 1))
        def _():
            out[...] = total.astype(out.dtype)


def run_weight(at, own_pairs, other_pairs, dv_pairs, n_z):
    n = len(own_pairs)
    count = own_pairs[0].shape[0] // n_z
    rows2 = own_pairs[0].shape[1]
    dvs = [x for pair_of in dv_pairs for x in pair_of]
    width = dvs[0].shape[1]
    shapes = [jax.ShapeDtypeStruct((count, width), F32 if d == 0 else BF16) for d in range(n_z)]
    pair_block = pl.BlockSpec((count, rows2), lambda d, at: (lax.rem(at[1] + d + 1, n_z), 0))
    return pl.pallas_call(
        functools.partial(weight_kernel, n_z, n),
        grid_spec=pltpu.PrefetchScalarGridSpec(
            num_scalar_prefetch=1,
            grid=(n_z,),
            in_specs=[pair_block] * (2 * n) + [pl.BlockSpec(dvs[0].shape, lambda d, at: (0, 0))] * (2 * n),
            out_specs=[pl.BlockSpec((count, width), lambda d, at: (0, 0))] * n_z,
        ),
        out_shape=shapes,
        compiler_params=pltpu.CompilerParams(vmem_limit_bytes=VMEM_BYTES),
        cost_estimate=small_cost(),
        name="weight",
    )(at, *own_pairs, *other_pairs, *dvs)


def tokens_kernel(n_fsdp, at_ref, dv_ref, w_ref, own_ref, *others):
    made = dot(dv_ref[...], w_ref[...], NT).astype(BF16)
    rows = own_ref.shape[0]
    own_ref[...] = made[:rows]
    for s, ref in enumerate(others):
        ref[...] = made[(s + 1) * rows : (s + 2) * rows]


def run_tokens(at, dv_rows, w, n_fsdp):
    slab, width = w.shape
    rows = dv_rows.shape[0] // n_fsdp
    tile = slab // 3 if slab % (3 * HD) == 0 else slab
    n_tiles = slab // tile
    return pl.pallas_call(
        functools.partial(tokens_kernel, n_fsdp),
        grid_spec=pltpu.PrefetchScalarGridSpec(
            num_scalar_prefetch=1,
            grid=(n_tiles,),
            in_specs=[
                pl.BlockSpec(dv_rows.shape, lambda j, at: (0, 0)),
                pl.BlockSpec((tile, width), lambda j, at: (j, 0)),
            ],
            out_specs=[pl.BlockSpec((rows, tile), lambda j, at: (0, at[0] * n_tiles + j))]
            + [pl.BlockSpec((rows, tile), lambda j, at: (0, j))] * (n_fsdp - 1),
        ),
        out_shape=[jax.ShapeDtypeStruct((rows, slab * n_fsdp), BF16)]
        + [jax.ShapeDtypeStruct((rows, slab), BF16)] * (n_fsdp - 1),
        compiler_params=pltpu.CompilerParams(vmem_limit_bytes=VMEM_BYTES),
        cost_estimate=small_cost(),
        name="tokens",
    )(at, dv_rows, w)


def shifted(x, by):
    length = lax.axis_size("ctx")
    return lax.ppermute(x, "ctx", [(i, i + by) for i in range(length) if 0 <= i + by < length])


def swapped(x):
    return lax.ppermute(x, "ctx", [(i, i ^ 1) for i in range(lax.axis_size("ctx"))])


def rotated(x, by):
    length = lax.axis_size("fsdp")
    return lax.ppermute(x, "fsdp", [(i, (i + by) % length) for i in range(length)])


def moved(x, flip, by):
    n_ctx, n_fsdp = lax.axis_size("ctx"), lax.axis_size("fsdp")
    pairs = [
        (c * n_fsdp + f, (c ^ (2 * flip)) * n_fsdp + (f + by) % n_fsdp)
        for c in range(n_ctx)
        for f in range(n_fsdp)
    ]
    return lax.ppermute(x, ("ctx", "fsdp"), pairs)


def relayed(my_y, far, got):
    return (far.astype(F32) + jnp.where(my_y == 1, got.astype(F32), 0.0)).astype(BF16)


def gathered_terms(my_y, mine, got, back):
    return (mine.astype(F32) + back.astype(F32) + jnp.where(my_y == 0, got.astype(F32), 0.0)).astype(BF16)


def cols(x, at, width):
    return lax.dynamic_slice_in_dim(x, at * width, width, x.ndim - 1)


def rows_of(x, at, count):
    return lax.dynamic_slice_in_dim(x, at * count, count, 0)


def placed(core, own, other, axis):
    both = jnp.concatenate([own, own], axis)
    return lax.dynamic_update_slice_in_dim(both, other, (1 - core) * own.shape[axis], axis)


def flipped(x):
    return lax.ppermute(x, "ctx", [(i, i ^ 2) for i in range(lax.axis_size("ctx"))])


def after(x, *earlier):
    return lax.optimization_barrier((x, *earlier))[0]


def shards(hidden, queries, key_heads, w_value, d_out, segments):
    shard_rows = hidden.shape[1]
    model = hidden.shape[2]
    kv_width = w_value.shape[1]
    n_ctx = lax.axis_size("ctx")
    n_fsdp = lax.axis_size("fsdp")
    chip_rows = 2 * shard_rows
    n_z = n_ctx // 4
    assert WINDOW == 2 * chip_rows
    my_ctx = lax.axis_index("ctx")
    my_fsdp = lax.axis_index("fsdp")
    core = my_ctx % 2
    core_arg = core.astype(jnp.int32).reshape(1)
    chip = my_ctx // 2
    my_y = chip % 2
    my_z = chip // 2
    half_kv = kv_width // 2
    slab = model // n_fsdp
    tokens = hidden[0]
    first = chip * chip_rows

    aligned = slab % HD == 0
    fsdp_arg = my_fsdp.astype(jnp.int32).reshape(1)
    zero_arg = jnp.zeros((1,), jnp.int32)
    half_q = queries.shape[2] // 2
    out_rows = model // (n_ctx * n_fsdp)
    places = [(flip, s) for flip in range(2) for s in range(n_fsdp)]

    cut = slab // HD // 2 * HD if aligned else slab
    parts_at = [(0, cut), (cut, slab)] if aligned else [(0, slab)]
    slabs = [
        [
            lax.dynamic_slice_in_dim(tokens, (my_fsdp + s) % n_fsdp * slab + low, high - low, 1)
            for low, high in parts_at
        ]
        for s in range(1, n_fsdp)
    ]
    sent = [[rotated(x, s + 1) for x in parts] for s, parts in enumerate(slabs)]

    own_tags = segments[0].astype(BF16)
    tag_row = lax.dynamic_update_slice_in_dim(jnp.zeros((half_kv,), BF16), own_tags, core * shard_rows, 0)
    tag_rows = jnp.concatenate([tag_row[None], jnp.zeros((15, half_kv), BF16)], 0)
    k_sent = jnp.concatenate([cols(key_heads[0], 1 - core, half_kv), tag_rows], 0)
    got = swapped(after(k_sent, *[parts[0] for parts in slabs]))

    if out_rows % 8 == 0:
        at = jnp.stack([my_y, my_fsdp]).astype(jnp.int32)
        pieces = run_pieces(after(at, k_sent, got), tokens, n_z, n_fsdp, out_rows)
    else:
        turned = tokens.T.reshape(n_z, 2, 2, n_fsdp, out_rows, shard_rows)
        pieces = []
        for flip, s in places:
            piece = lax.dynamic_index_in_dim(turned, my_y ^ flip, 1, keepdims=False)
            piece = lax.dynamic_index_in_dim(piece, (my_fsdp + s) % n_fsdp, 2, keepdims=False)
            pieces.append(piece.reshape(n_z * 2 * out_rows, shard_rows))
    by_place = dict(zip(places, pieces))

    k_own = jnp.concatenate(
        [
            placed(core, cols(key_heads[0], core, half_kv), got[:shard_rows], 0),
            tag_rows + got[shard_rows:],
        ],
        0,
    )
    k_far = shifted(k_own, 4)
    k_near = shifted(k_own, 2)
    over_y = {s: flipped(after(by_place[1, s], k_own)) for s in range(1, n_fsdp)}
    q_sent = jnp.concatenate([cols(queries[0], 1 - core, half_q), cols(d_out[0], 1 - core, half_q)], 1)
    q_other = swapped(after(q_sent, k_own))
    if aligned:
        value_own = run_product(after(fsdp_arg, q_sent, *pieces), [tokens], w_value, F32)
    else:
        value_own = dot(cols(tokens, my_fsdp, slab), w_value)
    keys = [k_far, k_near, k_own]

    span_tags = jnp.concatenate([k[chip_rows, :chip_rows] for k in keys], 0)
    key_at = jnp.arange(WINDOW + chip_rows, dtype=jnp.int32)
    chip_tags = k_own[chip_rows, :chip_rows]
    before = (span_tags[None, :] < chip_tags[:, None]) | (key_at + first < WINDOW)[None, :]
    low = jnp.sum(before.astype(jnp.int32), axis=1)
    low = jnp.maximum(low, jnp.arange(1, chip_rows + 1, dtype=jnp.int32))[None, :]

    if aligned:
        partial = [run_product(zero_arg, parts, w_value, BF16) for parts in sent]
    else:
        partial = [dot(parts[0], w_value).astype(BF16) for parts in sent]
    low = after(low, *partial, *over_y.values())
    e, inv, do_t, dv_far, dv_near, dv_mine = run_probs(
        core_arg, low, queries[0], q_other, d_out[0], keys, chip_rows, half_kv
    )
    dv_got = flipped(dv_near)

    value_back = [rotated(x, -s - 1) for s, x in enumerate(partial)]
    over_fsdp = {s: rotated(after(by_place[0, s], sent), s) for s in range(1, n_fsdp)}
    value_back = [after(x, dv_near) for x in value_back]
    value_sum = value_own
    for x in value_back:
        value_sum = value_sum + x.astype(F32)
    own_values = value_sum.astype(BF16)
    v_own = placed(core, cols(own_values, core, half_kv), swapped(cols(own_values, 1 - core, half_kv)), 0)

    over_y[0] = flipped(after(by_place[1, 0], k_near))
    v_own, over_y[0], over_fsdp = lax.optimization_barrier((v_own, over_y[0], over_fsdp))
    v_far = shifted(v_own, 4)
    own_pairs = [jnp.concatenate([by_place[0, 0], over_y[0]], 1)]
    other_pairs = [swapped(after(own_pairs[0], v_own))]
    relayed_y = {s: rotated(after(over_y[s], own_values), s) for s in range(1, n_fsdp)}

    dv_got = after(dv_got, v_own)
    dv_sent = relayed(my_y, dv_far, dv_got)
    dv_back = shifted(dv_sent, -4)
    v_sent = after(jnp.where(my_y == 0, v_own, v_far), dv_sent)
    v_near = flipped(v_sent)
    vals = [v_far, v_near, v_own]
    dv_chip = gathered_terms(my_y, dv_mine, dv_got, after(dv_back, v_sent))
    dv_fsdp = [dv_chip] + [rotated(dv_chip, s) for s in range(1, n_fsdp)]
    dv_over_y = [moved(dv_chip, 1, s) for s in range(n_fsdp)]
    v_near = after(v_near, dv_chip)
    for s in range(1, n_fsdp):
        own_pairs.append(jnp.concatenate([over_fsdp[s], after(relayed_y[s], v_near)], 1))
        other_pairs.append(swapped(own_pairs[s]))
    vals = [v_far, v_near, v_own]
    out, dq, other, dk_far, dk_near, dk_mine = run_grads(
        core_arg, e, inv, do_t, queries[0], q_other, keys, vals, chip_rows, half_kv
    )
    dk_back = [shifted(dk_near, -2), shifted(dk_far, -4)]

    dv_pairs = list(zip(dv_fsdp, dv_over_y))
    if out_rows % 8 == 0:
        at = after(jnp.stack([core, my_z]).astype(jnp.int32), dk_near)
        by_z = run_weight(at, own_pairs, other_pairs, dv_pairs, n_z)
    else:
        weight_term = 0.0
        for p in range(n_fsdp):
            for flip in range(2):
                window = slice(flip * shard_rows, (flip + 1) * shard_rows)
                weight_term += dot(own_pairs[p][:, window], rows_of(dv_pairs[p][flip], core, shard_rows))
                weight_term += dot(other_pairs[p][:, window], rows_of(dv_pairs[p][flip], 1 - core, shard_rows))
        weight_term = weight_term.reshape(n_z, 2 * out_rows, half_kv)
        by_z = [
            lax.dynamic_index_in_dim(weight_term, (my_z + d) % n_z, 0, keepdims=False).astype(BF16 if d else F32)
            for d in range(n_z)
        ]
    over_z = [
        lax.ppermute(by_z[d], "ctx", [(i, (i + 4 * d) % n_ctx) for i in range(n_ctx)]) for d in range(1, n_z)
    ]

    dv_fsdp = [after(x, dk_near) for x in dv_fsdp]
    dv_over_y = [after(x, dk_near) for x in dv_over_y]
    dv_fsdp = [after(x, by_z[0]) for x in dv_fsdp]
    dv_other = swapped(jnp.concatenate([rows_of(x, 1 - core, shard_rows) for x in dv_fsdp], 0))
    dv_rows = placed(
        core, jnp.concatenate([rows_of(x, core, shard_rows) for x in dv_fsdp], 0), dv_other, 1
    )
    if aligned:
        d_tokens, *made = run_tokens(fsdp_arg, dv_rows, w_value, n_fsdp)
    else:
        made = dot(dv_rows, w_value, NT).astype(BF16)
        made = [made[s * shard_rows : (s + 1) * shard_rows] for s in range(n_fsdp)]
        d_tokens = jnp.concatenate([made[0]] * n_fsdp, 1)
        made = made[1:]
    for s in range(1, n_fsdp):
        back = rotated(made[s - 1], -s)
        d_tokens = lax.dynamic_update_slice_in_dim(d_tokens, back, ((my_fsdp + s) % n_fsdp) * slab, 1)

    row_sum = by_z[0]
    for x in over_z:
        row_sum = row_sum + x.astype(F32)
    d_weight = placed(core, rows_of(row_sum, core, out_rows), swapped(rows_of(row_sum, 1 - core, out_rows)), 1)
    dk_back = [after(x, *made) for x in dk_back]
    dk_chip = (dk_mine.astype(F32) + dk_back[0].astype(F32) + dk_back[1].astype(F32)).astype(BF16)
    d_keys = placed(core, rows_of(dk_chip, core, shard_rows), swapped(rows_of(dk_chip, 1 - core, shard_rows)), 1)
    other = swapped(after(other, *made))
    out = lax.dynamic_update_slice_in_dim(out, other[0], (1 - core) * half_q, 1)
    dq = lax.dynamic_update_slice_in_dim(dq, other[1], (1 - core) * half_q, 1)
    return (out[None], dq[None], d_keys[None], d_tokens[None], d_weight)


def solution(mesh):
    in_specs = (
        P("fsdp", "ctx", None),
        P("fsdp", "ctx", None),
        P("fsdp", "ctx", None),
        P("fsdp", None),
        P("fsdp", "ctx", None),
        P("fsdp", "ctx"),
    )
    out_specs = (
        P("fsdp", "ctx", None),
        P("fsdp", "ctx", None),
        P("fsdp", "ctx", None),
        P("fsdp", "ctx", None),
        P(("ctx", "fsdp"), None),
    )
    return jax.shard_map(shards, mesh=mesh, in_specs=in_specs, out_specs=out_specs, check_vma=False)
```

```python
import functools
import math

import jax
import jax.numpy as jnp
from jax import lax
from jax.experimental import pallas as pl
from jax.experimental.pallas import tpu as pltpu
from jax.sharding import PartitionSpec as P

HQ = 16
HK = 8
HD = 128
WINDOW = 1024
GROUP = 2
NEG = -1e30
VMEM_BYTES = 58 * 1024 * 1024

score_scale = 1.0 / math.sqrt(168.0)
exp2_scale = score_scale / math.log(2.0)

BF16 = jnp.bfloat16
F32 = jnp.float32
NT = (((1,), (1,)), ((), ()))
TN = (((0,), (0,)), ((), ()))


def dot(a, b, dims=(((1,), (0,)), ((), ()))):
    return lax.dot_general(a, b, dims, preferred_element_type=F32)


def probs_kernel(blk, n_back, core_ref, low_ref, q_own, q_other, do_own, do_other, *refs):
    n_arr = n_back + 1
    k_refs = refs[:n_arr]
    e_ref, inv_ref, dot_ref = refs[n_arr : n_arr + 3]
    dv_refs = refs[n_arr + 3 : 2 * n_arr + 3]
    bias, s_scr, dv_acc, q_buf, do_buf = refs[2 * n_arr + 3 :]
    span_blocks = WINDOW // blk + 1
    core = core_ref[0]

    @pl.when(pl.program_id(0) == 0)
    def _():
        for qb in range(2):
            kpos = lax.broadcasted_iota(jnp.int32, (span_blocks * blk, blk), 0) + qb * blk
            qpos = lax.broadcasted_iota(jnp.int32, (span_blocks * blk, blk), 1) + (qb * blk + WINDOW)
            low = low_ref[:, qb * blk : (qb + 1) * blk]
            ok = (kpos >= low) & (kpos <= qpos)
            bias[qb] = jnp.where(ok, 0.0, NEG)

    q_buf[core] = q_own[...]
    q_buf[1 - core] = q_other[...]
    do_buf[core] = do_own[...]
    do_buf[1 - core] = do_other[...]

    def key_block(j):
        return k_refs[j // 2][(j % 2) * blk : (j % 2 + 1) * blk, :]

    def stacked(buf, qb):
        return jnp.concatenate([buf[qb, :, r * HD : (r + 1) * HD] for r in range(GROUP)], 0)

    for qb in range(2):
        qs = stacked(q_buf, qb)
        top = None
        for j in range(span_blocks):
            s = dot(key_block(qb + j), qs, NT)
            b = bias[qb, j * blk : (j + 1) * blk, :]
            s = s * exp2_scale + jnp.concatenate([b] * GROUP, 1)
            s_scr[j] = s
            part = jnp.max(s.reshape(blk // 8, 8, GROUP * blk), axis=0)
            top = part if top is None else jnp.maximum(top, part)
        top = jnp.max(top, axis=0, keepdims=True)
        total = None
        for j in range(span_blocks):
            e = jnp.exp2(s_scr[j] - top)
            part = jnp.sum(e.reshape(blk // 8, 8, GROUP * blk), axis=0)
            total = part if total is None else total + part
            e_ref[0, qb, j * blk : (j + 1) * blk, :] = e.astype(BF16)
        inv = 1.0 / jnp.sum(total, axis=0, keepdims=True)
        inv_ref[0, qb] = inv
        do_t = (stacked(do_buf, qb).astype(F32).T * inv).astype(BF16)
        dot_ref[0, qb] = do_t
        for j in range(span_blocks):
            term = dot(e_ref[0, qb, j * blk : (j + 1) * blk, :], do_t, NT)
            at = slice((qb + j) * blk, (qb + j + 1) * blk)
            if qb == 0 or j == span_blocks - 1:
                dv_acc[at, :] = term
            else:
                dv_acc[at, :] += term
    for a in range(n_arr):
        dv_refs[a][...] = dv_acc[a * 2 * blk : (a + 1) * 2 * blk, :].astype(BF16)


def grads_kernel(blk, n_back, core_ref, e_ref, inv_ref, dot_ref, q_own, q_other, *refs):
    n_arr = n_back + 1
    k_refs = refs[:n_arr]
    v_refs = refs[n_arr : 2 * n_arr]
    out_ref, dq_ref, other_ref = refs[2 * n_arr : 2 * n_arr + 3]
    dk_refs = refs[2 * n_arr + 3 : 3 * n_arr + 3]
    dk_acc, q_buf, out_buf, dq_buf = refs[3 * n_arr + 3 :]
    span_blocks = WINDOW // blk + 1
    core = core_ref[0]

    q_buf[core] = q_own[...]
    q_buf[1 - core] = q_other[...]

    def block_of(arrays, j):
        return arrays[j // 2][(j % 2) * blk : (j % 2 + 1) * blk, :]

    for qb in range(2):
        qs = jnp.concatenate([q_buf[qb, :, r * HD : (r + 1) * HD] for r in range(GROUP)], 0)
        do_t = dot_ref[0, qb]
        out_t = None
        for j in range(span_blocks):
            e = e_ref[0, qb, j * blk : (j + 1) * blk, :]
            part = dot(block_of(v_refs, qb + j), e, TN)
            out_t = part if out_t is None else out_t + part
        out_t = (out_t * inv_ref[0, qb]).astype(BF16).astype(F32)
        delta = jnp.sum(out_t * do_t.astype(F32), axis=0, keepdims=True)
        out = out_t.T.astype(BF16)
        dq_t = None
        for j in range(span_blocks):
            e = e_ref[0, qb, j * blk : (j + 1) * blk, :].astype(F32)
            dp = dot(block_of(v_refs, qb + j), do_t)
            ds = (e * (dp - delta)).astype(BF16)
            term = dot(ds, qs)
            at = slice((qb + j) * blk, (qb + j + 1) * blk)
            if qb == 0 or j == span_blocks - 1:
                dk_acc[at, :] = term
            else:
                dk_acc[at, :] += term
            part = dot(block_of(k_refs, qb + j), ds, TN)
            dq_t = part if dq_t is None else dq_t + part
        dq = (dq_t * score_scale).T.astype(BF16)
        for r in range(GROUP):
            out_buf[qb, :, r * HD : (r + 1) * HD] = out[r * blk : (r + 1) * blk, :]
            dq_buf[qb, :, r * HD : (r + 1) * HD] = dq[r * blk : (r + 1) * blk, :]
    out_ref[...] = out_buf[core]
    dq_ref[...] = dq_buf[core]
    other_ref[0] = out_buf[1 - core]
    other_ref[1] = dq_buf[1 - core]
    for a in range(n_arr):
        dk_refs[a][...] = (dk_acc[a * 2 * blk : (a + 1) * 2 * blk, :] * score_scale).astype(BF16)


def specs_of(rows, width):
    blk = rows // 2
    heads = width // HD
    span = WINDOW + blk
    lanes = GROUP * blk
    head = pl.BlockSpec((rows, HD), lambda g, c: (0, g))
    own = pl.BlockSpec((blk, GROUP * HD), lambda g, c: (0, c[0] * heads + g))
    return blk, heads, span, lanes, head, own


def run_probs(core, low, q, q_other, do, keys, rows, width):
    blk, heads, span, lanes, head, own = specs_of(rows, width)
    n_arr = len(keys)
    return pl.pallas_call(
        functools.partial(probs_kernel, blk, n_arr - 1),
        grid_spec=pltpu.PrefetchScalarGridSpec(
            num_scalar_prefetch=1,
            grid=(heads,),
            in_specs=[
                pl.BlockSpec((1, rows), lambda g, c: (0, 0)),
                own,
                pl.BlockSpec((blk, GROUP * HD), lambda g, c: (0, g)),
                own,
                pl.BlockSpec((blk, GROUP * HD), lambda g, c: (0, heads + g)),
            ]
            + [head] * n_arr,
            out_specs=[
                pl.BlockSpec((1, 2, span, lanes), lambda g, c: (g, 0, 0, 0)),
                pl.BlockSpec((1, 2, 1, lanes), lambda g, c: (g, 0, 0, 0)),
                pl.BlockSpec((1, 2, HD, lanes), lambda g, c: (g, 0, 0, 0)),
            ]
            + [head] * n_arr,
            scratch_shapes=[
                pltpu.VMEM((2, span, blk), F32),
                pltpu.VMEM((span // blk, blk, lanes), F32),
                pltpu.VMEM((WINDOW + rows, HD), F32),
                pltpu.VMEM((2, blk, GROUP * HD), BF16),
                pltpu.VMEM((2, blk, GROUP * HD), BF16),
            ],
        ),
        out_shape=[
            jax.ShapeDtypeStruct((heads, 2, span, lanes), BF16),
            jax.ShapeDtypeStruct((heads, 2, 1, lanes), F32),
            jax.ShapeDtypeStruct((heads, 2, HD, lanes), BF16),
        ]
        + [jax.ShapeDtypeStruct((rows, width), BF16)] * n_arr,
        compiler_params=pltpu.CompilerParams(vmem_limit_bytes=VMEM_BYTES),
        cost_estimate=small_cost(),
        name="probs",
    )(core, low, q, q_other, do, q_other, *keys)


def run_grads(core, e, inv, do_t, q, q_other, keys, values, rows, width):
    blk, heads, span, lanes, head, own = specs_of(rows, width)
    n_arr = len(keys)
    full = jax.ShapeDtypeStruct(q.shape, BF16)
    return pl.pallas_call(
        functools.partial(grads_kernel, blk, n_arr - 1),
        grid_spec=pltpu.PrefetchScalarGridSpec(
            num_scalar_prefetch=1,
            grid=(heads,),
            in_specs=[
                pl.BlockSpec((1, 2, span, lanes), lambda g, c: (g, 0, 0, 0)),
                pl.BlockSpec((1, 2, 1, lanes), lambda g, c: (g, 0, 0, 0)),
                pl.BlockSpec((1, 2, HD, lanes), lambda g, c: (g, 0, 0, 0)),
                own,
                pl.BlockSpec((blk, GROUP * HD), lambda g, c: (0, g)),
            ]
            + [head] * (2 * n_arr),
            out_specs=[own, own, pl.BlockSpec((2, blk, GROUP * HD), lambda g, c: (0, 0, g))] + [head] * n_arr,
            scratch_shapes=[
                pltpu.VMEM((WINDOW + rows, HD), F32),
                pltpu.VMEM((2, blk, GROUP * HD), BF16),
                pltpu.VMEM((2, blk, GROUP * HD), BF16),
                pltpu.VMEM((2, blk, GROUP * HD), BF16),
            ],
        ),
        out_shape=[full, full, jax.ShapeDtypeStruct((2, blk, GROUP * width), BF16)]
        + [jax.ShapeDtypeStruct((rows, width), BF16)] * n_arr,
        compiler_params=pltpu.CompilerParams(vmem_limit_bytes=VMEM_BYTES),
        cost_estimate=small_cost(),
        name="grads",
    )(core, e, inv, do_t, q, q_other, *keys, *values)


def small_cost():
    return pl.CostEstimate(flops=1 << 20, bytes_accessed=1 << 12, transcendentals=0)


def whole():
    return pl.BlockSpec(memory_space=pltpu.VMEM)


def pieces_kernel(dims, at_ref, x_ref, *refs):
    n_z, n_fsdp, out_rows = dims
    outs = refs[: 2 * n_fsdp]
    turned = refs[2 * n_fsdp]
    my_y, my_fsdp = at_ref[0], at_ref[1]
    for c in range(x_ref.shape[1] // HD):
        turned[c * HD : (c + 1) * HD, :] = x_ref[:, c * HD : (c + 1) * HD].astype(F32).T
    for p, out in enumerate(outs):
        flip, s = p // n_fsdp, p % n_fsdp
        y = lax.rem(my_y + flip, 2)
        f = lax.rem(my_fsdp + s, n_fsdp)
        for z in range(n_z):
            parts = []
            for core in range(2):
                block = ((z * 2 + y) * 2 + core) * n_fsdp + f
                parts.append(turned[pl.ds(pl.multiple_of(block * out_rows, 8), out_rows), :])
            out[z * 2 * out_rows : (z + 1) * 2 * out_rows, :] = jnp.concatenate(parts, 0).astype(BF16)


def run_pieces(at, tokens, n_z, n_fsdp, out_rows):
    rows, model = tokens.shape
    shape = jax.ShapeDtypeStruct((n_z * 2 * out_rows, rows), BF16)
    return pl.pallas_call(
        functools.partial(pieces_kernel, (n_z, n_fsdp, out_rows)),
        in_specs=[pl.BlockSpec(memory_space=pltpu.SMEM), whole()],
        out_specs=[whole()] * (2 * n_fsdp),
        out_shape=[shape] * (2 * n_fsdp),
        scratch_shapes=[pltpu.VMEM((model, rows), F32)],
        compiler_params=pltpu.CompilerParams(vmem_limit_bytes=VMEM_BYTES),
        cost_estimate=small_cost(),
        name="pieces",
    )(at, tokens)


def product_kernel(at_ref, *refs):
    *x_refs, w_ref, o_ref = refs
    total, first = None, 0
    for x in x_refs:
        term = dot(x[...], w_ref[first : first + x.shape[1], :])
        total = term if total is None else total + term
        first += x.shape[1]
    o_ref[...] = total.astype(o_ref.dtype)


def run_product(at, parts, w, kind):
    rows = parts[0].shape[0]
    depth, width = w.shape
    tile = 512
    if len(parts) == 1:
        x_specs = [pl.BlockSpec((rows, depth), lambda j, at: (0, at[0]))]
    else:
        x_specs = [pl.BlockSpec(x.shape, lambda j, at: (0, 0)) for x in parts]
    return pl.pallas_call(
        product_kernel,
        grid_spec=pltpu.PrefetchScalarGridSpec(
            num_scalar_prefetch=1,
            grid=(width // tile,),
            in_specs=x_specs + [pl.BlockSpec((depth, tile), lambda j, at: (0, j))],
            out_specs=pl.BlockSpec((rows, tile), lambda j, at: (0, j)),
        ),
        out_shape=jax.ShapeDtypeStruct((rows, width), kind),
        compiler_params=pltpu.CompilerParams(vmem_limit_bytes=VMEM_BYTES),
        cost_estimate=small_cost(),
        name="product",
    )(at, *parts, w)


def weight_kernel(n_z, n, at_ref, *refs):
    own_pairs, other_pairs = refs[:n], refs[n : 2 * n]
    dv_refs = refs[2 * n : 4 * n]
    outs = refs[4 * n :]
    core = at_ref[0]
    step = pl.program_id(0)
    rows = own_pairs[0].shape[1] // 2
    own = pl.ds(pl.multiple_of(core * rows, rows), rows)
    other = pl.ds(pl.multiple_of((1 - core) * rows, rows), rows)
    total = None
    for p in range(n):
        for flip in range(2):
            window = slice(flip * rows, (flip + 1) * rows)
            term = dot(own_pairs[p][:, window], dv_refs[2 * p + flip][own, :])
            term = term + dot(other_pairs[p][:, window], dv_refs[2 * p + flip][other, :])
            total = term if total is None else total + term
    for d, out in enumerate(outs):

        @pl.when(step == (n_z - 1 if d == 0 else d - 1))
        def _():
            out[...] = total.astype(out.dtype)


def run_weight(at, own_pairs, other_pairs, dv_pairs, n_z):
    n = len(own_pairs)
    count = own_pairs[0].shape[0] // n_z
    rows2 = own_pairs[0].shape[1]
    dvs = [x for pair_of in dv_pairs for x in pair_of]
    width = dvs[0].shape[1]
    shapes = [jax.ShapeDtypeStruct((count, width), F32 if d == 0 else BF16) for d in range(n_z)]
    pair_block = pl.BlockSpec((count, rows2), lambda d, at: (lax.rem(at[1] + d + 1, n_z), 0))
    return pl.pallas_call(
        functools.partial(weight_kernel, n_z, n),
        grid_spec=pltpu.PrefetchScalarGridSpec(
            num_scalar_prefetch=1,
            grid=(n_z,),
            in_specs=[pair_block] * (2 * n) + [pl.BlockSpec(dvs[0].shape, lambda d, at: (0, 0))] * (2 * n),
            out_specs=[pl.BlockSpec((count, width), lambda d, at: (0, 0))] * n_z,
        ),
        out_shape=shapes,
        compiler_params=pltpu.CompilerParams(vmem_limit_bytes=VMEM_BYTES),
        cost_estimate=small_cost(),
        name="weight",
    )(at, *own_pairs, *other_pairs, *dvs)


def tokens_kernel(n_fsdp, at_ref, dv_ref, w_ref, own_ref, *others):
    made = dot(dv_ref[...], w_ref[...], NT).astype(BF16)
    rows = own_ref.shape[0]
    own_ref[...] = made[:rows]
    for s, ref in enumerate(others):
        ref[...] = made[(s + 1) * rows : (s + 2) * rows]


def run_tokens(at, dv_rows, w, n_fsdp):
    slab, width = w.shape
    rows = dv_rows.shape[0] // n_fsdp
    tile = slab // 3 if slab % (3 * HD) == 0 else slab
    n_tiles = slab // tile
    return pl.pallas_call(
        functools.partial(tokens_kernel, n_fsdp),
        grid_spec=pltpu.PrefetchScalarGridSpec(
            num_scalar_prefetch=1,
            grid=(n_tiles,),
            in_specs=[
                pl.BlockSpec(dv_rows.shape, lambda j, at: (0, 0)),
                pl.BlockSpec((tile, width), lambda j, at: (j, 0)),
            ],
            out_specs=[pl.BlockSpec((rows, tile), lambda j, at: (0, at[0] * n_tiles + j))]
            + [pl.BlockSpec((rows, tile), lambda j, at: (0, j))] * (n_fsdp - 1),
        ),
        out_shape=[jax.ShapeDtypeStruct((rows, slab * n_fsdp), BF16)]
        + [jax.ShapeDtypeStruct((rows, slab), BF16)] * (n_fsdp - 1),
        compiler_params=pltpu.CompilerParams(vmem_limit_bytes=VMEM_BYTES),
        cost_estimate=small_cost(),
        name="tokens",
    )(at, dv_rows, w)


def shifted(x, by):
    length = lax.axis_size("ctx")
    return lax.ppermute(x, "ctx", [(i, i + by) for i in range(length) if 0 <= i + by < length])


def swapped(x):
    return lax.ppermute(x, "ctx", [(i, i ^ 1) for i in range(lax.axis_size("ctx"))])


def rotated(x, by):
    length = lax.axis_size("fsdp")
    return lax.ppermute(x, "fsdp", [(i, (i + by) % length) for i in range(length)])


def moved(x, flip, by):
    n_ctx, n_fsdp = lax.axis_size("ctx"), lax.axis_size("fsdp")
    pairs = [
        (c * n_fsdp + f, (c ^ (2 * flip)) * n_fsdp + (f + by) % n_fsdp)
        for c in range(n_ctx)
        for f in range(n_fsdp)
    ]
    return lax.ppermute(x, ("ctx", "fsdp"), pairs)


def relayed(my_y, far, got):
    return (far.astype(F32) + jnp.where(my_y == 1, got.astype(F32), 0.0)).astype(BF16)


def gathered_terms(my_y, mine, got, back):
    return (mine.astype(F32) + back.astype(F32) + jnp.where(my_y == 0, got.astype(F32), 0.0)).astype(BF16)


def cols(x, at, width):
    return lax.dynamic_slice_in_dim(x, at * width, width, x.ndim - 1)


def rows_of(x, at, count):
    return lax.dynamic_slice_in_dim(x, at * count, count, 0)


def placed(core, own, other, axis):
    both = jnp.concatenate([own, own], axis)
    return lax.dynamic_update_slice_in_dim(both, other, (1 - core) * own.shape[axis], axis)


def flipped(x):
    return lax.ppermute(x, "ctx", [(i, i ^ 2) for i in range(lax.axis_size("ctx"))])


def after(x, *earlier):
    return lax.optimization_barrier((x, *earlier))[0]


def shards(hidden, queries, key_heads, w_value, d_out, segments):
    shard_rows = hidden.shape[1]
    model = hidden.shape[2]
    kv_width = w_value.shape[1]
    n_ctx = lax.axis_size("ctx")
    n_fsdp = lax.axis_size("fsdp")
    chip_rows = 2 * shard_rows
    n_z = n_ctx // 4
    assert WINDOW == 2 * chip_rows
    my_ctx = lax.axis_index("ctx")
    my_fsdp = lax.axis_index("fsdp")
    core = my_ctx % 2
    core_arg = core.astype(jnp.int32).reshape(1)
    chip = my_ctx // 2
    my_y = chip % 2
    my_z = chip // 2
    half_kv = kv_width // 2
    slab = model // n_fsdp
    tokens = hidden[0]
    first = chip * chip_rows

    aligned = slab % HD == 0
    fsdp_arg = my_fsdp.astype(jnp.int32).reshape(1)
    zero_arg = jnp.zeros((1,), jnp.int32)
    half_q = queries.shape[2] // 2
    out_rows = model // (n_ctx * n_fsdp)
    places = [(flip, s) for flip in range(2) for s in range(n_fsdp)]

    cut = slab // HD // 2 * HD if aligned else slab
    parts_at = [(0, cut), (cut, slab)] if aligned else [(0, slab)]
    slabs = [
        [
            lax.dynamic_slice_in_dim(tokens, (my_fsdp + s) % n_fsdp * slab + low, high - low, 1)
            for low, high in parts_at
        ]
        for s in range(1, n_fsdp)
    ]
    sent = [[rotated(x, s + 1) for x in parts] for s, parts in enumerate(slabs)]

    own_tags = segments[0].astype(BF16)
    tag_row = lax.dynamic_update_slice_in_dim(jnp.zeros((half_kv,), BF16), own_tags, core * shard_rows, 0)
    tag_rows = jnp.concatenate([tag_row[None], jnp.zeros((15, half_kv), BF16)], 0)
    k_sent = jnp.concatenate([cols(key_heads[0], 1 - core, half_kv), tag_rows], 0)
    got = swapped(after(k_sent, *[parts[0] for parts in slabs]))

    if out_rows % 8 == 0:
        at = jnp.stack([my_y, my_fsdp]).astype(jnp.int32)
        pieces = run_pieces(after(at, k_sent, got), tokens, n_z, n_fsdp, out_rows)
    else:
        turned = tokens.T.reshape(n_z, 2, 2, n_fsdp, out_rows, shard_rows)
        pieces = []
        for flip, s in places:
            piece = lax.dynamic_index_in_dim(turned, my_y ^ flip, 1, keepdims=False)
            piece = lax.dynamic_index_in_dim(piece, (my_fsdp + s) % n_fsdp, 2, keepdims=False)
            pieces.append(piece.reshape(n_z * 2 * out_rows, shard_rows))
    by_place = dict(zip(places, pieces))

    k_own = jnp.concatenate(
        [
            placed(core, cols(key_heads[0], core, half_kv), got[:shard_rows], 0),
            tag_rows + got[shard_rows:],
        ],
        0,
    )
    k_far = shifted(k_own, 4)
    k_near = shifted(k_own, 2)
    over_y = {s: flipped(after(by_place[1, s], k_own)) for s in range(1, n_fsdp)}
    q_sent = jnp.concatenate([cols(queries[0], 1 - core, half_q), cols(d_out[0], 1 - core, half_q)], 1)
    q_other = swapped(after(q_sent, k_own))
    if aligned:
        value_own = run_product(after(fsdp_arg, q_sent, *pieces), [tokens], w_value, F32)
    else:
        value_own = dot(cols(tokens, my_fsdp, slab), w_value)
    keys = [k_far, k_near, k_own]

    span_tags = jnp.concatenate([k[chip_rows, :chip_rows] for k in keys], 0)
    key_at = jnp.arange(WINDOW + chip_rows, dtype=jnp.int32)
    chip_tags = k_own[chip_rows, :chip_rows]
    before = (span_tags[None, :] < chip_tags[:, None]) | (key_at + first < WINDOW)[None, :]
    low = jnp.sum(before.astype(jnp.int32), axis=1)
    low = jnp.maximum(low, jnp.arange(1, chip_rows + 1, dtype=jnp.int32))[None, :]

    if aligned:
        partial = [run_product(zero_arg, parts, w_value, BF16) for parts in sent]
    else:
        partial = [dot(parts[0], w_value).astype(BF16) for parts in sent]
    low = after(low, *partial)
    e, inv, do_t, dv_far, dv_near, dv_mine = run_probs(
        core_arg, low, queries[0], q_other, d_out[0], keys, chip_rows, half_kv
    )
    dv_got = flipped(dv_near)

    value_back = [rotated(x, -s - 1) for s, x in enumerate(partial)]
    over_fsdp = {s: rotated(after(by_place[0, s], sent), s) for s in range(1, n_fsdp)}
    value_back = [after(x, dv_near, over_y) for x in value_back]
    value_sum = value_own
    for x in value_back:
        value_sum = value_sum + x.astype(F32)
    own_values = value_sum.astype(BF16)
    v_own = placed(core, cols(own_values, core, half_kv), swapped(cols(own_values, 1 - core, half_kv)), 0)

    late_y = flipped(after(by_place[1, 0], k_near))
    v_own, late_y, over_fsdp = lax.optimization_barrier((v_own, late_y, over_fsdp))
    v_far = shifted(v_own, 4)
    own_pairs = [jnp.concatenate([by_place[0, 0], late_y], 1)]
    other_pairs = [swapped(after(own_pairs[0], v_own))]
    relayed_y = {s: rotated(after(over_y[s], own_values), s) for s in range(1, n_fsdp)}

    dv_got = after(dv_got, v_own)
    dv_sent = relayed(my_y, dv_far, dv_got)
    dv_back = shifted(dv_sent, -4)
    v_sent = after(jnp.where(my_y == 0, v_own, v_far), dv_sent)
    v_near = flipped(v_sent)
    vals = [v_far, v_near, v_own]
    dv_chip = gathered_terms(my_y, dv_mine, dv_got, after(dv_back, v_sent))
    dv_fsdp = [dv_chip] + [rotated(dv_chip, s) for s in range(1, n_fsdp)]
    dv_over_y = [moved(dv_chip, 1, s) for s in range(n_fsdp)]
    for s in range(1, n_fsdp):
        own_pairs.append(jnp.concatenate([over_fsdp[s], relayed_y[s]], 1))
        other_pairs.append(swapped(own_pairs[s]))
    vals = [v_far, v_near, v_own]
    v_near, dv_fsdp[1:] = lax.optimization_barrier((v_near, dv_fsdp[1:]))
    vals = [v_far, v_near, v_own]
    dv_sides = [
        jnp.concatenate([rows_of(x, at, shard_rows) for x in dv_fsdp], 0) for at in (core, 1 - core)
    ]
    dv_other = swapped(dv_sides[1])
    out, dq, other, dk_far, dk_near, dk_mine = run_grads(
        after(core_arg, *dv_sides), e, inv, do_t, queries[0], q_other, keys, vals, chip_rows, half_kv
    )
    dk_back = [shifted(dk_near, -2), shifted(dk_far, -4)]

    dv_over_y = [after(x, dk_near) for x in dv_over_y]
    dv_rows = placed(core, dv_sides[0], after(dv_other, dk_near), 1)
    dv_rows = after(dv_rows, *dv_over_y)
    if aligned:
        d_tokens, *made = run_tokens(fsdp_arg, dv_rows, w_value, n_fsdp)
    else:
        made = dot(dv_rows, w_value, NT).astype(BF16)
        made = [made[s * shard_rows : (s + 1) * shard_rows] for s in range(n_fsdp)]
        d_tokens = jnp.concatenate([made[0]] * n_fsdp, 1)
        made = made[1:]
    for s in range(1, n_fsdp):
        back = rotated(made[s - 1], -s)
        d_tokens = lax.dynamic_update_slice_in_dim(d_tokens, back, ((my_fsdp + s) % n_fsdp) * slab, 1)

    dv_pairs = list(zip(dv_fsdp, dv_over_y))
    if out_rows % 8 == 0:
        at = after(jnp.stack([core, my_z]).astype(jnp.int32), *made)
        by_z = run_weight(at, own_pairs, other_pairs, dv_pairs, n_z)
    else:
        weight_term = 0.0
        for p in range(n_fsdp):
            for flip in range(2):
                window = slice(flip * shard_rows, (flip + 1) * shard_rows)
                weight_term += dot(own_pairs[p][:, window], rows_of(dv_pairs[p][flip], core, shard_rows))
                weight_term += dot(other_pairs[p][:, window], rows_of(dv_pairs[p][flip], 1 - core, shard_rows))
        weight_term = weight_term.reshape(n_z, 2 * out_rows, half_kv)
        by_z = [
            lax.dynamic_index_in_dim(weight_term, (my_z + d) % n_z, 0, keepdims=False).astype(BF16 if d else F32)
            for d in range(n_z)
        ]
    by_z, dk_back = lax.optimization_barrier((list(by_z), dk_back))
    over_z = [
        lax.ppermute(by_z[d], "ctx", [(i, (i + 4 * d) % n_ctx) for i in range(n_ctx)]) for d in range(1, n_z)
    ]

    row_sum = by_z[0]
    for x in over_z:
        row_sum = row_sum + x.astype(F32)
    d_weight = placed(core, rows_of(row_sum, core, out_rows), swapped(rows_of(row_sum, 1 - core, out_rows)), 1)
    dk_chip = (dk_mine.astype(F32) + dk_back[0].astype(F32) + dk_back[1].astype(F32)).astype(BF16)
    d_keys = placed(core, rows_of(dk_chip, core, shard_rows), swapped(rows_of(dk_chip, 1 - core, shard_rows)), 1)
    other = swapped(after(other, *made))
    out = lax.dynamic_update_slice_in_dim(out, other[0], (1 - core) * half_q, 1)
    dq = lax.dynamic_update_slice_in_dim(dq, other[1], (1 - core) * half_q, 1)
    return (out[None], dq[None], d_keys[None], d_tokens[None], d_weight)


def solution(mesh):
    in_specs = (
        P("fsdp", "ctx", None),
        P("fsdp", "ctx", None),
        P("fsdp", "ctx", None),
        P("fsdp", None),
        P("fsdp", "ctx", None),
        P("fsdp", "ctx"),
    )
    out_specs = (
        P("fsdp", "ctx", None),
        P("fsdp", "ctx", None),
        P("fsdp", "ctx", None),
        P("fsdp", "ctx", None),
        P(("ctx", "fsdp"), None),
    )
    return jax.shard_map(shards, mesh=mesh, in_specs=in_specs, out_specs=out_specs, check_vma=False)
```

```python
import functools
import math

import jax
import jax.numpy as jnp
from jax import lax
from jax.experimental import pallas as pl
from jax.experimental.pallas import tpu as pltpu
from jax.sharding import PartitionSpec as P

HQ = 16
HK = 8
HD = 128
WINDOW = 1024
GROUP = 2
NEG = -1e30
VMEM_BYTES = 58 * 1024 * 1024

score_scale = 1.0 / math.sqrt(168.0)
exp2_scale = score_scale / math.log(2.0)

BF16 = jnp.bfloat16
F32 = jnp.float32
NT = (((1,), (1,)), ((), ()))
TN = (((0,), (0,)), ((), ()))


def dot(a, b, dims=(((1,), (0,)), ((), ()))):
    return lax.dot_general(a, b, dims, preferred_element_type=F32)


def probs_kernel(blk, n_back, core_ref, low_ref, q_own, q_other, do_own, do_other, *refs):
    n_arr = n_back + 1
    k_refs = refs[:n_arr]
    e_ref, inv_ref, dot_ref = refs[n_arr : n_arr + 3]
    dv_refs = refs[n_arr + 3 : 2 * n_arr + 3]
    bias, s_scr, dv_acc, q_buf, do_buf = refs[2 * n_arr + 3 :]
    span_blocks = WINDOW // blk + 1
    core = core_ref[0]

    @pl.when(pl.program_id(0) == 0)
    def _():
        for qb in range(2):
            kpos = lax.broadcasted_iota(jnp.int32, (span_blocks * blk, blk), 0) + qb * blk
            qpos = lax.broadcasted_iota(jnp.int32, (span_blocks * blk, blk), 1) + (qb * blk + WINDOW)
            low = low_ref[:, qb * blk : (qb + 1) * blk]
            ok = (kpos >= low) & (kpos <= qpos)
            bias[qb] = jnp.where(ok, 0.0, NEG)

    q_buf[core] = q_own[...]
    q_buf[1 - core] = q_other[...]
    do_buf[core] = do_own[...]
    do_buf[1 - core] = do_other[...]

    def key_block(j):
        return k_refs[j // 2][(j % 2) * blk : (j % 2 + 1) * blk, :]

    def stacked(buf, qb):
        return jnp.concatenate([buf[qb, :, r * HD : (r + 1) * HD] for r in range(GROUP)], 0)

    for qb in range(2):
        qs = stacked(q_buf, qb)
        top = None
        for j in range(span_blocks):
            s = dot(key_block(qb + j), qs, NT)
            b = bias[qb, j * blk : (j + 1) * blk, :]
            s = s * exp2_scale + jnp.concatenate([b] * GROUP, 1)
            s_scr[j] = s
            part = jnp.max(s.reshape(blk // 8, 8, GROUP * blk), axis=0)
            top = part if top is None else jnp.maximum(top, part)
        top = jnp.max(top, axis=0, keepdims=True)
        total = None
        for j in range(span_blocks):
            e = jnp.exp2(s_scr[j] - top)
            part = jnp.sum(e.reshape(blk // 8, 8, GROUP * blk), axis=0)
            total = part if total is None else total + part
            e_ref[0, qb, j * blk : (j + 1) * blk, :] = e.astype(BF16)
        inv = 1.0 / jnp.sum(total, axis=0, keepdims=True)
        inv_ref[0, qb] = inv
        do_t = (stacked(do_buf, qb).astype(F32).T * inv).astype(BF16)
        dot_ref[0, qb] = do_t
        for j in range(span_blocks):
            term = dot(e_ref[0, qb, j * blk : (j + 1) * blk, :], do_t, NT)
            at = slice((qb + j) * blk, (qb + j + 1) * blk)
            if qb == 0 or j == span_blocks - 1:
                dv_acc[at, :] = term
            else:
                dv_acc[at, :] += term
    for a in range(n_arr):
        dv_refs[a][...] = dv_acc[a * 2 * blk : (a + 1) * 2 * blk, :].astype(BF16)


def grads_kernel(blk, n_back, core_ref, e_ref, inv_ref, dot_ref, q_own, q_other, *refs):
    n_arr = n_back + 1
    k_refs = refs[:n_arr]
    v_refs = refs[n_arr : 2 * n_arr]
    out_ref, dq_ref, other_ref = refs[2 * n_arr : 2 * n_arr + 3]
    dk_refs = refs[2 * n_arr + 3 : 3 * n_arr + 3]
    dk_acc, q_buf, out_buf, dq_buf = refs[3 * n_arr + 3 :]
    span_blocks = WINDOW // blk + 1
    core = core_ref[0]

    q_buf[core] = q_own[...]
    q_buf[1 - core] = q_other[...]

    def block_of(arrays, j):
        return arrays[j // 2][(j % 2) * blk : (j % 2 + 1) * blk, :]

    for qb in range(2):
        qs = jnp.concatenate([q_buf[qb, :, r * HD : (r + 1) * HD] for r in range(GROUP)], 0)
        do_t = dot_ref[0, qb]
        out_t = None
        for j in range(span_blocks):
            e = e_ref[0, qb, j * blk : (j + 1) * blk, :]
            part = dot(block_of(v_refs, qb + j), e, TN)
            out_t = part if out_t is None else out_t + part
        out_t = (out_t * inv_ref[0, qb]).astype(BF16).astype(F32)
        delta = jnp.sum(out_t * do_t.astype(F32), axis=0, keepdims=True)
        out = out_t.T.astype(BF16)
        dq_t = None
        for j in range(span_blocks):
            e = e_ref[0, qb, j * blk : (j + 1) * blk, :].astype(F32)
            dp = dot(block_of(v_refs, qb + j), do_t)
            ds = (e * (dp - delta)).astype(BF16)
            term = dot(ds, qs)
            at = slice((qb + j) * blk, (qb + j + 1) * blk)
            if qb == 0 or j == span_blocks - 1:
                dk_acc[at, :] = term
            else:
                dk_acc[at, :] += term
            part = dot(block_of(k_refs, qb + j), ds, TN)
            dq_t = part if dq_t is None else dq_t + part
        dq = (dq_t * score_scale).T.astype(BF16)
        for r in range(GROUP):
            out_buf[qb, :, r * HD : (r + 1) * HD] = out[r * blk : (r + 1) * blk, :]
            dq_buf[qb, :, r * HD : (r + 1) * HD] = dq[r * blk : (r + 1) * blk, :]
    out_ref[...] = out_buf[core]
    dq_ref[...] = dq_buf[core]
    other_ref[0] = out_buf[1 - core]
    other_ref[1] = dq_buf[1 - core]
    for a in range(n_arr):
        dk_refs[a][...] = (dk_acc[a * 2 * blk : (a + 1) * 2 * blk, :] * score_scale).astype(BF16)


def specs_of(rows, width):
    blk = rows // 2
    heads = width // HD
    span = WINDOW + blk
    lanes = GROUP * blk
    head = pl.BlockSpec((rows, HD), lambda g, c: (0, g))
    own = pl.BlockSpec((blk, GROUP * HD), lambda g, c: (0, c[0] * heads + g))
    return blk, heads, span, lanes, head, own


def run_probs(core, low, q, q_other, do, keys, rows, width):
    blk, heads, span, lanes, head, own = specs_of(rows, width)
    n_arr = len(keys)
    return pl.pallas_call(
        functools.partial(probs_kernel, blk, n_arr - 1),
        grid_spec=pltpu.PrefetchScalarGridSpec(
            num_scalar_prefetch=1,
            grid=(heads,),
            in_specs=[
                pl.BlockSpec((1, rows), lambda g, c: (0, 0)),
                own,
                pl.BlockSpec((blk, GROUP * HD), lambda g, c: (0, g)),
                own,
                pl.BlockSpec((blk, GROUP * HD), lambda g, c: (0, heads + g)),
            ]
            + [head] * n_arr,
            out_specs=[
                pl.BlockSpec((1, 2, span, lanes), lambda g, c: (g, 0, 0, 0)),
                pl.BlockSpec((1, 2, 1, lanes), lambda g, c: (g, 0, 0, 0)),
                pl.BlockSpec((1, 2, HD, lanes), lambda g, c: (g, 0, 0, 0)),
            ]
            + [head] * n_arr,
            scratch_shapes=[
                pltpu.VMEM((2, span, blk), F32),
                pltpu.VMEM((span // blk, blk, lanes), F32),
                pltpu.VMEM((WINDOW + rows, HD), F32),
                pltpu.VMEM((2, blk, GROUP * HD), BF16),
                pltpu.VMEM((2, blk, GROUP * HD), BF16),
            ],
        ),
        out_shape=[
            jax.ShapeDtypeStruct((heads, 2, span, lanes), BF16),
            jax.ShapeDtypeStruct((heads, 2, 1, lanes), F32),
            jax.ShapeDtypeStruct((heads, 2, HD, lanes), BF16),
        ]
        + [jax.ShapeDtypeStruct((rows, width), BF16)] * n_arr,
        compiler_params=pltpu.CompilerParams(vmem_limit_bytes=VMEM_BYTES),
        cost_estimate=small_cost(),
        name="probs",
    )(core, low, q, q_other, do, q_other, *keys)


def run_grads(core, e, inv, do_t, q, q_other, keys, values, rows, width, low, high):
    blk, heads, span, lanes, _, _ = specs_of(rows, width)
    n_arr = len(keys)
    count = high - low
    head = pl.BlockSpec((rows, HD), lambda g, c: (0, low + g))
    head_out = pl.BlockSpec((rows, HD), lambda g, c: (0, g))
    group_out = pl.BlockSpec((blk, GROUP * HD), lambda g, c: (0, g))
    return pl.pallas_call(
        functools.partial(grads_kernel, blk, n_arr - 1),
        grid_spec=pltpu.PrefetchScalarGridSpec(
            num_scalar_prefetch=1,
            grid=(count,),
            in_specs=[
                pl.BlockSpec((1, 2, span, lanes), lambda g, c: (low + g, 0, 0, 0)),
                pl.BlockSpec((1, 2, 1, lanes), lambda g, c: (low + g, 0, 0, 0)),
                pl.BlockSpec((1, 2, HD, lanes), lambda g, c: (low + g, 0, 0, 0)),
                pl.BlockSpec((blk, GROUP * HD), lambda g, c: (0, c[0] * heads + low + g)),
                pl.BlockSpec((blk, GROUP * HD), lambda g, c: (0, low + g)),
            ]
            + [head] * (2 * n_arr),
            out_specs=[group_out, group_out, pl.BlockSpec((2, blk, GROUP * HD), lambda g, c: (0, 0, g))]
            + [head_out] * n_arr,
            scratch_shapes=[
                pltpu.VMEM((WINDOW + rows, HD), F32),
                pltpu.VMEM((2, blk, GROUP * HD), BF16),
                pltpu.VMEM((2, blk, GROUP * HD), BF16),
                pltpu.VMEM((2, blk, GROUP * HD), BF16),
            ],
        ),
        out_shape=[jax.ShapeDtypeStruct((blk, GROUP * HD * count), BF16)] * 2
        + [jax.ShapeDtypeStruct((2, blk, GROUP * HD * count), BF16)]
        + [jax.ShapeDtypeStruct((rows, HD * count), BF16)] * n_arr,
        compiler_params=pltpu.CompilerParams(vmem_limit_bytes=VMEM_BYTES),
        cost_estimate=small_cost(),
        name="grads",
    )(core, e, inv, do_t, q, q_other, *keys, *values)


def small_cost():
    return pl.CostEstimate(flops=1 << 20, bytes_accessed=1 << 12, transcendentals=0)


def whole():
    return pl.BlockSpec(memory_space=pltpu.VMEM)


def pieces_kernel(dims, at_ref, x_ref, *refs):
    n_z, n_fsdp, out_rows = dims
    outs = refs[: 2 * n_fsdp]
    turned = refs[2 * n_fsdp]
    my_y, my_fsdp = at_ref[0], at_ref[1]
    for c in range(x_ref.shape[1] // HD):
        turned[c * HD : (c + 1) * HD, :] = x_ref[:, c * HD : (c + 1) * HD].astype(F32).T
    for p, out in enumerate(outs):
        flip, s = p // n_fsdp, p % n_fsdp
        y = lax.rem(my_y + flip, 2)
        f = lax.rem(my_fsdp + s, n_fsdp)
        for z in range(n_z):
            parts = []
            for core in range(2):
                block = ((z * 2 + y) * 2 + core) * n_fsdp + f
                parts.append(turned[pl.ds(pl.multiple_of(block * out_rows, 8), out_rows), :])
            out[z * 2 * out_rows : (z + 1) * 2 * out_rows, :] = jnp.concatenate(parts, 0).astype(BF16)


def run_pieces(at, tokens, n_z, n_fsdp, out_rows):
    rows, model = tokens.shape
    shape = jax.ShapeDtypeStruct((n_z * 2 * out_rows, rows), BF16)
    return pl.pallas_call(
        functools.partial(pieces_kernel, (n_z, n_fsdp, out_rows)),
        in_specs=[pl.BlockSpec(memory_space=pltpu.SMEM), whole()],
        out_specs=[whole()] * (2 * n_fsdp),
        out_shape=[shape] * (2 * n_fsdp),
        scratch_shapes=[pltpu.VMEM((model, rows), F32)],
        compiler_params=pltpu.CompilerParams(vmem_limit_bytes=VMEM_BYTES),
        cost_estimate=small_cost(),
        name="pieces",
    )(at, tokens)


def product_kernel(at_ref, *refs):
    *x_refs, w_ref, o_ref = refs
    total, first = None, 0
    for x in x_refs:
        term = dot(x[...], w_ref[first : first + x.shape[1], :])
        total = term if total is None else total + term
        first += x.shape[1]
    o_ref[...] = total.astype(o_ref.dtype)


def run_product(at, parts, w, kind):
    rows = parts[0].shape[0]
    depth, width = w.shape
    tile = 512
    if len(parts) == 1:
        x_specs = [pl.BlockSpec((rows, depth), lambda j, at: (0, at[0]))]
    else:
        x_specs = [pl.BlockSpec(x.shape, lambda j, at: (0, 0)) for x in parts]
    return pl.pallas_call(
        product_kernel,
        grid_spec=pltpu.PrefetchScalarGridSpec(
            num_scalar_prefetch=1,
            grid=(width // tile,),
            in_specs=x_specs + [pl.BlockSpec((depth, tile), lambda j, at: (0, j))],
            out_specs=pl.BlockSpec((rows, tile), lambda j, at: (0, j)),
        ),
        out_shape=jax.ShapeDtypeStruct((rows, width), kind),
        compiler_params=pltpu.CompilerParams(vmem_limit_bytes=VMEM_BYTES),
        cost_estimate=small_cost(),
        name="product",
    )(at, *parts, w)


def weight_kernel(n_z, n, at_ref, *refs):
    own_pairs, other_pairs = refs[:n], refs[n : 2 * n]
    dv_refs = refs[2 * n : 4 * n]
    outs = refs[4 * n :]
    core = at_ref[0]
    step = pl.program_id(0)
    rows = own_pairs[0].shape[1] // 2
    own = pl.ds(pl.multiple_of(core * rows, rows), rows)
    other = pl.ds(pl.multiple_of((1 - core) * rows, rows), rows)
    total = None
    for p in range(n):
        for flip in range(2):
            window = slice(flip * rows, (flip + 1) * rows)
            term = dot(own_pairs[p][:, window], dv_refs[2 * p + flip][own, :])
            term = term + dot(other_pairs[p][:, window], dv_refs[2 * p + flip][other, :])
            total = term if total is None else total + term
    for d, out in enumerate(outs):

        @pl.when(step == (n_z - 1 if d == 0 else d - 1))
        def _():
            out[...] = total.astype(out.dtype)


def run_weight(at, own_pairs, other_pairs, dv_pairs, n_z):
    n = len(own_pairs)
    count = own_pairs[0].shape[0] // n_z
    rows2 = own_pairs[0].shape[1]
    dvs = [x for pair_of in dv_pairs for x in pair_of]
    width = dvs[0].shape[1]
    shapes = [jax.ShapeDtypeStruct((count, width), F32 if d == 0 else BF16) for d in range(n_z)]
    pair_block = pl.BlockSpec((count, rows2), lambda d, at: (lax.rem(at[1] + d + 1, n_z), 0))
    return pl.pallas_call(
        functools.partial(weight_kernel, n_z, n),
        grid_spec=pltpu.PrefetchScalarGridSpec(
            num_scalar_prefetch=1,
            grid=(n_z,),
            in_specs=[pair_block] * (2 * n) + [pl.BlockSpec(dvs[0].shape, lambda d, at: (0, 0))] * (2 * n),
            out_specs=[pl.BlockSpec((count, width), lambda d, at: (0, 0))] * n_z,
        ),
        out_shape=shapes,
        compiler_params=pltpu.CompilerParams(vmem_limit_bytes=VMEM_BYTES),
        cost_estimate=small_cost(),
        name="weight",
    )(at, *own_pairs, *other_pairs, *dvs)


def tokens_kernel(n_fsdp, at_ref, dv_ref, w_ref, own_ref, *others):
    made = dot(dv_ref[...], w_ref[...], NT).astype(BF16)
    rows = own_ref.shape[0]
    own_ref[...] = made[:rows]
    for s, ref in enumerate(others):
        ref[...] = made[(s + 1) * rows : (s + 2) * rows]


def run_tokens(at, dv_rows, w, n_fsdp):
    slab, width = w.shape
    rows = dv_rows.shape[0] // n_fsdp
    tile = slab // 3 if slab % (3 * HD) == 0 else slab
    n_tiles = slab // tile
    return pl.pallas_call(
        functools.partial(tokens_kernel, n_fsdp),
        grid_spec=pltpu.PrefetchScalarGridSpec(
            num_scalar_prefetch=1,
            grid=(n_tiles,),
            in_specs=[
                pl.BlockSpec(dv_rows.shape, lambda j, at: (0, 0)),
                pl.BlockSpec((tile, width), lambda j, at: (j, 0)),
            ],
            out_specs=[pl.BlockSpec((rows, tile), lambda j, at: (0, at[0] * n_tiles + j))]
            + [pl.BlockSpec((rows, tile), lambda j, at: (0, j))] * (n_fsdp - 1),
        ),
        out_shape=[jax.ShapeDtypeStruct((rows, slab * n_fsdp), BF16)]
        + [jax.ShapeDtypeStruct((rows, slab), BF16)] * (n_fsdp - 1),
        compiler_params=pltpu.CompilerParams(vmem_limit_bytes=VMEM_BYTES),
        cost_estimate=small_cost(),
        name="tokens",
    )(at, dv_rows, w)


def shifted(x, by):
    length = lax.axis_size("ctx")
    return lax.ppermute(x, "ctx", [(i, i + by) for i in range(length) if 0 <= i + by < length])


def swapped(x):
    return lax.ppermute(x, "ctx", [(i, i ^ 1) for i in range(lax.axis_size("ctx"))])


def rotated(x, by):
    length = lax.axis_size("fsdp")
    return lax.ppermute(x, "fsdp", [(i, (i + by) % length) for i in range(length)])


def moved(x, flip, by):
    n_ctx, n_fsdp = lax.axis_size("ctx"), lax.axis_size("fsdp")
    pairs = [
        (c * n_fsdp + f, (c ^ (2 * flip)) * n_fsdp + (f + by) % n_fsdp)
        for c in range(n_ctx)
        for f in range(n_fsdp)
    ]
    return lax.ppermute(x, ("ctx", "fsdp"), pairs)


def relayed(my_y, far, got):
    return (far.astype(F32) + jnp.where(my_y == 1, got.astype(F32), 0.0)).astype(BF16)


def gathered_terms(my_y, mine, got, back):
    return (mine.astype(F32) + back.astype(F32) + jnp.where(my_y == 0, got.astype(F32), 0.0)).astype(BF16)


def cols(x, at, width):
    return lax.dynamic_slice_in_dim(x, at * width, width, x.ndim - 1)


def rows_of(x, at, count):
    return lax.dynamic_slice_in_dim(x, at * count, count, 0)


def placed(core, own, other, axis):
    both = jnp.concatenate([own, own], axis)
    return lax.dynamic_update_slice_in_dim(both, other, (1 - core) * own.shape[axis], axis)


def flipped(x):
    return lax.ppermute(x, "ctx", [(i, i ^ 2) for i in range(lax.axis_size("ctx"))])


def after(x, *earlier):
    return lax.optimization_barrier((x, *earlier))[0]


def shards(hidden, queries, key_heads, w_value, d_out, segments):
    shard_rows = hidden.shape[1]
    model = hidden.shape[2]
    kv_width = w_value.shape[1]
    n_ctx = lax.axis_size("ctx")
    n_fsdp = lax.axis_size("fsdp")
    chip_rows = 2 * shard_rows
    n_z = n_ctx // 4
    assert WINDOW == 2 * chip_rows
    my_ctx = lax.axis_index("ctx")
    my_fsdp = lax.axis_index("fsdp")
    core = my_ctx % 2
    core_arg = core.astype(jnp.int32).reshape(1)
    chip = my_ctx // 2
    my_y = chip % 2
    my_z = chip // 2
    half_kv = kv_width // 2
    slab = model // n_fsdp
    tokens = hidden[0]
    first = chip * chip_rows

    aligned = slab % HD == 0
    fsdp_arg = my_fsdp.astype(jnp.int32).reshape(1)
    zero_arg = jnp.zeros((1,), jnp.int32)
    half_q = queries.shape[2] // 2
    out_rows = model // (n_ctx * n_fsdp)
    places = [(flip, s) for flip in range(2) for s in range(n_fsdp)]

    cut = slab // HD // 2 * HD if aligned else slab
    parts_at = [(0, cut), (cut, slab)] if aligned else [(0, slab)]
    slabs = [
        [
            lax.dynamic_slice_in_dim(tokens, (my_fsdp + s) % n_fsdp * slab + low, high - low, 1)
            for low, high in parts_at
        ]
        for s in range(1, n_fsdp)
    ]
    sent = [[rotated(x, s + 1) for x in parts] for s, parts in enumerate(slabs)]

    own_tags = segments[0].astype(BF16)
    tag_row = lax.dynamic_update_slice_in_dim(jnp.zeros((half_kv,), BF16), own_tags, core * shard_rows, 0)
    tag_rows = jnp.concatenate([tag_row[None], jnp.zeros((15, half_kv), BF16)], 0)
    k_sent = jnp.concatenate([cols(key_heads[0], 1 - core, half_kv), tag_rows], 0)
    got = swapped(after(k_sent, *[parts[0] for parts in slabs]))

    if out_rows % 8 == 0:
        at = jnp.stack([my_y, my_fsdp]).astype(jnp.int32)
        pieces = run_pieces(after(at, k_sent, got), tokens, n_z, n_fsdp, out_rows)
    else:
        turned = tokens.T.reshape(n_z, 2, 2, n_fsdp, out_rows, shard_rows)
        pieces = []
        for flip, s in places:
            piece = lax.dynamic_index_in_dim(turned, my_y ^ flip, 1, keepdims=False)
            piece = lax.dynamic_index_in_dim(piece, (my_fsdp + s) % n_fsdp, 2, keepdims=False)
            pieces.append(piece.reshape(n_z * 2 * out_rows, shard_rows))
    by_place = dict(zip(places, pieces))

    k_own = jnp.concatenate(
        [
            placed(core, cols(key_heads[0], core, half_kv), got[:shard_rows], 0),
            tag_rows + got[shard_rows:],
        ],
        0,
    )
    k_far = shifted(k_own, 4)
    k_near = shifted(k_own, 2)
    over_y = {s: flipped(after(by_place[1, s], k_own)) for s in range(1, n_fsdp)}
    q_sent = jnp.concatenate([cols(queries[0], 1 - core, half_q), cols(d_out[0], 1 - core, half_q)], 1)
    q_other = swapped(after(q_sent, k_own))
    if aligned:
        value_own = run_product(after(fsdp_arg, q_sent, *pieces), [tokens], w_value, F32)
    else:
        value_own = dot(cols(tokens, my_fsdp, slab), w_value)
    keys = [k_far, k_near, k_own]

    span_tags = jnp.concatenate([k[chip_rows, :chip_rows] for k in keys], 0)
    key_at = jnp.arange(WINDOW + chip_rows, dtype=jnp.int32)
    chip_tags = k_own[chip_rows, :chip_rows]
    before = (span_tags[None, :] < chip_tags[:, None]) | (key_at + first < WINDOW)[None, :]
    low = jnp.sum(before.astype(jnp.int32), axis=1)
    low = jnp.maximum(low, jnp.arange(1, chip_rows + 1, dtype=jnp.int32))[None, :]

    if aligned:
        partial = [run_product(zero_arg, parts, w_value, BF16) for parts in sent]
    else:
        partial = [dot(parts[0], w_value).astype(BF16) for parts in sent]
    low = after(low, *partial)
    e, inv, do_t, dv_far, dv_near, dv_mine = run_probs(
        core_arg, low, queries[0], q_other, d_out[0], keys, chip_rows, half_kv
    )
    dv_got = flipped(dv_near)

    value_back = [rotated(x, -s - 1) for s, x in enumerate(partial)]
    over_fsdp = {s: rotated(after(by_place[0, s], sent), s) for s in range(1, n_fsdp)}
    value_back = [after(x, dv_near, over_y) for x in value_back]
    value_sum = value_own
    for x in value_back:
        value_sum = value_sum + x.astype(F32)
    own_values = value_sum.astype(BF16)
    v_own = placed(core, cols(own_values, core, half_kv), swapped(cols(own_values, 1 - core, half_kv)), 0)

    late_y = flipped(after(by_place[1, 0], k_near))
    v_own, late_y, over_fsdp = lax.optimization_barrier((v_own, late_y, over_fsdp))
    v_far = shifted(v_own, 4)
    own_pairs = [jnp.concatenate([by_place[0, 0], late_y], 1)]
    other_pairs = [swapped(after(own_pairs[0], v_own))]
    relayed_y = {s: rotated(after(over_y[s], own_values), s) for s in range(1, n_fsdp)}

    dv_got = after(dv_got, v_own)
    dv_sent = relayed(my_y, dv_far, dv_got)
    dv_back = shifted(dv_sent, -4)
    v_sent = after(jnp.where(my_y == 0, v_own, v_far), dv_sent)
    v_near = flipped(v_sent)
    vals = [v_far, v_near, v_own]
    dv_chip = gathered_terms(my_y, dv_mine, dv_got, after(dv_back, v_sent))
    dv_fsdp = [dv_chip] + [rotated(dv_chip, s) for s in range(1, n_fsdp)]
    dv_over_y = [moved(dv_chip, 1, s) for s in range(n_fsdp)]
    for s in range(1, n_fsdp):
        own_pairs.append(jnp.concatenate([over_fsdp[s], relayed_y[s]], 1))
        other_pairs.append(swapped(own_pairs[s]))
    vals = [v_far, v_near, v_own]
    vals = [v_far, v_near, v_own]
    n_heads = half_kv // HD
    grad_args = (e, inv, do_t, queries[0], q_other, keys, vals, chip_rows, half_kv)
    early = run_grads(core_arg, *grad_args, 0, n_heads // 2)
    early_back = [shifted(early[4], -2), shifted(early[3], -4)]

    dv_fsdp[1:] = [after(x, early[4]) for x in dv_fsdp[1:]]
    dv_over_y = [after(x, early[4]) for x in dv_over_y]
    dv_sides = [
        jnp.concatenate([rows_of(x, at, shard_rows) for x in dv_fsdp], 0) for at in (core, 1 - core)
    ]
    dv_rows = placed(core, dv_sides[0], swapped(dv_sides[1]), 1)
    dv_rows = after(dv_rows, *dv_over_y)
    if aligned:
        d_tokens, *made = run_tokens(fsdp_arg, dv_rows, w_value, n_fsdp)
    else:
        made = dot(dv_rows, w_value, NT).astype(BF16)
        made = [made[s * shard_rows : (s + 1) * shard_rows] for s in range(n_fsdp)]
        d_tokens = jnp.concatenate([made[0]] * n_fsdp, 1)
        made = made[1:]
    for s in range(1, n_fsdp):
        back = rotated(made[s - 1], -s)
        d_tokens = lax.dynamic_update_slice_in_dim(d_tokens, back, ((my_fsdp + s) % n_fsdp) * slab, 1)

    dv_pairs = list(zip(dv_fsdp, dv_over_y))
    if out_rows % 8 == 0:
        at = after(jnp.stack([core, my_z]).astype(jnp.int32), *made)
        by_z = run_weight(at, own_pairs, other_pairs, dv_pairs, n_z)
    else:
        weight_term = 0.0
        for p in range(n_fsdp):
            for flip in range(2):
                window = slice(flip * shard_rows, (flip + 1) * shard_rows)
                weight_term += dot(own_pairs[p][:, window], rows_of(dv_pairs[p][flip], core, shard_rows))
                weight_term += dot(other_pairs[p][:, window], rows_of(dv_pairs[p][flip], 1 - core, shard_rows))
        weight_term = weight_term.reshape(n_z, 2 * out_rows, half_kv)
        by_z = [
            lax.dynamic_index_in_dim(weight_term, (my_z + d) % n_z, 0, keepdims=False).astype(BF16 if d else F32)
            for d in range(n_z)
        ]
    by_z, early_back = lax.optimization_barrier((list(by_z), early_back))
    over_z = [
        lax.ppermute(by_z[d], "ctx", [(i, (i + 4 * d) % n_ctx) for i in range(n_ctx)]) for d in range(1, n_z)
    ]

    late = run_grads(after(core_arg, by_z[0]), *grad_args, n_heads // 2, n_heads)
    late_back = [shifted(late[4], -2), shifted(late[3], -4)]
    over_z = [after(x, late[4]) for x in over_z]
    row_sum = by_z[0]
    for x in over_z:
        row_sum = row_sum + x.astype(F32)
    d_weight = placed(core, rows_of(row_sum, core, out_rows), swapped(rows_of(row_sum, 1 - core, out_rows)), 1)
    late_back = [after(x, over_z[0]) for x in late_back]
    dk_chip = jnp.concatenate(
        [
            (made_by[5].astype(F32) + back[0].astype(F32) + back[1].astype(F32)).astype(BF16)
            for made_by, back in ((early, early_back), (late, late_back))
        ],
        1,
    )
    d_keys = placed(core, rows_of(dk_chip, core, shard_rows), swapped(rows_of(dk_chip, 1 - core, shard_rows)), 1)
    out, dq, other = [jnp.concatenate((early[i], late[i]), early[i].ndim - 1) for i in range(3)]
    other = swapped(other)
    out = placed(core, out, other[0], 1)
    dq = placed(core, dq, other[1], 1)
    return (out[None], dq[None], d_keys[None], d_tokens[None], d_weight)


def solution(mesh):
    in_specs = (
        P("fsdp", "ctx", None),
        P("fsdp", "ctx", None),
        P("fsdp", "ctx", None),
        P("fsdp", None),
        P("fsdp", "ctx", None),
        P("fsdp", "ctx"),
    )
    out_specs = (
        P("fsdp", "ctx", None),
        P("fsdp", "ctx", None),
        P("fsdp", "ctx", None),
        P("fsdp", "ctx", None),
        P(("ctx", "fsdp"), None),
    )
    return jax.shard_map(shards, mesh=mesh, in_specs=in_specs, out_specs=out_specs, check_vma=False)
```

```python
import functools
import math

import jax
import jax.numpy as jnp
from jax import lax
from jax.experimental import pallas as pl
from jax.experimental.pallas import tpu as pltpu
from jax.sharding import PartitionSpec as P

HQ = 16
HK = 8
HD = 128
WINDOW = 1024
GROUP = 2
NEG = -1e30
VMEM_BYTES = 58 * 1024 * 1024

score_scale = 1.0 / math.sqrt(168.0)
exp2_scale = score_scale / math.log(2.0)

BF16 = jnp.bfloat16
F32 = jnp.float32
NT = (((1,), (1,)), ((), ()))
TN = (((0,), (0,)), ((), ()))


def dot(a, b, dims=(((1,), (0,)), ((), ()))):
    return lax.dot_general(a, b, dims, preferred_element_type=F32)


def probs_kernel(blk, n_back, core_ref, low_ref, q_own, q_other, do_own, do_other, *refs):
    n_arr = n_back + 1
    k_refs = refs[:n_arr]
    e_ref, inv_ref, dot_ref = refs[n_arr : n_arr + 3]
    dv_refs = refs[n_arr + 3 : 2 * n_arr + 3]
    bias, s_scr, dv_acc, q_buf, do_buf = refs[2 * n_arr + 3 :]
    span_blocks = WINDOW // blk + 1
    core = core_ref[0]

    @pl.when(pl.program_id(0) == 0)
    def _():
        for qb in range(2):
            kpos = lax.broadcasted_iota(jnp.int32, (span_blocks * blk, blk), 0) + qb * blk
            qpos = lax.broadcasted_iota(jnp.int32, (span_blocks * blk, blk), 1) + (qb * blk + WINDOW)
            low = low_ref[:, qb * blk : (qb + 1) * blk]
            ok = (kpos >= low) & (kpos <= qpos)
            bias[qb] = jnp.where(ok, 0.0, NEG)

    q_buf[core] = q_own[...]
    q_buf[1 - core] = q_other[...]
    do_buf[core] = do_own[...]
    do_buf[1 - core] = do_other[...]

    def key_block(j):
        return k_refs[j // 2][(j % 2) * blk : (j % 2 + 1) * blk, :]

    def stacked(buf, qb):
        return jnp.concatenate([buf[qb, :, r * HD : (r + 1) * HD] for r in range(GROUP)], 0)

    for qb in range(2):
        qs = stacked(q_buf, qb)
        top = None
        for j in range(span_blocks):
            s = dot(key_block(qb + j), qs, NT)
            b = bias[qb, j * blk : (j + 1) * blk, :]
            s = s * exp2_scale + jnp.concatenate([b] * GROUP, 1)
            s_scr[j] = s
            part = jnp.max(s.reshape(blk // 8, 8, GROUP * blk), axis=0)
            top = part if top is None else jnp.maximum(top, part)
        top = jnp.max(top, axis=0, keepdims=True)
        total = None
        for j in range(span_blocks):
            e = jnp.exp2(s_scr[j] - top)
            part = jnp.sum(e.reshape(blk // 8, 8, GROUP * blk), axis=0)
            total = part if total is None else total + part
            e_ref[0, qb, j * blk : (j + 1) * blk, :] = e.astype(BF16)
        inv = 1.0 / jnp.sum(total, axis=0, keepdims=True)
        inv_ref[0, qb] = inv
        do_t = (stacked(do_buf, qb).astype(F32).T * inv).astype(BF16)
        dot_ref[0, qb] = do_t
        for j in range(span_blocks):
            term = dot(e_ref[0, qb, j * blk : (j + 1) * blk, :], do_t, NT)
            at = slice((qb + j) * blk, (qb + j + 1) * blk)
            if qb == 0 or j == span_blocks - 1:
                dv_acc[at, :] = term
            else:
                dv_acc[at, :] += term
    for a in range(n_arr):
        dv_refs[a][...] = dv_acc[a * 2 * blk : (a + 1) * 2 * blk, :].astype(BF16)


def grads_kernel(blk, n_back, core_ref, e_ref, inv_ref, dot_ref, q_own, q_other, *refs):
    n_arr = n_back + 1
    k_refs = refs[:n_arr]
    v_refs = refs[n_arr : 2 * n_arr]
    out_ref, dq_ref, other_ref = refs[2 * n_arr : 2 * n_arr + 3]
    dk_refs = refs[2 * n_arr + 3 : 3 * n_arr + 3]
    dk_acc, q_buf, out_buf, dq_buf = refs[3 * n_arr + 3 :]
    span_blocks = WINDOW // blk + 1
    core = core_ref[0]

    q_buf[core] = q_own[...]
    q_buf[1 - core] = q_other[...]

    def block_of(arrays, j):
        return arrays[j // 2][(j % 2) * blk : (j % 2 + 1) * blk, :]

    for qb in range(2):
        qs = jnp.concatenate([q_buf[qb, :, r * HD : (r + 1) * HD] for r in range(GROUP)], 0)
        do_t = dot_ref[0, qb]
        out_t = None
        for j in range(span_blocks):
            e = e_ref[0, qb, j * blk : (j + 1) * blk, :]
            part = dot(block_of(v_refs, qb + j), e, TN)
            out_t = part if out_t is None else out_t + part
        out_t = (out_t * inv_ref[0, qb]).astype(BF16).astype(F32)
        delta = jnp.sum(out_t * do_t.astype(F32), axis=0, keepdims=True)
        out = out_t.T.astype(BF16)
        dq_t = None
        for j in range(span_blocks):
            e = e_ref[0, qb, j * blk : (j + 1) * blk, :].astype(F32)
            dp = dot(block_of(v_refs, qb + j), do_t)
            ds = (e * (dp - delta)).astype(BF16)
            term = dot(ds, qs)
            at = slice((qb + j) * blk, (qb + j + 1) * blk)
            if qb == 0 or j == span_blocks - 1:
                dk_acc[at, :] = term
            else:
                dk_acc[at, :] += term
            part = dot(block_of(k_refs, qb + j), ds, TN)
            dq_t = part if dq_t is None else dq_t + part
        dq = (dq_t * score_scale).T.astype(BF16)
        for r in range(GROUP):
            out_buf[qb, :, r * HD : (r + 1) * HD] = out[r * blk : (r + 1) * blk, :]
            dq_buf[qb, :, r * HD : (r + 1) * HD] = dq[r * blk : (r + 1) * blk, :]
    out_ref[...] = out_buf[core]
    dq_ref[...] = dq_buf[core]
    other_ref[0] = out_buf[1 - core]
    other_ref[1] = dq_buf[1 - core]
    for a in range(n_arr):
        dk_refs[a][...] = (dk_acc[a * 2 * blk : (a + 1) * 2 * blk, :] * score_scale).astype(BF16)


def specs_of(rows, width):
    blk = rows // 2
    heads = width // HD
    span = WINDOW + blk
    lanes = GROUP * blk
    head = pl.BlockSpec((rows, HD), lambda g, c: (0, g))
    own = pl.BlockSpec((blk, GROUP * HD), lambda g, c: (0, c[0] * heads + g))
    return blk, heads, span, lanes, head, own


def run_probs(core, low, q, q_other, do, keys, rows, width):
    blk, heads, span, lanes, head, own = specs_of(rows, width)
    n_arr = len(keys)
    return pl.pallas_call(
        functools.partial(probs_kernel, blk, n_arr - 1),
        grid_spec=pltpu.PrefetchScalarGridSpec(
            num_scalar_prefetch=1,
            grid=(heads,),
            in_specs=[
                pl.BlockSpec((1, rows), lambda g, c: (0, 0)),
                own,
                pl.BlockSpec((blk, GROUP * HD), lambda g, c: (0, g)),
                own,
                pl.BlockSpec((blk, GROUP * HD), lambda g, c: (0, heads + g)),
            ]
            + [head] * n_arr,
            out_specs=[
                pl.BlockSpec((1, 2, span, lanes), lambda g, c: (g, 0, 0, 0)),
                pl.BlockSpec((1, 2, 1, lanes), lambda g, c: (g, 0, 0, 0)),
                pl.BlockSpec((1, 2, HD, lanes), lambda g, c: (g, 0, 0, 0)),
            ]
            + [head] * n_arr,
            scratch_shapes=[
                pltpu.VMEM((2, span, blk), F32),
                pltpu.VMEM((span // blk, blk, lanes), F32),
                pltpu.VMEM((WINDOW + rows, HD), F32),
                pltpu.VMEM((2, blk, GROUP * HD), BF16),
                pltpu.VMEM((2, blk, GROUP * HD), BF16),
            ],
        ),
        out_shape=[
            jax.ShapeDtypeStruct((heads, 2, span, lanes), BF16),
            jax.ShapeDtypeStruct((heads, 2, 1, lanes), F32),
            jax.ShapeDtypeStruct((heads, 2, HD, lanes), BF16),
        ]
        + [jax.ShapeDtypeStruct((rows, width), BF16)] * n_arr,
        compiler_params=pltpu.CompilerParams(vmem_limit_bytes=VMEM_BYTES),
        cost_estimate=small_cost(),
        name="probs",
    )(core, low, q, q_other, do, q_other, *keys)


def run_grads(core, e, inv, do_t, q, q_other, keys, values, rows, width, low, high):
    blk, heads, span, lanes, _, _ = specs_of(rows, width)
    n_arr = len(keys)
    count = high - low
    head = pl.BlockSpec((rows, HD), lambda g, c: (0, low + g))
    head_out = pl.BlockSpec((rows, HD), lambda g, c: (0, g))
    group_out = pl.BlockSpec((blk, GROUP * HD), lambda g, c: (0, g))
    return pl.pallas_call(
        functools.partial(grads_kernel, blk, n_arr - 1),
        grid_spec=pltpu.PrefetchScalarGridSpec(
            num_scalar_prefetch=1,
            grid=(count,),
            in_specs=[
                pl.BlockSpec((1, 2, span, lanes), lambda g, c: (low + g, 0, 0, 0)),
                pl.BlockSpec((1, 2, 1, lanes), lambda g, c: (low + g, 0, 0, 0)),
                pl.BlockSpec((1, 2, HD, lanes), lambda g, c: (low + g, 0, 0, 0)),
                pl.BlockSpec((blk, GROUP * HD), lambda g, c: (0, c[0] * heads + low + g)),
                pl.BlockSpec((blk, GROUP * HD), lambda g, c: (0, low + g)),
            ]
            + [head] * (2 * n_arr),
            out_specs=[group_out, group_out, pl.BlockSpec((2, blk, GROUP * HD), lambda g, c: (0, 0, g))]
            + [head_out] * n_arr,
            scratch_shapes=[
                pltpu.VMEM((WINDOW + rows, HD), F32),
                pltpu.VMEM((2, blk, GROUP * HD), BF16),
                pltpu.VMEM((2, blk, GROUP * HD), BF16),
                pltpu.VMEM((2, blk, GROUP * HD), BF16),
            ],
        ),
        out_shape=[jax.ShapeDtypeStruct((blk, GROUP * HD * count), BF16)] * 2
        + [jax.ShapeDtypeStruct((2, blk, GROUP * HD * count), BF16)]
        + [jax.ShapeDtypeStruct((rows, HD * count), BF16)] * n_arr,
        compiler_params=pltpu.CompilerParams(vmem_limit_bytes=VMEM_BYTES),
        cost_estimate=small_cost(),
        name="grads",
    )(core, e, inv, do_t, q, q_other, *keys, *values)


def small_cost():
    return pl.CostEstimate(flops=1 << 20, bytes_accessed=1 << 12, transcendentals=0)


def whole():
    return pl.BlockSpec(memory_space=pltpu.VMEM)


def pieces_kernel(dims, at_ref, x_ref, *refs):
    n_z, n_fsdp, out_rows = dims
    outs = refs[: 2 * n_fsdp]
    turned = refs[2 * n_fsdp]
    my_y, my_fsdp = at_ref[0], at_ref[1]
    for c in range(x_ref.shape[1] // HD):
        turned[c * HD : (c + 1) * HD, :] = x_ref[:, c * HD : (c + 1) * HD].astype(F32).T
    for p, out in enumerate(outs):
        flip, s = p // n_fsdp, p % n_fsdp
        y = lax.rem(my_y + flip, 2)
        f = lax.rem(my_fsdp + s, n_fsdp)
        for z in range(n_z):
            parts = []
            for core in range(2):
                block = ((z * 2 + y) * 2 + core) * n_fsdp + f
                parts.append(turned[pl.ds(pl.multiple_of(block * out_rows, 8), out_rows), :])
            out[z * 2 * out_rows : (z + 1) * 2 * out_rows, :] = jnp.concatenate(parts, 0).astype(BF16)


def run_pieces(at, tokens, n_z, n_fsdp, out_rows):
    rows, model = tokens.shape
    shape = jax.ShapeDtypeStruct((n_z * 2 * out_rows, rows), BF16)
    return pl.pallas_call(
        functools.partial(pieces_kernel, (n_z, n_fsdp, out_rows)),
        in_specs=[pl.BlockSpec(memory_space=pltpu.SMEM), whole()],
        out_specs=[whole()] * (2 * n_fsdp),
        out_shape=[shape] * (2 * n_fsdp),
        scratch_shapes=[pltpu.VMEM((model, rows), F32)],
        compiler_params=pltpu.CompilerParams(vmem_limit_bytes=VMEM_BYTES),
        cost_estimate=small_cost(),
        name="pieces",
    )(at, tokens)


def product_kernel(at_ref, *refs):
    *x_refs, w_ref, o_ref = refs
    total, first = None, 0
    for x in x_refs:
        term = dot(x[...], w_ref[first : first + x.shape[1], :])
        total = term if total is None else total + term
        first += x.shape[1]
    o_ref[...] = total.astype(o_ref.dtype)


def run_product(at, parts, w, kind):
    rows = parts[0].shape[0]
    depth, width = w.shape
    tile = 512
    if len(parts) == 1:
        x_specs = [pl.BlockSpec((rows, depth), lambda j, at: (0, at[0]))]
    else:
        x_specs = [pl.BlockSpec(x.shape, lambda j, at: (0, 0)) for x in parts]
    return pl.pallas_call(
        product_kernel,
        grid_spec=pltpu.PrefetchScalarGridSpec(
            num_scalar_prefetch=1,
            grid=(width // tile,),
            in_specs=x_specs + [pl.BlockSpec((depth, tile), lambda j, at: (0, j))],
            out_specs=pl.BlockSpec((rows, tile), lambda j, at: (0, j)),
        ),
        out_shape=jax.ShapeDtypeStruct((rows, width), kind),
        compiler_params=pltpu.CompilerParams(vmem_limit_bytes=VMEM_BYTES),
        cost_estimate=small_cost(),
        name="product",
    )(at, *parts, w)


def weight_kernel(n_z, n, at_ref, *refs):
    own_pairs, other_pairs = refs[:n], refs[n : 2 * n]
    dv_refs = refs[2 * n : 4 * n]
    outs = refs[4 * n :]
    core = at_ref[0]
    step = pl.program_id(0)
    rows = own_pairs[0].shape[1] // 2
    own = pl.ds(pl.multiple_of(core * rows, rows), rows)
    other = pl.ds(pl.multiple_of((1 - core) * rows, rows), rows)
    total = None
    for p in range(n):
        for flip in range(2):
            window = slice(flip * rows, (flip + 1) * rows)
            term = dot(own_pairs[p][:, window], dv_refs[2 * p + flip][own, :])
            term = term + dot(other_pairs[p][:, window], dv_refs[2 * p + flip][other, :])
            total = term if total is None else total + term
    for d, out in enumerate(outs):

        @pl.when(step == (n_z - 1 if d == 0 else d - 1))
        def _():
            out[...] = total.astype(out.dtype)


def run_weight(at, own_pairs, other_pairs, dv_pairs, n_z):
    n = len(own_pairs)
    count = own_pairs[0].shape[0] // n_z
    rows2 = own_pairs[0].shape[1]
    dvs = [x for pair_of in dv_pairs for x in pair_of]
    width = dvs[0].shape[1]
    shapes = [jax.ShapeDtypeStruct((count, width), F32 if d == 0 else BF16) for d in range(n_z)]
    pair_block = pl.BlockSpec((count, rows2), lambda d, at: (lax.rem(at[1] + d + 1, n_z), 0))
    return pl.pallas_call(
        functools.partial(weight_kernel, n_z, n),
        grid_spec=pltpu.PrefetchScalarGridSpec(
            num_scalar_prefetch=1,
            grid=(n_z,),
            in_specs=[pair_block] * (2 * n) + [pl.BlockSpec(dvs[0].shape, lambda d, at: (0, 0))] * (2 * n),
            out_specs=[pl.BlockSpec((count, width), lambda d, at: (0, 0))] * n_z,
        ),
        out_shape=shapes,
        compiler_params=pltpu.CompilerParams(vmem_limit_bytes=VMEM_BYTES),
        cost_estimate=small_cost(),
        name="weight",
    )(at, *own_pairs, *other_pairs, *dvs)


def tokens_kernel(n_fsdp, at_ref, dv_ref, w_ref, own_ref, *others):
    made = dot(dv_ref[...], w_ref[...], NT).astype(BF16)
    rows = own_ref.shape[0]
    own_ref[...] = made[:rows]
    for s, ref in enumerate(others):
        ref[...] = made[(s + 1) * rows : (s + 2) * rows]


def run_tokens(at, dv_rows, w, n_fsdp):
    slab, width = w.shape
    rows = dv_rows.shape[0] // n_fsdp
    tile = slab // 3 if slab % (3 * HD) == 0 else slab
    n_tiles = slab // tile
    return pl.pallas_call(
        functools.partial(tokens_kernel, n_fsdp),
        grid_spec=pltpu.PrefetchScalarGridSpec(
            num_scalar_prefetch=1,
            grid=(n_tiles,),
            in_specs=[
                pl.BlockSpec(dv_rows.shape, lambda j, at: (0, 0)),
                pl.BlockSpec((tile, width), lambda j, at: (j, 0)),
            ],
            out_specs=[pl.BlockSpec((rows, tile), lambda j, at: (0, at[0] * n_tiles + j))]
            + [pl.BlockSpec((rows, tile), lambda j, at: (0, j))] * (n_fsdp - 1),
        ),
        out_shape=[jax.ShapeDtypeStruct((rows, slab * n_fsdp), BF16)]
        + [jax.ShapeDtypeStruct((rows, slab), BF16)] * (n_fsdp - 1),
        compiler_params=pltpu.CompilerParams(vmem_limit_bytes=VMEM_BYTES),
        cost_estimate=small_cost(),
        name="tokens",
    )(at, dv_rows, w)


def shifted(x, by):
    length = lax.axis_size("ctx")
    return lax.ppermute(x, "ctx", [(i, i + by) for i in range(length) if 0 <= i + by < length])


def swapped(x):
    return lax.ppermute(x, "ctx", [(i, i ^ 1) for i in range(lax.axis_size("ctx"))])


def rotated(x, by):
    length = lax.axis_size("fsdp")
    return lax.ppermute(x, "fsdp", [(i, (i + by) % length) for i in range(length)])


def moved(x, flip, by):
    n_ctx, n_fsdp = lax.axis_size("ctx"), lax.axis_size("fsdp")
    pairs = [
        (c * n_fsdp + f, (c ^ (2 * flip)) * n_fsdp + (f + by) % n_fsdp)
        for c in range(n_ctx)
        for f in range(n_fsdp)
    ]
    return lax.ppermute(x, ("ctx", "fsdp"), pairs)


def relayed(my_y, far, got):
    return (far.astype(F32) + jnp.where(my_y == 1, got.astype(F32), 0.0)).astype(BF16)


def gathered_terms(my_y, mine, got, back):
    return (mine.astype(F32) + back.astype(F32) + jnp.where(my_y == 0, got.astype(F32), 0.0)).astype(BF16)


def cols(x, at, width):
    return lax.dynamic_slice_in_dim(x, at * width, width, x.ndim - 1)


def rows_of(x, at, count):
    return lax.dynamic_slice_in_dim(x, at * count, count, 0)


def placed(core, own, other, axis):
    both = jnp.concatenate([own, own], axis)
    return lax.dynamic_update_slice_in_dim(both, other, (1 - core) * own.shape[axis], axis)


def flipped(x):
    return lax.ppermute(x, "ctx", [(i, i ^ 2) for i in range(lax.axis_size("ctx"))])


def after(x, *earlier):
    return lax.optimization_barrier((x, *earlier))[0]


def shards(hidden, queries, key_heads, w_value, d_out, segments):
    shard_rows = hidden.shape[1]
    model = hidden.shape[2]
    kv_width = w_value.shape[1]
    n_ctx = lax.axis_size("ctx")
    n_fsdp = lax.axis_size("fsdp")
    chip_rows = 2 * shard_rows
    n_z = n_ctx // 4
    assert WINDOW == 2 * chip_rows
    my_ctx = lax.axis_index("ctx")
    my_fsdp = lax.axis_index("fsdp")
    core = my_ctx % 2
    core_arg = core.astype(jnp.int32).reshape(1)
    chip = my_ctx // 2
    my_y = chip % 2
    my_z = chip // 2
    half_kv = kv_width // 2
    slab = model // n_fsdp
    tokens = hidden[0]
    first = chip * chip_rows

    aligned = slab % HD == 0
    fsdp_arg = my_fsdp.astype(jnp.int32).reshape(1)
    zero_arg = jnp.zeros((1,), jnp.int32)
    half_q = queries.shape[2] // 2
    out_rows = model // (n_ctx * n_fsdp)
    places = [(flip, s) for flip in range(2) for s in range(n_fsdp)]

    cut = slab // HD // 2 * HD if aligned else slab
    parts_at = [(0, cut), (cut, slab)] if aligned else [(0, slab)]
    slabs = [
        [
            lax.dynamic_slice_in_dim(tokens, (my_fsdp + s) % n_fsdp * slab + low, high - low, 1)
            for low, high in parts_at
        ]
        for s in range(1, n_fsdp)
    ]
    sent = [[rotated(x, s + 1) for x in parts] for s, parts in enumerate(slabs)]

    own_tags = segments[0].astype(BF16)
    tag_row = lax.dynamic_update_slice_in_dim(jnp.zeros((half_kv,), BF16), own_tags, core * shard_rows, 0)
    tag_rows = jnp.concatenate([tag_row[None], jnp.zeros((15, half_kv), BF16)], 0)
    k_sent = jnp.concatenate([cols(key_heads[0], 1 - core, half_kv), tag_rows], 0)
    got = swapped(after(k_sent, *[parts[0] for parts in slabs]))

    if out_rows % 8 == 0:
        at = jnp.stack([my_y, my_fsdp]).astype(jnp.int32)
        pieces = run_pieces(after(at, k_sent, got), tokens, n_z, n_fsdp, out_rows)
    else:
        turned = tokens.T.reshape(n_z, 2, 2, n_fsdp, out_rows, shard_rows)
        pieces = []
        for flip, s in places:
            piece = lax.dynamic_index_in_dim(turned, my_y ^ flip, 1, keepdims=False)
            piece = lax.dynamic_index_in_dim(piece, (my_fsdp + s) % n_fsdp, 2, keepdims=False)
            pieces.append(piece.reshape(n_z * 2 * out_rows, shard_rows))
    by_place = dict(zip(places, pieces))

    k_own = jnp.concatenate(
        [
            placed(core, cols(key_heads[0], core, half_kv), got[:shard_rows], 0),
            tag_rows + got[shard_rows:],
        ],
        0,
    )
    k_far = shifted(k_own, 4)
    k_near = shifted(k_own, 2)
    over_y = {s: flipped(after(by_place[1, s], k_own)) for s in range(1, n_fsdp)}
    q_sent = jnp.concatenate([cols(queries[0], 1 - core, half_q), cols(d_out[0], 1 - core, half_q)], 1)
    q_other = swapped(after(q_sent, k_own))
    if aligned:
        value_own = run_product(after(fsdp_arg, q_sent, *pieces), [tokens], w_value, F32)
    else:
        value_own = dot(cols(tokens, my_fsdp, slab), w_value)
    keys = [k_far, k_near, k_own]

    span_tags = jnp.concatenate([k[chip_rows, :chip_rows] for k in keys], 0)
    key_at = jnp.arange(WINDOW + chip_rows, dtype=jnp.int32)
    chip_tags = k_own[chip_rows, :chip_rows]
    before = (span_tags[None, :] < chip_tags[:, None]) | (key_at + first < WINDOW)[None, :]
    low = jnp.sum(before.astype(jnp.int32), axis=1)
    low = jnp.maximum(low, jnp.arange(1, chip_rows + 1, dtype=jnp.int32))[None, :]

    if aligned:
        partial = [run_product(zero_arg, parts, w_value, BF16) for parts in sent]
    else:
        partial = [dot(parts[0], w_value).astype(BF16) for parts in sent]
    low = after(low, *partial)
    e, inv, do_t, dv_far, dv_near, dv_mine = run_probs(
        core_arg, low, queries[0], q_other, d_out[0], keys, chip_rows, half_kv
    )
    dv_got = flipped(dv_near)

    value_back = [rotated(x, -s - 1) for s, x in enumerate(partial)]
    over_fsdp = {s: rotated(after(by_place[0, s], sent), s) for s in range(1, n_fsdp)}
    value_back = [after(x, dv_near, over_y) for x in value_back]
    value_sum = value_own
    for x in value_back:
        value_sum = value_sum + x.astype(F32)
    own_values = value_sum.astype(BF16)
    v_own = placed(core, cols(own_values, core, half_kv), swapped(cols(own_values, 1 - core, half_kv)), 0)

    late_y = flipped(after(by_place[1, 0], k_near))
    v_own, late_y, over_fsdp = lax.optimization_barrier((v_own, late_y, over_fsdp))
    v_far = shifted(v_own, 4)
    own_pairs = [jnp.concatenate([by_place[0, 0], late_y], 1)]
    other_pairs = [swapped(after(own_pairs[0], v_own))]
    relayed_y = {s: rotated(after(over_y[s], own_values), s) for s in range(1, n_fsdp)}

    dv_got = after(dv_got, v_own)
    dv_sent = relayed(my_y, dv_far, dv_got)
    dv_back = shifted(dv_sent, -4)
    v_sent = after(jnp.where(my_y == 0, v_own, v_far), dv_sent)
    v_near = flipped(v_sent)
    vals = [v_far, v_near, v_own]
    dv_chip = gathered_terms(my_y, dv_mine, dv_got, after(dv_back, v_sent))
    dv_fsdp = [dv_chip] + [rotated(dv_chip, s) for s in range(1, n_fsdp)]
    dv_over_y = [moved(dv_chip, 1, s) for s in range(n_fsdp)]
    for s in range(1, n_fsdp):
        own_pairs.append(jnp.concatenate([over_fsdp[s], relayed_y[s]], 1))
        other_pairs.append(swapped(own_pairs[s]))
    vals = [v_far, v_near, v_own]
    vals = [v_far, v_near, v_own]
    n_heads = half_kv // HD
    grad_args = (e, inv, do_t, queries[0], q_other, keys, vals, chip_rows, half_kv)
    early = run_grads(core_arg, *grad_args, 0, n_heads // 2)
    early_back = [shifted(early[4], -2), shifted(early[3], -4)]

    dv_fsdp[1:] = [after(x, early[4]) for x in dv_fsdp[1:]]
    dv_over_y = [after(x, early[4]) for x in dv_over_y]
    dv_pairs = list(zip(dv_fsdp, dv_over_y))
    if out_rows % 8 == 0:
        at = after(jnp.stack([core, my_z]).astype(jnp.int32), early[4])
        by_z = run_weight(at, own_pairs, other_pairs, dv_pairs, n_z)
    else:
        weight_term = 0.0
        for p in range(n_fsdp):
            for flip in range(2):
                window = slice(flip * shard_rows, (flip + 1) * shard_rows)
                weight_term += dot(own_pairs[p][:, window], rows_of(dv_pairs[p][flip], core, shard_rows))
                weight_term += dot(other_pairs[p][:, window], rows_of(dv_pairs[p][flip], 1 - core, shard_rows))
        weight_term = weight_term.reshape(n_z, 2 * out_rows, half_kv)
        by_z = [
            lax.dynamic_index_in_dim(weight_term, (my_z + d) % n_z, 0, keepdims=False).astype(BF16 if d else F32)
            for d in range(n_z)
        ]
    by_z, early_back = lax.optimization_barrier((list(by_z), early_back))
    over_z = [
        lax.ppermute(by_z[d], "ctx", [(i, (i + 4 * d) % n_ctx) for i in range(n_ctx)]) for d in range(1, n_z)
    ]

    dv_sides = [
        jnp.concatenate([rows_of(x, at, shard_rows) for x in dv_fsdp], 0) for at in (core, 1 - core)
    ]
    dv_rows = placed(core, dv_sides[0], swapped(dv_sides[1]), 1)
    dv_rows = after(dv_rows, by_z[0])
    if aligned:
        d_tokens, *made = run_tokens(fsdp_arg, dv_rows, w_value, n_fsdp)
    else:
        made = dot(dv_rows, w_value, NT).astype(BF16)
        made = [made[s * shard_rows : (s + 1) * shard_rows] for s in range(n_fsdp)]
        d_tokens = jnp.concatenate([made[0]] * n_fsdp, 1)
        made = made[1:]
    arrivals = []
    for s in range(1, n_fsdp):
        back = rotated(made[s - 1], -s)
        arrivals.append(back)
        d_tokens = lax.dynamic_update_slice_in_dim(d_tokens, back, ((my_fsdp + s) % n_fsdp) * slab, 1)

    late = run_grads(after(core_arg, *made), *grad_args, n_heads // 2, n_heads)
    late_back = [shifted(late[4], -2), shifted(late[3], -4)]
    late_back = [after(x, *arrivals) for x in late_back]
    over_z = [after(x, *late_back) for x in over_z]
    row_sum = by_z[0]
    for x in over_z:
        row_sum = row_sum + x.astype(F32)
    d_weight = placed(core, rows_of(row_sum, core, out_rows), swapped(rows_of(row_sum, 1 - core, out_rows)), 1)
    dk_chip = jnp.concatenate(
        [
            (made_by[5].astype(F32) + back[0].astype(F32) + back[1].astype(F32)).astype(BF16)
            for made_by, back in ((early, early_back), (late, late_back))
        ],
        1,
    )
    d_keys = placed(core, rows_of(dk_chip, core, shard_rows), swapped(rows_of(dk_chip, 1 - core, shard_rows)), 1)
    out, dq, other = [jnp.concatenate((early[i], late[i]), early[i].ndim - 1) for i in range(3)]
    other = swapped(other)
    out = placed(core, out, other[0], 1)
    dq = placed(core, dq, other[1], 1)
    return (out[None], dq[None], d_keys[None], d_tokens[None], d_weight)


def solution(mesh):
    in_specs = (
        P("fsdp", "ctx", None),
        P("fsdp", "ctx", None),
        P("fsdp", "ctx", None),
        P("fsdp", None),
        P("fsdp", "ctx", None),
        P("fsdp", "ctx"),
    )
    out_specs = (
        P("fsdp", "ctx", None),
        P("fsdp", "ctx", None),
        P("fsdp", "ctx", None),
        P("fsdp", "ctx", None),
        P(("ctx", "fsdp"), None),
    )
    return jax.shard_map(shards, mesh=mesh, in_specs=in_specs, out_specs=out_specs, check_vma=False)
```

```python
import functools
import math

import jax
import jax.numpy as jnp
from jax import lax
from jax.experimental import pallas as pl
from jax.experimental.pallas import tpu as pltpu
from jax.sharding import PartitionSpec as P

HQ = 16
HK = 8
HD = 128
WINDOW = 1024
GROUP = 2
NEG = -1e30
VMEM_BYTES = 58 * 1024 * 1024

score_scale = 1.0 / math.sqrt(168.0)
exp2_scale = score_scale / math.log(2.0)

BF16 = jnp.bfloat16
F32 = jnp.float32
NT = (((1,), (1,)), ((), ()))
TN = (((0,), (0,)), ((), ()))


def dot(a, b, dims=(((1,), (0,)), ((), ()))):
    return lax.dot_general(a, b, dims, preferred_element_type=F32)


def probs_kernel(blk, n_back, core_ref, low_ref, q_own, q_other, do_own, do_other, *refs):
    n_arr = n_back + 1
    k_refs = refs[:n_arr]
    e_ref, inv_ref, dot_ref = refs[n_arr : n_arr + 3]
    dv_refs = refs[n_arr + 3 : 2 * n_arr + 3]
    bias, s_scr, dv_acc, q_buf, do_buf = refs[2 * n_arr + 3 :]
    span_blocks = WINDOW // blk + 1
    core = core_ref[0]

    @pl.when(pl.program_id(0) == 0)
    def _():
        for qb in range(2):
            kpos = lax.broadcasted_iota(jnp.int32, (span_blocks * blk, blk), 0) + qb * blk
            qpos = lax.broadcasted_iota(jnp.int32, (span_blocks * blk, blk), 1) + (qb * blk + WINDOW)
            low = low_ref[:, qb * blk : (qb + 1) * blk]
            ok = (kpos >= low) & (kpos <= qpos)
            bias[qb] = jnp.where(ok, 0.0, NEG)

    q_buf[core] = q_own[...]
    q_buf[1 - core] = q_other[...]
    do_buf[core] = do_own[...]
    do_buf[1 - core] = do_other[...]

    def key_block(j):
        return k_refs[j // 2][(j % 2) * blk : (j % 2 + 1) * blk, :]

    def stacked(buf, qb):
        return jnp.concatenate([buf[qb, :, r * HD : (r + 1) * HD] for r in range(GROUP)], 0)

    for qb in range(2):
        qs = stacked(q_buf, qb)
        top = None
        for j in range(span_blocks):
            s = dot(key_block(qb + j), qs, NT)
            b = bias[qb, j * blk : (j + 1) * blk, :]
            s = s * exp2_scale + jnp.concatenate([b] * GROUP, 1)
            s_scr[j] = s
            part = jnp.max(s.reshape(blk // 8, 8, GROUP * blk), axis=0)
            top = part if top is None else jnp.maximum(top, part)
        top = jnp.max(top, axis=0, keepdims=True)
        total = None
        for j in range(span_blocks):
            e = jnp.exp2(s_scr[j] - top)
            part = jnp.sum(e.reshape(blk // 8, 8, GROUP * blk), axis=0)
            total = part if total is None else total + part
            e_ref[0, qb, j * blk : (j + 1) * blk, :] = e.astype(BF16)
        inv = 1.0 / jnp.sum(total, axis=0, keepdims=True)
        inv_ref[0, qb] = inv
        do_t = (stacked(do_buf, qb).astype(F32).T * inv).astype(BF16)
        dot_ref[0, qb] = do_t
        for j in range(span_blocks):
            term = dot(e_ref[0, qb, j * blk : (j + 1) * blk, :], do_t, NT)
            at = slice((qb + j) * blk, (qb + j + 1) * blk)
            if qb == 0 or j == span_blocks - 1:
                dv_acc[at, :] = term
            else:
                dv_acc[at, :] += term
    for a in range(n_arr):
        dv_refs[a][...] = dv_acc[a * 2 * blk : (a + 1) * 2 * blk, :].astype(BF16)


def grads_kernel(blk, n_back, core_ref, e_ref, inv_ref, dot_ref, q_own, q_other, *refs):
    n_arr = n_back + 1
    k_refs = refs[:n_arr]
    v_refs = refs[n_arr : 2 * n_arr]
    out_ref, dq_ref, other_ref = refs[2 * n_arr : 2 * n_arr + 3]
    dk_refs = refs[2 * n_arr + 3 : 3 * n_arr + 3]
    dk_acc, q_buf, out_buf, dq_buf = refs[3 * n_arr + 3 :]
    span_blocks = WINDOW // blk + 1
    core = core_ref[0]

    q_buf[core] = q_own[...]
    q_buf[1 - core] = q_other[...]

    def block_of(arrays, j):
        return arrays[j // 2][(j % 2) * blk : (j % 2 + 1) * blk, :]

    for qb in range(2):
        qs = jnp.concatenate([q_buf[qb, :, r * HD : (r + 1) * HD] for r in range(GROUP)], 0)
        do_t = dot_ref[0, qb]
        out_t = None
        for j in range(span_blocks):
            e = e_ref[0, qb, j * blk : (j + 1) * blk, :]
            part = dot(block_of(v_refs, qb + j), e, TN)
            out_t = part if out_t is None else out_t + part
        out_t = (out_t * inv_ref[0, qb]).astype(BF16).astype(F32)
        delta = jnp.sum(out_t * do_t.astype(F32), axis=0, keepdims=True)
        out = out_t.T.astype(BF16)
        dq_t = None
        for j in range(span_blocks):
            e = e_ref[0, qb, j * blk : (j + 1) * blk, :].astype(F32)
            dp = dot(block_of(v_refs, qb + j), do_t)
            ds = (e * (dp - delta)).astype(BF16)
            term = dot(ds, qs)
            at = slice((qb + j) * blk, (qb + j + 1) * blk)
            if qb == 0 or j == span_blocks - 1:
                dk_acc[at, :] = term
            else:
                dk_acc[at, :] += term
            part = dot(block_of(k_refs, qb + j), ds, TN)
            dq_t = part if dq_t is None else dq_t + part
        dq = (dq_t * score_scale).T.astype(BF16)
        for r in range(GROUP):
            out_buf[qb, :, r * HD : (r + 1) * HD] = out[r * blk : (r + 1) * blk, :]
            dq_buf[qb, :, r * HD : (r + 1) * HD] = dq[r * blk : (r + 1) * blk, :]
    out_ref[...] = out_buf[core]
    dq_ref[...] = dq_buf[core]
    other_ref[0] = out_buf[1 - core]
    other_ref[1] = dq_buf[1 - core]
    for a in range(n_arr):
        dk_refs[a][...] = (dk_acc[a * 2 * blk : (a + 1) * 2 * blk, :] * score_scale).astype(BF16)


def specs_of(rows, width):
    blk = rows // 2
    heads = width // HD
    span = WINDOW + blk
    lanes = GROUP * blk
    head = pl.BlockSpec((rows, HD), lambda g, c: (0, g))
    own = pl.BlockSpec((blk, GROUP * HD), lambda g, c: (0, c[0] * heads + g))
    return blk, heads, span, lanes, head, own


def run_probs(core, low, q, q_other, do, keys, rows, width):
    blk, heads, span, lanes, head, own = specs_of(rows, width)
    n_arr = len(keys)
    return pl.pallas_call(
        functools.partial(probs_kernel, blk, n_arr - 1),
        grid_spec=pltpu.PrefetchScalarGridSpec(
            num_scalar_prefetch=1,
            grid=(heads,),
            in_specs=[
                pl.BlockSpec((1, rows), lambda g, c: (0, 0)),
                own,
                pl.BlockSpec((blk, GROUP * HD), lambda g, c: (0, g)),
                own,
                pl.BlockSpec((blk, GROUP * HD), lambda g, c: (0, heads + g)),
            ]
            + [head] * n_arr,
            out_specs=[
                pl.BlockSpec((1, 2, span, lanes), lambda g, c: (g, 0, 0, 0)),
                pl.BlockSpec((1, 2, 1, lanes), lambda g, c: (g, 0, 0, 0)),
                pl.BlockSpec((1, 2, HD, lanes), lambda g, c: (g, 0, 0, 0)),
            ]
            + [head] * n_arr,
            scratch_shapes=[
                pltpu.VMEM((2, span, blk), F32),
                pltpu.VMEM((span // blk, blk, lanes), F32),
                pltpu.VMEM((WINDOW + rows, HD), F32),
                pltpu.VMEM((2, blk, GROUP * HD), BF16),
                pltpu.VMEM((2, blk, GROUP * HD), BF16),
            ],
        ),
        out_shape=[
            jax.ShapeDtypeStruct((heads, 2, span, lanes), BF16),
            jax.ShapeDtypeStruct((heads, 2, 1, lanes), F32),
            jax.ShapeDtypeStruct((heads, 2, HD, lanes), BF16),
        ]
        + [jax.ShapeDtypeStruct((rows, width), BF16)] * n_arr,
        compiler_params=pltpu.CompilerParams(vmem_limit_bytes=VMEM_BYTES),
        cost_estimate=small_cost(),
        name="probs",
    )(core, low, q, q_other, do, q_other, *keys)


def run_grads(core, e, inv, do_t, q, q_other, keys, values, rows, width):
    blk, heads, span, lanes, head, own = specs_of(rows, width)
    n_arr = len(keys)
    full = jax.ShapeDtypeStruct(q.shape, BF16)
    return pl.pallas_call(
        functools.partial(grads_kernel, blk, n_arr - 1),
        grid_spec=pltpu.PrefetchScalarGridSpec(
            num_scalar_prefetch=1,
            grid=(heads,),
            in_specs=[
                pl.BlockSpec((1, 2, span, lanes), lambda g, c: (g, 0, 0, 0)),
                pl.BlockSpec((1, 2, 1, lanes), lambda g, c: (g, 0, 0, 0)),
                pl.BlockSpec((1, 2, HD, lanes), lambda g, c: (g, 0, 0, 0)),
                own,
                pl.BlockSpec((blk, GROUP * HD), lambda g, c: (0, g)),
            ]
            + [head] * (2 * n_arr),
            out_specs=[own, own, pl.BlockSpec((2, blk, GROUP * HD), lambda g, c: (0, 0, g))] + [head] * n_arr,
            scratch_shapes=[
                pltpu.VMEM((WINDOW + rows, HD), F32),
                pltpu.VMEM((2, blk, GROUP * HD), BF16),
                pltpu.VMEM((2, blk, GROUP * HD), BF16),
                pltpu.VMEM((2, blk, GROUP * HD), BF16),
            ],
        ),
        out_shape=[full, full, jax.ShapeDtypeStruct((2, blk, GROUP * width), BF16)]
        + [jax.ShapeDtypeStruct((rows, width), BF16)] * n_arr,
        compiler_params=pltpu.CompilerParams(vmem_limit_bytes=VMEM_BYTES),
        cost_estimate=small_cost(),
        name="grads",
    )(core, e, inv, do_t, q, q_other, *keys, *values)


def small_cost():
    return pl.CostEstimate(flops=1 << 20, bytes_accessed=1 << 12, transcendentals=0)


def whole():
    return pl.BlockSpec(memory_space=pltpu.VMEM)


def pieces_kernel(dims, at_ref, x_ref, *refs):
    n_z, n_fsdp, out_rows = dims
    outs = refs[: 2 * n_fsdp]
    turned = refs[2 * n_fsdp]
    my_y, my_fsdp = at_ref[0], at_ref[1]
    for c in range(x_ref.shape[1] // HD):
        turned[c * HD : (c + 1) * HD, :] = x_ref[:, c * HD : (c + 1) * HD].astype(F32).T
    for p, out in enumerate(outs):
        flip, s = p // n_fsdp, p % n_fsdp
        y = lax.rem(my_y + flip, 2)
        f = lax.rem(my_fsdp + s, n_fsdp)
        for z in range(n_z):
            parts = []
            for core in range(2):
                block = ((z * 2 + y) * 2 + core) * n_fsdp + f
                parts.append(turned[pl.ds(pl.multiple_of(block * out_rows, 8), out_rows), :])
            out[z * 2 * out_rows : (z + 1) * 2 * out_rows, :] = jnp.concatenate(parts, 0).astype(BF16)


def run_pieces(at, tokens, n_z, n_fsdp, out_rows):
    rows, model = tokens.shape
    shape = jax.ShapeDtypeStruct((n_z * 2 * out_rows, rows), BF16)
    return pl.pallas_call(
        functools.partial(pieces_kernel, (n_z, n_fsdp, out_rows)),
        in_specs=[pl.BlockSpec(memory_space=pltpu.SMEM), whole()],
        out_specs=[whole()] * (2 * n_fsdp),
        out_shape=[shape] * (2 * n_fsdp),
        scratch_shapes=[pltpu.VMEM((model, rows), F32)],
        compiler_params=pltpu.CompilerParams(vmem_limit_bytes=VMEM_BYTES),
        cost_estimate=small_cost(),
        name="pieces",
    )(at, tokens)


def product_kernel(at_ref, *refs):
    *x_refs, w_ref, o_ref = refs
    total, first = None, 0
    for x in x_refs:
        term = dot(x[...], w_ref[first : first + x.shape[1], :])
        total = term if total is None else total + term
        first += x.shape[1]
    o_ref[...] = total.astype(o_ref.dtype)


def run_product(at, parts, w, kind):
    rows = parts[0].shape[0]
    depth, width = w.shape
    tile = 512
    if len(parts) == 1:
        x_specs = [pl.BlockSpec((rows, depth), lambda j, at: (0, at[0]))]
    else:
        x_specs = [pl.BlockSpec(x.shape, lambda j, at: (0, 0)) for x in parts]
    return pl.pallas_call(
        product_kernel,
        grid_spec=pltpu.PrefetchScalarGridSpec(
            num_scalar_prefetch=1,
            grid=(width // tile,),
            in_specs=x_specs + [pl.BlockSpec((depth, tile), lambda j, at: (0, j))],
            out_specs=pl.BlockSpec((rows, tile), lambda j, at: (0, j)),
        ),
        out_shape=jax.ShapeDtypeStruct((rows, width), kind),
        compiler_params=pltpu.CompilerParams(vmem_limit_bytes=VMEM_BYTES),
        cost_estimate=small_cost(),
        name="product",
    )(at, *parts, w)


def weight_kernel(n_z, n, at_ref, *refs):
    own_pairs, other_pairs = refs[:n], refs[n : 2 * n]
    dv_refs = refs[2 * n : 4 * n]
    outs = refs[4 * n :]
    core = at_ref[0]
    step = pl.program_id(0)
    rows = own_pairs[0].shape[1] // 2
    own = pl.ds(pl.multiple_of(core * rows, rows), rows)
    other = pl.ds(pl.multiple_of((1 - core) * rows, rows), rows)
    total = None
    for p in range(n):
        for flip in range(2):
            window = slice(flip * rows, (flip + 1) * rows)
            term = dot(own_pairs[p][:, window], dv_refs[2 * p + flip][own, :])
            term = term + dot(other_pairs[p][:, window], dv_refs[2 * p + flip][other, :])
            total = term if total is None else total + term
    for d, out in enumerate(outs):

        @pl.when(step == (n_z - 1 if d == 0 else d - 1))
        def _():
            out[...] = total.astype(out.dtype)


def run_weight(at, own_pairs, other_pairs, dv_pairs, n_z):
    n = len(own_pairs)
    count = own_pairs[0].shape[0] // n_z
    rows2 = own_pairs[0].shape[1]
    dvs = [x for pair_of in dv_pairs for x in pair_of]
    width = dvs[0].shape[1]
    shapes = [jax.ShapeDtypeStruct((count, width), F32 if d == 0 else BF16) for d in range(n_z)]
    pair_block = pl.BlockSpec((count, rows2), lambda d, at: (lax.rem(at[1] + d + 1, n_z), 0))
    return pl.pallas_call(
        functools.partial(weight_kernel, n_z, n),
        grid_spec=pltpu.PrefetchScalarGridSpec(
            num_scalar_prefetch=1,
            grid=(n_z,),
            in_specs=[pair_block] * (2 * n) + [pl.BlockSpec(dvs[0].shape, lambda d, at: (0, 0))] * (2 * n),
            out_specs=[pl.BlockSpec((count, width), lambda d, at: (0, 0))] * n_z,
        ),
        out_shape=shapes,
        compiler_params=pltpu.CompilerParams(vmem_limit_bytes=VMEM_BYTES),
        cost_estimate=small_cost(),
        name="weight",
    )(at, *own_pairs, *other_pairs, *dvs)


def tokens_kernel(n_fsdp, at_ref, dv_ref, w_ref, own_ref, *others):
    made = dot(dv_ref[...], w_ref[...], NT).astype(BF16)
    rows = own_ref.shape[0]
    own_ref[...] = made[:rows]
    for s, ref in enumerate(others):
        ref[...] = made[(s + 1) * rows : (s + 2) * rows]


def run_tokens(at, dv_rows, w, n_fsdp):
    slab, width = w.shape
    rows = dv_rows.shape[0] // n_fsdp
    tile = slab // 3 if slab % (3 * HD) == 0 else slab
    n_tiles = slab // tile
    return pl.pallas_call(
        functools.partial(tokens_kernel, n_fsdp),
        grid_spec=pltpu.PrefetchScalarGridSpec(
            num_scalar_prefetch=1,
            grid=(n_tiles,),
            in_specs=[
                pl.BlockSpec(dv_rows.shape, lambda j, at: (0, 0)),
                pl.BlockSpec((tile, width), lambda j, at: (j, 0)),
            ],
            out_specs=[pl.BlockSpec((rows, tile), lambda j, at: (0, at[0] * n_tiles + j))]
            + [pl.BlockSpec((rows, tile), lambda j, at: (0, j))] * (n_fsdp - 1),
        ),
        out_shape=[jax.ShapeDtypeStruct((rows, slab * n_fsdp), BF16)]
        + [jax.ShapeDtypeStruct((rows, slab), BF16)] * (n_fsdp - 1),
        compiler_params=pltpu.CompilerParams(vmem_limit_bytes=VMEM_BYTES),
        cost_estimate=small_cost(),
        name="tokens",
    )(at, dv_rows, w)


def shifted(x, by):
    length = lax.axis_size("ctx")
    return lax.ppermute(x, "ctx", [(i, i + by) for i in range(length) if 0 <= i + by < length])


def swapped(x):
    return lax.ppermute(x, "ctx", [(i, i ^ 1) for i in range(lax.axis_size("ctx"))])


def rotated(x, by):
    length = lax.axis_size("fsdp")
    return lax.ppermute(x, "fsdp", [(i, (i + by) % length) for i in range(length)])


def moved(x, flip, by):
    n_ctx, n_fsdp = lax.axis_size("ctx"), lax.axis_size("fsdp")
    pairs = [
        (c * n_fsdp + f, (c ^ (2 * flip)) * n_fsdp + (f + by) % n_fsdp)
        for c in range(n_ctx)
        for f in range(n_fsdp)
    ]
    return lax.ppermute(x, ("ctx", "fsdp"), pairs)


def relayed(my_y, far, got):
    return (far.astype(F32) + jnp.where(my_y == 1, got.astype(F32), 0.0)).astype(BF16)


def gathered_terms(my_y, mine, got, back):
    return (mine.astype(F32) + back.astype(F32) + jnp.where(my_y == 0, got.astype(F32), 0.0)).astype(BF16)


def cols(x, at, width):
    return lax.dynamic_slice_in_dim(x, at * width, width, x.ndim - 1)


def rows_of(x, at, count):
    return lax.dynamic_slice_in_dim(x, at * count, count, 0)


def placed(core, own, other, axis):
    both = jnp.concatenate([own, own], axis)
    return lax.dynamic_update_slice_in_dim(both, other, (1 - core) * own.shape[axis], axis)


def flipped(x):
    return lax.ppermute(x, "ctx", [(i, i ^ 2) for i in range(lax.axis_size("ctx"))])


def after(x, *earlier):
    return lax.optimization_barrier((x, *earlier))[0]


def shards(hidden, queries, key_heads, w_value, d_out, segments):
    shard_rows = hidden.shape[1]
    model = hidden.shape[2]
    kv_width = w_value.shape[1]
    n_ctx = lax.axis_size("ctx")
    n_fsdp = lax.axis_size("fsdp")
    chip_rows = 2 * shard_rows
    n_z = n_ctx // 4
    assert WINDOW == 2 * chip_rows
    my_ctx = lax.axis_index("ctx")
    my_fsdp = lax.axis_index("fsdp")
    core = my_ctx % 2
    core_arg = core.astype(jnp.int32).reshape(1)
    chip = my_ctx // 2
    my_y = chip % 2
    my_z = chip // 2
    half_kv = kv_width // 2
    slab = model // n_fsdp
    tokens = hidden[0]
    first = chip * chip_rows

    aligned = slab % HD == 0
    fsdp_arg = my_fsdp.astype(jnp.int32).reshape(1)
    zero_arg = jnp.zeros((1,), jnp.int32)
    half_q = queries.shape[2] // 2
    out_rows = model // (n_ctx * n_fsdp)
    places = [(flip, s) for flip in range(2) for s in range(n_fsdp)]

    cut = slab // HD // 2 * HD if aligned else slab
    parts_at = [(0, cut), (cut, slab)] if aligned else [(0, slab)]
    slabs = [
        [
            lax.dynamic_slice_in_dim(tokens, (my_fsdp + s) % n_fsdp * slab + low, high - low, 1)
            for low, high in parts_at
        ]
        for s in range(1, n_fsdp)
    ]
    sent = [[rotated(x, s + 1) for x in parts] for s, parts in enumerate(slabs)]

    own_tags = segments[0].astype(BF16)
    tag_row = lax.dynamic_update_slice_in_dim(jnp.zeros((half_kv,), BF16), own_tags, core * shard_rows, 0)
    tag_rows = jnp.concatenate([tag_row[None], jnp.zeros((15, half_kv), BF16)], 0)
    k_sent = jnp.concatenate([cols(key_heads[0], 1 - core, half_kv), tag_rows], 0)
    got = swapped(after(k_sent, *[parts[0] for parts in slabs]))

    if out_rows % 8 == 0:
        at = jnp.stack([my_y, my_fsdp]).astype(jnp.int32)
        pieces = run_pieces(after(at, k_sent, got), tokens, n_z, n_fsdp, out_rows)
    else:
        turned = tokens.T.reshape(n_z, 2, 2, n_fsdp, out_rows, shard_rows)
        pieces = []
        for flip, s in places:
            piece = lax.dynamic_index_in_dim(turned, my_y ^ flip, 1, keepdims=False)
            piece = lax.dynamic_index_in_dim(piece, (my_fsdp + s) % n_fsdp, 2, keepdims=False)
            pieces.append(piece.reshape(n_z * 2 * out_rows, shard_rows))
    by_place = dict(zip(places, pieces))

    k_own = jnp.concatenate(
        [
            placed(core, cols(key_heads[0], core, half_kv), got[:shard_rows], 0),
            tag_rows + got[shard_rows:],
        ],
        0,
    )
    k_far = shifted(k_own, 4)
    k_near = shifted(k_own, 2)
    over_y = {s: flipped(after(by_place[1, s], k_own)) for s in range(1, n_fsdp)}
    q_sent = jnp.concatenate([cols(queries[0], 1 - core, half_q), cols(d_out[0], 1 - core, half_q)], 1)
    q_other = swapped(after(q_sent, k_own))
    if aligned:
        value_own = run_product(after(fsdp_arg, q_sent, *pieces), [tokens], w_value, F32)
    else:
        value_own = dot(cols(tokens, my_fsdp, slab), w_value)
    keys = [k_far, k_near, k_own]

    span_tags = jnp.concatenate([k[chip_rows, :chip_rows] for k in keys], 0)
    key_at = jnp.arange(WINDOW + chip_rows, dtype=jnp.int32)
    chip_tags = k_own[chip_rows, :chip_rows]
    before = (span_tags[None, :] < chip_tags[:, None]) | (key_at + first < WINDOW)[None, :]
    low = jnp.sum(before.astype(jnp.int32), axis=1)
    low = jnp.maximum(low, jnp.arange(1, chip_rows + 1, dtype=jnp.int32))[None, :]

    if aligned:
        partial = [run_product(zero_arg, parts, w_value, BF16) for parts in sent]
    else:
        partial = [dot(parts[0], w_value).astype(BF16) for parts in sent]
    low = after(low, *partial)
    e, inv, do_t, dv_far, dv_near, dv_mine = run_probs(
        core_arg, low, queries[0], q_other, d_out[0], keys, chip_rows, half_kv
    )
    dv_got = flipped(dv_near)

    value_back = [rotated(x, -s - 1) for s, x in enumerate(partial)]
    over_fsdp = {s: rotated(after(by_place[0, s], sent), s) for s in range(1, n_fsdp)}
    value_back = [after(x, dv_near, over_y) for x in value_back]
    value_sum = value_own
    for x in value_back:
        value_sum = value_sum + x.astype(F32)
    own_values = value_sum.astype(BF16)
    v_own = placed(core, cols(own_values, core, half_kv), swapped(cols(own_values, 1 - core, half_kv)), 0)

    over_y[0] = flipped(after(by_place[1, 0], k_near))
    v_own, over_y[0], over_fsdp = lax.optimization_barrier((v_own, over_y[0], over_fsdp))
    v_far = shifted(v_own, 4)
    own_pairs = [jnp.concatenate([by_place[0, 0], over_y[0]], 1)]
    other_pairs = [swapped(after(own_pairs[0], v_own))]
    relayed_y = {s: rotated(after(over_y[s], own_values), s) for s in range(1, n_fsdp)}

    dv_got = after(dv_got, v_own)
    dv_sent = relayed(my_y, dv_far, dv_got)
    dv_back = shifted(dv_sent, -4)
    v_sent = after(jnp.where(my_y == 0, v_own, v_far), dv_sent)
    v_near = flipped(v_sent)
    vals = [v_far, v_near, v_own]
    dv_chip = gathered_terms(my_y, dv_mine, dv_got, after(dv_back, v_sent))
    dv_fsdp = [dv_chip] + [rotated(dv_chip, s) for s in range(1, n_fsdp)]
    dv_over_y = [moved(dv_chip, 1, s) for s in range(n_fsdp)]
    for s in range(1, n_fsdp):
        own_pairs.append(jnp.concatenate([over_fsdp[s], after(relayed_y[s], dv_chip)], 1))
        other_pairs.append(swapped(own_pairs[s]))
    v_near = after(v_near, dv_chip)
    vals = [v_far, v_near, v_own]
    out, dq, other, dk_far, dk_near, dk_mine = run_grads(
        core_arg, e, inv, do_t, queries[0], q_other, keys, vals, chip_rows, half_kv
    )
    dk_back = [shifted(dk_near, -2), shifted(dk_far, -4)]

    dv_fsdp = [after(x, dk_near) for x in dv_fsdp]
    dv_over_y = [after(x, dk_near) for x in dv_over_y]
    dv_other = swapped(jnp.concatenate([rows_of(x, 1 - core, shard_rows) for x in dv_fsdp], 0))
    dv_rows = placed(
        core, jnp.concatenate([rows_of(x, core, shard_rows) for x in dv_fsdp], 0), dv_other, 1
    )
    dv_rows = after(dv_rows, *dv_over_y)
    if aligned:
        d_tokens, *made = run_tokens(fsdp_arg, dv_rows, w_value, n_fsdp)
    else:
        made = dot(dv_rows, w_value, NT).astype(BF16)
        made = [made[s * shard_rows : (s + 1) * shard_rows] for s in range(n_fsdp)]
        d_tokens = jnp.concatenate([made[0]] * n_fsdp, 1)
        made = made[1:]
    for s in range(1, n_fsdp):
        back = rotated(made[s - 1], -s)
        d_tokens = lax.dynamic_update_slice_in_dim(d_tokens, back, ((my_fsdp + s) % n_fsdp) * slab, 1)

    dv_pairs = list(zip(dv_fsdp, dv_over_y))
    if out_rows % 8 == 0:
        at = after(jnp.stack([core, my_z]).astype(jnp.int32), *made)
        by_z = run_weight(at, own_pairs, other_pairs, dv_pairs, n_z)
    else:
        weight_term = 0.0
        for p in range(n_fsdp):
            for flip in range(2):
                window = slice(flip * shard_rows, (flip + 1) * shard_rows)
                weight_term += dot(own_pairs[p][:, window], rows_of(dv_pairs[p][flip], core, shard_rows))
                weight_term += dot(other_pairs[p][:, window], rows_of(dv_pairs[p][flip], 1 - core, shard_rows))
        weight_term = weight_term.reshape(n_z, 2 * out_rows, half_kv)
        by_z = [
            lax.dynamic_index_in_dim(weight_term, (my_z + d) % n_z, 0, keepdims=False).astype(BF16 if d else F32)
            for d in range(n_z)
        ]
    by_z, dk_back = lax.optimization_barrier((list(by_z), dk_back))
    over_z = [
        lax.ppermute(by_z[d], "ctx", [(i, (i + 4 * d) % n_ctx) for i in range(n_ctx)]) for d in range(1, n_z)
    ]

    row_sum = by_z[0]
    for x in over_z:
        row_sum = row_sum + x.astype(F32)
    d_weight = placed(core, rows_of(row_sum, core, out_rows), swapped(rows_of(row_sum, 1 - core, out_rows)), 1)

    dk_chip = (dk_mine.astype(F32) + dk_back[0].astype(F32) + dk_back[1].astype(F32)).astype(BF16)
    d_keys = placed(core, rows_of(dk_chip, core, shard_rows), swapped(rows_of(dk_chip, 1 - core, shard_rows)), 1)
    other = swapped(after(other, *made))
    out = lax.dynamic_update_slice_in_dim(out, other[0], (1 - core) * half_q, 1)
    dq = lax.dynamic_update_slice_in_dim(dq, other[1], (1 - core) * half_q, 1)
    return (out[None], dq[None], d_keys[None], d_tokens[None], d_weight)


def solution(mesh):
    in_specs = (
        P("fsdp", "ctx", None),
        P("fsdp", "ctx", None),
        P("fsdp", "ctx", None),
        P("fsdp", None),
        P("fsdp", "ctx", None),
        P("fsdp", "ctx"),
    )
    out_specs = (
        P("fsdp", "ctx", None),
        P("fsdp", "ctx", None),
        P("fsdp", "ctx", None),
        P("fsdp", "ctx", None),
        P(("ctx", "fsdp"), None),
    )
    return jax.shard_map(shards, mesh=mesh, in_specs=in_specs, out_specs=out_specs, check_vma=False)
```

```python
import functools
import math

import jax
import jax.numpy as jnp
from jax import lax
from jax.experimental import pallas as pl
from jax.experimental.pallas import tpu as pltpu
from jax.sharding import PartitionSpec as P

HQ = 16
HK = 8
HD = 128
WINDOW = 1024
GROUP = 2
NEG = -1e30
VMEM_BYTES = 58 * 1024 * 1024

score_scale = 1.0 / math.sqrt(168.0)
exp2_scale = score_scale / math.log(2.0)

BF16 = jnp.bfloat16
F32 = jnp.float32
NT = (((1,), (1,)), ((), ()))
TN = (((0,), (0,)), ((), ()))


def dot(a, b, dims=(((1,), (0,)), ((), ()))):
    return lax.dot_general(a, b, dims, preferred_element_type=F32)


def probs_kernel(blk, n_back, core_ref, low_ref, q_own, q_other, do_own, do_other, *refs):
    n_arr = n_back + 1
    k_refs = refs[:n_arr]
    e_ref, inv_ref, dot_ref = refs[n_arr : n_arr + 3]
    dv_refs = refs[n_arr + 3 : 2 * n_arr + 3]
    bias, s_scr, dv_acc, q_buf, do_buf = refs[2 * n_arr + 3 :]
    span_blocks = WINDOW // blk + 1
    core = core_ref[0]

    @pl.when(pl.program_id(0) == 0)
    def _():
        for qb in range(2):
            kpos = lax.broadcasted_iota(jnp.int32, (span_blocks * blk, blk), 0) + qb * blk
            qpos = lax.broadcasted_iota(jnp.int32, (span_blocks * blk, blk), 1) + (qb * blk + WINDOW)
            low = low_ref[:, qb * blk : (qb + 1) * blk]
            ok = (kpos >= low) & (kpos <= qpos)
            bias[qb] = jnp.where(ok, 0.0, NEG)

    q_buf[core] = q_own[...]
    q_buf[1 - core] = q_other[...]
    do_buf[core] = do_own[...]
    do_buf[1 - core] = do_other[...]

    def key_block(j):
        return k_refs[j // 2][(j % 2) * blk : (j % 2 + 1) * blk, :]

    def stacked(buf, qb):
        return jnp.concatenate([buf[qb, :, r * HD : (r + 1) * HD] for r in range(GROUP)], 0)

    for qb in range(2):
        qs = stacked(q_buf, qb)
        top = None
        for j in range(span_blocks):
            s = dot(key_block(qb + j), qs, NT)
            b = bias[qb, j * blk : (j + 1) * blk, :]
            s = s * exp2_scale + jnp.concatenate([b] * GROUP, 1)
            s_scr[j] = s
            part = jnp.max(s.reshape(blk // 8, 8, GROUP * blk), axis=0)
            top = part if top is None else jnp.maximum(top, part)
        top = jnp.max(top, axis=0, keepdims=True)
        total = None
        for j in range(span_blocks):
            e = jnp.exp2(s_scr[j] - top)
            part = jnp.sum(e.reshape(blk // 8, 8, GROUP * blk), axis=0)
            total = part if total is None else total + part
            e_ref[0, qb, j * blk : (j + 1) * blk, :] = e.astype(BF16)
        inv = 1.0 / jnp.sum(total, axis=0, keepdims=True)
        inv_ref[0, qb] = inv
        do_t = (stacked(do_buf, qb).astype(F32).T * inv).astype(BF16)
        dot_ref[0, qb] = do_t
        for j in range(span_blocks):
            term = dot(e_ref[0, qb, j * blk : (j + 1) * blk, :], do_t, NT)
            at = slice((qb + j) * blk, (qb + j + 1) * blk)
            if qb == 0 or j == span_blocks - 1:
                dv_acc[at, :] = term
            else:
                dv_acc[at, :] += term
    for a in range(n_arr):
        dv_refs[a][...] = dv_acc[a * 2 * blk : (a + 1) * 2 * blk, :].astype(BF16)


def grads_kernel(blk, n_back, core_ref, e_ref, inv_ref, dot_ref, q_own, q_other, *refs):
    n_arr = n_back + 1
    k_refs = refs[:n_arr]
    v_refs = refs[n_arr : 2 * n_arr]
    out_ref, dq_ref, other_ref = refs[2 * n_arr : 2 * n_arr + 3]
    dk_refs = refs[2 * n_arr + 3 : 3 * n_arr + 3]
    dk_acc, q_buf, out_buf, dq_buf = refs[3 * n_arr + 3 :]
    span_blocks = WINDOW // blk + 1
    core = core_ref[0]

    q_buf[core] = q_own[...]
    q_buf[1 - core] = q_other[...]

    def block_of(arrays, j):
        return arrays[j // 2][(j % 2) * blk : (j % 2 + 1) * blk, :]

    for qb in range(2):
        qs = jnp.concatenate([q_buf[qb, :, r * HD : (r + 1) * HD] for r in range(GROUP)], 0)
        do_t = dot_ref[0, qb]
        out_t = None
        for j in range(span_blocks):
            e = e_ref[0, qb, j * blk : (j + 1) * blk, :]
            part = dot(block_of(v_refs, qb + j), e, TN)
            out_t = part if out_t is None else out_t + part
        out_t = (out_t * inv_ref[0, qb]).astype(BF16).astype(F32)
        delta = jnp.sum(out_t * do_t.astype(F32), axis=0, keepdims=True)
        out = out_t.T.astype(BF16)
        dq_t = None
        for j in range(span_blocks):
            e = e_ref[0, qb, j * blk : (j + 1) * blk, :].astype(F32)
            dp = dot(block_of(v_refs, qb + j), do_t)
            ds = (e * (dp - delta)).astype(BF16)
            term = dot(ds, qs)
            at = slice((qb + j) * blk, (qb + j + 1) * blk)
            if qb == 0 or j == span_blocks - 1:
                dk_acc[at, :] = term
            else:
                dk_acc[at, :] += term
            part = dot(block_of(k_refs, qb + j), ds, TN)
            dq_t = part if dq_t is None else dq_t + part
        dq = (dq_t * score_scale).T.astype(BF16)
        for r in range(GROUP):
            out_buf[qb, :, r * HD : (r + 1) * HD] = out[r * blk : (r + 1) * blk, :]
            dq_buf[qb, :, r * HD : (r + 1) * HD] = dq[r * blk : (r + 1) * blk, :]
    out_ref[...] = out_buf[core]
    dq_ref[...] = dq_buf[core]
    other_ref[0] = out_buf[1 - core]
    other_ref[1] = dq_buf[1 - core]
    for a in range(n_arr):
        dk_refs[a][...] = (dk_acc[a * 2 * blk : (a + 1) * 2 * blk, :] * score_scale).astype(BF16)


def specs_of(rows, width):
    blk = rows // 2
    heads = width // HD
    span = WINDOW + blk
    lanes = GROUP * blk
    head = pl.BlockSpec((rows, HD), lambda g, c: (0, g))
    own = pl.BlockSpec((blk, GROUP * HD), lambda g, c: (0, c[0] * heads + g))
    return blk, heads, span, lanes, head, own


def run_probs(core, low, q, q_other, do, keys, rows, width):
    blk, heads, span, lanes, head, own = specs_of(rows, width)
    n_arr = len(keys)
    return pl.pallas_call(
        functools.partial(probs_kernel, blk, n_arr - 1),
        grid_spec=pltpu.PrefetchScalarGridSpec(
            num_scalar_prefetch=1,
            grid=(heads,),
            in_specs=[
                pl.BlockSpec((1, rows), lambda g, c: (0, 0)),
                own,
                pl.BlockSpec((blk, GROUP * HD), lambda g, c: (0, g)),
                own,
                pl.BlockSpec((blk, GROUP * HD), lambda g, c: (0, heads + g)),
            ]
            + [head] * n_arr,
            out_specs=[
                pl.BlockSpec((1, 2, span, lanes), lambda g, c: (g, 0, 0, 0)),
                pl.BlockSpec((1, 2, 1, lanes), lambda g, c: (g, 0, 0, 0)),
                pl.BlockSpec((1, 2, HD, lanes), lambda g, c: (g, 0, 0, 0)),
            ]
            + [head] * n_arr,
            scratch_shapes=[
                pltpu.VMEM((2, span, blk), F32),
                pltpu.VMEM((span // blk, blk, lanes), F32),
                pltpu.VMEM((WINDOW + rows, HD), F32),
                pltpu.VMEM((2, blk, GROUP * HD), BF16),
                pltpu.VMEM((2, blk, GROUP * HD), BF16),
            ],
        ),
        out_shape=[
            jax.ShapeDtypeStruct((heads, 2, span, lanes), BF16),
            jax.ShapeDtypeStruct((heads, 2, 1, lanes), F32),
            jax.ShapeDtypeStruct((heads, 2, HD, lanes), BF16),
        ]
        + [jax.ShapeDtypeStruct((rows, width), BF16)] * n_arr,
        compiler_params=pltpu.CompilerParams(vmem_limit_bytes=VMEM_BYTES),
        cost_estimate=small_cost(),
        name="probs",
    )(core, low, q, q_other, do, q_other, *keys)


def run_grads(core, e, inv, do_t, q, q_other, keys, values, rows, width):
    blk, heads, span, lanes, head, own = specs_of(rows, width)
    n_arr = len(keys)
    full = jax.ShapeDtypeStruct(q.shape, BF16)
    return pl.pallas_call(
        functools.partial(grads_kernel, blk, n_arr - 1),
        grid_spec=pltpu.PrefetchScalarGridSpec(
            num_scalar_prefetch=1,
            grid=(heads,),
            in_specs=[
                pl.BlockSpec((1, 2, span, lanes), lambda g, c: (g, 0, 0, 0)),
                pl.BlockSpec((1, 2, 1, lanes), lambda g, c: (g, 0, 0, 0)),
                pl.BlockSpec((1, 2, HD, lanes), lambda g, c: (g, 0, 0, 0)),
                own,
                pl.BlockSpec((blk, GROUP * HD), lambda g, c: (0, g)),
            ]
            + [head] * (2 * n_arr),
            out_specs=[own, own, pl.BlockSpec((2, blk, GROUP * HD), lambda g, c: (0, 0, g))] + [head] * n_arr,
            scratch_shapes=[
                pltpu.VMEM((WINDOW + rows, HD), F32),
                pltpu.VMEM((2, blk, GROUP * HD), BF16),
                pltpu.VMEM((2, blk, GROUP * HD), BF16),
                pltpu.VMEM((2, blk, GROUP * HD), BF16),
            ],
        ),
        out_shape=[full, full, jax.ShapeDtypeStruct((2, blk, GROUP * width), BF16)]
        + [jax.ShapeDtypeStruct((rows, width), BF16)] * n_arr,
        compiler_params=pltpu.CompilerParams(vmem_limit_bytes=VMEM_BYTES),
        cost_estimate=small_cost(),
        name="grads",
    )(core, e, inv, do_t, q, q_other, *keys, *values)


def small_cost():
    return pl.CostEstimate(flops=1 << 20, bytes_accessed=1 << 12, transcendentals=0)


def whole():
    return pl.BlockSpec(memory_space=pltpu.VMEM)


def pieces_kernel(dims, at_ref, x_ref, *refs):
    n_z, n_fsdp, out_rows = dims
    outs = refs[: 2 * n_fsdp]
    turned = refs[2 * n_fsdp]
    my_y, my_fsdp = at_ref[0], at_ref[1]
    for c in range(x_ref.shape[1] // HD):
        turned[c * HD : (c + 1) * HD, :] = x_ref[:, c * HD : (c + 1) * HD].astype(F32).T
    for p, out in enumerate(outs):
        flip, s = p // n_fsdp, p % n_fsdp
        y = lax.rem(my_y + flip, 2)
        f = lax.rem(my_fsdp + s, n_fsdp)
        for z in range(n_z):
            parts = []
            for core in range(2):
                block = ((z * 2 + y) * 2 + core) * n_fsdp + f
                parts.append(turned[pl.ds(pl.multiple_of(block * out_rows, 8), out_rows), :])
            out[z * 2 * out_rows : (z + 1) * 2 * out_rows, :] = jnp.concatenate(parts, 0).astype(BF16)


def run_pieces(at, tokens, n_z, n_fsdp, out_rows):
    rows, model = tokens.shape
    shape = jax.ShapeDtypeStruct((n_z * 2 * out_rows, rows), BF16)
    return pl.pallas_call(
        functools.partial(pieces_kernel, (n_z, n_fsdp, out_rows)),
        in_specs=[pl.BlockSpec(memory_space=pltpu.SMEM), whole()],
        out_specs=[whole()] * (2 * n_fsdp),
        out_shape=[shape] * (2 * n_fsdp),
        scratch_shapes=[pltpu.VMEM((model, rows), F32)],
        compiler_params=pltpu.CompilerParams(vmem_limit_bytes=VMEM_BYTES),
        cost_estimate=small_cost(),
        name="pieces",
    )(at, tokens)


def product_kernel(at_ref, *refs):
    *x_refs, w_ref, o_ref = refs
    total, first = None, 0
    for x in x_refs:
        term = dot(x[...], w_ref[first : first + x.shape[1], :])
        total = term if total is None else total + term
        first += x.shape[1]
    o_ref[...] = total.astype(o_ref.dtype)


def run_product(at, parts, w, kind):
    rows = parts[0].shape[0]
    depth, width = w.shape
    tile = width
    if len(parts) == 1:
        x_specs = [pl.BlockSpec((rows, depth), lambda j, at: (0, at[0]))]
    else:
        x_specs = [pl.BlockSpec(x.shape, lambda j, at: (0, 0)) for x in parts]
    return pl.pallas_call(
        product_kernel,
        grid_spec=pltpu.PrefetchScalarGridSpec(
            num_scalar_prefetch=1,
            grid=(width // tile,),
            in_specs=x_specs + [pl.BlockSpec((depth, tile), lambda j, at: (0, j))],
            out_specs=pl.BlockSpec((rows, tile), lambda j, at: (0, j)),
        ),
        out_shape=jax.ShapeDtypeStruct((rows, width), kind),
        compiler_params=pltpu.CompilerParams(vmem_limit_bytes=VMEM_BYTES),
        cost_estimate=small_cost(),
        name="product",
    )(at, *parts, w)


def weight_kernel(n_z, n, at_ref, *refs):
    own_pairs, other_pairs = refs[:n], refs[n : 2 * n]
    dv_refs = refs[2 * n : 4 * n]
    outs = refs[4 * n :]
    core = at_ref[0]
    step = pl.program_id(0)
    rows = own_pairs[0].shape[1] // 2
    own = pl.ds(pl.multiple_of(core * rows, rows), rows)
    other = pl.ds(pl.multiple_of((1 - core) * rows, rows), rows)
    total = None
    for p in range(n):
        for flip in range(2):
            window = slice(flip * rows, (flip + 1) * rows)
            term = dot(own_pairs[p][:, window], dv_refs[2 * p + flip][own, :])
            term = term + dot(other_pairs[p][:, window], dv_refs[2 * p + flip][other, :])
            total = term if total is None else total + term
    for d, out in enumerate(outs):

        @pl.when(step == (n_z - 1 if d == 0 else d - 1))
        def _():
            out[...] = total.astype(out.dtype)


def run_weight(at, own_pairs, other_pairs, dv_pairs, n_z):
    n = len(own_pairs)
    count = own_pairs[0].shape[0] // n_z
    rows2 = own_pairs[0].shape[1]
    dvs = [x for pair_of in dv_pairs for x in pair_of]
    width = dvs[0].shape[1]
    shapes = [jax.ShapeDtypeStruct((count, width), F32 if d == 0 else BF16) for d in range(n_z)]
    pair_block = pl.BlockSpec((count, rows2), lambda d, at: (lax.rem(at[1] + d + 1, n_z), 0))
    return pl.pallas_call(
        functools.partial(weight_kernel, n_z, n),
        grid_spec=pltpu.PrefetchScalarGridSpec(
            num_scalar_prefetch=1,
            grid=(n_z,),
            in_specs=[pair_block] * (2 * n) + [pl.BlockSpec(dvs[0].shape, lambda d, at: (0, 0))] * (2 * n),
            out_specs=[pl.BlockSpec((count, width), lambda d, at: (0, 0))] * n_z,
        ),
        out_shape=shapes,
        compiler_params=pltpu.CompilerParams(vmem_limit_bytes=VMEM_BYTES),
        cost_estimate=small_cost(),
        name="weight",
    )(at, *own_pairs, *other_pairs, *dvs)


def tokens_kernel(n_fsdp, at_ref, dv_ref, w_ref, own_ref, *others):
    made = dot(dv_ref[...], w_ref[...], NT).astype(BF16)
    rows = own_ref.shape[0]
    own_ref[...] = made[:rows]
    for s, ref in enumerate(others):
        ref[...] = made[(s + 1) * rows : (s + 2) * rows]


def run_tokens(at, dv_rows, w, n_fsdp):
    slab, width = w.shape
    rows = dv_rows.shape[0] // n_fsdp
    tile = slab // 3 if slab % (3 * HD) == 0 else slab
    n_tiles = slab // tile
    return pl.pallas_call(
        functools.partial(tokens_kernel, n_fsdp),
        grid_spec=pltpu.PrefetchScalarGridSpec(
            num_scalar_prefetch=1,
            grid=(n_tiles,),
            in_specs=[
                pl.BlockSpec(dv_rows.shape, lambda j, at: (0, 0)),
                pl.BlockSpec((tile, width), lambda j, at: (j, 0)),
            ],
            out_specs=[pl.BlockSpec((rows, tile), lambda j, at: (0, at[0] * n_tiles + j))]
            + [pl.BlockSpec((rows, tile), lambda j, at: (0, j))] * (n_fsdp - 1),
        ),
        out_shape=[jax.ShapeDtypeStruct((rows, slab * n_fsdp), BF16)]
        + [jax.ShapeDtypeStruct((rows, slab), BF16)] * (n_fsdp - 1),
        compiler_params=pltpu.CompilerParams(vmem_limit_bytes=VMEM_BYTES),
        cost_estimate=small_cost(),
        name="tokens",
    )(at, dv_rows, w)


def shifted(x, by):
    length = lax.axis_size("ctx")
    return lax.ppermute(x, "ctx", [(i, i + by) for i in range(length) if 0 <= i + by < length])


def swapped(x):
    return lax.ppermute(x, "ctx", [(i, i ^ 1) for i in range(lax.axis_size("ctx"))])


def rotated(x, by):
    length = lax.axis_size("fsdp")
    return lax.ppermute(x, "fsdp", [(i, (i + by) % length) for i in range(length)])


def moved(x, flip, by):
    n_ctx, n_fsdp = lax.axis_size("ctx"), lax.axis_size("fsdp")
    pairs = [
        (c * n_fsdp + f, (c ^ (2 * flip)) * n_fsdp + (f + by) % n_fsdp)
        for c in range(n_ctx)
        for f in range(n_fsdp)
    ]
    return lax.ppermute(x, ("ctx", "fsdp"), pairs)


def relayed(my_y, far, got):
    return (far.astype(F32) + jnp.where(my_y == 1, got.astype(F32), 0.0)).astype(BF16)


def gathered_terms(my_y, mine, got, back):
    return (mine.astype(F32) + back.astype(F32) + jnp.where(my_y == 0, got.astype(F32), 0.0)).astype(BF16)


def cols(x, at, width):
    return lax.dynamic_slice_in_dim(x, at * width, width, x.ndim - 1)


def rows_of(x, at, count):
    return lax.dynamic_slice_in_dim(x, at * count, count, 0)


def placed(core, own, other, axis):
    both = jnp.concatenate([own, own], axis)
    return lax.dynamic_update_slice_in_dim(both, other, (1 - core) * own.shape[axis], axis)


def flipped(x):
    return lax.ppermute(x, "ctx", [(i, i ^ 2) for i in range(lax.axis_size("ctx"))])


def after(x, *earlier):
    return lax.optimization_barrier((x, *earlier))[0]


def shards(hidden, queries, key_heads, w_value, d_out, segments):
    shard_rows = hidden.shape[1]
    model = hidden.shape[2]
    kv_width = w_value.shape[1]
    n_ctx = lax.axis_size("ctx")
    n_fsdp = lax.axis_size("fsdp")
    chip_rows = 2 * shard_rows
    n_z = n_ctx // 4
    assert WINDOW == 2 * chip_rows
    my_ctx = lax.axis_index("ctx")
    my_fsdp = lax.axis_index("fsdp")
    core = my_ctx % 2
    core_arg = core.astype(jnp.int32).reshape(1)
    chip = my_ctx // 2
    my_y = chip % 2
    my_z = chip // 2
    half_kv = kv_width // 2
    slab = model // n_fsdp
    tokens = hidden[0]
    first = chip * chip_rows

    aligned = slab % HD == 0
    fsdp_arg = my_fsdp.astype(jnp.int32).reshape(1)
    zero_arg = jnp.zeros((1,), jnp.int32)
    half_q = queries.shape[2] // 2
    out_rows = model // (n_ctx * n_fsdp)
    places = [(flip, s) for flip in range(2) for s in range(n_fsdp)]

    cut = slab // HD // 2 * HD if aligned else slab
    parts_at = [(0, cut), (cut, slab)] if aligned else [(0, slab)]
    slabs = [
        [
            lax.dynamic_slice_in_dim(tokens, (my_fsdp + s) % n_fsdp * slab + low, high - low, 1)
            for low, high in parts_at
        ]
        for s in range(1, n_fsdp)
    ]
    sent = [[rotated(x, s + 1) for x in parts] for s, parts in enumerate(slabs)]

    own_tags = segments[0].astype(BF16)
    tag_row = lax.dynamic_update_slice_in_dim(jnp.zeros((half_kv,), BF16), own_tags, core * shard_rows, 0)
    tag_rows = jnp.concatenate([tag_row[None], jnp.zeros((15, half_kv), BF16)], 0)
    k_sent = jnp.concatenate([cols(key_heads[0], 1 - core, half_kv), tag_rows], 0)
    got = swapped(after(k_sent, *[parts[0] for parts in slabs]))

    if out_rows % 8 == 0:
        at = jnp.stack([my_y, my_fsdp]).astype(jnp.int32)
        pieces = run_pieces(after(at, k_sent, got), tokens, n_z, n_fsdp, out_rows)
    else:
        turned = tokens.T.reshape(n_z, 2, 2, n_fsdp, out_rows, shard_rows)
        pieces = []
        for flip, s in places:
            piece = lax.dynamic_index_in_dim(turned, my_y ^ flip, 1, keepdims=False)
            piece = lax.dynamic_index_in_dim(piece, (my_fsdp + s) % n_fsdp, 2, keepdims=False)
            pieces.append(piece.reshape(n_z * 2 * out_rows, shard_rows))
    by_place = dict(zip(places, pieces))

    k_own = jnp.concatenate(
        [
            placed(core, cols(key_heads[0], core, half_kv), got[:shard_rows], 0),
            tag_rows + got[shard_rows:],
        ],
        0,
    )
    k_far = shifted(k_own, 4)
    k_near = shifted(k_own, 2)
    over_y = {s: flipped(after(by_place[1, s], k_own)) for s in range(1, n_fsdp)}
    q_sent = jnp.concatenate([cols(queries[0], 1 - core, half_q), cols(d_out[0], 1 - core, half_q)], 1)
    q_other = swapped(after(q_sent, k_own))
    if aligned:
        value_own = run_product(after(fsdp_arg, q_sent, *pieces), [tokens], w_value, F32)
    else:
        value_own = dot(cols(tokens, my_fsdp, slab), w_value)
    keys = [k_far, k_near, k_own]

    span_tags = jnp.concatenate([k[chip_rows, :chip_rows] for k in keys], 0)
    key_at = jnp.arange(WINDOW + chip_rows, dtype=jnp.int32)
    chip_tags = k_own[chip_rows, :chip_rows]
    before = (span_tags[None, :] < chip_tags[:, None]) | (key_at + first < WINDOW)[None, :]
    low = jnp.sum(before.astype(jnp.int32), axis=1)
    low = jnp.maximum(low, jnp.arange(1, chip_rows + 1, dtype=jnp.int32))[None, :]

    if aligned:
        partial = [run_product(zero_arg, parts, w_value, BF16) for parts in sent]
    else:
        partial = [dot(parts[0], w_value).astype(BF16) for parts in sent]
    low = after(low, *partial)
    e, inv, do_t, dv_far, dv_near, dv_mine = run_probs(
        core_arg, low, queries[0], q_other, d_out[0], keys, chip_rows, half_kv
    )
    dv_got = flipped(dv_near)

    value_back = [rotated(x, -s - 1) for s, x in enumerate(partial)]
    over_fsdp = {s: rotated(after(by_place[0, s], sent), s) for s in range(1, n_fsdp)}
    value_back = [after(x, dv_near, over_y) for x in value_back]
    value_sum = value_own
    for x in value_back:
        value_sum = value_sum + x.astype(F32)
    own_values = value_sum.astype(BF16)
    v_own = placed(core, cols(own_values, core, half_kv), swapped(cols(own_values, 1 - core, half_kv)), 0)

    over_y[0] = flipped(after(by_place[1, 0], k_near))
    v_own, over_y[0], over_fsdp = lax.optimization_barrier((v_own, over_y[0], over_fsdp))
    v_far = shifted(v_own, 4)
    own_pairs = [jnp.concatenate([by_place[0, 0], over_y[0]], 1)]
    other_pairs = [swapped(after(own_pairs[0], v_own))]
    relayed_y = {s: rotated(after(over_y[s], own_values), s) for s in range(1, n_fsdp)}

    dv_got = after(dv_got, v_own)
    dv_sent = relayed(my_y, dv_far, dv_got)
    dv_back = shifted(dv_sent, -4)
    v_sent = after(jnp.where(my_y == 0, v_own, v_far), dv_sent)
    v_near = flipped(v_sent)
    vals = [v_far, v_near, v_own]
    dv_chip = gathered_terms(my_y, dv_mine, dv_got, after(dv_back, v_sent))
    dv_fsdp = [dv_chip] + [rotated(dv_chip, s) for s in range(1, n_fsdp)]
    dv_over_y = [moved(dv_chip, 1, s) for s in range(n_fsdp)]
    for s in range(1, n_fsdp):
        own_pairs.append(jnp.concatenate([over_fsdp[s], after(relayed_y[s], dv_chip)], 1))
        other_pairs.append(swapped(own_pairs[s]))
    v_near = after(v_near, dv_chip)
    vals = [v_far, v_near, v_own]
    out, dq, other, dk_far, dk_near, dk_mine = run_grads(
        core_arg, e, inv, do_t, queries[0], q_other, keys, vals, chip_rows, half_kv
    )
    dk_back = [shifted(dk_near, -2), shifted(dk_far, -4)]

    dv_fsdp = [after(x, dk_near) for x in dv_fsdp]
    dv_other = swapped(jnp.concatenate([rows_of(x, 1 - core, shard_rows) for x in dv_fsdp], 0))
    dv_rows = placed(
        core, jnp.concatenate([rows_of(x, core, shard_rows) for x in dv_fsdp], 0), dv_other, 1
    )
    if aligned:
        d_tokens, *made = run_tokens(fsdp_arg, dv_rows, w_value, n_fsdp)
    else:
        made = dot(dv_rows, w_value, NT).astype(BF16)
        made = [made[s * shard_rows : (s + 1) * shard_rows] for s in range(n_fsdp)]
        d_tokens = jnp.concatenate([made[0]] * n_fsdp, 1)
        made = made[1:]
    for s in range(1, n_fsdp):
        back = rotated(made[s - 1], -s)
        d_tokens = lax.dynamic_update_slice_in_dim(d_tokens, back, ((my_fsdp + s) % n_fsdp) * slab, 1)

    dv_over_y = [after(x, *made) for x in dv_over_y]
    dv_pairs = list(zip(dv_fsdp, dv_over_y))
    if out_rows % 8 == 0:
        at = after(jnp.stack([core, my_z]).astype(jnp.int32), *made)
        by_z = run_weight(at, own_pairs, other_pairs, dv_pairs, n_z)
    else:
        weight_term = 0.0
        for p in range(n_fsdp):
            for flip in range(2):
                window = slice(flip * shard_rows, (flip + 1) * shard_rows)
                weight_term += dot(own_pairs[p][:, window], rows_of(dv_pairs[p][flip], core, shard_rows))
                weight_term += dot(other_pairs[p][:, window], rows_of(dv_pairs[p][flip], 1 - core, shard_rows))
        weight_term = weight_term.reshape(n_z, 2 * out_rows, half_kv)
        by_z = [
            lax.dynamic_index_in_dim(weight_term, (my_z + d) % n_z, 0, keepdims=False).astype(BF16 if d else F32)
            for d in range(n_z)
        ]
    by_z, dk_back = lax.optimization_barrier((list(by_z), dk_back))
    over_z = [
        lax.ppermute(by_z[d], "ctx", [(i, (i + 4 * d) % n_ctx) for i in range(n_ctx)]) for d in range(1, n_z)
    ]

    row_sum = by_z[0]
    for x in over_z:
        row_sum = row_sum + x.astype(F32)
    d_weight = placed(core, rows_of(row_sum, core, out_rows), swapped(rows_of(row_sum, 1 - core, out_rows)), 1)

    dk_chip = (dk_mine.astype(F32) + dk_back[0].astype(F32) + dk_back[1].astype(F32)).astype(BF16)
    d_keys = placed(core, rows_of(dk_chip, core, shard_rows), swapped(rows_of(dk_chip, 1 - core, shard_rows)), 1)
    other = swapped(after(other, *made))
    out = lax.dynamic_update_slice_in_dim(out, other[0], (1 - core) * half_q, 1)
    dq = lax.dynamic_update_slice_in_dim(dq, other[1], (1 - core) * half_q, 1)
    return (out[None], dq[None], d_keys[None], d_tokens[None], d_weight)


def solution(mesh):
    in_specs = (
        P("fsdp", "ctx", None),
        P("fsdp", "ctx", None),
        P("fsdp", "ctx", None),
        P("fsdp", None),
        P("fsdp", "ctx", None),
        P("fsdp", "ctx"),
    )
    out_specs = (
        P("fsdp", "ctx", None),
        P("fsdp", "ctx", None),
        P("fsdp", "ctx", None),
        P("fsdp", "ctx", None),
        P(("ctx", "fsdp"), None),
    )
    return jax.shard_map(shards, mesh=mesh, in_specs=in_specs, out_specs=out_specs, check_vma=False)
```

```python
import functools
import math

import jax
import jax.numpy as jnp
from jax import lax
from jax.experimental import pallas as pl
from jax.experimental.pallas import tpu as pltpu
from jax.sharding import PartitionSpec as P

HQ = 16
HK = 8
HD = 128
WINDOW = 1024
GROUP = 2
NEG = -1e30
VMEM_BYTES = 58 * 1024 * 1024

score_scale = 1.0 / math.sqrt(168.0)
exp2_scale = score_scale / math.log(2.0)

BF16 = jnp.bfloat16
F32 = jnp.float32
NT = (((1,), (1,)), ((), ()))
TN = (((0,), (0,)), ((), ()))


def dot(a, b, dims=(((1,), (0,)), ((), ()))):
    return lax.dot_general(a, b, dims, preferred_element_type=F32)


def probs_kernel(blk, n_back, core_ref, low_ref, q_own, q_other, do_own, do_other, *refs):
    n_arr = n_back + 1
    k_refs = refs[:n_arr]
    e_ref, inv_ref, dot_ref = refs[n_arr : n_arr + 3]
    dv_refs = refs[n_arr + 3 : 2 * n_arr + 3]
    bias, s_scr, dv_acc, q_buf, do_buf = refs[2 * n_arr + 3 :]
    span_blocks = WINDOW // blk + 1
    core = core_ref[0]

    @pl.when(pl.program_id(0) == 0)
    def _():
        for qb in range(2):
            kpos = lax.broadcasted_iota(jnp.int32, (span_blocks * blk, blk), 0) + qb * blk
            qpos = lax.broadcasted_iota(jnp.int32, (span_blocks * blk, blk), 1) + (qb * blk + WINDOW)
            low = low_ref[:, qb * blk : (qb + 1) * blk]
            ok = (kpos >= low) & (kpos <= qpos)
            bias[qb] = jnp.where(ok, 0.0, NEG)

    q_buf[core] = q_own[...]
    q_buf[1 - core] = q_other[...]
    do_buf[core] = do_own[...]
    do_buf[1 - core] = do_other[...]

    def key_block(j):
        return k_refs[j // 2][(j % 2) * blk : (j % 2 + 1) * blk, :]

    def stacked(buf, qb):
        return jnp.concatenate([buf[qb, :, r * HD : (r + 1) * HD] for r in range(GROUP)], 0)

    for qb in range(2):
        qs = stacked(q_buf, qb)
        top = None
        for j in range(span_blocks):
            s = dot(key_block(qb + j), qs, NT)
            b = bias[qb, j * blk : (j + 1) * blk, :]
            s = s * exp2_scale + jnp.concatenate([b] * GROUP, 1)
            s_scr[j] = s
            part = jnp.max(s.reshape(blk // 8, 8, GROUP * blk), axis=0)
            top = part if top is None else jnp.maximum(top, part)
        top = jnp.max(top, axis=0, keepdims=True)
        total = None
        for j in range(span_blocks):
            e = jnp.exp2(s_scr[j] - top)
            part = jnp.sum(e.reshape(blk // 8, 8, GROUP * blk), axis=0)
            total = part if total is None else total + part
            e_ref[0, qb, j * blk : (j + 1) * blk, :] = e.astype(BF16)
        inv = 1.0 / jnp.sum(total, axis=0, keepdims=True)
        inv_ref[0, qb] = inv
        do_t = (stacked(do_buf, qb).astype(F32).T * inv).astype(BF16)
        dot_ref[0, qb] = do_t
        for j in range(span_blocks):
            term = dot(e_ref[0, qb, j * blk : (j + 1) * blk, :], do_t, NT)
            at = slice((qb + j) * blk, (qb + j + 1) * blk)
            if qb == 0 or j == span_blocks - 1:
                dv_acc[at, :] = term
            else:
                dv_acc[at, :] += term
    for a in range(n_arr):
        dv_refs[a][...] = dv_acc[a * 2 * blk : (a + 1) * 2 * blk, :].astype(BF16)


def grads_kernel(blk, n_back, core_ref, e_ref, inv_ref, dot_ref, q_own, q_other, *refs):
    n_arr = n_back + 1
    k_refs = refs[:n_arr]
    v_refs = refs[n_arr : 2 * n_arr]
    out_ref, dq_ref, other_ref = refs[2 * n_arr : 2 * n_arr + 3]
    dk_refs = refs[2 * n_arr + 3 : 3 * n_arr + 3]
    dk_acc, q_buf, out_buf, dq_buf = refs[3 * n_arr + 3 :]
    span_blocks = WINDOW // blk + 1
    core = core_ref[0]

    q_buf[core] = q_own[...]
    q_buf[1 - core] = q_other[...]

    def block_of(arrays, j):
        return arrays[j // 2][(j % 2) * blk : (j % 2 + 1) * blk, :]

    for qb in range(2):
        qs = jnp.concatenate([q_buf[qb, :, r * HD : (r + 1) * HD] for r in range(GROUP)], 0)
        do_t = dot_ref[0, qb]
        out_t = None
        for j in range(span_blocks):
            e = e_ref[0, qb, j * blk : (j + 1) * blk, :]
            part = dot(block_of(v_refs, qb + j), e, TN)
            out_t = part if out_t is None else out_t + part
        out_t = (out_t * inv_ref[0, qb]).astype(BF16).astype(F32)
        delta = jnp.sum(out_t * do_t.astype(F32), axis=0, keepdims=True)
        out = out_t.T.astype(BF16)
        dq_t = None
        for j in range(span_blocks):
            e = e_ref[0, qb, j * blk : (j + 1) * blk, :].astype(F32)
            dp = dot(block_of(v_refs, qb + j), do_t)
            ds = (e * (dp - delta)).astype(BF16)
            term = dot(ds, qs)
            at = slice((qb + j) * blk, (qb + j + 1) * blk)
            if qb == 0 or j == span_blocks - 1:
                dk_acc[at, :] = term
            else:
                dk_acc[at, :] += term
            part = dot(block_of(k_refs, qb + j), ds, TN)
            dq_t = part if dq_t is None else dq_t + part
        dq = (dq_t * score_scale).T.astype(BF16)
        for r in range(GROUP):
            out_buf[qb, :, r * HD : (r + 1) * HD] = out[r * blk : (r + 1) * blk, :]
            dq_buf[qb, :, r * HD : (r + 1) * HD] = dq[r * blk : (r + 1) * blk, :]
    out_ref[...] = out_buf[core]
    dq_ref[...] = dq_buf[core]
    other_ref[0] = out_buf[1 - core]
    other_ref[1] = dq_buf[1 - core]
    for a in range(n_arr):
        dk_refs[a][...] = (dk_acc[a * 2 * blk : (a + 1) * 2 * blk, :] * score_scale).astype(BF16)


def specs_of(rows, width):
    blk = rows // 2
    heads = width // HD
    span = WINDOW + blk
    lanes = GROUP * blk
    head = pl.BlockSpec((rows, HD), lambda g, c: (0, g))
    own = pl.BlockSpec((blk, GROUP * HD), lambda g, c: (0, c[0] * heads + g))
    return blk, heads, span, lanes, head, own


def run_probs(core, low, q, q_other, do, keys, rows, width):
    blk, heads, span, lanes, head, own = specs_of(rows, width)
    n_arr = len(keys)
    return pl.pallas_call(
        functools.partial(probs_kernel, blk, n_arr - 1),
        grid_spec=pltpu.PrefetchScalarGridSpec(
            num_scalar_prefetch=1,
            grid=(heads,),
            in_specs=[
                pl.BlockSpec((1, rows), lambda g, c: (0, 0)),
                own,
                pl.BlockSpec((blk, GROUP * HD), lambda g, c: (0, g)),
                own,
                pl.BlockSpec((blk, GROUP * HD), lambda g, c: (0, heads + g)),
            ]
            + [head] * n_arr,
            out_specs=[
                pl.BlockSpec((1, 2, span, lanes), lambda g, c: (g, 0, 0, 0)),
                pl.BlockSpec((1, 2, 1, lanes), lambda g, c: (g, 0, 0, 0)),
                pl.BlockSpec((1, 2, HD, lanes), lambda g, c: (g, 0, 0, 0)),
            ]
            + [head] * n_arr,
            scratch_shapes=[
                pltpu.VMEM((2, span, blk), F32),
                pltpu.VMEM((span // blk, blk, lanes), F32),
                pltpu.VMEM((WINDOW + rows, HD), F32),
                pltpu.VMEM((2, blk, GROUP * HD), BF16),
                pltpu.VMEM((2, blk, GROUP * HD), BF16),
            ],
        ),
        out_shape=[
            jax.ShapeDtypeStruct((heads, 2, span, lanes), BF16),
            jax.ShapeDtypeStruct((heads, 2, 1, lanes), F32),
            jax.ShapeDtypeStruct((heads, 2, HD, lanes), BF16),
        ]
        + [jax.ShapeDtypeStruct((rows, width), BF16)] * n_arr,
        compiler_params=pltpu.CompilerParams(vmem_limit_bytes=VMEM_BYTES),
        cost_estimate=small_cost(),
        name="probs",
    )(core, low, q, q_other, do, q_other, *keys)


def run_grads(core, e, inv, do_t, q, q_other, keys, values, rows, width):
    blk, heads, span, lanes, head, own = specs_of(rows, width)
    n_arr = len(keys)
    full = jax.ShapeDtypeStruct(q.shape, BF16)
    return pl.pallas_call(
        functools.partial(grads_kernel, blk, n_arr - 1),
        grid_spec=pltpu.PrefetchScalarGridSpec(
            num_scalar_prefetch=1,
            grid=(heads,),
            in_specs=[
                pl.BlockSpec((1, 2, span, lanes), lambda g, c: (g, 0, 0, 0)),
                pl.BlockSpec((1, 2, 1, lanes), lambda g, c: (g, 0, 0, 0)),
                pl.BlockSpec((1, 2, HD, lanes), lambda g, c: (g, 0, 0, 0)),
                own,
                pl.BlockSpec((blk, GROUP * HD), lambda g, c: (0, g)),
            ]
            + [head] * (2 * n_arr),
            out_specs=[own, own, pl.BlockSpec((2, blk, GROUP * HD), lambda g, c: (0, 0, g))] + [head] * n_arr,
            scratch_shapes=[
                pltpu.VMEM((WINDOW + rows, HD), F32),
                pltpu.VMEM((2, blk, GROUP * HD), BF16),
                pltpu.VMEM((2, blk, GROUP * HD), BF16),
                pltpu.VMEM((2, blk, GROUP * HD), BF16),
            ],
        ),
        out_shape=[full, full, jax.ShapeDtypeStruct((2, blk, GROUP * width), BF16)]
        + [jax.ShapeDtypeStruct((rows, width), BF16)] * n_arr,
        compiler_params=pltpu.CompilerParams(vmem_limit_bytes=VMEM_BYTES),
        cost_estimate=small_cost(),
        name="grads",
    )(core, e, inv, do_t, q, q_other, *keys, *values)


def small_cost():
    return pl.CostEstimate(flops=1 << 20, bytes_accessed=1 << 12, transcendentals=0)


def whole():
    return pl.BlockSpec(memory_space=pltpu.VMEM)


def pieces_kernel(dims, at_ref, x_ref, *refs):
    n_z, n_fsdp, out_rows = dims
    outs = refs[: 2 * n_fsdp]
    turned = refs[2 * n_fsdp]
    my_y, my_fsdp = at_ref[0], at_ref[1]
    for c in range(x_ref.shape[1] // HD):
        turned[c * HD : (c + 1) * HD, :] = x_ref[:, c * HD : (c + 1) * HD].astype(F32).T
    for p, out in enumerate(outs):
        flip, s = p // n_fsdp, p % n_fsdp
        y = lax.rem(my_y + flip, 2)
        f = lax.rem(my_fsdp + s, n_fsdp)
        for z in range(n_z):
            parts = []
            for core in range(2):
                block = ((z * 2 + y) * 2 + core) * n_fsdp + f
                parts.append(turned[pl.ds(pl.multiple_of(block * out_rows, 8), out_rows), :])
            out[z * 2 * out_rows : (z + 1) * 2 * out_rows, :] = jnp.concatenate(parts, 0).astype(BF16)


def run_pieces(at, tokens, n_z, n_fsdp, out_rows):
    rows, model = tokens.shape
    shape = jax.ShapeDtypeStruct((n_z * 2 * out_rows, rows), BF16)
    return pl.pallas_call(
        functools.partial(pieces_kernel, (n_z, n_fsdp, out_rows)),
        in_specs=[pl.BlockSpec(memory_space=pltpu.SMEM), whole()],
        out_specs=[whole()] * (2 * n_fsdp),
        out_shape=[shape] * (2 * n_fsdp),
        scratch_shapes=[pltpu.VMEM((model, rows), F32)],
        compiler_params=pltpu.CompilerParams(vmem_limit_bytes=VMEM_BYTES),
        cost_estimate=small_cost(),
        name="pieces",
    )(at, tokens)


def product_kernel(at_ref, *refs):
    *x_refs, w_ref, o_ref = refs
    total, first = None, 0
    for x in x_refs:
        term = dot(x[...], w_ref[first : first + x.shape[1], :])
        total = term if total is None else total + term
        first += x.shape[1]
    o_ref[...] = total.astype(o_ref.dtype)


def run_product(at, parts, w, kind):
    rows = parts[0].shape[0]
    depth, width = w.shape
    tile = width
    if len(parts) == 1:
        x_specs = [pl.BlockSpec((rows, depth), lambda j, at: (0, at[0]))]
    else:
        x_specs = [pl.BlockSpec(x.shape, lambda j, at: (0, 0)) for x in parts]
    return pl.pallas_call(
        product_kernel,
        grid_spec=pltpu.PrefetchScalarGridSpec(
            num_scalar_prefetch=1,
            grid=(width // tile,),
            in_specs=x_specs + [pl.BlockSpec((depth, tile), lambda j, at: (0, j))],
            out_specs=pl.BlockSpec((rows, tile), lambda j, at: (0, j)),
        ),
        out_shape=jax.ShapeDtypeStruct((rows, width), kind),
        compiler_params=pltpu.CompilerParams(vmem_limit_bytes=VMEM_BYTES),
        cost_estimate=small_cost(),
        name="product",
    )(at, *parts, w)


def weight_kernel(n_z, n, at_ref, *refs):
    own_pairs, other_pairs = refs[:n], refs[n : 2 * n]
    dv_refs = refs[2 * n : 4 * n]
    outs = refs[4 * n :]
    core = at_ref[0]
    step = pl.program_id(0)
    rows = own_pairs[0].shape[1] // 2
    own = pl.ds(pl.multiple_of(core * rows, rows), rows)
    other = pl.ds(pl.multiple_of((1 - core) * rows, rows), rows)
    total = None
    for p in range(n):
        for flip in range(2):
            window = slice(flip * rows, (flip + 1) * rows)
            term = dot(own_pairs[p][:, window], dv_refs[2 * p + flip][own, :])
            term = term + dot(other_pairs[p][:, window], dv_refs[2 * p + flip][other, :])
            total = term if total is None else total + term
    for d, out in enumerate(outs):

        @pl.when(step == (n_z - 1 if d == 0 else d - 1))
        def _():
            out[...] = total.astype(out.dtype)


def run_weight(at, own_pairs, other_pairs, dv_pairs, n_z):
    n = len(own_pairs)
    count = own_pairs[0].shape[0] // n_z
    rows2 = own_pairs[0].shape[1]
    dvs = [x for pair_of in dv_pairs for x in pair_of]
    width = dvs[0].shape[1]
    shapes = [jax.ShapeDtypeStruct((count, width), F32 if d == 0 else BF16) for d in range(n_z)]
    pair_block = pl.BlockSpec((count, rows2), lambda d, at: (lax.rem(at[1] + d + 1, n_z), 0))
    return pl.pallas_call(
        functools.partial(weight_kernel, n_z, n),
        grid_spec=pltpu.PrefetchScalarGridSpec(
            num_scalar_prefetch=1,
            grid=(n_z,),
            in_specs=[pair_block] * (2 * n) + [pl.BlockSpec(dvs[0].shape, lambda d, at: (0, 0))] * (2 * n),
            out_specs=[pl.BlockSpec((count, width), lambda d, at: (0, 0))] * n_z,
        ),
        out_shape=shapes,
        compiler_params=pltpu.CompilerParams(vmem_limit_bytes=VMEM_BYTES),
        cost_estimate=small_cost(),
        name="weight",
    )(at, *own_pairs, *other_pairs, *dvs)


def tokens_kernel(n_fsdp, at_ref, dv_ref, w_ref, own_ref, *others):
    made = dot(dv_ref[...], w_ref[...], NT).astype(BF16)
    rows = own_ref.shape[0]
    own_ref[...] = made[:rows]
    for s, ref in enumerate(others):
        ref[...] = made[(s + 1) * rows : (s + 2) * rows]


def run_tokens(at, dv_rows, w, n_fsdp):
    slab, width = w.shape
    rows = dv_rows.shape[0] // n_fsdp
    tile = slab // 3 if slab % (3 * HD) == 0 else slab
    n_tiles = slab // tile
    return pl.pallas_call(
        functools.partial(tokens_kernel, n_fsdp),
        grid_spec=pltpu.PrefetchScalarGridSpec(
            num_scalar_prefetch=1,
            grid=(n_tiles,),
            in_specs=[
                pl.BlockSpec(dv_rows.shape, lambda j, at: (0, 0)),
                pl.BlockSpec((tile, width), lambda j, at: (j, 0)),
            ],
            out_specs=[pl.BlockSpec((rows, tile), lambda j, at: (0, at[0] * n_tiles + j))]
            + [pl.BlockSpec((rows, tile), lambda j, at: (0, j))] * (n_fsdp - 1),
        ),
        out_shape=[jax.ShapeDtypeStruct((rows, slab * n_fsdp), BF16)]
        + [jax.ShapeDtypeStruct((rows, slab), BF16)] * (n_fsdp - 1),
        compiler_params=pltpu.CompilerParams(vmem_limit_bytes=VMEM_BYTES),
        cost_estimate=small_cost(),
        name="tokens",
    )(at, dv_rows, w)


def shifted(x, by):
    length = lax.axis_size("ctx")
    return lax.ppermute(x, "ctx", [(i, i + by) for i in range(length) if 0 <= i + by < length])


def swapped(x):
    return lax.ppermute(x, "ctx", [(i, i ^ 1) for i in range(lax.axis_size("ctx"))])


def rotated(x, by):
    length = lax.axis_size("fsdp")
    return lax.ppermute(x, "fsdp", [(i, (i + by) % length) for i in range(length)])


def moved(x, flip, by):
    n_ctx, n_fsdp = lax.axis_size("ctx"), lax.axis_size("fsdp")
    pairs = [
        (c * n_fsdp + f, (c ^ (2 * flip)) * n_fsdp + (f + by) % n_fsdp)
        for c in range(n_ctx)
        for f in range(n_fsdp)
    ]
    return lax.ppermute(x, ("ctx", "fsdp"), pairs)


def relayed(my_y, far, got):
    return (far.astype(F32) + jnp.where(my_y == 1, got.astype(F32), 0.0)).astype(BF16)


def gathered_terms(my_y, mine, got, back):
    return (mine.astype(F32) + back.astype(F32) + jnp.where(my_y == 0, got.astype(F32), 0.0)).astype(BF16)


def cols(x, at, width):
    return lax.dynamic_slice_in_dim(x, at * width, width, x.ndim - 1)


def rows_of(x, at, count):
    return lax.dynamic_slice_in_dim(x, at * count, count, 0)


def placed(core, own, other, axis):
    both = jnp.concatenate([own, own], axis)
    return lax.dynamic_update_slice_in_dim(both, other, (1 - core) * own.shape[axis], axis)


def flipped(x):
    return lax.ppermute(x, "ctx", [(i, i ^ 2) for i in range(lax.axis_size("ctx"))])


def after(x, *earlier):
    return lax.optimization_barrier((x, *earlier))[0]


def shards(hidden, queries, key_heads, w_value, d_out, segments):
    shard_rows = hidden.shape[1]
    model = hidden.shape[2]
    kv_width = w_value.shape[1]
    n_ctx = lax.axis_size("ctx")
    n_fsdp = lax.axis_size("fsdp")
    chip_rows = 2 * shard_rows
    n_z = n_ctx // 4
    assert WINDOW == 2 * chip_rows
    my_ctx = lax.axis_index("ctx")
    my_fsdp = lax.axis_index("fsdp")
    core = my_ctx % 2
    core_arg = core.astype(jnp.int32).reshape(1)
    chip = my_ctx // 2
    my_y = chip % 2
    my_z = chip // 2
    half_kv = kv_width // 2
    slab = model // n_fsdp
    tokens = hidden[0]
    first = chip * chip_rows

    aligned = slab % HD == 0
    fsdp_arg = my_fsdp.astype(jnp.int32).reshape(1)
    zero_arg = jnp.zeros((1,), jnp.int32)
    half_q = queries.shape[2] // 2
    out_rows = model // (n_ctx * n_fsdp)
    places = [(flip, s) for flip in range(2) for s in range(n_fsdp)]

    cut = slab // HD // 2 * HD if aligned else slab
    parts_at = [(0, cut), (cut, slab)] if aligned else [(0, slab)]
    slabs = [
        [
            lax.dynamic_slice_in_dim(tokens, (my_fsdp + s) % n_fsdp * slab + low, high - low, 1)
            for low, high in parts_at
        ]
        for s in range(1, n_fsdp)
    ]
    sent = [[rotated(x, s + 1) for x in parts] for s, parts in enumerate(slabs)]

    own_tags = segments[0].astype(BF16)
    tag_row = lax.dynamic_update_slice_in_dim(jnp.zeros((half_kv,), BF16), own_tags, core * shard_rows, 0)
    tag_rows = jnp.concatenate([tag_row[None], jnp.zeros((15, half_kv), BF16)], 0)
    k_sent = jnp.concatenate([cols(key_heads[0], 1 - core, half_kv), tag_rows], 0)
    got = swapped(after(k_sent, *[parts[0] for parts in slabs]))

    if out_rows % 8 == 0:
        at = jnp.stack([my_y, my_fsdp]).astype(jnp.int32)
        pieces = run_pieces(after(at, k_sent, got), tokens, n_z, n_fsdp, out_rows)
    else:
        turned = tokens.T.reshape(n_z, 2, 2, n_fsdp, out_rows, shard_rows)
        pieces = []
        for flip, s in places:
            piece = lax.dynamic_index_in_dim(turned, my_y ^ flip, 1, keepdims=False)
            piece = lax.dynamic_index_in_dim(piece, (my_fsdp + s) % n_fsdp, 2, keepdims=False)
            pieces.append(piece.reshape(n_z * 2 * out_rows, shard_rows))
    by_place = dict(zip(places, pieces))

    k_own = jnp.concatenate(
        [
            placed(core, cols(key_heads[0], core, half_kv), got[:shard_rows], 0),
            tag_rows + got[shard_rows:],
        ],
        0,
    )
    k_far = shifted(k_own, 4)
    k_near = shifted(k_own, 2)
    over_y = {s: flipped(after(by_place[1, s], k_own)) for s in range(1, n_fsdp)}
    q_sent = jnp.concatenate([cols(queries[0], 1 - core, half_q), cols(d_out[0], 1 - core, half_q)], 1)
    q_other = swapped(after(q_sent, k_own))
    if aligned:
        value_own = run_product(after(fsdp_arg, q_sent, *pieces), [tokens], w_value, F32)
    else:
        value_own = dot(cols(tokens, my_fsdp, slab), w_value)
    keys = [k_far, k_near, k_own]

    span_tags = jnp.concatenate([k[chip_rows, :chip_rows] for k in keys], 0)
    key_at = jnp.arange(WINDOW + chip_rows, dtype=jnp.int32)
    chip_tags = k_own[chip_rows, :chip_rows]
    before = (span_tags[None, :] < chip_tags[:, None]) | (key_at + first < WINDOW)[None, :]
    low = jnp.sum(before.astype(jnp.int32), axis=1)
    low = jnp.maximum(low, jnp.arange(1, chip_rows + 1, dtype=jnp.int32))[None, :]

    if aligned:
        partial = [run_product(zero_arg, parts, w_value, BF16) for parts in sent]
    else:
        partial = [dot(parts[0], w_value).astype(BF16) for parts in sent]
    low = after(low, *partial)
    e, inv, do_t, dv_far, dv_near, dv_mine = run_probs(
        core_arg, low, queries[0], q_other, d_out[0], keys, chip_rows, half_kv
    )
    dv_got = flipped(dv_near)

    value_back = [rotated(x, -s - 1) for s, x in enumerate(partial)]
    over_fsdp = {s: rotated(after(by_place[0, s], sent), s) for s in range(1, n_fsdp)}
    value_back = [after(x, dv_near, over_y) for x in value_back]
    value_sum = value_own
    for x in value_back:
        value_sum = value_sum + x.astype(F32)
    own_values = value_sum.astype(BF16)
    v_own = placed(core, cols(own_values, core, half_kv), swapped(cols(own_values, 1 - core, half_kv)), 0)

    over_y[0] = flipped(after(by_place[1, 0], k_near))
    v_own, over_y[0], over_fsdp = lax.optimization_barrier((v_own, over_y[0], over_fsdp))
    v_far = shifted(v_own, 4)
    own_pairs = [jnp.concatenate([by_place[0, 0], over_y[0]], 1)]
    other_pairs = [swapped(after(own_pairs[0], v_own))]
    relayed_y = {s: rotated(after(over_y[s], own_values), s) for s in range(1, n_fsdp)}

    dv_got = after(dv_got, v_own)
    dv_sent = relayed(my_y, dv_far, dv_got)
    dv_back = shifted(dv_sent, -4)
    v_sent = after(jnp.where(my_y == 0, v_own, v_far), dv_sent)
    v_near = flipped(v_sent)
    vals = [v_far, v_near, v_own]
    dv_chip = gathered_terms(my_y, dv_mine, dv_got, after(dv_back, v_sent))
    dv_fsdp = [dv_chip] + [rotated(dv_chip, s) for s in range(1, n_fsdp)]
    dv_over_y = [moved(dv_chip, 1, s) for s in range(n_fsdp)]
    for s in range(1, n_fsdp):
        own_pairs.append(jnp.concatenate([over_fsdp[s], after(relayed_y[s], dv_chip)], 1))
        other_pairs.append(swapped(own_pairs[s]))
    v_near = after(v_near, dv_chip)
    vals = [v_far, v_near, v_own]
    out, dq, other, dk_far, dk_near, dk_mine = run_grads(
        core_arg, e, inv, do_t, queries[0], q_other, keys, vals, chip_rows, half_kv
    )
    dk_back = [shifted(dk_near, -2), shifted(dk_far, -4)]

    dv_fsdp = [after(x, dk_near) for x in dv_fsdp]
    dv_over_y = [after(x, dk_near) for x in dv_over_y]
    dv_other = swapped(jnp.concatenate([rows_of(x, 1 - core, shard_rows) for x in dv_fsdp], 0))
    dv_rows = placed(
        core, jnp.concatenate([rows_of(x, core, shard_rows) for x in dv_fsdp], 0), dv_other, 1
    )
    dv_rows = after(dv_rows, *dv_over_y)
    if aligned:
        d_tokens, *made = run_tokens(fsdp_arg, dv_rows, w_value, n_fsdp)
    else:
        made = dot(dv_rows, w_value, NT).astype(BF16)
        made = [made[s * shard_rows : (s + 1) * shard_rows] for s in range(n_fsdp)]
        d_tokens = jnp.concatenate([made[0]] * n_fsdp, 1)
        made = made[1:]
    for s in range(1, n_fsdp):
        back = rotated(made[s - 1], -s)
        d_tokens = lax.dynamic_update_slice_in_dim(d_tokens, back, ((my_fsdp + s) % n_fsdp) * slab, 1)

    dv_pairs = list(zip(dv_fsdp, dv_over_y))
    if out_rows % 8 == 0:
        at = after(jnp.stack([core, my_z]).astype(jnp.int32), *made)
        by_z = run_weight(at, own_pairs, other_pairs, dv_pairs, n_z)
    else:
        weight_term = 0.0
        for p in range(n_fsdp):
            for flip in range(2):
                window = slice(flip * shard_rows, (flip + 1) * shard_rows)
                weight_term += dot(own_pairs[p][:, window], rows_of(dv_pairs[p][flip], core, shard_rows))
                weight_term += dot(other_pairs[p][:, window], rows_of(dv_pairs[p][flip], 1 - core, shard_rows))
        weight_term = weight_term.reshape(n_z, 2 * out_rows, half_kv)
        by_z = [
            lax.dynamic_index_in_dim(weight_term, (my_z + d) % n_z, 0, keepdims=False).astype(BF16 if d else F32)
            for d in range(n_z)
        ]
    by_z, dk_back = lax.optimization_barrier((list(by_z), dk_back))
    over_z = [
        lax.ppermute(by_z[d], "ctx", [(i, (i + 4 * d) % n_ctx) for i in range(n_ctx)]) for d in range(1, n_z)
    ]

    row_sum = by_z[0]
    for x in over_z:
        row_sum = row_sum + x.astype(F32)
    d_weight = placed(core, rows_of(row_sum, core, out_rows), swapped(rows_of(row_sum, 1 - core, out_rows)), 1)

    dk_chip = (dk_mine.astype(F32) + dk_back[0].astype(F32) + dk_back[1].astype(F32)).astype(BF16)
    d_keys = placed(core, rows_of(dk_chip, core, shard_rows), swapped(rows_of(dk_chip, 1 - core, shard_rows)), 1)
    other = swapped(after(other, *made))
    out = lax.dynamic_update_slice_in_dim(out, other[0], (1 - core) * half_q, 1)
    dq = lax.dynamic_update_slice_in_dim(dq, other[1], (1 - core) * half_q, 1)
    return (out[None], dq[None], d_keys[None], d_tokens[None], d_weight)


def solution(mesh):
    in_specs = (
        P("fsdp", "ctx", None),
        P("fsdp", "ctx", None),
        P("fsdp", "ctx", None),
        P("fsdp", None),
        P("fsdp", "ctx", None),
        P("fsdp", "ctx"),
    )
    out_specs = (
        P("fsdp", "ctx", None),
        P("fsdp", "ctx", None),
        P("fsdp", "ctx", None),
        P("fsdp", "ctx", None),
        P(("ctx", "fsdp"), None),
    )
    return jax.shard_map(shards, mesh=mesh, in_specs=in_specs, out_specs=out_specs, check_vma=False)
```
